32 devices in a mesh: heads: 2 (over core), seq: 16 (over z, y, x).
Axes of the slice: x: 2, y: 2, z: 4, core: 2. Of those that a mesh axis runs over, the one named last changes fastest.
Arguments:
- tokens: bfloat16 [16384, 768], P('seq'), may hold values from -6 to 6
- gain_attn: bfloat16 [768], replicated, may hold values from 0.5 to 1.5
- w_query: bfloat16 [768, 768], P(None, 'heads'), may hold values from -0.21875 to 0.21875
- w_key: bfloat16 [768, 768], P(None, 'heads'), may hold values from -0.21875 to 0.21875
- w_value: bfloat16 [768, 768], P(None, 'heads'), may hold values from -0.21875 to 0.21875
- w_out: bfloat16 [768, 768], P('heads'), may hold values from -1.25 to 1.25
- bias_table: bfloat16 [32, 12], P(None, 'heads'), may hold values from -4 to 4
- gain_ffn: bfloat16 [768], replicated, may hold values from 0.5 to 1.5
- w_router: bfloat16 [768, 16], replicated, may hold values from -0.21875 to 0.21875
- w_inner: bfloat16 [16, 768, 3072], P('seq', None, 'heads'), may hold values from -0.21875 to 0.21875
- w_outer: bfloat16 [16, 3072, 768], P('seq', 'heads'), may hold values from -6 to 6
- routes: int32 [16384, 1], P('seq'), may hold values from 0 to 15
- seq_lengths: int32 [80], P('seq'), may hold values from 64 to 512, as said below
- out_grad: bfloat16 [16384, 768], P('seq'), may hold values from -6 to 6
Outputs:
- out: bfloat16 [16384, 768], P('seq', 'heads')
- input_grad: float32 [16384, 768], P('seq')
- gain_attn_grad: float32 [768], replicated
- query_w_grad: float32 [768, 768], P(None, 'heads')
- key_w_grad: float32 [768, 768], P(None, 'heads')
- value_w_grad: float32 [768, 768], P(None, 'heads')
- out_w_grad: float32 [768, 768], P('heads')
- table_grad: float32 [32, 12], P(None, 'heads')
- gain_ffn_grad: float32 [768], replicated
- router_grad: float32 [768, 16], replicated
- inner_grad: float32 [16, 768, 3072], P('seq', None, 'heads')
- outer_grad: float32 [16, 3072, 768], P('seq', 'heads')
The draws below stay inside these ranges and needn't reach their ends.
Inputs may be any that keep to these rules, and one draw needn't show every extreme that they name: `seq_lengths`: sequence k of an index of seq: the first 4 come from the bucket of 128 slots and hold at least 64 tokens, the other 1 from the bucket of 512 slots and hold at least 256; on every index of seq one of them fills its bucket.
All inputs are finite; a program needn't handle non-finite values.
Results may differ from the reference program's by a relative error of at most 0.017.
Values may be sent and summed in bfloat16 or wider, within the bound.
No kernel may reach another device: no remote copies, remote signals or barrier semaphores. Data moves between devices by JAX's collectives and lax.ppermute only.
A program may use at most 128 MiB of HBM per device.

```python
import jax
import jax.numpy as jnp
from jax import lax

D = 768
HEADS = 12
HEAD_DIM = 64
FF = 3072
BUCKETS = 32
SHORT_LEN = 128
LONG_LEN = 512
SHORT_DEV = 4
LONG_DEV = 1
TOK_DEV = 1024
TOKENS = 16384
SEQS = 80
EXPERTS = 16
CAP = 80
N_SEQ = 16


def draw_seq_lengths(key, part):
    key = jax.random.fold_in(key, 11)
    first, second, third = jax.random.split(key, 3)
    per_device = SHORT_DEV + LONG_DEV
    devices = SEQS // per_device
    short_part = jax.random.randint(first, (devices, SHORT_DEV), SHORT_LEN // 2, SHORT_LEN + 1)
    long_part = jax.random.randint(second, (devices, LONG_DEV), LONG_LEN // 2, LONG_LEN + 1)
    drawn = jnp.concatenate([short_part, long_part], axis=1)
    full_sizes = jnp.concatenate([jnp.full((SHORT_DEV,), SHORT_LEN), jnp.full((LONG_DEV,), LONG_LEN)])
    chosen = jax.random.randint(third, (devices, 1), 0, per_device)
    places = jnp.arange(per_device)[None, :]
    return jnp.where(places == chosen, full_sizes[None, :], drawn).reshape(-1).astype(jnp.int32)


def levels(rng, shape, cuts, least, high):
    loudness = 1.0
    for position, shards_of in cuts:
        draws = jax.random.uniform(jax.random.fold_in(jax.random.fold_in(rng, 6), position), (shards_of,), jnp.float32, least / len(cuts), high / len(cuts))
        loudness = loudness * jnp.repeat(jnp.exp(draws), shape[position] // shards_of).reshape((-1,) + (1,) * (len(shape) - 1 - position))
    return loudness


def picks_of(stream_key, rows, count, top, lift):
    ranking = jax.random.permutation(jax.random.fold_in(stream_key, 1), count)
    boost = ranking
    for power in range(3):
        boost = boost * boost // count
    boost = boost * lift // count
    tickets = jax.random.randint(jax.random.fold_in(stream_key, 2), (rows, count), 0, 4096) + boost
    holders = jax.random.permutation(jax.random.fold_in(stream_key, 3), rows)[jnp.arange(count) % rows]
    tickets = jnp.where(jnp.arange(rows)[:, None] == holders[None, :], 1 << 14, tickets)
    merit = tickets * count + jnp.arange(count)
    return lax.top_k(merit.astype(jnp.int32), top)[1].astype(jnp.int32)


def scatter_about(own_key, dims, scale, most, cuts=(), kind=jnp.bfloat16):
    values = jax.random.normal(own_key, dims, jnp.float32) * scale
    if len(cuts) > 0:
        values = levels(own_key, dims, cuts, -0.22, 0.18) * values
    return jnp.clip(values, min=-most, max=most).astype(kind)


def setup_inputs(seed: int = 0) -> dict:
    streams_of = jax.random.split(jax.random.key(seed), 15)
    return {
        "tokens": scatter_about(streams_of[0], (TOKENS, D), 1.0, 6.0, ((0, 16),)),
        "gain_attn": jnp.clip(1.0 + 0.1 * jax.random.normal(streams_of[1], (D,), jnp.float32), 0.5, 1.5).astype(jnp.bfloat16),
        "w_query": scatter_about(streams_of[2], (D, HEADS * HEAD_DIM), D ** -0.5, 0.21875, ((1, 2),)),
        "w_key": scatter_about(streams_of[3], (D, HEADS * HEAD_DIM), D ** -0.5, 0.21875, ((1, 2),)),
        "w_value": scatter_about(streams_of[4], (D, HEADS * HEAD_DIM), D ** -0.5, 0.21875, ((1, 2),)),
        "w_out": scatter_about(streams_of[5], (HEADS * HEAD_DIM, D), (D // 32) ** -0.5, 1.25, ((0, 2),)),
        "bias_table": scatter_about(streams_of[6], (BUCKETS, HEADS), 1.0, 4.0, ((1, 2),)),
        "gain_ffn": jnp.clip(1.0 + 0.1 * jax.random.normal(streams_of[7], (D,), jnp.float32), 0.5, 1.5).astype(jnp.bfloat16),
        "w_router": scatter_about(streams_of[8], (D, EXPERTS), D ** -0.5, 0.21875),
        "w_inner": scatter_about(streams_of[9], (EXPERTS, D, FF), D ** -0.5, 0.21875, ((0, 16), (2, 2))),
        "w_outer": scatter_about(streams_of[10], (EXPERTS, FF, D), (1.5 * EXPERTS * FF ** -0.5), 6.0, ((0, 16), (1, 2))),
        "routes": picks_of(streams_of[11], TOKENS, EXPERTS, 1, 512),
        "seq_lengths": draw_seq_lengths(jax.random.fold_in(streams_of[14], 71), 0),
        "out_grad": scatter_about(streams_of[13], (TOKENS, D), 1.0, 6.0, ((0, 16),)),
    }


@jax.custom_vjp
def low(v):
    return lax.optimization_barrier(v.astype(jnp.bfloat16)).astype(jnp.float32)

@jax.custom_vjp
def low_back(v):
    return v

def low_keep(v):
    return (low(v), None)

def low_pass(kept, grad):
    return (grad,)

def back_keep(v):
    return (v, None)

def back_low(kept, grad):
    return (low(grad),)
low.defvjp(low_keep, low_pass)
low_back.defvjp(back_keep, back_low)
epsilon = 1e-06
highest = lax.Precision.HIGHEST
far_limits = (12, 16, 23, 32, 46, 64, 91)

def bucket_of(span):
    places = jnp.arange(span, dtype=jnp.int32)
    offset = places[None, :] - places[:, None]
    distance = jnp.abs(offset)
    far_bucket = jnp.full((span, span), 8, jnp.int32)
    for limit in far_limits:
        far_bucket = far_bucket + (distance >= limit).astype(jnp.int32)
    near_far = jnp.where(distance < 8, distance, far_bucket)
    return near_far + jnp.where(offset > 0, 16, 0).astype(jnp.int32)

def bucket_hot(span, count):
    return (bucket_of(span)[:, :, None] == jnp.arange(count, dtype=jnp.int32)[None, None, :]).astype(jnp.float32)

def rms_scale(values, gain):
    return values * lax.rsqrt(lax.optimization_barrier(jnp.mean(values * values, axis=-1, keepdims=True)) + epsilon) * gain

def softmax_rows(scores):
    top_value = lax.optimization_barrier(jnp.max(scores, axis=-1, keepdims=True))
    weights = jnp.exp(scores - top_value)
    return weights / lax.optimization_barrier(jnp.sum(weights, axis=-1, keepdims=True))

def attend(query_rows, key_rows, value_rows, lengths, bias):
    raw_scores = jnp.einsum('gihd,gjhd->ghij', query_rows, key_rows, precision=highest)
    places = jnp.arange(raw_scores.shape[-1], dtype=jnp.int32)
    live = places[None, None, None, :] < lengths[:, None, None, None]
    scores = low_back(jnp.where(live, raw_scores * HEAD_DIM ** (-0.5) + bias[None], -1000000000.0))
    probs = low(softmax_rows(scores))
    return jnp.einsum('ghij,gjhd->gihd', probs, value_rows, precision=highest)

def bucket_attention(query_rows, key_rows, value_rows, lengths, table, span, group):
    bias = jnp.einsum('ijb,bh->hij', bucket_hot(span, table.shape[0]), table, precision=highest)
    count = query_rows.shape[0] // group

    def one_block(parts):
        return attend(parts[0], parts[1], parts[2], parts[3], bias)

    def grouped(array):
        return array.reshape((count, group) + array.shape[1:])
    mixed = lax.map(jax.checkpoint(one_block), (grouped(query_rows), grouped(key_rows), grouped(value_rows), grouped(lengths)))
    return mixed.reshape(query_rows.shape)

def expert_rows(parts):
    rows, inner_w, outer_w = parts
    pre_act = low_back(jnp.dot(rows, inner_w, precision=highest))
    hidden = low(jax.nn.gelu(pre_act, approximate=True))
    return low_back(low(jnp.dot(hidden, outer_w, precision=highest)))

def owner_of(slot_index):
    return jnp.full((EXPERTS * CAP,), -1, jnp.int32).at[slot_index].set(jnp.arange(TOK_DEV, dtype=jnp.int32), mode='drop')

def pick_rows(rows, owner):
    return jnp.where(owner[:, None] >= 0, rows[jnp.maximum(owner, 0)], 0.0)

def take_rows(buffer, slot_index, kept):
    return jnp.where(kept[:, None], buffer[jnp.minimum(slot_index, EXPERTS * CAP - 1)], 0.0)

def reference(tokens, gain_attn, w_query, w_key, w_value, w_out, bias_table, gain_ffn, w_router, w_inner, w_outer, routes, seq_lengths, out_grad):
    route_dev = routes[:, 0].reshape(N_SEQ, TOK_DEV)
    hot_int = (route_dev[:, :, None] == jnp.arange(EXPERTS, dtype=jnp.int32)[None, None, :]).astype(jnp.int32)
    before = lax.optimization_barrier(jnp.sum(hot_int * (jnp.cumsum(hot_int, axis=1, dtype=jnp.int32) - 1), axis=-1, dtype=jnp.int32))
    kept = before < CAP
    slot_index = jnp.where(kept, route_dev * CAP + before, EXPERTS * CAP).astype(jnp.int32)
    owners = jax.vmap(owner_of)(slot_index)
    hits = hot_int.reshape(TOKENS, EXPERTS).astype(jnp.float32)
    lengths_dev = seq_lengths.reshape(N_SEQ, SHORT_DEV + LONG_DEV)
    short_lengths = lengths_dev[:, :SHORT_DEV].reshape(-1)
    long_lengths = lengths_dev[:, SHORT_DEV:].reshape(-1)
    short_tok = SHORT_DEV * SHORT_LEN

    def split_heads(rows):
        per_device = rows.reshape(N_SEQ, TOK_DEV, HEADS, HEAD_DIM)
        short_part = per_device[:, :short_tok].reshape(N_SEQ * SHORT_DEV, SHORT_LEN, HEADS, HEAD_DIM)
        long_part = per_device[:, short_tok:].reshape(N_SEQ * LONG_DEV, LONG_LEN, HEADS, HEAD_DIM)
        return (short_part, long_part)

    def layer(inputs, gain_one, query_w, key_w, value_w, out_w, table, gain_two, router_w, inner_w, outer_w):
        normed = low(rms_scale(inputs, gain_one))
        query_rows = split_heads(low_back(low(jnp.dot(normed, query_w, precision=highest))))
        key_rows = split_heads(low_back(low(jnp.dot(normed, key_w, precision=highest))))
        value_rows = split_heads(low_back(low(jnp.dot(normed, value_w, precision=highest))))
        short_out = bucket_attention(query_rows[0], key_rows[0], value_rows[0], short_lengths, table, SHORT_LEN, 4)
        long_out = bucket_attention(query_rows[1], key_rows[1], value_rows[1], long_lengths, table, LONG_LEN, 1)
        mixed = jnp.concatenate([short_out.reshape(N_SEQ, short_tok, HEADS * HEAD_DIM), long_out.reshape(N_SEQ, LONG_DEV * LONG_LEN, HEADS * HEAD_DIM)], axis=1)
        heads_out = low_back(low(mixed.reshape(TOKENS, HEADS * HEAD_DIM)))
        attn = low_back(jnp.dot(heads_out, out_w, precision=highest))
        residual = inputs + attn
        second = low(rms_scale(residual, gain_two))
        logits = low_back(jnp.dot(second, router_w, precision=highest))
        gate = lax.optimization_barrier(jnp.sum(softmax_rows(logits) * hits, axis=-1))
        sent = jax.vmap(pick_rows)(second.reshape(N_SEQ, TOK_DEV, D), owners)
        arrived = low_back(sent.reshape(N_SEQ, EXPERTS, CAP, D).transpose(1, 0, 2, 3).reshape(EXPERTS, N_SEQ * CAP, D))
        expert_out = lax.map(jax.checkpoint(expert_rows), (arrived, inner_w, outer_w))
        returned = expert_out.reshape(EXPERTS, N_SEQ, CAP, D).transpose(1, 0, 2, 3).reshape(N_SEQ, EXPERTS * CAP, D)
        token_out = jax.vmap(take_rows)(returned, slot_index, kept).reshape(TOKENS, D)
        return residual + gate[:, None] * token_out
    floats = (tokens, gain_attn, w_query, w_key, w_value, w_out, bias_table, gain_ffn, w_router, w_inner, w_outer)
    result, pullback = jax.vjp(layer, *[array.astype(jnp.float32) for array in floats])
    grads = pullback(out_grad.astype(jnp.float32))
    return (result.astype(jnp.bfloat16), grads[0], grads[1], grads[2], grads[3], grads[4], grads[5], grads[6], grads[7], grads[8], grads[9], grads[10])
```

```python
from functools import partial

import jax
import jax.numpy as jnp
from jax import lax
from jax.sharding import PartitionSpec as P

SHORT_LEN = 128
LONG_LEN = 512
SHORT_DEV = 4
LONG_DEV = 1


epsilon = 1e-06
highest = lax.Precision.HIGHEST
far_limits = (12, 16, 23, 32, 46, 64, 91)


def bucket_of(span):
    places = jnp.arange(span, dtype=jnp.int32)
    offset = places[None, :] - places[:, None]
    distance = jnp.abs(offset)
    far_bucket = jnp.full((span, span), 8, jnp.int32)
    for limit in far_limits:
        far_bucket = far_bucket + (distance >= limit).astype(jnp.int32)
    near_far = jnp.where(distance < 8, distance, far_bucket)
    return near_far + jnp.where(offset > 0, 16, 0).astype(jnp.int32)


def bucket_hot(span, count):
    return (
        bucket_of(span)[:, :, None] == jnp.arange(count, dtype=jnp.int32)[None, None, :]
    ).astype(jnp.float32)


def rms_scale(values, gain):
    return values * lax.rsqrt(jnp.mean(values * values, axis=-1, keepdims=True) + epsilon) * gain


def contract_rows(left, right):
    return lax.dot_general(
        left, right, (((0,), (0,)), ((), ())), preferred_element_type=jnp.float32
    )


def contract_cols(left, right):
    return lax.dot_general(
        left, right, (((1,), (1,)), ((), ())), preferred_element_type=jnp.float32
    )


def scores_of(query_rows, key_rows, lengths, bias, scale):
    raw_scores = jnp.einsum(
        "gihd,gjhd->ghij", query_rows, key_rows, preferred_element_type=jnp.float32
    )
    places = jnp.arange(raw_scores.shape[-1], dtype=jnp.int32)
    live = places[None, None, None, :] < lengths[:, None, None, None]
    return jnp.where(live, raw_scores * scale + bias[None], -1000000000.0)


def attend_forward(parts, bias, scale):
    query_rows, key_rows, value_rows, lengths = parts
    scores = scores_of(query_rows, key_rows, lengths, bias, scale)
    top_value = jnp.max(scores, axis=-1, keepdims=True)
    weights = jnp.exp(scores - top_value)
    total = jnp.sum(weights, axis=-1, keepdims=True)
    probs = (weights / total).astype(jnp.bfloat16)
    mixed = jnp.einsum("ghij,gjhd->gihd", probs, value_rows, preferred_element_type=jnp.float32)
    return (mixed.astype(jnp.bfloat16), (top_value + jnp.log(total))[..., 0])


def attend_backward(carry, parts, bias, scale):
    query_rows, key_rows, value_rows, lengths, mixed_grad, log_total = parts
    scores = scores_of(query_rows, key_rows, lengths, bias, scale)
    probs = jnp.exp(scores - log_total[..., None])
    value_grad = jnp.einsum(
        "ghij,gihd->gjhd",
        probs.astype(jnp.bfloat16),
        mixed_grad,
        preferred_element_type=jnp.float32,
    )
    prob_grad = jnp.einsum(
        "gihd,gjhd->ghij", mixed_grad, value_rows, preferred_element_type=jnp.float32
    )
    score_grad = probs * (prob_grad - jnp.sum(probs * prob_grad, axis=-1, keepdims=True))
    rounded = score_grad.astype(jnp.bfloat16)
    query_grad = (
        jnp.einsum("ghij,gjhd->gihd", rounded, key_rows, preferred_element_type=jnp.float32) * scale
    )
    key_grad = (
        jnp.einsum("ghij,gihd->gjhd", rounded, query_rows, preferred_element_type=jnp.float32)
        * scale
    )
    carry = carry + jnp.sum(rounded.astype(jnp.float32), axis=0)
    return (
        carry,
        (
            query_grad.astype(jnp.bfloat16),
            key_grad.astype(jnp.bfloat16),
            value_grad.astype(jnp.bfloat16),
        ),
    )


def table_part(score_total, hot_table):
    flat_hot = hot_table.reshape(-1, hot_table.shape[-1])
    flat_scores = score_total.reshape(score_total.shape[0], -1)
    return lax.dot_general(
        flat_hot,
        flat_scores,
        (((0,), (1,)), ((), ())),
        precision=highest,
        preferred_element_type=jnp.float32,
    )


def swap_heads(rows):
    return lax.ppermute(rows, "heads", [(0, 1), (1, 0)])


def bit_of(bit):
    return (lax.axis_index("seq") >> bit) & 1


def trade(rows, bit):
    count = lax.axis_size("seq")
    return lax.ppermute(rows, "seq", [(i, i ^ (1 << bit)) for i in range(count)])


def sum_scattered(rows, bits):
    for bit in bits:
        span = rows.shape[0] // 2
        mine = bit_of(bit)
        sent = lax.dynamic_slice_in_dim(rows, (1 - mine) * span, span, 0)
        kept = lax.dynamic_slice_in_dim(rows, mine * span, span, 0)
        got = trade(sent, bit)
        rows = (kept.astype(jnp.float32) + got.astype(jnp.float32)).astype(jnp.bfloat16)
    return rows


def gathered(rows, bits):
    for bit in reversed(bits):
        got = trade(rows, bit)
        upper = bit_of(bit) == 1
        rows = jnp.concatenate([jnp.where(upper, got, rows), jnp.where(upper, rows, got)], axis=0)
    return rows


def sum_everywhere(rows, bits):
    return gathered(sum_scattered(rows.astype(jnp.bfloat16), bits), bits).astype(jnp.float32)


def sum_small(rows, bits):
    for bit in bits:
        rows = rows + trade(rows, bit)
    return rows


def on_device(
    tokens,
    gain_attn,
    w_query,
    w_key,
    w_value,
    w_out,
    bias_table,
    gain_ffn,
    w_router,
    w_inner,
    w_outer,
    routes,
    seq_lengths,
    out_grad,
):
    tok_count, width = tokens.shape
    heads_local = bias_table.shape[1]
    bucket_count = bias_table.shape[0]
    head_size = w_query.shape[1] // heads_local
    experts = w_router.shape[1]
    capacity = max(2, 5 * tok_count // (4 * experts))
    senders = lax.axis_size("seq")
    bits = list(range(senders.bit_length() - 1))
    scale = head_size ** (-0.5)
    short_tok = SHORT_DEV * SHORT_LEN
    short_blocks = SHORT_DEV // 4
    slots = experts * capacity
    half = width // 2
    core = lax.axis_index("heads")
    own_start = core * half
    other_start = (1 - core) * half

    def own_half(rows):
        return lax.dynamic_slice_in_dim(rows, own_start, half, 1)

    def other_half(rows):
        return lax.dynamic_slice_in_dim(rows, other_start, half, 1)

    def both_halves(own):
        other = swap_heads(own)
        first = core == 0
        return jnp.concatenate([jnp.where(first, own, other), jnp.where(first, other, own)], axis=1)

    def summed_half(rows):
        got = swap_heads(other_half(rows).astype(jnp.bfloat16))
        return (own_half(rows) + got.astype(jnp.float32)).astype(jnp.bfloat16)

    def exchange(rows):
        return lax.all_to_all(
            rows.reshape(senders, capacity, half), "seq", split_axis=0, concat_axis=0, tiled=True
        ).reshape(slots, half)

    inputs = tokens.astype(jnp.float32)
    gain_one = gain_attn.astype(jnp.float32)
    gain_two = gain_ffn.astype(jnp.float32)
    incoming = out_grad.astype(jnp.float32)

    chosen = routes[:, 0]
    hot_tok = (chosen[:, None] == jnp.arange(experts, dtype=jnp.int32)[None, :]).astype(jnp.bfloat16)
    places = jnp.arange(tok_count, dtype=jnp.int32)
    earlier = (places[None, :] < places[:, None]).astype(jnp.bfloat16)
    before = jnp.sum(
        hot_tok.astype(jnp.float32)
        * jnp.dot(earlier, hot_tok, preferred_element_type=jnp.float32),
        axis=-1,
    ).astype(jnp.int32)
    slot_index = jnp.where(before < capacity, chosen * capacity + before, slots)
    slot_places = jnp.arange(slots, dtype=jnp.int32)
    to_slot = (slot_places[:, None] == slot_index[None, :]).astype(jnp.bfloat16)
    to_token = (slot_index[:, None] == slot_places[None, :]).astype(jnp.bfloat16)
    grad_half = exchange(
        jnp.dot(to_slot, own_half(out_grad), preferred_element_type=jnp.float32).astype(jnp.bfloat16)
    )

    normed = rms_scale(inputs, gain_one).astype(jnp.bfloat16)
    query_rows = jnp.dot(normed, w_query, preferred_element_type=jnp.float32).astype(jnp.bfloat16)
    key_rows = jnp.dot(normed, w_key, preferred_element_type=jnp.float32).astype(jnp.bfloat16)
    value_rows = jnp.dot(normed, w_value, preferred_element_type=jnp.float32).astype(jnp.bfloat16)

    def short_shape(rows):
        return rows[:short_tok].reshape(short_blocks, 4, SHORT_LEN, heads_local, head_size)

    def long_shape(rows):
        return rows[short_tok:].reshape(LONG_DEV, 1, LONG_LEN, heads_local, head_size)

    short_lengths = seq_lengths[:SHORT_DEV].reshape(short_blocks, 4)
    long_lengths = seq_lengths[SHORT_DEV:].reshape(LONG_DEV, 1)
    short_hot = bucket_hot(SHORT_LEN, bucket_count)
    long_hot = bucket_hot(LONG_LEN, bucket_count)
    short_bias = jnp.einsum(
        "ijb,bh->hij",
        short_hot.astype(jnp.bfloat16),
        bias_table,
        preferred_element_type=jnp.float32,
    )
    long_bias = jnp.einsum(
        "ijb,bh->hij", long_hot.astype(jnp.bfloat16), bias_table, preferred_element_type=jnp.float32
    )
    short_parts = (
        short_shape(query_rows),
        short_shape(key_rows),
        short_shape(value_rows),
        short_lengths,
    )
    long_parts = (
        long_shape(query_rows),
        long_shape(key_rows),
        long_shape(value_rows),
        long_lengths,
    )
    short_mixed, short_log = lax.map(
        partial(attend_forward, bias=short_bias, scale=scale), short_parts
    )
    long_mixed, long_log = lax.map(partial(attend_forward, bias=long_bias, scale=scale), long_parts)
    mixed = jnp.concatenate(
        [short_mixed.reshape(short_tok, -1), long_mixed.reshape(tok_count - short_tok, -1)], axis=0
    )
    attn_part = jnp.dot(mixed, w_out, preferred_element_type=jnp.float32)
    residual = inputs + (attn_part + swap_heads(attn_part))
    second = rms_scale(residual, gain_two).astype(jnp.bfloat16)
    arrived_half = exchange(
        jnp.dot(to_slot, own_half(second), preferred_element_type=jnp.float32).astype(jnp.bfloat16)
    )

    inner = w_inner[0]
    outer = w_outer[0]
    grad_arrived = both_halves(grad_half)
    hidden_grad = contract_cols(grad_arrived, outer)

    def gate_of(rows, hits):
        logits = jnp.dot(rows, w_router, preferred_element_type=jnp.float32)
        top_logit = jnp.max(logits, axis=-1, keepdims=True)
        exp_logit = jnp.exp(logits - top_logit)
        router_probs = exp_logit / jnp.sum(exp_logit, axis=-1, keepdims=True)
        return router_probs, jnp.sum(router_probs * hits, axis=-1, keepdims=True)

    arrived = both_halves(arrived_half)
    own_hit = (jnp.arange(experts, dtype=jnp.int32) == lax.axis_index("seq")).astype(jnp.float32)[None]
    router_probs, gate = gate_of(arrived, own_hit)
    expert_pre = jnp.dot(arrived, inner, preferred_element_type=jnp.float32)
    hidden_wide, gelu_back = jax.vjp(partial(jax.nn.gelu, approximate=True), expert_pre)
    expert_hidden = hidden_wide.astype(jnp.bfloat16)
    gate_grad = jnp.sum(expert_hidden.astype(jnp.float32) * hidden_grad, axis=-1, keepdims=True)
    logit_grad = (router_probs * (gate_grad * (own_hit - gate))).astype(jnp.bfloat16)
    pre_grad = gelu_back(gate * hidden_grad)[0].astype(jnp.bfloat16)
    row_part = contract_cols(pre_grad, inner) + contract_cols(logit_grad, w_router)
    grad_back = both_halves(exchange(summed_half(row_part)))

    expert_part = jnp.dot(expert_hidden, outer, preferred_element_type=jnp.float32)
    returned = exchange(summed_half(expert_part))
    router_part = contract_rows(logit_grad, arrived)
    outer_grad = contract_rows(
        expert_hidden, (gate * grad_arrived.astype(jnp.float32)).astype(jnp.bfloat16)
    )
    inner_grad = contract_rows(arrived, pre_grad)

    second_grad = jnp.dot(to_token, grad_back, preferred_element_type=jnp.float32)
    ffn_back = jax.vjp(rms_scale, residual, gain_two)[1]
    residual_grad, gain_two_grad = ffn_back(second_grad)
    residual_grad = residual_grad + incoming
    attn_grad = residual_grad.astype(jnp.bfloat16)
    out_w_grad = contract_rows(mixed, attn_grad)
    mixed_grad = contract_cols(attn_grad, w_out).astype(jnp.bfloat16)
    short_zero = jnp.zeros((heads_local, SHORT_LEN, SHORT_LEN), jnp.float32)
    long_zero = jnp.zeros((heads_local, LONG_LEN, LONG_LEN), jnp.float32)
    short_total, short_grads = lax.scan(
        partial(attend_backward, bias=short_bias, scale=scale),
        short_zero,
        short_parts + (short_shape(mixed_grad), short_log),
    )
    long_total, long_grads = lax.scan(
        partial(attend_backward, bias=long_bias, scale=scale),
        long_zero,
        long_parts + (long_shape(mixed_grad), long_log),
    )
    table_grad = table_part(short_total, short_hot) + table_part(long_total, long_hot)

    def joined(index):
        return jnp.concatenate(
            [
                short_grads[index].reshape(short_tok, -1),
                long_grads[index].reshape(tok_count - short_tok, -1),
            ],
            axis=0,
        )

    query_grad = joined(0)
    key_grad = joined(1)
    value_grad = joined(2)
    query_w_grad = contract_rows(normed, query_grad)
    key_w_grad = contract_rows(normed, key_grad)
    value_w_grad = contract_rows(normed, value_grad)
    gain_one_part = (
        jnp.sum(
            query_w_grad * w_query.astype(jnp.float32)
            + key_w_grad * w_key.astype(jnp.float32)
            + value_w_grad * w_value.astype(jnp.float32),
            axis=1,
        )
        / gain_one
    )

    turns = [bits[k:] + bits[:k] for k in range(3)]
    third = width // 3
    out_w_sum = jnp.concatenate(
        [
            sum_everywhere(out_w_grad[:, k * third : (k + 1) * third], turns[k])
            for k in range(3)
        ],
        axis=1,
    )
    query_w_sum = sum_everywhere(query_w_grad, turns[0])
    key_w_sum = sum_everywhere(key_w_grad, turns[1])
    value_w_sum = sum_everywhere(value_w_grad, turns[2])
    pair_part = jnp.concatenate([router_part, gain_one_part[None]], axis=0)
    pair_part = pair_part + swap_heads(pair_part)
    table_row = jnp.pad(table_grad.reshape(-1), (0, width - table_grad.size))
    small = sum_small(
        jnp.concatenate([pair_part, gain_two_grad[None], table_row[None]], axis=0), bits
    )

    normed_part = (
        contract_cols(query_grad, w_query)
        + contract_cols(key_grad, w_key)
        + contract_cols(value_grad, w_value)
    ).astype(jnp.bfloat16)
    normed_grad = normed_part.astype(jnp.float32) + swap_heads(normed_part).astype(jnp.float32)
    attn_back = jax.vjp(rms_scale, inputs, gain_one)[1]
    input_grad = residual_grad + attn_back(normed_grad)[0]

    token_hits = hot_tok.astype(jnp.float32)
    token_gate = gate_of(second, token_hits)[1]
    token_out = jnp.dot(to_token, returned, preferred_element_type=jnp.float32)
    output = (own_half(residual) + token_gate * token_out).astype(jnp.bfloat16)
    return (
        output,
        input_grad,
        small[experts],
        query_w_sum,
        key_w_sum,
        value_w_sum,
        out_w_sum,
        small[experts + 2, : table_grad.size].reshape(table_grad.shape),
        small[experts + 1],
        small[:experts].T,
        inner_grad[None],
        outer_grad[None],
    )


def solution(mesh):
    in_specs = (
        P("seq", None),
        P(),
        P(None, "heads"),
        P(None, "heads"),
        P(None, "heads"),
        P("heads", None),
        P(None, "heads"),
        P(),
        P(),
        P("seq", None, "heads"),
        P("seq", "heads", None),
        P("seq", None),
        P("seq"),
        P("seq", None),
    )
    out_specs = (
        P("seq", "heads"),
        P("seq", None),
        P(),
        P(None, "heads"),
        P(None, "heads"),
        P(None, "heads"),
        P("heads", None),
        P(None, "heads"),
        P(),
        P(),
        P("seq", None, "heads"),
        P("seq", "heads", None),
    )
    return jax.shard_map(
        on_device, mesh=mesh, in_specs=in_specs, out_specs=out_specs, check_vma=False
    )
```

```python
from functools import partial

import jax
import jax.numpy as jnp
from jax import lax
from jax.experimental import pallas as pl
from jax.experimental.pallas import tpu as pltpu
from jax.sharding import PartitionSpec as P

SHORT_LEN = 128
LONG_LEN = 512
SHORT_DEV = 4
LONG_DEV = 1


epsilon = 1e-06
highest = lax.Precision.HIGHEST
far_limits = (12, 16, 23, 32, 46, 64, 91)


def vmem(count):
    return [pl.BlockSpec(memory_space=pltpu.VMEM)] * count


def params(mib=48):
    return pltpu.CompilerParams(vmem_limit_bytes=mib * 1024 * 1024)


def dot_nn(left, right):
    return jnp.dot(left, right, preferred_element_type=jnp.float32)


def dot_nt(left, right):
    return lax.dot_general(
        left, right, (((1,), (1,)), ((), ())), preferred_element_type=jnp.float32
    )


def inverse_rms(values):
    return lax.rsqrt(jnp.mean(values * values, axis=-1, keepdims=True) + epsilon)


def diagonal_buckets(offset):
    distance = jnp.abs(offset)
    far_bucket = jnp.full(offset.shape, 8, jnp.int32)
    for limit in far_limits:
        far_bucket = far_bucket + (distance >= limit).astype(jnp.int32)
    return jnp.where(distance < 8, distance, far_bucket) + jnp.where(offset > 0, 16, 0)


def attend_kernel(
    lengths_ref,
    tokens_ref,
    gain_ref,
    wq_ref,
    wk_ref,
    wv_ref,
    wo_ref,
    table_ref,
    part_ref,
    normed_ref,
    q_ref,
    k_ref,
    v_ref,
    mixed_ref,
    long_ref,
    short_ref,
    diag_ref,
):
    tok_count, width = tokens_ref.shape
    pairs = wq_ref.shape[1] // 128
    short_tok = SHORT_DEV * SHORT_LEN
    tile = 256
    gain = gain_ref[...]
    for start in range(0, tok_count, tile):
        rows = slice(start, start + tile)
        values = tokens_ref[rows, :].astype(jnp.float32)
        normed = (values * inverse_rms(values) * gain).astype(jnp.bfloat16)
        normed_ref[rows, :] = normed
        q_ref[rows, :] = (
            dot_nn(normed, wq_ref[...]).astype(jnp.bfloat16) * jnp.bfloat16(0.125)
        )
        k_ref[rows, :] = dot_nn(normed, wk_ref[...]).astype(jnp.bfloat16)
        v_ref[rows, :] = dot_nn(normed, wv_ref[...]).astype(jnp.bfloat16)
    offset = lax.broadcasted_iota(jnp.int32, (table_ref.shape[1], 512), 1) - 256
    hot = (
        diagonal_buckets(offset)
        == lax.broadcasted_iota(jnp.int32, (table_ref.shape[1], 512), 0)
    ).astype(jnp.float32)
    diag_ref[...] = dot_nn(table_ref[...], hot.astype(jnp.bfloat16))
    lane = lax.broadcasted_iota(jnp.int32, (1, 128), 1)
    key_place = lax.broadcasted_iota(jnp.int32, (1, LONG_LEN), 1)
    live_long = key_place < lengths_ref[SHORT_DEV]

    def softmax(scores):
        weights = jnp.exp(scores - jnp.max(scores, axis=1, keepdims=True))
        return (weights * (1.0 / jnp.sum(weights, axis=1, keepdims=True))).astype(jnp.bfloat16)

    def one_pair(pair, carry):
        lanes = pl.ds(pl.multiple_of(pair * 128, 128), 128)
        tiles = []
        for sub in range(2):
            row = diag_ref[pl.ds(pair * 2 + sub, 1), :]
            spread = pltpu.roll(
                jnp.broadcast_to(row, (128, 512)), 256, 1, stride=1, stride_axis=0
            )
            tiles.append(
                (
                    spread[:, 0:128],
                    spread[:, 128:256],
                    spread[:, 384:512],
                    jnp.broadcast_to(row[:, 511:512], (128, 128)),
                    jnp.broadcast_to(row[:, 0:1], (128, 128)),
                )
            )
        for block in range(SHORT_DEV):
            rows = slice(block * 128, block * 128 + 128)
            queries = q_ref[rows, lanes]
            keys = k_ref[rows, lanes]
            values = v_ref[rows, lanes]
            live = key_place[:, :128] < lengths_ref[block]
            out = []
            for sub in range(2):
                masked = jnp.where((lane >= 64) == (sub == 1), queries, 0)
                scores = jnp.where(live, dot_nt(masked, keys) + tiles[sub][0], -1000000000.0)
                probs = softmax(scores)
                short_ref[pair * 2 + sub, rows, :] = probs
                out.append(dot_nn(probs, values))
            mixed_ref[rows, lanes] = jnp.where(lane < 64, out[0], out[1]).astype(jnp.bfloat16)
        keys = k_ref[short_tok:, lanes]
        values = v_ref[short_tok:, lanes]
        for block in range(LONG_LEN // 128):
            places = slice(block * 128, block * 128 + 128)
            rows = slice(short_tok + block * 128, short_tok + block * 128 + 128)
            queries = q_ref[rows, lanes]
            out = []
            for sub in range(2):
                masked = jnp.where((lane >= 64) == (sub == 1), queries, 0)
                same, above, below, far_above, far_below = tiles[sub]
                bias = jnp.concatenate(
                    [
                        same
                        if other == block
                        else above
                        if other == block + 1
                        else below
                        if other == block - 1
                        else far_above
                        if other > block
                        else far_below
                        for other in range(LONG_LEN // 128)
                    ],
                    axis=1,
                )
                scores = jnp.where(live_long, dot_nt(masked, keys) + bias, -1000000000.0)
                probs = softmax(scores)
                long_ref[pair * 2 + sub, places, :] = probs
                out.append(dot_nn(probs, values))
            mixed_ref[rows, lanes] = jnp.where(lane < 64, out[0], out[1]).astype(jnp.bfloat16)
        return carry

    lax.fori_loop(0, pairs, one_pair, 0)
    for start in range(0, tok_count, tile):
        rows = slice(start, start + tile)
        part_ref[rows, :] = dot_nn(mixed_ref[rows, :], wo_ref[...])


def attend(lengths, tokens, gain, w_query, w_key, w_value, w_out, table):
    tok_count, width = tokens.shape
    own = w_query.shape[1]
    heads = own // 64
    heads_pad = -(-heads // 8) * 8
    table = jnp.pad(table.T, ((0, heads_pad - heads), (0, 0)))
    short_tok = SHORT_DEV * SHORT_LEN
    flops = 2 * tok_count * width * own * 4 + 4 * heads * (512 * 512 + short_tok * 128) * 64
    return pl.pallas_call(
        attend_kernel,
        out_shape=[
            jax.ShapeDtypeStruct((tok_count, width), jnp.float32),
            jax.ShapeDtypeStruct((tok_count, width), jnp.bfloat16),
            jax.ShapeDtypeStruct((tok_count, own), jnp.bfloat16),
            jax.ShapeDtypeStruct((tok_count, own), jnp.bfloat16),
            jax.ShapeDtypeStruct((tok_count, own), jnp.bfloat16),
            jax.ShapeDtypeStruct((tok_count, own), jnp.bfloat16),
            jax.ShapeDtypeStruct((heads, LONG_LEN, LONG_LEN), jnp.bfloat16),
            jax.ShapeDtypeStruct((heads, short_tok, SHORT_LEN), jnp.bfloat16),
        ],
        in_specs=[pl.BlockSpec(memory_space=pltpu.SMEM)] + vmem(7),
        out_specs=vmem(8),
        scratch_shapes=[pltpu.VMEM((heads_pad, 512), jnp.float32)],
        compiler_params=params(),
        cost_estimate=pl.CostEstimate(
            flops=flops, bytes_accessed=16000000, transcendentals=heads * 512 * 640
        ),
        name="attend",
    )(lengths, tokens, gain.astype(jnp.float32)[None], w_query, w_key, w_value, w_out, table)


def attend_back_kernel(
    hg_ref,
    q_ref,
    k_ref,
    v_ref,
    mixed_ref,
    long_ref,
    short_ref,
    qg_ref,
    kg_ref,
    vg_ref,
    diag_ref,
    sg_ref,
):
    short_tok = SHORT_DEV * SHORT_LEN
    lane = lax.broadcasted_iota(jnp.int32, (1, 128), 1)

    def flip(rows):
        return jnp.transpose(rows.astype(jnp.float32)).astype(jnp.bfloat16)

    def unsheared(tile):
        row = lax.broadcasted_iota(jnp.int32, (128, 1), 0)
        for bit in range(7):
            moved = pltpu.roll(tile, tile.shape[1] - (1 << bit), 1)
            tile = jnp.where(((row >> bit) & 1) == 1, moved, tile)
        return tile

    def score_part(heads_rows, values, probs, mixed):
        delta = jnp.sum(heads_rows.astype(jnp.float32) * mixed.astype(jnp.float32), axis=1, keepdims=True)
        return probs.astype(jnp.float32) * (dot_nt(heads_rows, values) - delta)

    for sub in range(2):
        own = (lane >= 64) == (sub == 1)
        same = jnp.zeros((128, 128), jnp.float32)
        above = same
        below = same
        far_above = same
        far_below = same
        for block in range(SHORT_DEV):
            rows = slice(block * 128, block * 128 + 128)
            heads_rows = jnp.where(own, hg_ref[rows, :], 0)
            part = score_part(heads_rows, v_ref[rows, :], short_ref[sub, rows, :], mixed_ref[rows, :])
            same = same + part
            part = part.astype(jnp.bfloat16)
            lanes = slice(64 * sub, 64 * sub + 64)
            qg_ref[rows, lanes] = (dot_nn(part, k_ref[rows, :])[:, lanes] * 0.125).astype(jnp.bfloat16)
            kg_t = dot_nn(flip(q_ref[rows, :])[lanes, :], part)
            vg_t = dot_nn(flip(hg_ref[rows, :])[lanes, :], short_ref[sub, rows, :])
            both = jnp.transpose(jnp.concatenate([kg_t, vg_t], axis=0))
            kg_ref[rows, lanes] = both[:, :64].astype(jnp.bfloat16)
            vg_ref[rows, lanes] = both[:, 64:].astype(jnp.bfloat16)
        for block in range(LONG_LEN // 128):
            places = slice(block * 128, block * 128 + 128)
            rows = slice(short_tok + block * 128, short_tok + block * 128 + 128)
            heads_rows = jnp.where(own, hg_ref[rows, :], 0)
            part = score_part(heads_rows, v_ref[short_tok:, :], long_ref[sub, places, :], mixed_ref[rows, :])
            for other in range(LONG_LEN // 128):
                piece = part[:, other * 128 : other * 128 + 128]
                if other == block:
                    same = same + piece
                elif other == block + 1:
                    above = above + piece
                elif other == block - 1:
                    below = below + piece
                elif other > block:
                    far_above = far_above + piece
                else:
                    far_below = far_below + piece
            part = part.astype(jnp.bfloat16)
            sg_ref[places, :] = part
            lanes = slice(64 * sub, 64 * sub + 64)
            qg_ref[rows, lanes] = (dot_nn(part, k_ref[short_tok:, :])[:, lanes] * 0.125).astype(jnp.bfloat16)
        rows = slice(short_tok, short_tok + LONG_LEN)
        kg_t = dot_nn(flip(q_ref[rows, :])[lanes, :], sg_ref[...])
        vg_t = dot_nn(flip(hg_ref[rows, :])[lanes, :], long_ref[sub])
        both = jnp.transpose(jnp.concatenate([kg_t, vg_t], axis=0))
        kg_ref[rows, lanes] = both[:, :64].astype(jnp.bfloat16)
        vg_ref[rows, lanes] = both[:, 64:].astype(jnp.bfloat16)
        sheared = unsheared(
            jnp.concatenate([same, above, jnp.zeros((128, 128), jnp.float32), below], axis=1)
        )
        whole = jnp.concatenate([sheared, far_above, far_below], axis=1)
        diag_ref[0, sub : sub + 1, :] = jnp.sum(whole, axis=0, keepdims=True)


def attend_back(heads_grad, query_rows, key_rows, value_rows, mixed, long_probs, short_probs):
    tok_count, own = query_rows.shape
    pairs = own // 128
    short_tok = SHORT_DEV * SHORT_LEN
    rows_spec = pl.BlockSpec((tok_count, 128), lambda pair: (0, pair))
    flops = 10 * pairs * 2 * (512 * 512 + short_tok * 128) * 64
    qg, kg, vg, diag = pl.pallas_call(
        attend_back_kernel,
        grid=(pairs,),
        out_shape=[jax.ShapeDtypeStruct((tok_count, own), jnp.bfloat16)] * 3
        + [jax.ShapeDtypeStruct((pairs, 2, 768), jnp.float32)],
        in_specs=[rows_spec] * 5
        + [
            pl.BlockSpec((2, LONG_LEN, LONG_LEN), lambda pair: (pair, 0, 0)),
            pl.BlockSpec((2, short_tok, SHORT_LEN), lambda pair: (pair, 0, 0)),
        ],
        out_specs=[rows_spec] * 3 + [pl.BlockSpec((1, 2, 768), lambda pair: (pair, 0, 0))],
        scratch_shapes=[pltpu.VMEM((LONG_LEN, LONG_LEN), jnp.bfloat16)],
        compiler_params=params(),
        cost_estimate=pl.CostEstimate(flops=flops, bytes_accessed=12000000, transcendentals=0),
        name="attend_back",
    )(heads_grad, query_rows, key_rows, value_rows, mixed, long_probs, short_probs)
    return qg, kg, vg, diag.reshape(pairs * 2, 768)


def table_from(diag, bucket_count):
    lane = jnp.arange(768, dtype=jnp.int32)
    offset = jnp.where(lane < 256, lane, lane - 512)
    offset = jnp.where(lane >= 640, -256, jnp.where(lane >= 512, 256, offset))
    hot = (diagonal_buckets(offset)[:, None] == jnp.arange(bucket_count)[None, :]).astype(jnp.float32)
    return lax.dot_general(
        hot, diag, (((0,), (1,)), ((), ())), precision=highest, preferred_element_type=jnp.float32
    )


def dispatch_rows(send_ref, slot_row, half_rows):
    slots = send_ref.shape[0]
    tok_count = slot_row.shape[1]
    for base in range(0, slots, 256):
        span = min(256, slots - base)
        place = lax.broadcasted_iota(jnp.int32, (span, tok_count), 0) + base
        hot = jnp.where(place == slot_row, 1.0, 0.0).astype(jnp.bfloat16)
        send_ref[base : base + span, :] = dot_nn(hot, half_rows).astype(jnp.bfloat16)


def half_lanes(core, half):
    return pl.ds(pl.multiple_of(core * half, half), half)


def route_kernel(capacity, where_ref, routes_ref, grad_ref, row_ref, col_ref, send_ref):
    tok_count = routes_ref.shape[1]
    slots, half = send_ref.shape
    experts = slots // capacity
    routes = routes_ref[...]
    expert = lax.broadcasted_iota(jnp.int32, (experts, tok_count), 0)
    lane = lax.broadcasted_iota(jnp.int32, (1, tok_count), 1)
    hot = jnp.where(expert == routes, 1.0, 0.0)
    total = hot
    step = 1
    while step < tok_count:
        total = total + jnp.where(lane >= step, pltpu.roll(total, step, 1), 0.0)
        step *= 2
    before = jnp.sum(hot * total, axis=0, keepdims=True).astype(jnp.int32) - 1
    slot = jnp.where(before < capacity, routes * capacity + before, slots)
    row_ref[...] = slot
    wide = jnp.broadcast_to(slot.astype(jnp.float32), (128, tok_count))
    col_ref[...] = jnp.transpose(wide).astype(jnp.int32)
    dispatch_rows(send_ref, slot, grad_ref[:, half_lanes(where_ref[0], half)])


def route(where, routes, out_grad, experts, capacity):
    tok_count, width = out_grad.shape
    slots = experts * capacity
    return pl.pallas_call(
        partial(route_kernel, capacity),
        out_shape=[
            jax.ShapeDtypeStruct((1, tok_count), jnp.int32),
            jax.ShapeDtypeStruct((tok_count, 128), jnp.int32),
            jax.ShapeDtypeStruct((slots, width // 2), jnp.bfloat16),
        ],
        in_specs=[pl.BlockSpec(memory_space=pltpu.SMEM)] + vmem(2),
        out_specs=vmem(3),
        compiler_params=params(),
        cost_estimate=pl.CostEstimate(
            flops=slots * tok_count * width, bytes_accessed=4000000, transcendentals=0
        ),
        name="route",
    )(where, routes.reshape(1, tok_count), out_grad)


def second_kernel(
    where_ref, tokens_ref, own_ref, other_ref, gain_ref, row_ref, residual_ref, send_ref, second_ref
):
    step = pl.program_id(0)
    tile = tokens_ref.shape[0]
    half = send_ref.shape[1]
    residual = tokens_ref[...].astype(jnp.float32) + (own_ref[...] + other_ref[...])
    residual_ref[...] = residual
    second_ref[pl.ds(pl.multiple_of(step * tile, tile), tile), :] = (
        residual * inverse_rms(residual) * gain_ref[...]
    ).astype(jnp.bfloat16)

    @pl.when(step == pl.num_programs(0) - 1)
    def _():
        dispatch_rows(send_ref, row_ref[...], second_ref[:, half_lanes(where_ref[0], half)])


def second_rows(where, tokens, own, other, gain, slot_row, slots):
    tok_count, width = tokens.shape
    tile = 256
    rows = pl.BlockSpec((tile, width), lambda step: (step, 0))
    return pl.pallas_call(
        second_kernel,
        grid=(tok_count // tile,),
        out_shape=[
            jax.ShapeDtypeStruct((tok_count, width), jnp.float32),
            jax.ShapeDtypeStruct((slots, width // 2), jnp.bfloat16),
        ],
        in_specs=[
            pl.BlockSpec(memory_space=pltpu.SMEM),
            rows,
            rows,
            rows,
            pl.BlockSpec((1, width), lambda step: (0, 0)),
            pl.BlockSpec((1, tok_count), lambda step: (0, 0)),
        ],
        out_specs=[rows, pl.BlockSpec((slots, width // 2), lambda step: (0, 0))],
        scratch_shapes=[pltpu.VMEM((tok_count, width), jnp.bfloat16)],
        compiler_params=params(),
        cost_estimate=pl.CostEstimate(
            flops=slots * tok_count * width, bytes_accessed=13000000, transcendentals=0
        ),
        name="second",
    )(where, tokens, own, other, gain.astype(jnp.float32)[None], slot_row)


def hidden_grad_kernel(where_ref, own_ref, other_ref, outer_ref, out_ref):
    half = own_ref.shape[1]
    core = where_ref[0]
    out_ref[...] = dot_nt(own_ref[...], outer_ref[:, half_lanes(core, half)]) + dot_nt(
        other_ref[...], outer_ref[:, half_lanes(1 - core, half)]
    )


def hidden_grad_of(where, own, other, outer):
    slots, half = own.shape
    hidden = outer.shape[0]
    tile = 256
    rows = pl.BlockSpec((tile, half), lambda step: (step, 0))
    return pl.pallas_call(
        hidden_grad_kernel,
        grid=(slots // tile,),
        out_shape=jax.ShapeDtypeStruct((slots, hidden), jnp.float32),
        in_specs=[
            pl.BlockSpec(memory_space=pltpu.SMEM),
            rows,
            rows,
            pl.BlockSpec(outer.shape, lambda step: (0, 0)),
        ],
        out_specs=pl.BlockSpec((tile, hidden), lambda step: (step, 0)),
        compiler_params=params(),
        cost_estimate=pl.CostEstimate(
            flops=4 * slots * half * hidden, bytes_accessed=12000000, transcendentals=0
        ),
        name="hidden_grad",
    )(where, own, other, outer)


def expert_kernel(
    where_ref,
    own_ref,
    other_ref,
    grad_own_ref,
    grad_other_ref,
    hg_ref,
    inner_ref,
    router_ref,
    hidden_ref,
    pre_grad_ref,
    keep_ref,
    send_ref,
    arrived_ref,
    gated_ref,
    logit_ref,
):
    core = where_ref[0]
    half = own_ref.shape[1]
    experts = router_ref.shape[1]
    own_lanes = half_lanes(core, half)
    other_lanes = half_lanes(1 - core, half)
    own = own_ref[...]
    other = other_ref[...]
    arrived_ref[:, own_lanes] = own
    arrived_ref[:, other_lanes] = other
    logits = dot_nn(own, router_ref[own_lanes, :]) + dot_nn(other, router_ref[other_lanes, :])
    exp_logit = jnp.exp(logits - jnp.max(logits, axis=1, keepdims=True))
    probs = exp_logit * (1.0 / jnp.sum(exp_logit, axis=1, keepdims=True))
    hit = jnp.where(
        lax.broadcasted_iota(jnp.int32, (1, experts), 1) == where_ref[1], 1.0, 0.0
    )
    gate = jnp.sum(probs * hit, axis=1, keepdims=True)
    gated_ref[:, own_lanes] = (gate * grad_own_ref[...].astype(jnp.float32)).astype(jnp.bfloat16)
    gated_ref[:, other_lanes] = (gate * grad_other_ref[...].astype(jnp.float32)).astype(jnp.bfloat16)
    pre = dot_nn(own, inner_ref[own_lanes, :]) + dot_nn(other, inner_ref[other_lanes, :])
    hg = hg_ref[...]
    square = pre * pre
    curve = 0.7978845608028654
    bend = jnp.tanh(pre * (curve + (curve * 0.044715) * square))
    grown = 0.5 + 0.5 * bend
    hidden = (pre * grown).astype(jnp.bfloat16)
    hidden_ref[...] = hidden
    gate_grad = jnp.sum(hidden.astype(jnp.float32) * hg, axis=1, keepdims=True)
    slope = grown + (0.5 * pre) * (1.0 - bend * bend) * (curve + (3 * curve * 0.044715) * square)
    pre_grad = (slope * (gate * hg)).astype(jnp.bfloat16)
    pre_grad_ref[...] = pre_grad
    logit = (probs * (gate_grad * (hit - gate))).astype(jnp.bfloat16)
    logit_ref[...] = logit
    send_ref[...] = (
        dot_nt(pre_grad, inner_ref[other_lanes, :]) + dot_nt(logit, router_ref[other_lanes, :])
    ).astype(jnp.bfloat16)
    keep_ref[...] = dot_nt(pre_grad, inner_ref[own_lanes, :]) + dot_nt(
        logit, router_ref[own_lanes, :]
    )


def expert(where, own, other, grad_own, grad_other, hidden_grad, inner, router):
    slots, half = own.shape
    width, hidden = inner.shape
    experts = router.shape[1]
    tile = 256
    halves = pl.BlockSpec((tile, half), lambda step: (step, 0))
    wide = pl.BlockSpec((tile, width), lambda step: (step, 0))
    units = pl.BlockSpec((tile, hidden), lambda step: (step, 0))
    return pl.pallas_call(
        expert_kernel,
        grid=(slots // tile,),
        out_shape=[
            jax.ShapeDtypeStruct((slots, hidden), jnp.bfloat16),
            jax.ShapeDtypeStruct((slots, hidden), jnp.bfloat16),
            jax.ShapeDtypeStruct((slots, half), jnp.float32),
            jax.ShapeDtypeStruct((slots, half), jnp.bfloat16),
            jax.ShapeDtypeStruct((slots, width), jnp.bfloat16),
            jax.ShapeDtypeStruct((slots, width), jnp.bfloat16),
            jax.ShapeDtypeStruct((slots, experts), jnp.bfloat16),
        ],
        in_specs=[
            pl.BlockSpec(memory_space=pltpu.SMEM),
            halves,
            halves,
            halves,
            halves,
            units,
            pl.BlockSpec(inner.shape, lambda step: (0, 0)),
            pl.BlockSpec(router.shape, lambda step: (0, 0)),
        ],
        out_specs=[
            units,
            units,
            halves,
            halves,
            wide,
            wide,
            pl.BlockSpec((tile, experts), lambda step: (step, 0)),
        ],
        compiler_params=params(),
        cost_estimate=pl.CostEstimate(
            flops=4 * slots * width * hidden, bytes_accessed=30000000, transcendentals=slots * hidden
        ),
        name="expert",
    )(where, own, other, grad_own, grad_other, hidden_grad, inner, router)


def expert_out_kernel(where_ref, hidden_ref, outer_ref, keep_ref, send_ref):
    core = where_ref[0]
    half = keep_ref.shape[1]
    hidden = hidden_ref[...]
    send_ref[...] = dot_nn(hidden, outer_ref[:, half_lanes(1 - core, half)]).astype(jnp.bfloat16)
    keep_ref[...] = dot_nn(hidden, outer_ref[:, half_lanes(core, half)])


def expert_out_of(where, hidden, outer):
    slots, units = hidden.shape
    half = outer.shape[1] // 2
    tile = 256
    halves = pl.BlockSpec((tile, half), lambda step: (step, 0))
    return pl.pallas_call(
        expert_out_kernel,
        grid=(slots // tile,),
        out_shape=[
            jax.ShapeDtypeStruct((slots, half), jnp.float32),
            jax.ShapeDtypeStruct((slots, half), jnp.bfloat16),
        ],
        in_specs=[
            pl.BlockSpec(memory_space=pltpu.SMEM),
            pl.BlockSpec((tile, units), lambda step: (step, 0)),
            pl.BlockSpec(outer.shape, lambda step: (0, 0)),
        ],
        out_specs=[halves, halves],
        compiler_params=params(),
        cost_estimate=pl.CostEstimate(
            flops=4 * slots * half * units, bytes_accessed=9000000, transcendentals=0
        ),
        name="expert_out",
    )(where, hidden, outer)


def residual_back_kernel(
    where_ref,
    col_ref,
    own_ref,
    other_ref,
    residual_ref,
    grad_ref,
    gain_ref,
    wo_ref,
    out_ref,
    attn_ref,
    heads_ref,
    gain_out_ref,
    whole_ref,
):
    core = where_ref[0]
    slots, half = own_ref.shape
    tile = residual_ref.shape[0]
    place = lax.broadcasted_iota(jnp.int32, (tile, slots), 1)
    hot = jnp.where(place == col_ref[:, :1], 1.0, 0.0).astype(jnp.bfloat16)
    whole_ref[:, half_lanes(core, half)] = dot_nn(hot, own_ref[...])
    whole_ref[:, half_lanes(1 - core, half)] = dot_nn(hot, other_ref[...])
    ybar = whole_ref[...]
    values = residual_ref[...]
    scale = inverse_rms(values)
    scaled = values * scale
    pulled = ybar * gain_ref[...]

    @pl.when(pl.program_id(0) == 0)
    def _():
        gain_out_ref[...] = jnp.zeros_like(gain_out_ref)

    gain_out_ref[...] += jnp.sum(ybar * scaled, axis=0, keepdims=True)
    back = scale * (pulled - scaled * jnp.mean(pulled * scaled, axis=1, keepdims=True))
    out = back + grad_ref[...].astype(jnp.float32)
    out_ref[...] = out
    attn = out.astype(jnp.bfloat16)
    attn_ref[...] = attn
    heads_ref[...] = dot_nt(attn, wo_ref[...]).astype(jnp.bfloat16)


def residual_back(where, slot_col, own, other, residual, out_grad, gain, w_out):
    tok_count, width = residual.shape
    slots, half = own.shape
    heads_width = w_out.shape[0]
    tile = 256
    rows = pl.BlockSpec((tile, width), lambda step: (step, 0))
    whole = lambda shape: pl.BlockSpec(shape, lambda step: (0, 0))
    return pl.pallas_call(
        residual_back_kernel,
        grid=(tok_count // tile,),
        out_shape=[
            jax.ShapeDtypeStruct((tok_count, width), jnp.float32),
            jax.ShapeDtypeStruct((tok_count, width), jnp.bfloat16),
            jax.ShapeDtypeStruct((tok_count, heads_width), jnp.bfloat16),
            jax.ShapeDtypeStruct((1, width), jnp.float32),
        ],
        in_specs=[
            pl.BlockSpec(memory_space=pltpu.SMEM),
            pl.BlockSpec((tile, 128), lambda step: (step, 0)),
            whole(own.shape),
            whole(other.shape),
            rows,
            rows,
            whole((1, width)),
            whole(w_out.shape),
        ],
        out_specs=[
            rows,
            rows,
            pl.BlockSpec((tile, heads_width), lambda step: (step, 0)),
            whole((1, width)),
        ],
        scratch_shapes=[pltpu.VMEM((tile, width), jnp.float32)],
        compiler_params=params(),
        cost_estimate=pl.CostEstimate(
            flops=tok_count * width * (2 * slots + 2 * heads_width),
            bytes_accessed=14000000,
            transcendentals=0,
        ),
        name="residual_back",
    )(where, slot_col, own, other, residual, out_grad, gain.astype(jnp.float32)[None], w_out)


def output_kernel(
    capacity, where_ref, col_ref, returned_ref, residual_ref, gain_ref, router_ref, out_ref
):
    slots, half = returned_ref.shape
    tile = residual_ref.shape[0]
    experts = router_ref.shape[1]
    col = col_ref[:, :1]
    place = lax.broadcasted_iota(jnp.int32, (tile, slots), 1)
    hot = jnp.where(place == col, 1.0, 0.0).astype(jnp.bfloat16)
    token_out = dot_nn(hot, returned_ref[...])
    residual = residual_ref[...]
    second = (residual * inverse_rms(residual) * gain_ref[...]).astype(jnp.bfloat16)
    logits = dot_nn(second, router_ref[...])
    exp_logit = jnp.exp(logits - jnp.max(logits, axis=1, keepdims=True))
    first = lax.broadcasted_iota(jnp.int32, (1, experts), 1) * capacity
    hit = jnp.where((col >= first) & (col < first + capacity), exp_logit, 0.0)
    gate = jnp.sum(hit, axis=1, keepdims=True) / jnp.sum(exp_logit, axis=1, keepdims=True)
    own = residual_ref[:, half_lanes(where_ref[0], half)]
    out_ref[...] = (own + gate * token_out).astype(jnp.bfloat16)


def output_of(where, slot_col, returned, residual, gain, router, capacity):
    tok_count, width = residual.shape
    slots, half = returned.shape
    tile = 256
    whole = lambda shape: pl.BlockSpec(shape, lambda step: (0, 0))
    return pl.pallas_call(
        partial(output_kernel, capacity),
        grid=(tok_count // tile,),
        out_shape=jax.ShapeDtypeStruct((tok_count, half), jnp.bfloat16),
        in_specs=[
            pl.BlockSpec(memory_space=pltpu.SMEM),
            pl.BlockSpec((tile, 128), lambda step: (step, 0)),
            whole(returned.shape),
            pl.BlockSpec((tile, width), lambda step: (step, 0)),
            whole((1, width)),
            whole(router.shape),
        ],
        out_specs=pl.BlockSpec((tile, half), lambda step: (step, 0)),
        compiler_params=params(),
        cost_estimate=pl.CostEstimate(
            flops=2 * tok_count * half * slots, bytes_accessed=6000000, transcendentals=0
        ),
        name="output",
    )(where, slot_col, returned, residual, gain.astype(jnp.float32)[None], router)


def input_back_kernel(tokens_ref, own_ref, other_ref, gain_ref, residual_ref, out_ref):
    ybar = own_ref[...].astype(jnp.float32) + other_ref[...].astype(jnp.float32)
    values = tokens_ref[...].astype(jnp.float32)
    scale = inverse_rms(values)
    scaled = values * scale
    pulled = ybar * gain_ref[...]
    out_ref[...] = residual_ref[...] + scale * (
        pulled - scaled * jnp.mean(pulled * scaled, axis=1, keepdims=True)
    )


def input_back(tokens, own, other, gain, residual_grad):
    tok_count, width = tokens.shape
    tile = 256
    rows = pl.BlockSpec((tile, width), lambda step: (step, 0))
    return pl.pallas_call(
        input_back_kernel,
        grid=(tok_count // tile,),
        out_shape=jax.ShapeDtypeStruct((tok_count, width), jnp.float32),
        in_specs=[rows, rows, rows, pl.BlockSpec((1, width), lambda step: (0, 0)), rows],
        out_specs=rows,
        compiler_params=params(),
        cost_estimate=pl.CostEstimate(
            flops=10 * tok_count * width, bytes_accessed=11000000, transcendentals=0
        ),
        name="input_back",
    )(tokens, own, other, gain.astype(jnp.float32)[None], residual_grad)


def weights_kernel(
    normed_ref, qg_ref, kg_ref, vg_ref, mixed_ref, attn_ref, wq_ref, wk_ref, wv_ref, gain_ref,
    stack_ref, gain_out_ref,
):
    width = normed_ref.shape[1]
    own = mixed_ref.shape[1]
    tile = 256
    for start in range(0, width, tile):
        rows = slice(start, start + tile)
        normed = normed_ref[:, rows]
        total = jnp.zeros((tile, 1), jnp.float32)
        for index, (grad_ref, w_ref) in enumerate(((qg_ref, wq_ref), (kg_ref, wk_ref), (vg_ref, wv_ref))):
            grad = contract_rows(normed, grad_ref[...])
            total = total + jnp.sum(grad * w_ref[rows, :].astype(jnp.float32), axis=1, keepdims=True)
            stack_ref[index * width + start : index * width + start + tile, :] = grad.astype(jnp.bfloat16)
        gain_out_ref[:, rows] = jnp.transpose(jnp.broadcast_to(total, (tile, 128)))[:8, :]
    gain_out_ref[...] = gain_out_ref[...] / gain_ref[...]
    for start in range(0, own, 128):
        grad = contract_rows(mixed_ref[:, start : start + 128], attn_ref[...]).astype(jnp.bfloat16)
        for part in range(width // own):
            base = 3 * width + part * own + start
            stack_ref[base : base + 128, :] = grad[:, part * own : part * own + own]


def weight_grads(normed, qg, kg, vg, mixed, attn_grad, w_query, w_key, w_value, gain):
    tok_count, width = normed.shape
    own = qg.shape[1]
    return pl.pallas_call(
        weights_kernel,
        out_shape=[
            jax.ShapeDtypeStruct((4 * width, own), jnp.bfloat16),
            jax.ShapeDtypeStruct((8, width), jnp.float32),
        ],
        in_specs=vmem(10),
        out_specs=vmem(2),
        compiler_params=params(),
        cost_estimate=pl.CostEstimate(
            flops=8 * tok_count * width * own, bytes_accessed=12000000, transcendentals=0
        ),
        name="weight_grads",
    )(normed, qg, kg, vg, mixed, attn_grad, w_query, w_key, w_value, gain.astype(jnp.float32)[None])


def split_kernel(count, bits_ref, *refs):
    for part in range(count):
        whole = refs[part]
        span = whole.shape[0] // 2
        mine = bits_ref[part]
        refs[count + part][...] = whole[pl.ds((1 - mine) * span, span)]
        refs[2 * count + part][...] = whole[pl.ds(mine * span, span)]


def split(bits, parts):
    count = len(parts)
    halves = [jax.ShapeDtypeStruct((p.shape[0] // 2,) + p.shape[1:], p.dtype) for p in parts]
    out = pl.pallas_call(
        partial(split_kernel, count),
        out_shape=halves + halves,
        in_specs=[pl.BlockSpec(memory_space=pltpu.SMEM)] + vmem(count),
        out_specs=vmem(2 * count),
        compiler_params=params(),
        name="split",
    )(bits, *parts)
    return out[:count], out[count:]


def fold_kernel(count, bits_ref, *refs):
    kept, got, sent, keep = (refs[count * k : count * (k + 1)] for k in range(4))
    for part in range(count):
        span = kept[part].shape[0] // 2
        mine = bits_ref[part]
        for ref, start in ((sent[part], (1 - mine) * span), (keep[part], mine * span)):
            rows = pl.ds(start, span)
            ref[...] = (
                kept[part][rows].astype(jnp.float32) + got[part][rows].astype(jnp.float32)
            ).astype(jnp.bfloat16)


def fold(bits, kept, got):
    count = len(kept)
    halves = [jax.ShapeDtypeStruct((p.shape[0] // 2,) + p.shape[1:], p.dtype) for p in kept]
    out = pl.pallas_call(
        partial(fold_kernel, count),
        out_shape=halves + halves,
        in_specs=[pl.BlockSpec(memory_space=pltpu.SMEM)] + vmem(2 * count),
        out_specs=vmem(2 * count),
        compiler_params=params(),
        name="fold",
    )(bits, *kept, *got)
    return out[:count], out[count:]


def join_kernel(count, bits_ref, *refs):
    own, got, out = (refs[count * k : count * (k + 1)] for k in range(3))
    for part in range(count):
        span = own[part].shape[0]
        mine = bits_ref[part]
        out[part][pl.ds(mine * span, span)] = own[part][...]
        out[part][pl.ds((1 - mine) * span, span)] = got[part][...]


def join(bits, own, got):
    count = len(own)
    return pl.pallas_call(
        partial(join_kernel, count),
        out_shape=[jax.ShapeDtypeStruct((p.shape[0] * 2,) + p.shape[1:], p.dtype) for p in own],
        in_specs=[pl.BlockSpec(memory_space=pltpu.SMEM)] + vmem(2 * count),
        out_specs=vmem(count),
        compiler_params=params(),
        name="join",
    )(bits, *own, *got)


def swap_heads(rows):
    return lax.ppermute(rows, "heads", [(0, 1), (1, 0)])


def trade(rows, bit):
    count = lax.axis_size("seq")
    return lax.ppermute(rows, "seq", [(i, i ^ (1 << bit)) for i in range(count)])


def sum_over_seq(parts, turns, small):
    place = lax.axis_index("seq")
    depth = len(turns[0])
    bits = [jnp.stack([(place >> turn[k]) & 1 for turn in turns]).astype(jnp.int32) for k in range(depth)]
    sent, kept = split(bits[0], parts)
    for k in range(depth):
        got = [trade(rows, turn[k]) for rows, turn in zip(sent, turns)]
        small = small + trade(small, turns[0][k])
        if k + 1 < depth:
            sent, kept = fold(bits[k + 1], kept, got)
    rows = [
        (own.astype(jnp.float32) + other.astype(jnp.float32)).astype(jnp.bfloat16)
        for own, other in zip(kept, got)
    ]
    for k in reversed(range(depth)):
        got = [trade(own, turn[k]) for own, turn in zip(rows, turns)]
        rows = join(bits[k], rows, got)
    return rows, small


def contract_rows(left, right):
    return lax.dot_general(
        left, right, (((0,), (0,)), ((), ())), preferred_element_type=jnp.float32
    )


def contract_cols(left, right):
    return lax.dot_general(
        left, right, (((1,), (1,)), ((), ())), preferred_element_type=jnp.float32
    )


def on_device(
    tokens,
    gain_attn,
    w_query,
    w_key,
    w_value,
    w_out,
    bias_table,
    gain_ffn,
    w_router,
    w_inner,
    w_outer,
    routes,
    seq_lengths,
    out_grad,
):
    tok_count, width = tokens.shape
    bucket_count = bias_table.shape[0]
    experts = w_router.shape[1]
    capacity = max(2, 5 * tok_count // (4 * experts))
    senders = lax.axis_size("seq")
    bits = list(range(senders.bit_length() - 1))
    slots = experts * capacity
    half = width // 2
    own = w_query.shape[1]
    where = jnp.stack([lax.axis_index("heads"), lax.axis_index("seq")]).astype(jnp.int32)

    def exchange(rows):
        return lax.all_to_all(
            rows.reshape(senders, capacity, half), "seq", split_axis=0, concat_axis=0, tiled=True
        ).reshape(slots, half)

    def summed(keep, send):
        return (keep + swap_heads(send).astype(jnp.float32)).astype(jnp.bfloat16)

    slot_row, slot_col, grad_sent = route(where, routes, out_grad, experts, capacity)
    grad_sent, tokens = lax.optimization_barrier((grad_sent, tokens))
    grad_own = exchange(grad_sent)
    attn_part, normed, query_rows, key_rows, value_rows, mixed, long_probs, short_probs = attend(
        seq_lengths, tokens, gain_attn, w_query, w_key, w_value, w_out, bias_table
    )
    attn_part, grad_own = lax.optimization_barrier((attn_part, grad_own))
    residual, second_sent = second_rows(
        where, tokens, attn_part, swap_heads(attn_part), gain_ffn, slot_row, slots
    )
    arrived_own = exchange(second_sent)

    inner = w_inner[0]
    outer = w_outer[0]
    grad_other = swap_heads(grad_own)
    hidden_grad = hidden_grad_of(where, grad_own, grad_other, outer)
    arrived_own, hidden_grad = lax.optimization_barrier((arrived_own, hidden_grad))
    arrived_other = swap_heads(arrived_own)
    hidden, pre_grad, keep, send, arrived, gated, logit_grad = expert(
        where, arrived_own, arrived_other, grad_own, grad_other, hidden_grad, inner, w_router
    )
    back_own = exchange(summed(keep, send))

    out_keep, out_send = expert_out_of(where, hidden, outer)
    out_sum = summed(out_keep, out_send)
    router_part = contract_rows(logit_grad, arrived)
    outer_grad = contract_rows(hidden, gated)
    inner_grad = contract_rows(arrived, pre_grad)
    back_own, out_sum, router_part, outer_grad, inner_grad = lax.optimization_barrier(
        (back_own, out_sum, router_part, outer_grad, inner_grad)
    )
    returned = exchange(out_sum)

    residual_grad, attn_grad, heads_grad, gain_two_part = residual_back(
        where, slot_col, back_own, swap_heads(back_own), residual, out_grad, gain_ffn, w_out
    )
    query_grad, key_grad, value_grad, diag = attend_back(
        heads_grad, query_rows, key_rows, value_rows, mixed, long_probs, short_probs
    )
    table_grad = table_from(diag, bucket_count)
    stack, gain_one_part = weight_grads(
        normed, query_grad, key_grad, value_grad, mixed, attn_grad, w_query, w_key, w_value, gain_attn
    )

    turns = [bits[k:] + bits[:k] for k in range(3)]
    rows = stack.shape[0] // 3
    parts = [
        stack[k * rows : (k + 1) * rows].reshape(senders, rows // senders, own) for k in range(3)
    ]
    pair_part = jnp.concatenate([router_part, gain_one_part[:1]], axis=0)
    pair_part = pair_part + swap_heads(pair_part)
    table_row = jnp.pad(table_grad.reshape(1, -1), ((0, 0), (0, width - table_grad.size)))
    small = jnp.concatenate([pair_part, gain_two_part, table_row], axis=0)
    parts, small = sum_over_seq(parts, turns, small)
    total = jnp.concatenate([part.reshape(rows, own) for part in parts], axis=0).astype(jnp.float32)

    normed_part = (
        contract_cols(query_grad, w_query)
        + contract_cols(key_grad, w_key)
        + contract_cols(value_grad, w_value)
    ).astype(jnp.bfloat16)
    input_grad = input_back(tokens, normed_part, swap_heads(normed_part), gain_attn, residual_grad)
    output = output_of(where, slot_col, returned, residual, gain_ffn, w_router, capacity)
    return (
        output,
        input_grad,
        small[experts],
        total[:width],
        total[width : 2 * width],
        total[2 * width : 3 * width],
        jnp.concatenate(
            [total[3 * width + k * own : 3 * width + (k + 1) * own] for k in range(width // own)], axis=1
        ),
        small[experts + 2, : table_grad.size].reshape(table_grad.shape),
        small[experts + 1],
        small[:experts].T,
        inner_grad[None],
        outer_grad[None],
    )


def solution(mesh):
    in_specs = (
        P("seq", None),
        P(),
        P(None, "heads"),
        P(None, "heads"),
        P(None, "heads"),
        P("heads", None),
        P(None, "heads"),
        P(),
        P(),
        P("seq", None, "heads"),
        P("seq", "heads", None),
        P("seq", None),
        P("seq"),
        P("seq", None),
    )
    out_specs = (
        P("seq", "heads"),
        P("seq", None),
        P(),
        P(None, "heads"),
        P(None, "heads"),
        P(None, "heads"),
        P("heads", None),
        P(None, "heads"),
        P(),
        P(),
        P("seq", None, "heads"),
        P("seq", "heads", None),
    )
    return jax.shard_map(
        on_device, mesh=mesh, in_specs=in_specs, out_specs=out_specs, check_vma=False
    )
```

```python
from functools import partial

import jax
import jax.numpy as jnp
from jax import lax
from jax.experimental import pallas as pl
from jax.experimental.pallas import tpu as pltpu
from jax.sharding import PartitionSpec as P

SHORT_LEN = 128
LONG_LEN = 512
SHORT_DEV = 4
LONG_DEV = 1


epsilon = 1e-06
highest = lax.Precision.HIGHEST
far_limits = (12, 16, 23, 32, 46, 64, 91)


def vmem(count):
    return [pl.BlockSpec(memory_space=pltpu.VMEM)] * count


def params(mib=48):
    return pltpu.CompilerParams(vmem_limit_bytes=mib * 1024 * 1024)


def dot_nn(left, right):
    return jnp.dot(left, right, preferred_element_type=jnp.float32)


def dot_nt(left, right):
    return lax.dot_general(
        left, right, (((1,), (1,)), ((), ())), preferred_element_type=jnp.float32
    )


def inverse_rms(values):
    return lax.rsqrt(jnp.mean(values * values, axis=-1, keepdims=True) + epsilon)


def diagonal_buckets(offset):
    distance = jnp.abs(offset)
    far_bucket = jnp.full(offset.shape, 8, jnp.int32)
    for limit in far_limits:
        far_bucket = far_bucket + (distance >= limit).astype(jnp.int32)
    return jnp.where(distance < 8, distance, far_bucket) + jnp.where(offset > 0, 16, 0)


def attend_kernel(
    lengths_ref,
    tokens_ref,
    gain_ref,
    wq_ref,
    wk_ref,
    wv_ref,
    wo_ref,
    table_ref,
    part_ref,
    normed_ref,
    q_ref,
    k_ref,
    v_ref,
    mixed_ref,
    long_ref,
    short_ref,
    diag_ref,
):
    tok_count, width = tokens_ref.shape
    pairs = wq_ref.shape[1] // 128
    short_tok = SHORT_DEV * SHORT_LEN
    tile = 256
    gain = gain_ref[...]
    for start in range(0, tok_count, tile):
        rows = slice(start, start + tile)
        values = tokens_ref[rows, :].astype(jnp.float32)
        normed = (values * inverse_rms(values) * gain).astype(jnp.bfloat16)
        normed_ref[rows, :] = normed
        q_ref[rows, :] = (
            dot_nn(normed, wq_ref[...]).astype(jnp.bfloat16) * jnp.bfloat16(0.125)
        )
        k_ref[rows, :] = dot_nn(normed, wk_ref[...]).astype(jnp.bfloat16)
        v_ref[rows, :] = dot_nn(normed, wv_ref[...]).astype(jnp.bfloat16)
    offset = lax.broadcasted_iota(jnp.int32, (table_ref.shape[1], 512), 1) - 256
    hot = (
        diagonal_buckets(offset)
        == lax.broadcasted_iota(jnp.int32, (table_ref.shape[1], 512), 0)
    ).astype(jnp.float32)
    diag_ref[...] = dot_nn(table_ref[...], hot.astype(jnp.bfloat16))
    lane = lax.broadcasted_iota(jnp.int32, (1, 128), 1)
    key_place = lax.broadcasted_iota(jnp.int32, (1, LONG_LEN), 1)
    live_long = key_place < lengths_ref[SHORT_DEV]

    def softmax(scores):
        weights = jnp.exp(scores - jnp.max(scores, axis=1, keepdims=True))
        return (weights * (1.0 / jnp.sum(weights, axis=1, keepdims=True))).astype(jnp.bfloat16)

    def one_pair(pair, carry):
        lanes = pl.ds(pl.multiple_of(pair * 128, 128), 128)
        tiles = []
        for sub in range(2):
            row = diag_ref[pl.ds(pair * 2 + sub, 1), :]
            spread = pltpu.roll(
                jnp.broadcast_to(row, (128, 512)), 256, 1, stride=1, stride_axis=0
            )
            tiles.append(
                (
                    spread[:, 0:128],
                    spread[:, 128:256],
                    spread[:, 384:512],
                    jnp.broadcast_to(row[:, 511:512], (128, 128)),
                    jnp.broadcast_to(row[:, 0:1], (128, 128)),
                )
            )
        for block in range(SHORT_DEV):
            rows = slice(block * 128, block * 128 + 128)
            queries = q_ref[rows, lanes]
            keys = k_ref[rows, lanes]
            values = v_ref[rows, lanes]
            live = key_place[:, :128] < lengths_ref[block]
            out = []
            for sub in range(2):
                masked = jnp.where((lane >= 64) == (sub == 1), queries, 0)
                scores = jnp.where(live, dot_nt(masked, keys) + tiles[sub][0], -1000000000.0)
                probs = softmax(scores)
                short_ref[pair * 2 + sub, rows, :] = probs
                out.append(dot_nn(probs, values))
            mixed_ref[rows, lanes] = jnp.where(lane < 64, out[0], out[1]).astype(jnp.bfloat16)
        keys = k_ref[short_tok:, lanes]
        values = v_ref[short_tok:, lanes]
        for block in range(LONG_LEN // 128):
            places = slice(block * 128, block * 128 + 128)
            rows = slice(short_tok + block * 128, short_tok + block * 128 + 128)
            queries = q_ref[rows, lanes]
            out = []
            for sub in range(2):
                masked = jnp.where((lane >= 64) == (sub == 1), queries, 0)
                same, above, below, far_above, far_below = tiles[sub]
                bias = jnp.concatenate(
                    [
                        same
                        if other == block
                        else above
                        if other == block + 1
                        else below
                        if other == block - 1
                        else far_above
                        if other > block
                        else far_below
                        for other in range(LONG_LEN // 128)
                    ],
                    axis=1,
                )
                scores = jnp.where(live_long, dot_nt(masked, keys) + bias, -1000000000.0)
                probs = softmax(scores)
                long_ref[pair * 2 + sub, places, :] = probs
                out.append(dot_nn(probs, values))
            mixed_ref[rows, lanes] = jnp.where(lane < 64, out[0], out[1]).astype(jnp.bfloat16)
        return carry

    lax.fori_loop(0, pairs, one_pair, 0)
    for start in range(0, tok_count, tile):
        rows = slice(start, start + tile)
        part_ref[rows, :] = dot_nn(mixed_ref[rows, :], wo_ref[...])


def attend(lengths, tokens, gain, w_query, w_key, w_value, w_out, table):
    tok_count, width = tokens.shape
    own = w_query.shape[1]
    heads = own // 64
    heads_pad = -(-heads // 8) * 8
    table = jnp.pad(table.T, ((0, heads_pad - heads), (0, 0)))
    short_tok = SHORT_DEV * SHORT_LEN
    flops = 2 * tok_count * width * own * 4 + 4 * heads * (512 * 512 + short_tok * 128) * 64
    return pl.pallas_call(
        attend_kernel,
        out_shape=[
            jax.ShapeDtypeStruct((tok_count, width), jnp.float32),
            jax.ShapeDtypeStruct((tok_count, width), jnp.bfloat16),
            jax.ShapeDtypeStruct((tok_count, own), jnp.bfloat16),
            jax.ShapeDtypeStruct((tok_count, own), jnp.bfloat16),
            jax.ShapeDtypeStruct((tok_count, own), jnp.bfloat16),
            jax.ShapeDtypeStruct((tok_count, own), jnp.bfloat16),
            jax.ShapeDtypeStruct((heads, LONG_LEN, LONG_LEN), jnp.bfloat16),
            jax.ShapeDtypeStruct((heads, short_tok, SHORT_LEN), jnp.bfloat16),
        ],
        in_specs=[pl.BlockSpec(memory_space=pltpu.SMEM)] + vmem(7),
        out_specs=vmem(8),
        scratch_shapes=[pltpu.VMEM((heads_pad, 512), jnp.float32)],
        compiler_params=params(),
        cost_estimate=pl.CostEstimate(
            flops=flops, bytes_accessed=16000000, transcendentals=heads * 512 * 640
        ),
        name="attend",
    )(lengths, tokens, gain.astype(jnp.float32)[None], w_query, w_key, w_value, w_out, table)


def attend_back_kernel(
    hg_ref,
    q_ref,
    k_ref,
    v_ref,
    mixed_ref,
    long_ref,
    short_ref,
    qg_ref,
    kg_ref,
    vg_ref,
    diag_ref,
    sg_ref,
):
    short_tok = SHORT_DEV * SHORT_LEN
    lane = lax.broadcasted_iota(jnp.int32, (1, 128), 1)

    def flip(rows):
        return jnp.transpose(rows.astype(jnp.float32)).astype(jnp.bfloat16)

    def unsheared(tile):
        row = lax.broadcasted_iota(jnp.int32, (128, 1), 0)
        for bit in range(7):
            moved = pltpu.roll(tile, tile.shape[1] - (1 << bit), 1)
            tile = jnp.where(((row >> bit) & 1) == 1, moved, tile)
        return tile

    def score_part(heads_rows, values, probs, mixed):
        delta = jnp.sum(heads_rows.astype(jnp.float32) * mixed.astype(jnp.float32), axis=1, keepdims=True)
        return probs.astype(jnp.float32) * (dot_nt(heads_rows, values) - delta)

    for sub in range(2):
        own = (lane >= 64) == (sub == 1)
        same = jnp.zeros((128, 128), jnp.float32)
        above = same
        below = same
        far_above = same
        far_below = same
        for block in range(SHORT_DEV):
            rows = slice(block * 128, block * 128 + 128)
            heads_rows = jnp.where(own, hg_ref[rows, :], 0)
            part = score_part(heads_rows, v_ref[rows, :], short_ref[sub, rows, :], mixed_ref[rows, :])
            same = same + part
            part = part.astype(jnp.bfloat16)
            lanes = slice(64 * sub, 64 * sub + 64)
            qg_ref[rows, lanes] = (dot_nn(part, k_ref[rows, :])[:, lanes] * 0.125).astype(jnp.bfloat16)
            kg_t = dot_nn(flip(q_ref[rows, :])[lanes, :], part)
            vg_t = dot_nn(flip(hg_ref[rows, :])[lanes, :], short_ref[sub, rows, :])
            both = jnp.transpose(jnp.concatenate([kg_t, vg_t], axis=0))
            kg_ref[rows, lanes] = both[:, :64].astype(jnp.bfloat16)
            vg_ref[rows, lanes] = both[:, 64:].astype(jnp.bfloat16)
        for block in range(LONG_LEN // 128):
            places = slice(block * 128, block * 128 + 128)
            rows = slice(short_tok + block * 128, short_tok + block * 128 + 128)
            heads_rows = jnp.where(own, hg_ref[rows, :], 0)
            part = score_part(heads_rows, v_ref[short_tok:, :], long_ref[sub, places, :], mixed_ref[rows, :])
            for other in range(LONG_LEN // 128):
                piece = part[:, other * 128 : other * 128 + 128]
                if other == block:
                    same = same + piece
                elif other == block + 1:
                    above = above + piece
                elif other == block - 1:
                    below = below + piece
                elif other > block:
                    far_above = far_above + piece
                else:
                    far_below = far_below + piece
            part = part.astype(jnp.bfloat16)
            sg_ref[places, :] = part
            lanes = slice(64 * sub, 64 * sub + 64)
            qg_ref[rows, lanes] = (dot_nn(part, k_ref[short_tok:, :])[:, lanes] * 0.125).astype(jnp.bfloat16)
        rows = slice(short_tok, short_tok + LONG_LEN)
        kg_t = dot_nn(flip(q_ref[rows, :])[lanes, :], sg_ref[...])
        vg_t = dot_nn(flip(hg_ref[rows, :])[lanes, :], long_ref[sub])
        both = jnp.transpose(jnp.concatenate([kg_t, vg_t], axis=0))
        kg_ref[rows, lanes] = both[:, :64].astype(jnp.bfloat16)
        vg_ref[rows, lanes] = both[:, 64:].astype(jnp.bfloat16)
        sheared = unsheared(
            jnp.concatenate([same, above, jnp.zeros((128, 128), jnp.float32), below], axis=1)
        )
        whole = jnp.concatenate([sheared, far_above, far_below], axis=1)
        diag_ref[0, sub : sub + 1, :] = jnp.sum(whole, axis=0, keepdims=True)


def attend_back(heads_grad, query_rows, key_rows, value_rows, mixed, long_probs, short_probs):
    tok_count, own = query_rows.shape
    pairs = own // 128
    short_tok = SHORT_DEV * SHORT_LEN
    rows_spec = pl.BlockSpec((tok_count, 128), lambda pair: (0, pair))
    flops = 10 * pairs * 2 * (512 * 512 + short_tok * 128) * 64
    qg, kg, vg, diag = pl.pallas_call(
        attend_back_kernel,
        grid=(pairs,),
        out_shape=[jax.ShapeDtypeStruct((tok_count, own), jnp.bfloat16)] * 3
        + [jax.ShapeDtypeStruct((pairs, 2, 768), jnp.float32)],
        in_specs=[rows_spec] * 5
        + [
            pl.BlockSpec((2, LONG_LEN, LONG_LEN), lambda pair: (pair, 0, 0)),
            pl.BlockSpec((2, short_tok, SHORT_LEN), lambda pair: (pair, 0, 0)),
        ],
        out_specs=[rows_spec] * 3 + [pl.BlockSpec((1, 2, 768), lambda pair: (pair, 0, 0))],
        scratch_shapes=[pltpu.VMEM((LONG_LEN, LONG_LEN), jnp.bfloat16)],
        compiler_params=params(),
        cost_estimate=pl.CostEstimate(flops=flops, bytes_accessed=12000000, transcendentals=0),
        name="attend_back",
    )(heads_grad, query_rows, key_rows, value_rows, mixed, long_probs, short_probs)
    return qg, kg, vg, diag.reshape(pairs * 2, 768)


def table_from(diag, bucket_count):
    lane = jnp.arange(768, dtype=jnp.int32)
    offset = jnp.where(lane < 256, lane, lane - 512)
    offset = jnp.where(lane >= 640, -256, jnp.where(lane >= 512, 256, offset))
    hot = (diagonal_buckets(offset)[:, None] == jnp.arange(bucket_count)[None, :]).astype(jnp.float32)
    return lax.dot_general(
        hot, diag, (((0,), (1,)), ((), ())), precision=highest, preferred_element_type=jnp.float32
    )


def dispatch_rows(send_ref, slot_row, half_rows):
    slots = send_ref.shape[0]
    tok_count = slot_row.shape[1]
    for base in range(0, slots, 256):
        span = min(256, slots - base)
        place = lax.broadcasted_iota(jnp.int32, (span, tok_count), 0) + base
        hot = jnp.where(place == slot_row, 1.0, 0.0).astype(jnp.bfloat16)
        send_ref[base : base + span, :] = dot_nn(hot, half_rows).astype(jnp.bfloat16)


def half_lanes(core, half):
    return pl.ds(pl.multiple_of(core * half, half), half)


def route_kernel(capacity, where_ref, routes_ref, grad_ref, row_ref, col_ref, send_ref):
    tok_count = routes_ref.shape[1]
    slots, half = send_ref.shape
    experts = slots // capacity
    routes = routes_ref[...]
    expert = lax.broadcasted_iota(jnp.int32, (experts, tok_count), 0)
    lane = lax.broadcasted_iota(jnp.int32, (1, tok_count), 1)
    hot = jnp.where(expert == routes, 1.0, 0.0)
    total = hot
    step = 1
    while step < tok_count:
        total = total + jnp.where(lane >= step, pltpu.roll(total, step, 1), 0.0)
        step *= 2
    before = jnp.sum(hot * total, axis=0, keepdims=True).astype(jnp.int32) - 1
    slot = jnp.where(before < capacity, routes * capacity + before, slots)
    row_ref[...] = slot
    wide = jnp.broadcast_to(slot.astype(jnp.float32), (128, tok_count))
    col_ref[...] = jnp.transpose(wide).astype(jnp.int32)
    dispatch_rows(send_ref, slot, grad_ref[:, half_lanes(where_ref[0], half)])


def route(where, routes, out_grad, experts, capacity):
    tok_count, width = out_grad.shape
    slots = experts * capacity
    return pl.pallas_call(
        partial(route_kernel, capacity),
        out_shape=[
            jax.ShapeDtypeStruct((1, tok_count), jnp.int32),
            jax.ShapeDtypeStruct((tok_count, 128), jnp.int32),
            jax.ShapeDtypeStruct((slots, width // 2), jnp.bfloat16),
        ],
        in_specs=[pl.BlockSpec(memory_space=pltpu.SMEM)] + vmem(2),
        out_specs=vmem(3),
        compiler_params=params(),
        cost_estimate=pl.CostEstimate(
            flops=slots * tok_count * width, bytes_accessed=4000000, transcendentals=0
        ),
        name="route",
    )(where, routes.reshape(1, tok_count), out_grad)


def second_kernel(
    where_ref, tokens_ref, own_ref, other_ref, gain_ref, row_ref, residual_ref, send_ref, second_ref
):
    step = pl.program_id(0)
    tile = tokens_ref.shape[0]
    half = send_ref.shape[1]
    residual = tokens_ref[...].astype(jnp.float32) + (own_ref[...] + other_ref[...])
    residual_ref[...] = residual
    second_ref[pl.ds(pl.multiple_of(step * tile, tile), tile), :] = (
        residual * inverse_rms(residual) * gain_ref[...]
    ).astype(jnp.bfloat16)

    @pl.when(step == pl.num_programs(0) - 1)
    def _():
        dispatch_rows(send_ref, row_ref[...], second_ref[:, half_lanes(where_ref[0], half)])


def second_rows(where, tokens, own, other, gain, slot_row, slots):
    tok_count, width = tokens.shape
    tile = 256
    rows = pl.BlockSpec((tile, width), lambda step: (step, 0))
    return pl.pallas_call(
        second_kernel,
        grid=(tok_count // tile,),
        out_shape=[
            jax.ShapeDtypeStruct((tok_count, width), jnp.float32),
            jax.ShapeDtypeStruct((slots, width // 2), jnp.bfloat16),
        ],
        in_specs=[
            pl.BlockSpec(memory_space=pltpu.SMEM),
            rows,
            rows,
            rows,
            pl.BlockSpec((1, width), lambda step: (0, 0)),
            pl.BlockSpec((1, tok_count), lambda step: (0, 0)),
        ],
        out_specs=[rows, pl.BlockSpec((slots, width // 2), lambda step: (0, 0))],
        scratch_shapes=[pltpu.VMEM((tok_count, width), jnp.bfloat16)],
        compiler_params=params(),
        cost_estimate=pl.CostEstimate(
            flops=slots * tok_count * width, bytes_accessed=13000000, transcendentals=0
        ),
        name="second",
    )(where, tokens, own, other, gain.astype(jnp.float32)[None], slot_row)


def hidden_grad_kernel(where_ref, own_ref, other_ref, outer_ref, out_ref):
    half = own_ref.shape[1]
    core = where_ref[0]
    out_ref[...] = dot_nt(own_ref[...], outer_ref[:, half_lanes(core, half)]) + dot_nt(
        other_ref[...], outer_ref[:, half_lanes(1 - core, half)]
    )


def hidden_grad_of(where, own, other, outer):
    slots, half = own.shape
    hidden = outer.shape[0]
    tile = 256
    rows = pl.BlockSpec((tile, half), lambda step: (step, 0))
    return pl.pallas_call(
        hidden_grad_kernel,
        grid=(slots // tile,),
        out_shape=jax.ShapeDtypeStruct((slots, hidden), jnp.float32),
        in_specs=[
            pl.BlockSpec(memory_space=pltpu.SMEM),
            rows,
            rows,
            pl.BlockSpec(outer.shape, lambda step: (0, 0)),
        ],
        out_specs=pl.BlockSpec((tile, hidden), lambda step: (step, 0)),
        compiler_params=params(),
        cost_estimate=pl.CostEstimate(
            flops=4 * slots * half * hidden, bytes_accessed=12000000, transcendentals=0
        ),
        name="hidden_grad",
    )(where, own, other, outer)


def expert_kernel(
    where_ref,
    own_ref,
    other_ref,
    grad_own_ref,
    grad_other_ref,
    hg_ref,
    inner_ref,
    router_ref,
    hidden_ref,
    pre_grad_ref,
    keep_ref,
    send_ref,
    arrived_ref,
    gated_ref,
    logit_ref,
):
    core = where_ref[0]
    half = own_ref.shape[1]
    experts = router_ref.shape[1]
    own_lanes = half_lanes(core, half)
    other_lanes = half_lanes(1 - core, half)
    own = own_ref[...]
    other = other_ref[...]
    arrived_ref[:, own_lanes] = own
    arrived_ref[:, other_lanes] = other
    logits = dot_nn(own, router_ref[own_lanes, :]) + dot_nn(other, router_ref[other_lanes, :])
    exp_logit = jnp.exp(logits - jnp.max(logits, axis=1, keepdims=True))
    probs = exp_logit * (1.0 / jnp.sum(exp_logit, axis=1, keepdims=True))
    hit = jnp.where(
        lax.broadcasted_iota(jnp.int32, (1, experts), 1) == where_ref[1], 1.0, 0.0
    )
    gate = jnp.sum(probs * hit, axis=1, keepdims=True)
    gated_ref[:, own_lanes] = (gate * grad_own_ref[...].astype(jnp.float32)).astype(jnp.bfloat16)
    gated_ref[:, other_lanes] = (gate * grad_other_ref[...].astype(jnp.float32)).astype(jnp.bfloat16)
    pre = dot_nn(own, inner_ref[own_lanes, :]) + dot_nn(other, inner_ref[other_lanes, :])
    hg = hg_ref[...]
    square = pre * pre
    curve = 0.7978845608028654
    bend = jnp.tanh(pre * (curve + (curve * 0.044715) * square))
    grown = 0.5 + 0.5 * bend
    hidden = (pre * grown).astype(jnp.bfloat16)
    hidden_ref[...] = hidden
    gate_grad = jnp.sum(hidden.astype(jnp.float32) * hg, axis=1, keepdims=True)
    slope = grown + (0.5 * pre) * (1.0 - bend * bend) * (curve + (3 * curve * 0.044715) * square)
    pre_grad = (slope * (gate * hg)).astype(jnp.bfloat16)
    pre_grad_ref[...] = pre_grad
    logit = (probs * (gate_grad * (hit - gate))).astype(jnp.bfloat16)
    logit_ref[...] = logit
    send_ref[...] = (
        dot_nt(pre_grad, inner_ref[other_lanes, :]) + dot_nt(logit, router_ref[other_lanes, :])
    ).astype(jnp.bfloat16)
    keep_ref[...] = dot_nt(pre_grad, inner_ref[own_lanes, :]) + dot_nt(
        logit, router_ref[own_lanes, :]
    )


def expert(where, own, other, grad_own, grad_other, hidden_grad, inner, router):
    slots, half = own.shape
    width, hidden = inner.shape
    experts = router.shape[1]
    tile = 256
    halves = pl.BlockSpec((tile, half), lambda step: (step, 0))
    wide = pl.BlockSpec((tile, width), lambda step: (step, 0))
    units = pl.BlockSpec((tile, hidden), lambda step: (step, 0))
    return pl.pallas_call(
        expert_kernel,
        grid=(slots // tile,),
        out_shape=[
            jax.ShapeDtypeStruct((slots, hidden), jnp.bfloat16),
            jax.ShapeDtypeStruct((slots, hidden), jnp.bfloat16),
            jax.ShapeDtypeStruct((slots, half), jnp.float32),
            jax.ShapeDtypeStruct((slots, half), jnp.bfloat16),
            jax.ShapeDtypeStruct((slots, width), jnp.bfloat16),
            jax.ShapeDtypeStruct((slots, width), jnp.bfloat16),
            jax.ShapeDtypeStruct((slots, experts), jnp.bfloat16),
        ],
        in_specs=[
            pl.BlockSpec(memory_space=pltpu.SMEM),
            halves,
            halves,
            halves,
            halves,
            units,
            pl.BlockSpec(inner.shape, lambda step: (0, 0)),
            pl.BlockSpec(router.shape, lambda step: (0, 0)),
        ],
        out_specs=[
            units,
            units,
            halves,
            halves,
            wide,
            wide,
            pl.BlockSpec((tile, experts), lambda step: (step, 0)),
        ],
        compiler_params=params(),
        cost_estimate=pl.CostEstimate(
            flops=4 * slots * width * hidden, bytes_accessed=30000000, transcendentals=slots * hidden
        ),
        name="expert",
    )(where, own, other, grad_own, grad_other, hidden_grad, inner, router)


def expert_out_kernel(where_ref, hidden_ref, outer_ref, keep_ref, send_ref):
    core = where_ref[0]
    half = keep_ref.shape[1]
    hidden = hidden_ref[...]
    send_ref[...] = dot_nn(hidden, outer_ref[:, half_lanes(1 - core, half)]).astype(jnp.bfloat16)
    keep_ref[...] = dot_nn(hidden, outer_ref[:, half_lanes(core, half)])


def expert_out_of(where, hidden, outer):
    slots, units = hidden.shape
    half = outer.shape[1] // 2
    tile = 256
    halves = pl.BlockSpec((tile, half), lambda step: (step, 0))
    return pl.pallas_call(
        expert_out_kernel,
        grid=(slots // tile,),
        out_shape=[
            jax.ShapeDtypeStruct((slots, half), jnp.float32),
            jax.ShapeDtypeStruct((slots, half), jnp.bfloat16),
        ],
        in_specs=[
            pl.BlockSpec(memory_space=pltpu.SMEM),
            pl.BlockSpec((tile, units), lambda step: (step, 0)),
            pl.BlockSpec(outer.shape, lambda step: (0, 0)),
        ],
        out_specs=[halves, halves],
        compiler_params=params(),
        cost_estimate=pl.CostEstimate(
            flops=4 * slots * half * units, bytes_accessed=9000000, transcendentals=0
        ),
        name="expert_out",
    )(where, hidden, outer)


def residual_back_kernel(
    where_ref,
    col_ref,
    own_ref,
    other_ref,
    residual_ref,
    grad_ref,
    gain_ref,
    wo_ref,
    out_ref,
    attn_ref,
    heads_ref,
    gain_out_ref,
    whole_ref,
):
    core = where_ref[0]
    slots, half = own_ref.shape
    tile = residual_ref.shape[0]
    place = lax.broadcasted_iota(jnp.int32, (tile, slots), 1)
    hot = jnp.where(place == col_ref[:, :1], 1.0, 0.0).astype(jnp.bfloat16)
    whole_ref[:, half_lanes(core, half)] = dot_nn(hot, own_ref[...])
    whole_ref[:, half_lanes(1 - core, half)] = dot_nn(hot, other_ref[...])
    ybar = whole_ref[...]
    values = residual_ref[...]
    scale = inverse_rms(values)
    scaled = values * scale
    pulled = ybar * gain_ref[...]

    @pl.when(pl.program_id(0) == 0)
    def _():
        gain_out_ref[...] = jnp.zeros_like(gain_out_ref)

    gain_out_ref[...] += jnp.sum(ybar * scaled, axis=0, keepdims=True)
    back = scale * (pulled - scaled * jnp.mean(pulled * scaled, axis=1, keepdims=True))
    out = back + grad_ref[...].astype(jnp.float32)
    out_ref[...] = out
    attn = out.astype(jnp.bfloat16)
    attn_ref[...] = attn
    heads_ref[...] = dot_nt(attn, wo_ref[...]).astype(jnp.bfloat16)


def residual_back(where, slot_col, own, other, residual, out_grad, gain, w_out):
    tok_count, width = residual.shape
    slots, half = own.shape
    heads_width = w_out.shape[0]
    tile = 256
    rows = pl.BlockSpec((tile, width), lambda step: (step, 0))
    whole = lambda shape: pl.BlockSpec(shape, lambda step: (0, 0))
    return pl.pallas_call(
        residual_back_kernel,
        grid=(tok_count // tile,),
        out_shape=[
            jax.ShapeDtypeStruct((tok_count, width), jnp.float32),
            jax.ShapeDtypeStruct((tok_count, width), jnp.bfloat16),
            jax.ShapeDtypeStruct((tok_count, heads_width), jnp.bfloat16),
            jax.ShapeDtypeStruct((1, width), jnp.float32),
        ],
        in_specs=[
            pl.BlockSpec(memory_space=pltpu.SMEM),
            pl.BlockSpec((tile, 128), lambda step: (step, 0)),
            whole(own.shape),
            whole(other.shape),
            rows,
            rows,
            whole((1, width)),
            whole(w_out.shape),
        ],
        out_specs=[
            rows,
            rows,
            pl.BlockSpec((tile, heads_width), lambda step: (step, 0)),
            whole((1, width)),
        ],
        scratch_shapes=[pltpu.VMEM((tile, width), jnp.float32)],
        compiler_params=params(),
        cost_estimate=pl.CostEstimate(
            flops=tok_count * width * (2 * slots + 2 * heads_width),
            bytes_accessed=14000000,
            transcendentals=0,
        ),
        name="residual_back",
    )(where, slot_col, own, other, residual, out_grad, gain.astype(jnp.float32)[None], w_out)


def output_kernel(
    capacity, where_ref, col_ref, returned_ref, residual_ref, gain_ref, router_ref, out_ref
):
    slots, half = returned_ref.shape
    tile = residual_ref.shape[0]
    experts = router_ref.shape[1]
    col = col_ref[:, :1]
    place = lax.broadcasted_iota(jnp.int32, (tile, slots), 1)
    hot = jnp.where(place == col, 1.0, 0.0).astype(jnp.bfloat16)
    token_out = dot_nn(hot, returned_ref[...])
    residual = residual_ref[...]
    second = (residual * inverse_rms(residual) * gain_ref[...]).astype(jnp.bfloat16)
    logits = dot_nn(second, router_ref[...])
    exp_logit = jnp.exp(logits - jnp.max(logits, axis=1, keepdims=True))
    first = lax.broadcasted_iota(jnp.int32, (1, experts), 1) * capacity
    hit = jnp.where((col >= first) & (col < first + capacity), exp_logit, 0.0)
    gate = jnp.sum(hit, axis=1, keepdims=True) / jnp.sum(exp_logit, axis=1, keepdims=True)
    own = residual_ref[:, half_lanes(where_ref[0], half)]
    out_ref[...] = (own + gate * token_out).astype(jnp.bfloat16)


def output_of(where, slot_col, returned, residual, gain, router, capacity):
    tok_count, width = residual.shape
    slots, half = returned.shape
    tile = 256
    whole = lambda shape: pl.BlockSpec(shape, lambda step: (0, 0))
    return pl.pallas_call(
        partial(output_kernel, capacity),
        grid=(tok_count // tile,),
        out_shape=jax.ShapeDtypeStruct((tok_count, half), jnp.bfloat16),
        in_specs=[
            pl.BlockSpec(memory_space=pltpu.SMEM),
            pl.BlockSpec((tile, 128), lambda step: (step, 0)),
            whole(returned.shape),
            pl.BlockSpec((tile, width), lambda step: (step, 0)),
            whole((1, width)),
            whole(router.shape),
        ],
        out_specs=pl.BlockSpec((tile, half), lambda step: (step, 0)),
        compiler_params=params(),
        cost_estimate=pl.CostEstimate(
            flops=2 * tok_count * half * slots, bytes_accessed=6000000, transcendentals=0
        ),
        name="output",
    )(where, slot_col, returned, residual, gain.astype(jnp.float32)[None], router)


def input_back_kernel(tokens_ref, own_ref, other_ref, gain_ref, residual_ref, out_ref):
    ybar = own_ref[...].astype(jnp.float32) + other_ref[...].astype(jnp.float32)
    values = tokens_ref[...].astype(jnp.float32)
    scale = inverse_rms(values)
    scaled = values * scale
    pulled = ybar * gain_ref[...]
    out_ref[...] = residual_ref[...] + scale * (
        pulled - scaled * jnp.mean(pulled * scaled, axis=1, keepdims=True)
    )


def input_back(tokens, own, other, gain, residual_grad):
    tok_count, width = tokens.shape
    tile = 256
    rows = pl.BlockSpec((tile, width), lambda step: (step, 0))
    return pl.pallas_call(
        input_back_kernel,
        grid=(tok_count // tile,),
        out_shape=jax.ShapeDtypeStruct((tok_count, width), jnp.float32),
        in_specs=[rows, rows, rows, pl.BlockSpec((1, width), lambda step: (0, 0)), rows],
        out_specs=rows,
        compiler_params=params(),
        cost_estimate=pl.CostEstimate(
            flops=10 * tok_count * width, bytes_accessed=11000000, transcendentals=0
        ),
        name="input_back",
    )(tokens, own, other, gain.astype(jnp.float32)[None], residual_grad)


def weights_kernel(
    normed_ref, qg_ref, kg_ref, vg_ref, mixed_ref, attn_ref, wq_ref, wk_ref, wv_ref, gain_ref,
    stack_ref, gain_out_ref,
):
    width = normed_ref.shape[1]
    own = mixed_ref.shape[1]
    tile = 256
    for start in range(0, width, tile):
        rows = slice(start, start + tile)
        normed = normed_ref[:, rows]
        total = jnp.zeros((tile, 1), jnp.float32)
        for index, (grad_ref, w_ref) in enumerate(((qg_ref, wq_ref), (kg_ref, wk_ref), (vg_ref, wv_ref))):
            grad = contract_rows(normed, grad_ref[...])
            total = total + jnp.sum(grad * w_ref[rows, :].astype(jnp.float32), axis=1, keepdims=True)
            stack_ref[index * width + start : index * width + start + tile, :] = grad.astype(jnp.bfloat16)
        gain_out_ref[:, rows] = jnp.transpose(jnp.broadcast_to(total, (tile, 128)))[:8, :]
    gain_out_ref[...] = gain_out_ref[...] / gain_ref[...]
    for start in range(0, own, 128):
        grad = contract_rows(mixed_ref[:, start : start + 128], attn_ref[...]).astype(jnp.bfloat16)
        for part in range(width // own):
            base = 3 * width + part * own + start
            stack_ref[base : base + 128, :] = grad[:, part * own : part * own + own]


def weight_grads(normed, qg, kg, vg, mixed, attn_grad, w_query, w_key, w_value, gain):
    tok_count, width = normed.shape
    own = qg.shape[1]
    return pl.pallas_call(
        weights_kernel,
        out_shape=[
            jax.ShapeDtypeStruct((4 * width, own), jnp.bfloat16),
            jax.ShapeDtypeStruct((8, width), jnp.float32),
        ],
        in_specs=vmem(10),
        out_specs=vmem(2),
        compiler_params=params(),
        cost_estimate=pl.CostEstimate(
            flops=8 * tok_count * width * own, bytes_accessed=12000000, transcendentals=0
        ),
        name="weight_grads",
    )(normed, qg, kg, vg, mixed, attn_grad, w_query, w_key, w_value, gain.astype(jnp.float32)[None])


def split_kernel(count, bits_ref, *refs):
    for part in range(count):
        whole = refs[part]
        span = whole.shape[0] // 2
        mine = bits_ref[part]
        refs[count + part][...] = whole[pl.ds((1 - mine) * span, span)]
        refs[2 * count + part][...] = whole[pl.ds(mine * span, span)]


def split(bits, parts):
    count = len(parts)
    halves = [jax.ShapeDtypeStruct((p.shape[0] // 2,) + p.shape[1:], p.dtype) for p in parts]
    out = pl.pallas_call(
        partial(split_kernel, count),
        out_shape=halves + halves,
        in_specs=[pl.BlockSpec(memory_space=pltpu.SMEM)] + vmem(count),
        out_specs=vmem(2 * count),
        compiler_params=params(16),
        name="split",
    )(bits, *parts)
    return out[:count], out[count:]


def fold_kernel(count, bits_ref, *refs):
    kept, got, sent, keep = (refs[count * k : count * (k + 1)] for k in range(4))
    for part in range(count):
        span = kept[part].shape[0] // 2
        mine = bits_ref[part]
        for ref, start in ((sent[part], (1 - mine) * span), (keep[part], mine * span)):
            rows = pl.ds(start, span)
            ref[...] = (
                kept[part][rows].astype(jnp.float32) + got[part][rows].astype(jnp.float32)
            ).astype(jnp.bfloat16)


def fold(bits, kept, got):
    count = len(kept)
    halves = [jax.ShapeDtypeStruct((p.shape[0] // 2,) + p.shape[1:], p.dtype) for p in kept]
    out = pl.pallas_call(
        partial(fold_kernel, count),
        out_shape=halves + halves,
        in_specs=[pl.BlockSpec(memory_space=pltpu.SMEM)] + vmem(2 * count),
        out_specs=vmem(2 * count),
        compiler_params=params(16),
        name="fold",
    )(bits, *kept, *got)
    return out[:count], out[count:]


def join_kernel(count, bits_ref, *refs):
    own, got, out = (refs[count * k : count * (k + 1)] for k in range(3))
    for part in range(count):
        span = own[part].shape[0]
        mine = bits_ref[part]
        out[part][pl.ds(mine * span, span)] = own[part][...]
        out[part][pl.ds((1 - mine) * span, span)] = got[part][...]


def join(bits, own, got):
    count = len(own)
    return pl.pallas_call(
        partial(join_kernel, count),
        out_shape=[jax.ShapeDtypeStruct((p.shape[0] * 2,) + p.shape[1:], p.dtype) for p in own],
        in_specs=[pl.BlockSpec(memory_space=pltpu.SMEM)] + vmem(2 * count),
        out_specs=vmem(count),
        compiler_params=params(16),
        name="join",
    )(bits, *own, *got)


def pack_kernel(count, *refs):
    kept, got = refs[:count], refs[count : 2 * count]
    span = kept[0].shape[0]
    for part in range(count):
        refs[-1][part * span : (part + 1) * span] = (
            kept[part][...].astype(jnp.float32) + got[part][...].astype(jnp.float32)
        ).astype(jnp.bfloat16)


def pack(kept, got):
    count = len(kept)
    shape = kept[0].shape
    return pl.pallas_call(
        partial(pack_kernel, count),
        out_shape=jax.ShapeDtypeStruct((count * shape[0],) + shape[1:], jnp.bfloat16),
        in_specs=vmem(2 * count),
        out_specs=vmem(1)[0],
        compiler_params=params(16),
        name="pack",
    )(*kept, *got)


def unpack_kernel(own_ref, got_ref, *out):
    span = out[0].shape[0]
    for part, ref in enumerate(out):
        rows = slice(part * span, (part + 1) * span)
        ref[...] = (own_ref[rows].astype(jnp.float32) + got_ref[rows].astype(jnp.float32)).astype(
            jnp.bfloat16
        )


def unpack(own, got, count):
    shape = (own.shape[0] // count,) + own.shape[1:]
    return pl.pallas_call(
        unpack_kernel,
        out_shape=[jax.ShapeDtypeStruct(shape, jnp.bfloat16)] * count,
        in_specs=vmem(2),
        out_specs=vmem(count),
        compiler_params=params(16),
        name="unpack",
    )(own, got)


def finish_kernel(count, bits_ref, *refs):
    own, got = refs[:count], refs[count : 2 * count]
    query_ref, key_ref, value_ref, out_ref, whole_ref = refs[2 * count :]
    span = own[0].shape[0]
    rows = 2 * span * own[0].shape[1]
    width, lanes = query_ref.shape
    for part in range(count):
        mine = bits_ref[part]
        whole_ref[pl.ds(mine * span, span)] = own[part][...].astype(jnp.float32)
        whole_ref[pl.ds((1 - mine) * span, span)] = got[part][...].astype(jnp.float32)
        flat = whole_ref[...].reshape(rows, lanes)
        for index, ref in enumerate((query_ref, key_ref, value_ref)):
            first = max(index * width, part * rows)
            last = min((index + 1) * width, (part + 1) * rows)
            if first < last:
                ref[first - index * width : last - index * width, :] = flat[
                    first - part * rows : last - part * rows
                ]
        for index in range(width // lanes):
            base = 3 * width + index * lanes
            first = max(base, part * rows)
            last = min(base + lanes, (part + 1) * rows)
            if first < last:
                out_ref[first - base : last - base, index * lanes : (index + 1) * lanes] = flat[
                    first - part * rows : last - part * rows
                ]


def finish(bits, own, got, width):
    count = len(own)
    span, rows, lanes = own[0].shape
    return pl.pallas_call(
        partial(finish_kernel, count),
        out_shape=[jax.ShapeDtypeStruct((width, lanes), jnp.float32)] * 3
        + [jax.ShapeDtypeStruct((lanes, width), jnp.float32)],
        in_specs=[pl.BlockSpec(memory_space=pltpu.SMEM)] + vmem(2 * count),
        out_specs=vmem(4),
        scratch_shapes=[pltpu.VMEM((2 * span, rows, lanes), jnp.float32)],
        compiler_params=params(24),
        name="finish",
    )(bits, *own, *got)


def swap_heads(rows):
    return lax.ppermute(rows, "heads", [(0, 1), (1, 0)])


def trade(rows, bit):
    count = lax.axis_size("seq")
    return lax.ppermute(rows, "seq", [(i, i ^ (1 << bit)) for i in range(count)])


def together(*groups):
    return lax.optimization_barrier(groups)


def contract_rows(left, right):
    return lax.dot_general(
        left, right, (((0,), (0,)), ((), ())), preferred_element_type=jnp.float32
    )


def contract_cols(left, right):
    return lax.dot_general(
        left, right, (((1,), (1,)), ((), ())), preferred_element_type=jnp.float32
    )


def on_device(
    tokens,
    gain_attn,
    w_query,
    w_key,
    w_value,
    w_out,
    bias_table,
    gain_ffn,
    w_router,
    w_inner,
    w_outer,
    routes,
    seq_lengths,
    out_grad,
):
    tok_count, width = tokens.shape
    bucket_count = bias_table.shape[0]
    experts = w_router.shape[1]
    capacity = max(2, 5 * tok_count // (4 * experts))
    senders = lax.axis_size("seq")
    bits = list(range(senders.bit_length() - 1))
    slots = experts * capacity
    half = width // 2
    own = w_query.shape[1]
    where = jnp.stack([lax.axis_index("heads"), lax.axis_index("seq")]).astype(jnp.int32)

    def exchange(rows):
        return lax.all_to_all(
            rows.reshape(senders, capacity, half), "seq", split_axis=0, concat_axis=0, tiled=True
        ).reshape(slots, half)

    def summed(keep, send):
        return (keep + swap_heads(send).astype(jnp.float32)).astype(jnp.bfloat16)

    slot_row, slot_col, grad_sent = route(where, routes, out_grad, experts, capacity)
    grad_sent, tokens = together(grad_sent, tokens)
    grad_own = exchange(grad_sent)
    attn_part, normed, query_rows, key_rows, value_rows, mixed, long_probs, short_probs = attend(
        seq_lengths, tokens, gain_attn, w_query, w_key, w_value, w_out, bias_table
    )
    attn_part, grad_own = together(attn_part, grad_own)
    residual, second_sent = second_rows(
        where, tokens, attn_part, swap_heads(attn_part), gain_ffn, slot_row, slots
    )
    arrived_own = exchange(second_sent)

    inner = w_inner[0]
    outer = w_outer[0]
    grad_other = swap_heads(grad_own)
    hidden_grad = hidden_grad_of(where, grad_own, grad_other, outer)
    arrived_own, hidden_grad = together(arrived_own, hidden_grad)
    arrived_other = swap_heads(arrived_own)
    hidden, pre_grad, keep, send, arrived, gated, logit_grad = expert(
        where, arrived_own, arrived_other, grad_own, grad_other, hidden_grad, inner, w_router
    )
    back_sum, hidden = together(summed(keep, send), hidden)
    back_own = exchange(back_sum)
    out_keep, out_send = expert_out_of(where, hidden, outer)
    out_sum = summed(out_keep, out_send)
    router_part = contract_rows(logit_grad, arrived)
    outer_grad = contract_rows(hidden, gated)
    inner_grad = contract_rows(arrived, pre_grad)
    back_own, out_sum, router_part, outer_grad, inner_grad = together(
        back_own, out_sum, router_part, outer_grad, inner_grad
    )
    returned = exchange(out_sum)

    residual_grad, attn_grad, heads_grad, gain_two_part = residual_back(
        where, slot_col, back_own, swap_heads(back_own), residual, out_grad, gain_ffn, w_out
    )
    query_grad, key_grad, value_grad, diag = attend_back(
        heads_grad, query_rows, key_rows, value_rows, mixed, long_probs, short_probs
    )
    query_grad, returned = together(query_grad, returned)
    stack, gain_one_part = weight_grads(
        normed, query_grad, key_grad, value_grad, mixed, attn_grad, w_query, w_key, w_value, gain_attn
    )

    depth = len(bits) - 1
    turns = [bits[k * depth // 3 : depth] + bits[: k * depth // 3] for k in range(3)]
    place = lax.axis_index("seq")
    mine = [jnp.stack([(place >> turn[k]) & 1 for turn in turns]).astype(jnp.int32) for k in range(depth)]
    rows = stack.shape[0] // 3
    parts = [
        stack[k * rows : (k + 1) * rows].reshape(senders, rows // senders, own) for k in range(3)
    ]

    def trades(arrays, k):
        return [trade(array, turn[k]) for array, turn in zip(arrays, turns)]

    table_grad = table_from(diag, bucket_count)
    pair_part = jnp.concatenate([router_part, gain_one_part[:1]], axis=0)
    table_row = jnp.pad(table_grad.reshape(1, -1), ((0, 0), (0, width - table_grad.size)))
    own_part = jnp.concatenate([gain_two_part, table_row], axis=0)
    sent, kept = split(mine[0], parts)
    for k in range(depth):
        got = trades(sent, k)
        if k == 0:
            pair_part = pair_part + swap_heads(pair_part)
            small = jnp.concatenate([pair_part, own_part], axis=0)
            output = output_of(where, slot_col, returned, residual, gain_ffn, w_router, capacity)
            got, output, small = together(got, output, small)
        else:
            small = small + trade(small, bits[k - 1])
            if k == 1:
                normed_part = (
                    contract_cols(query_grad, w_query)
                    + contract_cols(key_grad, w_key)
                    + contract_cols(value_grad, w_value)
                ).astype(jnp.bfloat16)
                got, normed_part, small = together(got, normed_part, small)
            else:
                got, small = together(got, small)
        if k + 1 < depth:
            sent, kept = fold(mine[k + 1], kept, got)
    packed = pack(kept, got)
    got = trade(packed, bits[-1])
    normed_other = swap_heads(normed_part)
    for bit in bits[depth - 1 : -1]:
        small = small + trade(small, bit)
    got, small, normed_other = together(got, small, normed_other)
    summed_parts = unpack(packed, got, 3)
    for k in reversed(range(1, depth)):
        summed_parts = join(mine[k], summed_parts, trades(summed_parts, k))
    got = trades(summed_parts, 0)
    small = small + trade(small, bits[-1])
    input_grad = input_back(tokens, normed_part, normed_other, gain_attn, residual_grad)
    got, input_grad, small = together(got, input_grad, small)
    query_w_grad, key_w_grad, value_w_grad, out_w_grad = finish(mine[0], summed_parts, got, width)
    return (
        output,
        input_grad,
        small[experts],
        query_w_grad,
        key_w_grad,
        value_w_grad,
        out_w_grad,
        small[experts + 2, : table_grad.size].reshape(table_grad.shape),
        small[experts + 1],
        small[:experts].T,
        inner_grad[None],
        outer_grad[None],
    )


def solution(mesh):
    in_specs = (
        P("seq", None),
        P(),
        P(None, "heads"),
        P(None, "heads"),
        P(None, "heads"),
        P("heads", None),
        P(None, "heads"),
        P(),
        P(),
        P("seq", None, "heads"),
        P("seq", "heads", None),
        P("seq", None),
        P("seq"),
        P("seq", None),
    )
    out_specs = (
        P("seq", "heads"),
        P("seq", None),
        P(),
        P(None, "heads"),
        P(None, "heads"),
        P(None, "heads"),
        P("heads", None),
        P(None, "heads"),
        P(),
        P(),
        P("seq", None, "heads"),
        P("seq", "heads", None),
    )
    return jax.shard_map(
        on_device, mesh=mesh, in_specs=in_specs, out_specs=out_specs, check_vma=False
    )
```

```python
from functools import partial

import jax
import jax.numpy as jnp
from jax import lax
from jax.experimental import pallas as pl
from jax.experimental.pallas import tpu as pltpu
from jax.sharding import PartitionSpec as P

SHORT_LEN = 128
LONG_LEN = 512
SHORT_DEV = 4
LONG_DEV = 1


epsilon = 1e-06
highest = lax.Precision.HIGHEST
far_limits = (12, 16, 23, 32, 46, 64, 91)


def vmem(count):
    return [pl.BlockSpec(memory_space=pltpu.VMEM)] * count


def params(mib=16):
    return pltpu.CompilerParams(vmem_limit_bytes=mib * 1024 * 1024)


def dot_nn(left, right):
    return jnp.dot(left, right, preferred_element_type=jnp.float32)


def dot_nt(left, right):
    return lax.dot_general(
        left, right, (((1,), (1,)), ((), ())), preferred_element_type=jnp.float32
    )


def inverse_rms(values):
    return lax.rsqrt(jnp.mean(values * values, axis=-1, keepdims=True) + epsilon)


def diagonal_buckets(offset):
    distance = jnp.abs(offset)
    far_bucket = jnp.full(offset.shape, 8, jnp.int32)
    for limit in far_limits:
        far_bucket = far_bucket + (distance >= limit).astype(jnp.int32)
    return jnp.where(distance < 8, distance, far_bucket) + jnp.where(offset > 0, 16, 0)


def in_hbm(array):
    return pltpu.with_memory_space_constraint(array, pltpu.HBM)


def start_copies(pairs):
    copies = [pltpu.make_async_copy(*triple) for triple in pairs]
    for copy in copies:
        copy.start()
    return copies


def attend_kernel(
    block_rows,
    lengths_ref,
    tokens_hbm,
    gain_ref,
    wq_hbm,
    wk_hbm,
    wv_hbm,
    wo_hbm,
    table_ref,
    part_hbm,
    normed_hbm,
    q_hbm,
    k_hbm,
    v_hbm,
    mixed_hbm,
    long_hbm,
    short_hbm,
    tokens_ref,
    wq_ref,
    wk_ref,
    wv_ref,
    wo_ref,
    part_ref,
    normed_ref,
    q_ref,
    k_ref,
    v_ref,
    mixed_ref,
    long_ref,
    short_ref,
    diag_ref,
    in_sems,
    out_sems,
):
    tok_count, width = tokens_ref.shape
    pairs = wq_ref.shape[1] // 128
    short_tok = SHORT_DEV * SHORT_LEN
    tile = 256
    steps = tok_count // tile
    tiles_in = []
    for step in range(steps):
        rows = slice(step * tile, step * tile + tile)
        tiles_in.append((tokens_hbm.at[rows], tokens_ref.at[rows], in_sems.at[step]))
    weights = [(wq_hbm, wq_ref), (wk_hbm, wk_ref), (wv_hbm, wv_ref), (wo_hbm, wo_ref)]
    triples = [tiles_in[0]]
    triples += [(src, dst, in_sems.at[steps + index]) for index, (src, dst) in enumerate(weights[:3])]
    triples += tiles_in[1:]
    triples += [(weights[3][0], weights[3][1], in_sems.at[steps + 3])]
    copies = start_copies(triples)
    tile_copies = [copies[0]] + copies[4 : 3 + steps]
    weight_copies = copies[1:4] + copies[3 + steps :]
    outs = []

    offset = lax.broadcasted_iota(jnp.int32, (table_ref.shape[1], 512), 1) - 256
    hot = jnp.where(
        diagonal_buckets(offset)
        == lax.broadcasted_iota(jnp.int32, (table_ref.shape[1], 512), 0),
        1.0,
        0.0,
    )
    diag_ref[...] = dot_nn(table_ref[...], hot.astype(jnp.bfloat16))
    gain = gain_ref[...]
    for step in range(steps):
        rows = slice(step * tile, step * tile + tile)
        tile_copies[step].wait()
        values = tokens_ref[rows, :].astype(jnp.float32)
        normed = (values * inverse_rms(values) * gain).astype(jnp.bfloat16)
        normed_ref[rows, :] = normed
        if step == 0:
            for copy in weight_copies[:3]:
                copy.wait()
        q_ref[rows, :] = dot_nn(normed, wq_ref[...]).astype(jnp.bfloat16) * jnp.bfloat16(0.125)
        k_ref[rows, :] = dot_nn(normed, wk_ref[...]).astype(jnp.bfloat16)
        v_ref[rows, :] = dot_nn(normed, wv_ref[...]).astype(jnp.bfloat16)
    outs += start_copies(
        [
            (normed_ref, normed_hbm, out_sems.at[0]),
            (q_ref, q_hbm, out_sems.at[1]),
            (k_ref, k_hbm, out_sems.at[2]),
            (v_ref, v_hbm, out_sems.at[3]),
        ]
    )
    lane = lax.broadcasted_iota(jnp.int32, (1, 128), 1)
    key_place = lax.broadcasted_iota(jnp.int32, (1, LONG_LEN), 1)
    live_long = key_place < lengths_ref[SHORT_DEV]

    def softmax(scores):
        weights = jnp.exp(scores - jnp.max(scores, axis=1, keepdims=True))
        return (weights * (1.0 / jnp.sum(weights, axis=1, keepdims=True))).astype(jnp.bfloat16)

    def one_pair(pair):
        lanes = slice(pair * 128, pair * 128 + 128)
        tiles = []
        for sub in range(2):
            row = diag_ref[pair * 2 + sub : pair * 2 + sub + 1, :]
            spread = pltpu.roll(
                jnp.broadcast_to(row, (128, 512)), 256, 1, stride=1, stride_axis=0
            )
            tiles.append(
                (
                    spread[:, 0:128],
                    spread[:, 128:256],
                    spread[:, 384:512],
                    jnp.broadcast_to(row[:, 511:512], (128, 128)),
                    jnp.broadcast_to(row[:, 0:1], (128, 128)),
                )
            )
        out = []
        for sub in range(2):
            scores = []
            for block in range(SHORT_DEV):
                rows = slice(block * 128, block * 128 + 128)
                masked = jnp.where((lane >= 64) == (sub == 1), q_ref[rows, lanes], 0)
                live = key_place[:, :128] < lengths_ref[block]
                scores.append(
                    jnp.where(
                        live, dot_nt(masked, k_ref[rows, lanes]) + tiles[sub][0], -1000000000.0
                    )
                )
            probs = softmax(jnp.concatenate(scores, axis=0))
            short_ref[pair * 2 + sub] = probs
            mixed = []
            for block in range(SHORT_DEV):
                rows = slice(block * 128, block * 128 + 128)
                mixed.append(dot_nn(probs[rows], v_ref[rows, lanes]))
            out.append(jnp.concatenate(mixed, axis=0))
        mixed_ref[:short_tok, lanes] = jnp.where(lane < 64, out[0], out[1]).astype(jnp.bfloat16)
        keys = k_ref[short_tok:, lanes]
        values = v_ref[short_tok:, lanes]
        for start in range(0, LONG_LEN, block_rows):
            places = slice(start, start + block_rows)
            rows = slice(short_tok + start, short_tok + start + block_rows)
            queries = q_ref[rows, lanes]
            out = []
            for sub in range(2):
                masked = jnp.where((lane >= 64) == (sub == 1), queries, 0)
                same, above, below, far_above, far_below = tiles[sub]
                bias = jnp.concatenate(
                    [
                        jnp.concatenate(
                            [
                                same
                                if other == block
                                else above
                                if other == block + 1
                                else below
                                if other == block - 1
                                else far_above
                                if other > block
                                else far_below
                                for other in range(LONG_LEN // 128)
                            ],
                            axis=1,
                        )
                        for block in range(start // 128, (start + block_rows) // 128)
                    ],
                    axis=0,
                )
                scores = jnp.where(live_long, dot_nt(masked, keys) + bias, -1000000000.0)
                probs = softmax(scores)
                long_ref[pair * 2 + sub, places, :] = probs
                out.append(dot_nn(probs, values))
            mixed_ref[rows, lanes] = jnp.where(lane < 64, out[0], out[1]).astype(jnp.bfloat16)

    for pair in range(pairs):
        one_pair(pair)
        both = slice(pair * 2, pair * 2 + 2)
        outs += start_copies(
            [
                (long_ref.at[both], long_hbm.at[both], out_sems.at[4 + 2 * pair]),
                (short_ref.at[both], short_hbm.at[both], out_sems.at[5 + 2 * pair]),
            ]
        )
    weight_copies[3].wait()
    base = 4 + 2 * pairs
    outs += start_copies([(mixed_ref, mixed_hbm, out_sems.at[base])])
    for step in range(steps):
        rows = slice(step * tile, step * tile + tile)
        part_ref[rows, :] = dot_nn(mixed_ref[rows, :], wo_ref[...]).astype(part_ref.dtype)
        outs += start_copies([(part_ref.at[rows], part_hbm.at[rows], out_sems.at[base + 1 + step])])
    for copy in outs:
        copy.wait()


def attend(lengths, tokens, gain, w_query, w_key, w_value, w_out, table, block_rows=512):
    tok_count, width = tokens.shape
    own = w_query.shape[1]
    heads = own // 64
    heads_pad = -(-heads // 8) * 8
    table = jnp.pad(table.T, ((0, heads_pad - heads), (0, 0)))
    short_tok = SHORT_DEV * SHORT_LEN
    flops = 2 * tok_count * width * own * 4 + 4 * heads * (512 * 512 + short_tok * 128) * 64
    hbm = pl.BlockSpec(memory_space=pltpu.HBM)
    out_shapes = [
        ((tok_count, width), jnp.bfloat16),
        ((tok_count, width), jnp.bfloat16),
        ((tok_count, own), jnp.bfloat16),
        ((tok_count, own), jnp.bfloat16),
        ((tok_count, own), jnp.bfloat16),
        ((tok_count, own), jnp.bfloat16),
        ((heads, LONG_LEN, LONG_LEN), jnp.bfloat16),
        ((heads, short_tok, SHORT_LEN), jnp.bfloat16),
    ]
    steps = tok_count // 256
    return pl.pallas_call(
        partial(attend_kernel, block_rows),
        out_shape=[jax.ShapeDtypeStruct(shape, dtype) for shape, dtype in out_shapes],
        in_specs=[pl.BlockSpec(memory_space=pltpu.SMEM), hbm]
        + vmem(1)
        + [hbm] * 4
        + vmem(1),
        out_specs=[hbm] * 8,
        scratch_shapes=[pltpu.VMEM(tokens.shape, jnp.bfloat16)]
        + [pltpu.VMEM(w.shape, jnp.bfloat16) for w in (w_query, w_key, w_value, w_out)]
        + [pltpu.VMEM(shape, dtype) for shape, dtype in out_shapes]
        + [
            pltpu.VMEM((heads_pad, 512), jnp.float32),
            pltpu.SemaphoreType.DMA((steps + 4,)),
            pltpu.SemaphoreType.DMA((5 + 2 * (heads // 2) + steps,)),
        ],
        compiler_params=params(24),
        cost_estimate=pl.CostEstimate(
            flops=flops, bytes_accessed=16000000, transcendentals=heads * 512 * 640
        ),
        name="attend",
    )(
        lengths,
        in_hbm(tokens),
        gain.astype(jnp.float32)[None],
        in_hbm(w_query),
        in_hbm(w_key),
        in_hbm(w_value),
        in_hbm(w_out),
        table,
    )


def attend_back_kernel(
    block_rows,
    hg_ref,
    q_ref,
    k_ref,
    v_ref,
    mixed_ref,
    long_ref,
    short_ref,
    qg_ref,
    kg_ref,
    vg_ref,
    tiles_ref,
    far_ref,
    sg_ref,
):
    tok_count = q_ref.shape[0]
    short_tok = SHORT_DEV * SHORT_LEN
    lane = lax.broadcasted_iota(jnp.int32, (1, 128), 1)
    blocks = LONG_LEN // 128
    heads_grad = hg_ref[...]
    products = heads_grad.astype(jnp.float32) * mixed_ref[...].astype(jnp.float32)
    q_t = jnp.transpose(q_ref[...])
    hg_t = jnp.transpose(heads_grad)
    qg = []
    kg_t = []
    vg_t = []
    for sub in range(2):
        own = (lane >= 64) == (sub == 1)
        rows_t = slice(64 * sub, 64 * sub + 64)
        masked = jnp.where(own, heads_grad, 0)
        delta = jnp.sum(jnp.where(own, products, 0.0), axis=1, keepdims=True)
        grads = [
            dot_nt(masked[block * 128 : block * 128 + 128], v_ref[block * 128 : block * 128 + 128, :])
            for block in range(SHORT_DEV)
        ]
        probs = short_ref[sub]
        part = probs.astype(jnp.float32) * (jnp.concatenate(grads, axis=0) - delta[:short_tok])
        same = part[:128]
        for block in range(1, SHORT_DEV):
            same = same + part[block * 128 : block * 128 + 128]
        part = part.astype(jnp.bfloat16)
        qg_parts = []
        kg_parts = []
        vg_parts = []
        for block in range(SHORT_DEV):
            rows = slice(block * 128, block * 128 + 128)
            qg_parts.append(dot_nn(part[rows], k_ref[rows, :]))
            kg_parts.append(dot_nn(q_t[rows_t, rows], part[rows]))
            vg_parts.append(dot_nn(hg_t[rows_t, rows], probs[rows]))
        above = jnp.zeros((128, 128), jnp.float32)
        below = above
        far_above = above
        far_below = above
        for start in range(0, LONG_LEN, block_rows):
            places = slice(start, start + block_rows)
            rows = slice(short_tok + start, short_tok + start + block_rows)
            part = long_ref[sub, places, :].astype(jnp.float32) * (
                dot_nt(masked[rows], v_ref[short_tok:, :]) - delta[rows]
            )
            for block in range(start // 128, (start + block_rows) // 128):
                for other in range(blocks):
                    first = block * 128 - start
                    piece = part[first : first + 128, other * 128 : other * 128 + 128]
                    if other == block:
                        same = same + piece
                    elif other == block + 1:
                        above = above + piece
                    elif other == block - 1:
                        below = below + piece
                    elif other > block:
                        far_above = far_above + piece
                    else:
                        far_below = far_below + piece
            part = part.astype(jnp.bfloat16)
            sg_ref[places, :] = part
            qg_parts.append(dot_nn(part, k_ref[short_tok:, :]))
        kg_parts.append(dot_nn(q_t[rows_t, short_tok:], sg_ref[...]))
        vg_parts.append(dot_nn(hg_t[rows_t, short_tok:], long_ref[sub]))
        qg.append(jnp.concatenate(qg_parts, axis=0))
        kg_t.append(jnp.concatenate(kg_parts, axis=1))
        vg_t.append(jnp.concatenate(vg_parts, axis=1))
        tiles_ref[sub, :, 0:128] = same
        tiles_ref[sub, :, 128:256] = above
        tiles_ref[sub, :, 256:384] = below
        far_ref[sub, 0:1, :] = jnp.sum(far_above, axis=0, keepdims=True)
        far_ref[sub, 1:2, :] = jnp.sum(far_below, axis=0, keepdims=True)
    qg_ref[...] = (jnp.where(lane < 64, qg[0], qg[1]) * 0.125).astype(jnp.bfloat16)
    kg_ref[...] = jnp.transpose(jnp.concatenate(kg_t, axis=0).astype(jnp.bfloat16))
    vg_ref[...] = jnp.transpose(jnp.concatenate(vg_t, axis=0).astype(jnp.bfloat16))


def attend_back(heads_grad, query_rows, key_rows, value_rows, mixed, long_probs, short_probs):
    tok_count, own = query_rows.shape
    pairs = own // 128
    short_tok = SHORT_DEV * SHORT_LEN
    rows_spec = pl.BlockSpec((tok_count, 128), lambda pair: (0, pair))
    flops = 10 * pairs * 2 * (512 * 512 + short_tok * 128) * 64
    return pl.pallas_call(
        partial(attend_back_kernel, LONG_LEN),
        grid=(pairs,),
        out_shape=[jax.ShapeDtypeStruct((tok_count, own), jnp.bfloat16)] * 3
        + [
            jax.ShapeDtypeStruct((pairs * 2, 128, 384), jnp.float32),
            jax.ShapeDtypeStruct((pairs * 2, 2, 128), jnp.float32),
        ],
        in_specs=[rows_spec] * 5
        + [
            pl.BlockSpec((2, LONG_LEN, LONG_LEN), lambda pair: (pair, 0, 0)),
            pl.BlockSpec((2, short_tok, SHORT_LEN), lambda pair: (pair, 0, 0)),
        ],
        out_specs=[rows_spec] * 3
        + [
            pl.BlockSpec((2, 128, 384), lambda pair: (pair, 0, 0)),
            pl.BlockSpec((2, 2, 128), lambda pair: (pair, 0, 0)),
        ],
        scratch_shapes=[pltpu.VMEM((LONG_LEN, LONG_LEN), jnp.bfloat16)],
        compiler_params=params(24),
        cost_estimate=pl.CostEstimate(flops=flops, bytes_accessed=12000000, transcendentals=0),
        name="attend_back",
    )(
        in_hbm(heads_grad),
        in_hbm(query_rows),
        in_hbm(key_rows),
        in_hbm(value_rows),
        in_hbm(mixed),
        in_hbm(long_probs),
        in_hbm(short_probs),
    )


def table_kernel(tiles_ref, far_ref, out_ref):
    row = lax.broadcasted_iota(jnp.int32, (128, 1), 0)
    heads = tiles_ref.shape[0]
    for head in range(heads):
        tile = jnp.concatenate(
            [
                tiles_ref[head, :, 0:256],
                jnp.zeros((128, 128), jnp.float32),
                tiles_ref[head, :, 256:384],
            ],
            axis=1,
        )
        for bit in range(7):
            moved = pltpu.roll(tile, 512 - (1 << bit), 1)
            tile = jnp.where(((row >> bit) & 1) == 1, moved, tile)
        out_ref[head : head + 1, 0:512] = jnp.sum(tile, axis=0, keepdims=True)
        out_ref[head : head + 1, 512:640] = far_ref[head, 0:1, :]
        out_ref[head : head + 1, 640:768] = far_ref[head, 1:2, :]


def table_diagonals(tiles, far):
    heads = tiles.shape[0]
    return pl.pallas_call(
        table_kernel,
        out_shape=jax.ShapeDtypeStruct((heads, 768), jnp.float32),
        in_specs=vmem(2),
        out_specs=vmem(1)[0],
        compiler_params=params(16),
        cost_estimate=pl.CostEstimate(flops=heads * 128 * 512 * 14, bytes_accessed=1300000, transcendentals=0),
        name="table",
    )(tiles, far)


def table_from(diag, bucket_count):
    lane = jnp.arange(768, dtype=jnp.int32)
    offset = jnp.where(lane < 256, lane, lane - 512)
    offset = jnp.where(lane >= 640, -256, jnp.where(lane >= 512, 256, offset))
    hot = (diagonal_buckets(offset)[:, None] == jnp.arange(bucket_count)[None, :]).astype(jnp.float32)
    return lax.dot_general(
        hot, diag, (((0,), (1,)), ((), ())), precision=highest, preferred_element_type=jnp.float32
    )


def dispatch_rows(send_ref, slot_row, half_rows):
    slots = send_ref.shape[0]
    tok_count = slot_row.shape[1]
    for base in range(0, slots, 256):
        span = min(256, slots - base)
        place = lax.broadcasted_iota(jnp.int32, (span, tok_count), 0) + base
        hot = jnp.where(place == slot_row, 1.0, 0.0).astype(jnp.bfloat16)
        send_ref[base : base + span, :] = dot_nn(hot, half_rows).astype(jnp.bfloat16)


def half_lanes(core, half):
    return pl.ds(pl.multiple_of(core * half, half), half)


def route_kernel(capacity, where_ref, routes_ref, grad_ref, row_ref, col_ref, send_ref):
    tok_count = routes_ref.shape[1]
    slots, half = send_ref.shape
    experts = slots // capacity
    routes = routes_ref[...]
    expert = lax.broadcasted_iota(jnp.int32, (experts, tok_count), 0)
    lane = lax.broadcasted_iota(jnp.int32, (1, tok_count), 1)
    hot = jnp.where(expert == routes, 1.0, 0.0)
    total = hot
    step = 1
    while step < tok_count:
        total = total + jnp.where(lane >= step, pltpu.roll(total, step, 1), 0.0)
        step *= 2
    before = jnp.sum(hot * total, axis=0, keepdims=True).astype(jnp.int32) - 1
    slot = jnp.where(before < capacity, routes * capacity + before, slots)
    row_ref[...] = slot
    wide = jnp.broadcast_to(slot.astype(jnp.float32), (128, tok_count))
    col_ref[...] = jnp.transpose(wide).astype(jnp.int32)
    dispatch_rows(send_ref, slot, grad_ref[:, half_lanes(where_ref[0], half)])


def route(where, routes, out_grad, experts, capacity):
    tok_count, width = out_grad.shape
    slots = experts * capacity
    return pl.pallas_call(
        partial(route_kernel, capacity),
        out_shape=[
            jax.ShapeDtypeStruct((1, tok_count), jnp.int32),
            jax.ShapeDtypeStruct((tok_count, 128), jnp.int32),
            jax.ShapeDtypeStruct((slots, width // 2), jnp.bfloat16),
        ],
        in_specs=[pl.BlockSpec(memory_space=pltpu.SMEM)] + vmem(2),
        out_specs=vmem(3),
        compiler_params=params(),
        cost_estimate=pl.CostEstimate(
            flops=slots * tok_count * width, bytes_accessed=4000000, transcendentals=0
        ),
        name="route",
    )(where, routes.reshape(1, tok_count), out_grad)


def second_kernel(
    where_ref, tokens_ref, own_ref, other_ref, gain_ref, row_ref, residual_ref, send_ref, second_ref
):
    step = pl.program_id(0)
    tile = tokens_ref.shape[0]
    half = send_ref.shape[1]
    residual = tokens_ref[...].astype(jnp.float32) + (
        own_ref[...].astype(jnp.float32) + other_ref[...].astype(jnp.float32)
    )
    residual_ref[...] = residual
    second_ref[pl.ds(pl.multiple_of(step * tile, tile), tile), :] = (
        residual * inverse_rms(residual) * gain_ref[...]
    ).astype(jnp.bfloat16)

    @pl.when(step == pl.num_programs(0) - 1)
    def _():
        dispatch_rows(send_ref, row_ref[...], second_ref[:, half_lanes(where_ref[0], half)])


def second_rows(where, tokens, own, other, gain, slot_row, slots):
    tok_count, width = tokens.shape
    tile = 256
    rows = pl.BlockSpec((tile, width), lambda step: (step, 0))
    return pl.pallas_call(
        second_kernel,
        grid=(tok_count // tile,),
        out_shape=[
            jax.ShapeDtypeStruct((tok_count, width), jnp.float32),
            jax.ShapeDtypeStruct((slots, width // 2), jnp.bfloat16),
        ],
        in_specs=[
            pl.BlockSpec(memory_space=pltpu.SMEM),
            rows,
            rows,
            rows,
            pl.BlockSpec((1, width), lambda step: (0, 0)),
            pl.BlockSpec((1, tok_count), lambda step: (0, 0)),
        ],
        out_specs=[rows, pl.BlockSpec((slots, width // 2), lambda step: (0, 0))],
        scratch_shapes=[pltpu.VMEM((tok_count, width), jnp.bfloat16)],
        compiler_params=params(),
        cost_estimate=pl.CostEstimate(
            flops=slots * tok_count * width, bytes_accessed=13000000, transcendentals=0
        ),
        name="second",
    )(where, tokens, own, other, gain.astype(jnp.float32)[None], slot_row)


def hidden_grad_kernel(where_ref, own_ref, other_ref, outer_ref, out_ref):
    half = own_ref.shape[1]
    core = where_ref[0]
    out_ref[...] = dot_nt(own_ref[...], outer_ref[:, half_lanes(core, half)]) + dot_nt(
        other_ref[...], outer_ref[:, half_lanes(1 - core, half)]
    )


def hidden_grad_of(where, own, other, outer):
    slots, half = own.shape
    hidden = outer.shape[0]
    tile = 256
    rows = pl.BlockSpec((tile, half), lambda step: (step, 0))
    return pl.pallas_call(
        hidden_grad_kernel,
        grid=(slots // tile,),
        out_shape=jax.ShapeDtypeStruct((slots, hidden), jnp.float32),
        in_specs=[
            pl.BlockSpec(memory_space=pltpu.SMEM),
            rows,
            rows,
            pl.BlockSpec(outer.shape, lambda step: (0, 0)),
        ],
        out_specs=pl.BlockSpec((tile, hidden), lambda step: (step, 0)),
        compiler_params=params(),
        cost_estimate=pl.CostEstimate(
            flops=4 * slots * half * hidden, bytes_accessed=12000000, transcendentals=0
        ),
        name="hidden_grad",
    )(where, own, other, outer)


def expert_kernel(
    where_ref,
    own_ref,
    other_ref,
    grad_own_ref,
    grad_other_ref,
    hg_ref,
    inner_ref,
    router_ref,
    hidden_ref,
    pre_grad_ref,
    keep_ref,
    send_ref,
    arrived_ref,
    gated_ref,
    logit_ref,
):
    core = where_ref[0]
    half = own_ref.shape[1]
    experts = router_ref.shape[1]
    own_lanes = half_lanes(core, half)
    other_lanes = half_lanes(1 - core, half)
    own = own_ref[...]
    other = other_ref[...]
    arrived_ref[:, own_lanes] = own
    arrived_ref[:, other_lanes] = other
    logits = dot_nn(own, router_ref[own_lanes, :]) + dot_nn(other, router_ref[other_lanes, :])
    exp_logit = jnp.exp(logits - jnp.max(logits, axis=1, keepdims=True))
    probs = exp_logit * (1.0 / jnp.sum(exp_logit, axis=1, keepdims=True))
    hit = jnp.where(
        lax.broadcasted_iota(jnp.int32, (1, experts), 1) == where_ref[1], 1.0, 0.0
    )
    gate = jnp.sum(probs * hit, axis=1, keepdims=True)
    gated_ref[:, own_lanes] = (gate * grad_own_ref[...].astype(jnp.float32)).astype(jnp.bfloat16)
    gated_ref[:, other_lanes] = (gate * grad_other_ref[...].astype(jnp.float32)).astype(jnp.bfloat16)
    pre = dot_nn(own, inner_ref[own_lanes, :]) + dot_nn(other, inner_ref[other_lanes, :])
    hg = hg_ref[...]
    square = pre * pre
    curve = 0.7978845608028654
    bend = jnp.tanh(pre * (curve + (curve * 0.044715) * square))
    grown = 0.5 + 0.5 * bend
    hidden = (pre * grown).astype(jnp.bfloat16)
    hidden_ref[...] = hidden
    gate_grad = jnp.sum(hidden.astype(jnp.float32) * hg, axis=1, keepdims=True)
    slope = grown + (0.5 * pre) * (1.0 - bend * bend) * (curve + (3 * curve * 0.044715) * square)
    pre_grad = (slope * (gate * hg)).astype(jnp.bfloat16)
    pre_grad_ref[...] = pre_grad
    logit = (probs * (gate_grad * (hit - gate))).astype(jnp.bfloat16)
    logit_ref[...] = logit
    send_ref[...] = (
        dot_nt(pre_grad, inner_ref[other_lanes, :]) + dot_nt(logit, router_ref[other_lanes, :])
    ).astype(jnp.bfloat16)
    keep_ref[...] = dot_nt(pre_grad, inner_ref[own_lanes, :]) + dot_nt(
        logit, router_ref[own_lanes, :]
    )


def expert(where, own, other, grad_own, grad_other, hidden_grad, inner, router):
    slots, half = own.shape
    width, hidden = inner.shape
    experts = router.shape[1]
    tile = 256
    halves = pl.BlockSpec((tile, half), lambda step: (step, 0))
    wide = pl.BlockSpec((tile, width), lambda step: (step, 0))
    units = pl.BlockSpec((tile, hidden), lambda step: (step, 0))
    return pl.pallas_call(
        expert_kernel,
        grid=(slots // tile,),
        out_shape=[
            jax.ShapeDtypeStruct((slots, hidden), jnp.bfloat16),
            jax.ShapeDtypeStruct((slots, hidden), jnp.bfloat16),
            jax.ShapeDtypeStruct((slots, half), jnp.float32),
            jax.ShapeDtypeStruct((slots, half), jnp.bfloat16),
            jax.ShapeDtypeStruct((slots, width), jnp.bfloat16),
            jax.ShapeDtypeStruct((slots, width), jnp.bfloat16),
            jax.ShapeDtypeStruct((slots, experts), jnp.bfloat16),
        ],
        in_specs=[
            pl.BlockSpec(memory_space=pltpu.SMEM),
            halves,
            halves,
            halves,
            halves,
            units,
            pl.BlockSpec(inner.shape, lambda step: (0, 0)),
            pl.BlockSpec(router.shape, lambda step: (0, 0)),
        ],
        out_specs=[
            units,
            units,
            halves,
            halves,
            wide,
            wide,
            pl.BlockSpec((tile, experts), lambda step: (step, 0)),
        ],
        compiler_params=params(),
        cost_estimate=pl.CostEstimate(
            flops=4 * slots * width * hidden, bytes_accessed=30000000, transcendentals=slots * hidden
        ),
        name="expert",
    )(where, own, other, grad_own, grad_other, hidden_grad, inner, router)


def expert_out_kernel(where_ref, hidden_ref, outer_ref, keep_ref, send_ref):
    core = where_ref[0]
    half = keep_ref.shape[1]
    hidden = hidden_ref[...]
    send_ref[...] = dot_nn(hidden, outer_ref[:, half_lanes(1 - core, half)]).astype(jnp.bfloat16)
    keep_ref[...] = dot_nn(hidden, outer_ref[:, half_lanes(core, half)])


def expert_out_of(where, hidden, outer):
    slots, units = hidden.shape
    half = outer.shape[1] // 2
    tile = 256
    halves = pl.BlockSpec((tile, half), lambda step: (step, 0))
    return pl.pallas_call(
        expert_out_kernel,
        grid=(slots // tile,),
        out_shape=[
            jax.ShapeDtypeStruct((slots, half), jnp.float32),
            jax.ShapeDtypeStruct((slots, half), jnp.bfloat16),
        ],
        in_specs=[
            pl.BlockSpec(memory_space=pltpu.SMEM),
            pl.BlockSpec((tile, units), lambda step: (step, 0)),
            pl.BlockSpec(outer.shape, lambda step: (0, 0)),
        ],
        out_specs=[halves, halves],
        compiler_params=params(),
        cost_estimate=pl.CostEstimate(
            flops=4 * slots * half * units, bytes_accessed=9000000, transcendentals=0
        ),
        name="expert_out",
    )(where, hidden, outer)


def residual_back_kernel(
    where_ref,
    col_ref,
    own_ref,
    other_ref,
    residual_ref,
    grad_ref,
    gain_ref,
    wo_ref,
    out_ref,
    attn_ref,
    heads_ref,
    gain_out_ref,
    whole_ref,
):
    core = where_ref[0]
    slots, half = own_ref.shape
    tile = residual_ref.shape[0]
    place = lax.broadcasted_iota(jnp.int32, (tile, slots), 1)
    hot = jnp.where(place == col_ref[:, :1], 1.0, 0.0).astype(jnp.bfloat16)
    whole_ref[:, half_lanes(core, half)] = dot_nn(hot, own_ref[...])
    whole_ref[:, half_lanes(1 - core, half)] = dot_nn(hot, other_ref[...])
    ybar = whole_ref[...]
    values = residual_ref[...]
    scale = inverse_rms(values)
    scaled = values * scale
    pulled = ybar * gain_ref[...]

    @pl.when(pl.program_id(0) == 0)
    def _():
        gain_out_ref[...] = jnp.zeros_like(gain_out_ref)

    gain_out_ref[...] += jnp.sum(ybar * scaled, axis=0, keepdims=True)
    back = scale * (pulled - scaled * jnp.mean(pulled * scaled, axis=1, keepdims=True))
    out = back + grad_ref[...].astype(jnp.float32)
    out_ref[...] = out
    attn = out.astype(jnp.bfloat16)
    attn_ref[...] = attn
    heads_ref[...] = dot_nt(attn, wo_ref[...]).astype(jnp.bfloat16)


def residual_back(where, slot_col, own, other, residual, out_grad, gain, w_out):
    tok_count, width = residual.shape
    slots, half = own.shape
    heads_width = w_out.shape[0]
    tile = 256
    rows = pl.BlockSpec((tile, width), lambda step: (step, 0))
    whole = lambda shape: pl.BlockSpec(shape, lambda step: (0, 0))
    return pl.pallas_call(
        residual_back_kernel,
        grid=(tok_count // tile,),
        out_shape=[
            jax.ShapeDtypeStruct((tok_count, width), jnp.float32),
            jax.ShapeDtypeStruct((tok_count, width), jnp.bfloat16),
            jax.ShapeDtypeStruct((tok_count, heads_width), jnp.bfloat16),
            jax.ShapeDtypeStruct((1, width), jnp.float32),
        ],
        in_specs=[
            pl.BlockSpec(memory_space=pltpu.SMEM),
            pl.BlockSpec((tile, 128), lambda step: (step, 0)),
            whole(own.shape),
            whole(other.shape),
            rows,
            rows,
            whole((1, width)),
            whole(w_out.shape),
        ],
        out_specs=[
            rows,
            rows,
            pl.BlockSpec((tile, heads_width), lambda step: (step, 0)),
            whole((1, width)),
        ],
        scratch_shapes=[pltpu.VMEM((tile, width), jnp.float32)],
        compiler_params=params(),
        cost_estimate=pl.CostEstimate(
            flops=tok_count * width * (2 * slots + 2 * heads_width),
            bytes_accessed=14000000,
            transcendentals=0,
        ),
        name="residual_back",
    )(where, slot_col, own, other, residual, out_grad, gain.astype(jnp.float32)[None], w_out)


def output_kernel(
    capacity, where_ref, col_ref, returned_ref, residual_ref, gain_ref, router_ref, out_ref
):
    slots, half = returned_ref.shape
    tile = residual_ref.shape[0]
    experts = router_ref.shape[1]
    col = col_ref[:, :1]
    place = lax.broadcasted_iota(jnp.int32, (tile, slots), 1)
    hot = jnp.where(place == col, 1.0, 0.0).astype(jnp.bfloat16)
    token_out = dot_nn(hot, returned_ref[...])
    residual = residual_ref[...]
    second = (residual * inverse_rms(residual) * gain_ref[...]).astype(jnp.bfloat16)
    logits = dot_nn(second, router_ref[...])
    exp_logit = jnp.exp(logits - jnp.max(logits, axis=1, keepdims=True))
    first = lax.broadcasted_iota(jnp.int32, (1, experts), 1) * capacity
    hit = jnp.where((col >= first) & (col < first + capacity), exp_logit, 0.0)
    gate = jnp.sum(hit, axis=1, keepdims=True) / jnp.sum(exp_logit, axis=1, keepdims=True)
    own = residual_ref[:, half_lanes(where_ref[0], half)]
    out_ref[...] = (own + gate * token_out).astype(jnp.bfloat16)


def output_of(where, slot_col, returned, residual, gain, router, capacity):
    tok_count, width = residual.shape
    slots, half = returned.shape
    tile = 256
    whole = lambda shape: pl.BlockSpec(shape, lambda step: (0, 0))
    return pl.pallas_call(
        partial(output_kernel, capacity),
        grid=(tok_count // tile,),
        out_shape=jax.ShapeDtypeStruct((tok_count, half), jnp.bfloat16),
        in_specs=[
            pl.BlockSpec(memory_space=pltpu.SMEM),
            pl.BlockSpec((tile, 128), lambda step: (step, 0)),
            whole(returned.shape),
            pl.BlockSpec((tile, width), lambda step: (step, 0)),
            whole((1, width)),
            whole(router.shape),
        ],
        out_specs=pl.BlockSpec((tile, half), lambda step: (step, 0)),
        compiler_params=params(),
        cost_estimate=pl.CostEstimate(
            flops=2 * tok_count * half * slots, bytes_accessed=6000000, transcendentals=0
        ),
        name="output",
    )(where, slot_col, returned, residual, gain.astype(jnp.float32)[None], router)


def normed_back_kernel(qg_ref, kg_ref, vg_ref, wq_ref, wk_ref, wv_ref, out_ref):
    tile = 256
    for start in range(0, out_ref.shape[0], tile):
        rows = slice(start, start + tile)
        out_ref[rows, :] = (
            dot_nt(qg_ref[rows, :], wq_ref[...])
            + dot_nt(kg_ref[rows, :], wk_ref[...])
            + dot_nt(vg_ref[rows, :], wv_ref[...])
        ).astype(jnp.bfloat16)


def normed_back(qg, kg, vg, w_query, w_key, w_value):
    tok_count, own = qg.shape
    width = w_query.shape[0]
    return pl.pallas_call(
        normed_back_kernel,
        out_shape=jax.ShapeDtypeStruct((tok_count, width), jnp.bfloat16),
        in_specs=vmem(6),
        out_specs=vmem(1)[0],
        compiler_params=params(16),
        cost_estimate=pl.CostEstimate(
            flops=6 * tok_count * own * width, bytes_accessed=6000000, transcendentals=0
        ),
        name="normed_back",
    )(qg, kg, vg, w_query, w_key, w_value)


def input_back_kernel(tokens_ref, own_ref, other_ref, gain_ref, residual_ref, out_ref):
    ybar = own_ref[...].astype(jnp.float32) + other_ref[...].astype(jnp.float32)
    values = tokens_ref[...].astype(jnp.float32)
    scale = inverse_rms(values)
    scaled = values * scale
    pulled = ybar * gain_ref[...]
    out_ref[...] = residual_ref[...] + scale * (
        pulled - scaled * jnp.mean(pulled * scaled, axis=1, keepdims=True)
    )


def input_back(tokens, own, other, gain, residual_grad):
    tok_count, width = tokens.shape
    tile = 256
    rows = pl.BlockSpec((tile, width), lambda step: (step, 0))
    return pl.pallas_call(
        input_back_kernel,
        grid=(tok_count // tile,),
        out_shape=jax.ShapeDtypeStruct((tok_count, width), jnp.float32),
        in_specs=[rows, rows, rows, pl.BlockSpec((1, width), lambda step: (0, 0)), rows],
        out_specs=rows,
        compiler_params=params(),
        cost_estimate=pl.CostEstimate(
            flops=10 * tok_count * width, bytes_accessed=11000000, transcendentals=0
        ),
        name="input_back",
    )(tokens, own, other, gain.astype(jnp.float32)[None], residual_grad)


def weights_kernel(
    normed_ref, qg_ref, kg_ref, vg_ref, mixed_ref, attn_ref, wq_ref, wk_ref, wv_ref, gain_ref,
    stack_ref, gain_out_ref,
):
    width = normed_ref.shape[1]
    own = mixed_ref.shape[1]
    tile = 256
    for start in range(0, width, tile):
        rows = slice(start, start + tile)
        normed = normed_ref[:, rows]
        total = jnp.zeros((tile, 1), jnp.float32)
        for index, (grad_ref, w_ref) in enumerate(((qg_ref, wq_ref), (kg_ref, wk_ref), (vg_ref, wv_ref))):
            grad = contract_rows(normed, grad_ref[...])
            total = total + jnp.sum(grad * w_ref[rows, :].astype(jnp.float32), axis=1, keepdims=True)
            stack_ref[index * width + start : index * width + start + tile, :] = grad.astype(jnp.bfloat16)
        gain_out_ref[:, rows] = jnp.transpose(jnp.broadcast_to(total, (tile, 128)))[:8, :]
    gain_out_ref[...] = gain_out_ref[...] / gain_ref[...]
    for start in range(0, own, 128):
        grad = contract_rows(mixed_ref[:, start : start + 128], attn_ref[...]).astype(jnp.bfloat16)
        for part in range(width // own):
            base = 3 * width + part * own + start
            stack_ref[base : base + 128, :] = grad[:, part * own : part * own + own]


def weight_grads(normed, qg, kg, vg, mixed, attn_grad, w_query, w_key, w_value, gain):
    tok_count, width = normed.shape
    own = qg.shape[1]
    return pl.pallas_call(
        weights_kernel,
        out_shape=[
            jax.ShapeDtypeStruct((4 * width, own), jnp.bfloat16),
            jax.ShapeDtypeStruct((8, width), jnp.float32),
        ],
        in_specs=vmem(10),
        out_specs=vmem(2),
        compiler_params=params(),
        cost_estimate=pl.CostEstimate(
            flops=8 * tok_count * width * own, bytes_accessed=12000000, transcendentals=0
        ),
        name="weight_grads",
    )(normed, qg, kg, vg, mixed, attn_grad, w_query, w_key, w_value, gain.astype(jnp.float32)[None])


def split_kernel(count, bits_ref, *refs):
    for part in range(count):
        whole = refs[part]
        span = whole.shape[0] // 2
        mine = bits_ref[part]
        refs[count + part][...] = whole[pl.ds((1 - mine) * span, span)]
        refs[2 * count + part][...] = whole[pl.ds(mine * span, span)]


def split(bits, parts):
    count = len(parts)
    halves = [jax.ShapeDtypeStruct((p.shape[0] // 2,) + p.shape[1:], p.dtype) for p in parts]
    out = pl.pallas_call(
        partial(split_kernel, count),
        out_shape=halves + halves,
        in_specs=[pl.BlockSpec(memory_space=pltpu.SMEM)] + vmem(count),
        out_specs=vmem(2 * count),
        compiler_params=params(16),
        name="split",
    )(bits, *parts)
    return out[:count], out[count:]


def fold_kernel(count, bits_ref, *refs):
    kept, got, sent, keep = (refs[count * k : count * (k + 1)] for k in range(4))
    for part in range(count):
        span = kept[part].shape[0] // 2
        mine = bits_ref[part]
        for ref, start in ((sent[part], (1 - mine) * span), (keep[part], mine * span)):
            rows = pl.ds(start, span)
            ref[...] = (
                kept[part][rows].astype(jnp.float32) + got[part][rows].astype(jnp.float32)
            ).astype(jnp.bfloat16)


def fold(bits, kept, got):
    count = len(kept)
    halves = [jax.ShapeDtypeStruct((p.shape[0] // 2,) + p.shape[1:], p.dtype) for p in kept]
    out = pl.pallas_call(
        partial(fold_kernel, count),
        out_shape=halves + halves,
        in_specs=[pl.BlockSpec(memory_space=pltpu.SMEM)] + vmem(2 * count),
        out_specs=vmem(2 * count),
        compiler_params=params(16),
        name="fold",
    )(bits, *kept, *got)
    return out[:count], out[count:]


def join_kernel(count, bits_ref, *refs):
    own, got, out = (refs[count * k : count * (k + 1)] for k in range(3))
    for part in range(count):
        span = own[part].shape[0]
        mine = bits_ref[part]
        out[part][pl.ds(mine * span, span)] = own[part][...]
        out[part][pl.ds((1 - mine) * span, span)] = got[part][...]


def join(bits, own, got):
    count = len(own)
    return pl.pallas_call(
        partial(join_kernel, count),
        out_shape=[jax.ShapeDtypeStruct((p.shape[0] * 2,) + p.shape[1:], p.dtype) for p in own],
        in_specs=[pl.BlockSpec(memory_space=pltpu.SMEM)] + vmem(2 * count),
        out_specs=vmem(count),
        compiler_params=params(16),
        name="join",
    )(bits, *own, *got)


def pack_kernel(count, *refs):
    kept, got = refs[:count], refs[count : 2 * count]
    span = kept[0].shape[0]
    for part in range(count):
        refs[-1][part * span : (part + 1) * span] = (
            kept[part][...].astype(jnp.float32) + got[part][...].astype(jnp.float32)
        ).astype(jnp.bfloat16)


def pack(kept, got):
    count = len(kept)
    shape = kept[0].shape
    return pl.pallas_call(
        partial(pack_kernel, count),
        out_shape=jax.ShapeDtypeStruct((count * shape[0],) + shape[1:], jnp.bfloat16),
        in_specs=vmem(2 * count),
        out_specs=vmem(1)[0],
        compiler_params=params(16),
        name="pack",
    )(*kept, *got)


def unpack_kernel(own_ref, got_ref, *out):
    span = out[0].shape[0]
    for part, ref in enumerate(out):
        rows = slice(part * span, (part + 1) * span)
        ref[...] = (own_ref[rows].astype(jnp.float32) + got_ref[rows].astype(jnp.float32)).astype(
            jnp.bfloat16
        )


def unpack(own, got, count):
    shape = (own.shape[0] // count,) + own.shape[1:]
    return pl.pallas_call(
        unpack_kernel,
        out_shape=[jax.ShapeDtypeStruct(shape, jnp.bfloat16)] * count,
        in_specs=vmem(2),
        out_specs=vmem(count),
        compiler_params=params(16),
        name="unpack",
    )(own, got)


def finish_kernel(count, bits_ref, *refs):
    own, got = refs[:count], refs[count : 2 * count]
    query_ref, key_ref, value_ref, out_ref, whole_ref = refs[2 * count :]
    span = own[0].shape[0]
    rows = 2 * span * own[0].shape[1]
    width, lanes = query_ref.shape
    for part in range(count):
        mine = bits_ref[part]
        whole_ref[pl.ds(mine * span, span)] = own[part][...].astype(jnp.float32)
        whole_ref[pl.ds((1 - mine) * span, span)] = got[part][...].astype(jnp.float32)
        flat = whole_ref[...].reshape(rows, lanes)
        for index, ref in enumerate((query_ref, key_ref, value_ref)):
            first = max(index * width, part * rows)
            last = min((index + 1) * width, (part + 1) * rows)
            if first < last:
                ref[first - index * width : last - index * width, :] = flat[
                    first - part * rows : last - part * rows
                ]
        for index in range(width // lanes):
            base = 3 * width + index * lanes
            first = max(base, part * rows)
            last = min(base + lanes, (part + 1) * rows)
            if first < last:
                out_ref[first - base : last - base, index * lanes : (index + 1) * lanes] = flat[
                    first - part * rows : last - part * rows
                ]


def finish(bits, own, got, width):
    count = len(own)
    span, rows, lanes = own[0].shape
    return pl.pallas_call(
        partial(finish_kernel, count),
        out_shape=[jax.ShapeDtypeStruct((width, lanes), jnp.float32)] * 3
        + [jax.ShapeDtypeStruct((lanes, width), jnp.float32)],
        in_specs=[pl.BlockSpec(memory_space=pltpu.SMEM)] + vmem(2 * count),
        out_specs=vmem(4),
        scratch_shapes=[pltpu.VMEM((2 * span, rows, lanes), jnp.float32)],
        compiler_params=params(24),
        name="finish",
    )(bits, *own, *got)


def swap_heads(rows):
    return lax.ppermute(rows, "heads", [(0, 1), (1, 0)])


def trade(rows, bit):
    count = lax.axis_size("seq")
    return lax.ppermute(rows, "seq", [(i, i ^ (1 << bit)) for i in range(count)])


def together(*groups):
    return lax.optimization_barrier(groups)


def contract_rows(left, right):
    return lax.dot_general(
        left, right, (((0,), (0,)), ((), ())), preferred_element_type=jnp.float32
    )


def on_device(
    tokens,
    gain_attn,
    w_query,
    w_key,
    w_value,
    w_out,
    bias_table,
    gain_ffn,
    w_router,
    w_inner,
    w_outer,
    routes,
    seq_lengths,
    out_grad,
):
    tok_count, width = tokens.shape
    bucket_count = bias_table.shape[0]
    experts = w_router.shape[1]
    capacity = max(2, 5 * tok_count // (4 * experts))
    senders = lax.axis_size("seq")
    bits = list(range(senders.bit_length() - 1))
    slots = experts * capacity
    half = width // 2
    own = w_query.shape[1]
    where = jnp.stack([lax.axis_index("heads"), lax.axis_index("seq")]).astype(jnp.int32)

    def exchange(rows):
        return lax.all_to_all(
            rows.reshape(senders, capacity, half), "seq", split_axis=0, concat_axis=0, tiled=True
        ).reshape(slots, half)

    def summed(keep, send):
        return (keep + swap_heads(send).astype(jnp.float32)).astype(jnp.bfloat16)

    slot_row, slot_col, grad_sent = route(where, routes, out_grad, experts, capacity)
    grad_sent, tokens = together(grad_sent, tokens)
    grad_own = exchange(grad_sent)
    attn_part, normed, query_rows, key_rows, value_rows, mixed, long_probs, short_probs = attend(
        seq_lengths, tokens, gain_attn, w_query, w_key, w_value, w_out, bias_table
    )
    attn_part, grad_own = together(attn_part, grad_own)
    residual, second_sent = second_rows(
        where, tokens, attn_part, swap_heads(attn_part), gain_ffn, slot_row, slots
    )
    arrived_own = exchange(second_sent)

    inner = w_inner[0]
    outer = w_outer[0]
    grad_other = swap_heads(grad_own)
    hidden_grad = hidden_grad_of(where, grad_own, grad_other, outer)
    arrived_own, hidden_grad = together(arrived_own, hidden_grad)
    arrived_other = swap_heads(arrived_own)
    hidden, pre_grad, keep, send, arrived, gated, logit_grad = expert(
        where, arrived_own, arrived_other, grad_own, grad_other, hidden_grad, inner, w_router
    )
    back_sum, hidden, pre_grad, logit_grad = together(
        summed(keep, send), hidden, pre_grad, logit_grad
    )
    back_own = exchange(back_sum)
    out_keep, out_send = expert_out_of(where, hidden, outer)
    out_sum = summed(out_keep, out_send)
    router_part = contract_rows(logit_grad, arrived)
    outer_grad = contract_rows(hidden, gated)
    inner_grad = contract_rows(arrived, pre_grad)
    back_own, out_sum, router_part, outer_grad, inner_grad = together(
        back_own, out_sum, router_part, outer_grad, inner_grad
    )
    returned = exchange(out_sum)

    residual_grad, attn_grad, heads_grad, gain_two_part = residual_back(
        where, slot_col, back_own, swap_heads(back_own), residual, out_grad, gain_ffn, w_out
    )
    query_grad, key_grad, value_grad, tiles, far = attend_back(
        heads_grad, query_rows, key_rows, value_rows, mixed, long_probs, short_probs
    )
    query_grad, returned = together(query_grad, returned)
    stack, gain_one_part = weight_grads(
        normed, query_grad, key_grad, value_grad, mixed, attn_grad, w_query, w_key, w_value, gain_attn
    )
    stack, query_grad, tiles = together(stack, query_grad, tiles)

    depth = len(bits) - 1
    turns = [bits[k * depth // 3 : depth] + bits[: k * depth // 3] for k in range(3)]
    place = lax.axis_index("seq")
    mine = [jnp.stack([(place >> turn[k]) & 1 for turn in turns]).astype(jnp.int32) for k in range(depth)]
    rows = stack.shape[0] // 3
    parts = [
        stack[k * rows : (k + 1) * rows].reshape(senders, rows // senders, own) for k in range(3)
    ]

    def trades(arrays, k):
        return [trade(array, turn[k]) for array, turn in zip(arrays, turns)]

    table_grad = table_from(table_diagonals(tiles, far), bucket_count)
    pair_part = jnp.concatenate([router_part, gain_one_part[:1]], axis=0)
    table_row = jnp.pad(table_grad.reshape(1, -1), ((0, 0), (0, width - table_grad.size)))
    own_part = jnp.concatenate([gain_two_part, table_row], axis=0)
    sent, kept = split(mine[0], parts)
    for k in range(depth):
        got = trades(sent, k)
        if k == 0:
            pair_part = pair_part + swap_heads(pair_part)
            small = jnp.concatenate([pair_part, own_part], axis=0)
            output = output_of(where, slot_col, returned, residual, gain_ffn, w_router, capacity)
            got, output, small = together(got, output, small)
        else:
            small = small + trade(small, bits[k - 1])
            if k == 1:
                normed_part = normed_back(
                    query_grad, key_grad, value_grad, w_query, w_key, w_value
                )
                got, normed_part, small = together(got, normed_part, small)
            else:
                got, small = together(got, small)
        if k + 1 < depth:
            sent, kept = fold(mine[k + 1], kept, got)
    packed = pack(kept, got)
    got = trade(packed, bits[-1])
    normed_other = swap_heads(normed_part)
    for bit in bits[depth - 1 : -1]:
        small = small + trade(small, bit)
    got, small, normed_other = together(got, small, normed_other)
    summed_parts = unpack(packed, got, 3)
    for k in reversed(range(1, depth)):
        summed_parts = join(mine[k], summed_parts, trades(summed_parts, k))
    got = trades(summed_parts, 0)
    small = small + trade(small, bits[-1])
    input_grad = input_back(tokens, normed_part, normed_other, gain_attn, residual_grad)
    got, input_grad, small = together(got, input_grad, small)
    query_w_grad, key_w_grad, value_w_grad, out_w_grad = finish(mine[0], summed_parts, got, width)
    return (
        output,
        input_grad,
        small[experts],
        query_w_grad,
        key_w_grad,
        value_w_grad,
        out_w_grad,
        small[experts + 2, : table_grad.size].reshape(table_grad.shape),
        small[experts + 1],
        small[:experts].T,
        inner_grad[None],
        outer_grad[None],
    )


def solution(mesh):
    in_specs = (
        P("seq", None),
        P(),
        P(None, "heads"),
        P(None, "heads"),
        P(None, "heads"),
        P("heads", None),
        P(None, "heads"),
        P(),
        P(),
        P("seq", None, "heads"),
        P("seq", "heads", None),
        P("seq", None),
        P("seq"),
        P("seq", None),
    )
    out_specs = (
        P("seq", "heads"),
        P("seq", None),
        P(),
        P(None, "heads"),
        P(None, "heads"),
        P(None, "heads"),
        P("heads", None),
        P(None, "heads"),
        P(),
        P(),
        P("seq", None, "heads"),
        P("seq", "heads", None),
    )
    return jax.shard_map(
        on_device, mesh=mesh, in_specs=in_specs, out_specs=out_specs, check_vma=False
    )
```

```python
from functools import partial

import jax
import jax.numpy as jnp
from jax import lax
from jax.experimental import pallas as pl
from jax.experimental.pallas import tpu as pltpu
from jax.sharding import PartitionSpec as P

SHORT_LEN = 128
LONG_LEN = 512
SHORT_DEV = 4
LONG_DEV = 1


epsilon = 1e-06
highest = lax.Precision.HIGHEST
far_limits = (12, 16, 23, 32, 46, 64, 91)


def vmem(count):
    return [pl.BlockSpec(memory_space=pltpu.VMEM)] * count


def params(mib=16):
    return pltpu.CompilerParams(vmem_limit_bytes=mib * 1024 * 1024)


def dot_nn(left, right):
    return jnp.dot(left, right, preferred_element_type=jnp.float32)


def dot_nt(left, right):
    return lax.dot_general(
        left, right, (((1,), (1,)), ((), ())), preferred_element_type=jnp.float32
    )


def inverse_rms(values):
    return lax.rsqrt(jnp.mean(values * values, axis=-1, keepdims=True) + epsilon)


def diagonal_buckets(offset):
    distance = jnp.abs(offset)
    far_bucket = jnp.full(offset.shape, 8, jnp.int32)
    for limit in far_limits:
        far_bucket = far_bucket + (distance >= limit).astype(jnp.int32)
    return jnp.where(distance < 8, distance, far_bucket) + jnp.where(offset > 0, 16, 0)


def hbm_out(shape, dtype):
    return pltpu.HBM(shape, dtype)


def in_hbm(array):
    return pltpu.with_memory_space_constraint(array, pltpu.HBM)


def start_copies(pairs):
    copies = [pltpu.make_async_copy(*triple) for triple in pairs]
    for copy in copies:
        copy.start()
    return copies


def attend_kernel(
    block_rows,
    lengths_ref,
    tokens_hbm,
    gain_ref,
    wq_hbm,
    wk_hbm,
    wv_hbm,
    wo_hbm,
    table_ref,
    part_hbm,
    normed_hbm,
    q_hbm,
    k_hbm,
    v_hbm,
    mixed_hbm,
    long_hbm,
    short_hbm,
    tokens_ref,
    wq_ref,
    wk_ref,
    wv_ref,
    wo_ref,
    part_ref,
    normed_ref,
    q_ref,
    k_ref,
    v_ref,
    mixed_ref,
    long_ref,
    short_ref,
    diag_ref,
    in_sems,
    out_sems,
):
    tok_count, width = tokens_ref.shape
    pairs = wq_ref.shape[1] // 128
    short_tok = SHORT_DEV * SHORT_LEN
    tile = 256
    steps = tok_count // tile
    tiles_in = []
    for step in range(steps):
        rows = slice(step * tile, step * tile + tile)
        tiles_in.append((tokens_hbm.at[rows], tokens_ref.at[rows], in_sems.at[step]))
    weights = [(wq_hbm, wq_ref), (wk_hbm, wk_ref), (wv_hbm, wv_ref), (wo_hbm, wo_ref)]
    triples = [tiles_in[0]]
    triples += [(src, dst, in_sems.at[steps + index]) for index, (src, dst) in enumerate(weights[:3])]
    triples += tiles_in[1:]
    triples += [(weights[3][0], weights[3][1], in_sems.at[steps + 3])]
    copies = start_copies(triples)
    tile_copies = [copies[0]] + copies[4 : 3 + steps]
    weight_copies = copies[1:4] + copies[3 + steps :]
    outs = []

    offset = lax.broadcasted_iota(jnp.int32, (table_ref.shape[1], 512), 1) - 256
    hot = jnp.where(
        diagonal_buckets(offset)
        == lax.broadcasted_iota(jnp.int32, (table_ref.shape[1], 512), 0),
        1.0,
        0.0,
    )
    diag_ref[...] = dot_nn(table_ref[...], hot.astype(jnp.bfloat16))
    gain = gain_ref[...]
    for step in range(steps):
        rows = slice(step * tile, step * tile + tile)
        tile_copies[step].wait()
        values = tokens_ref[rows, :].astype(jnp.float32)
        normed = (values * inverse_rms(values) * gain).astype(jnp.bfloat16)
        normed_ref[rows, :] = normed
        if step == 0:
            for copy in weight_copies[:3]:
                copy.wait()
        q_ref[rows, :] = dot_nn(normed, wq_ref[...]).astype(jnp.bfloat16) * jnp.bfloat16(0.125)
        k_ref[rows, :] = dot_nn(normed, wk_ref[...]).astype(jnp.bfloat16)
        v_ref[rows, :] = dot_nn(normed, wv_ref[...]).astype(jnp.bfloat16)
    outs += start_copies(
        [
            (normed_ref, normed_hbm, out_sems.at[0]),
            (q_ref, q_hbm, out_sems.at[1]),
            (k_ref, k_hbm, out_sems.at[2]),
            (v_ref, v_hbm, out_sems.at[3]),
        ]
    )
    lane = lax.broadcasted_iota(jnp.int32, (1, 128), 1)
    key_place = lax.broadcasted_iota(jnp.int32, (1, LONG_LEN), 1)
    live_long = key_place < lengths_ref[SHORT_DEV]

    def softmax(scores):
        weights = jnp.exp(scores - jnp.max(scores, axis=1, keepdims=True))
        return (weights * (1.0 / jnp.sum(weights, axis=1, keepdims=True))).astype(jnp.bfloat16)

    def one_pair(pair):
        lanes = slice(pair * 128, pair * 128 + 128)
        tiles = []
        for sub in range(2):
            row = diag_ref[pair * 2 + sub : pair * 2 + sub + 1, :]
            spread = pltpu.roll(
                jnp.broadcast_to(row, (128, 512)), 256, 1, stride=1, stride_axis=0
            )
            tiles.append(
                (
                    spread[:, 0:128],
                    spread[:, 128:256],
                    spread[:, 384:512],
                    jnp.broadcast_to(row[:, 511:512], (128, 128)),
                    jnp.broadcast_to(row[:, 0:1], (128, 128)),
                )
            )
        out = []
        for sub in range(2):
            scores = []
            for block in range(SHORT_DEV):
                rows = slice(block * 128, block * 128 + 128)
                masked = jnp.where((lane >= 64) == (sub == 1), q_ref[rows, lanes], 0)
                live = key_place[:, :128] < lengths_ref[block]
                scores.append(
                    jnp.where(
                        live, dot_nt(masked, k_ref[rows, lanes]) + tiles[sub][0], -1000000000.0
                    )
                )
            probs = softmax(jnp.concatenate(scores, axis=0))
            short_ref[pair * 2 + sub] = probs
            mixed = []
            for block in range(SHORT_DEV):
                rows = slice(block * 128, block * 128 + 128)
                mixed.append(dot_nn(probs[rows], v_ref[rows, lanes]))
            out.append(jnp.concatenate(mixed, axis=0))
        mixed_ref[:short_tok, lanes] = jnp.where(lane < 64, out[0], out[1]).astype(jnp.bfloat16)
        keys = k_ref[short_tok:, lanes]
        values = v_ref[short_tok:, lanes]
        for start in range(0, LONG_LEN, block_rows):
            places = slice(start, start + block_rows)
            rows = slice(short_tok + start, short_tok + start + block_rows)
            queries = q_ref[rows, lanes]
            out = []
            for sub in range(2):
                masked = jnp.where((lane >= 64) == (sub == 1), queries, 0)
                same, above, below, far_above, far_below = tiles[sub]
                bias = jnp.concatenate(
                    [
                        jnp.concatenate(
                            [
                                same
                                if other == block
                                else above
                                if other == block + 1
                                else below
                                if other == block - 1
                                else far_above
                                if other > block
                                else far_below
                                for other in range(LONG_LEN // 128)
                            ],
                            axis=1,
                        )
                        for block in range(start // 128, (start + block_rows) // 128)
                    ],
                    axis=0,
                )
                scores = jnp.where(live_long, dot_nt(masked, keys) + bias, -1000000000.0)
                probs = softmax(scores)
                long_ref[pair * 2 + sub, places, :] = probs
                out.append(dot_nn(probs, values))
            mixed_ref[rows, lanes] = jnp.where(lane < 64, out[0], out[1]).astype(jnp.bfloat16)

    for pair in range(pairs):
        one_pair(pair)
        both = slice(pair * 2, pair * 2 + 2)
        outs += start_copies(
            [
                (long_ref.at[both], long_hbm.at[both], out_sems.at[4 + 2 * pair]),
                (short_ref.at[both], short_hbm.at[both], out_sems.at[5 + 2 * pair]),
            ]
        )
    weight_copies[3].wait()
    base = 4 + 2 * pairs
    outs += start_copies([(mixed_ref, mixed_hbm, out_sems.at[base])])
    for step in range(steps):
        rows = slice(step * tile, step * tile + tile)
        part_ref[rows, :] = dot_nn(mixed_ref[rows, :], wo_ref[...]).astype(part_ref.dtype)
        outs += start_copies([(part_ref.at[rows], part_hbm.at[rows], out_sems.at[base + 1 + step])])
    for copy in outs:
        copy.wait()


def attend(lengths, tokens, gain, w_query, w_key, w_value, w_out, table, block_rows=512):
    tok_count, width = tokens.shape
    own = w_query.shape[1]
    heads = own // 64
    heads_pad = -(-heads // 8) * 8
    table = jnp.pad(table.T, ((0, heads_pad - heads), (0, 0)))
    short_tok = SHORT_DEV * SHORT_LEN
    flops = 2 * tok_count * width * own * 4 + 4 * heads * (512 * 512 + short_tok * 128) * 64
    hbm = pl.BlockSpec(memory_space=pltpu.HBM)
    out_shapes = [
        ((tok_count, width), jnp.bfloat16),
        ((tok_count, width), jnp.bfloat16),
        ((tok_count, own), jnp.bfloat16),
        ((tok_count, own), jnp.bfloat16),
        ((tok_count, own), jnp.bfloat16),
        ((tok_count, own), jnp.bfloat16),
        ((heads, LONG_LEN, LONG_LEN), jnp.bfloat16),
        ((heads, short_tok, SHORT_LEN), jnp.bfloat16),
    ]
    steps = tok_count // 256
    return pl.pallas_call(
        partial(attend_kernel, block_rows),
        out_shape=[jax.ShapeDtypeStruct(*out_shapes[0])]
        + [hbm_out(shape, dtype) for shape, dtype in out_shapes[1:]],
        in_specs=[pl.BlockSpec(memory_space=pltpu.SMEM), hbm]
        + vmem(1)
        + [hbm] * 4
        + vmem(1),
        out_specs=[hbm] * 8,
        scratch_shapes=[pltpu.VMEM(tokens.shape, jnp.bfloat16)]
        + [pltpu.VMEM(w.shape, jnp.bfloat16) for w in (w_query, w_key, w_value, w_out)]
        + [pltpu.VMEM(shape, dtype) for shape, dtype in out_shapes]
        + [
            pltpu.VMEM((heads_pad, 512), jnp.float32),
            pltpu.SemaphoreType.DMA((steps + 4,)),
            pltpu.SemaphoreType.DMA((5 + 2 * (heads // 2) + steps,)),
        ],
        compiler_params=params(24),
        cost_estimate=pl.CostEstimate(
            flops=flops, bytes_accessed=16000000, transcendentals=heads * 512 * 640
        ),
        name="attend",
    )(
        lengths,
        in_hbm(tokens),
        gain.astype(jnp.float32)[None],
        in_hbm(w_query),
        in_hbm(w_key),
        in_hbm(w_value),
        in_hbm(w_out),
        table,
    )


def attend_back_kernel(
    block_rows,
    hg_ref,
    q_ref,
    k_ref,
    v_ref,
    mixed_ref,
    long_ref,
    short_ref,
    qg_ref,
    kg_ref,
    vg_ref,
    tiles_ref,
    far_ref,
    sg_ref,
):
    tok_count = q_ref.shape[0]
    short_tok = SHORT_DEV * SHORT_LEN
    lane = lax.broadcasted_iota(jnp.int32, (1, 128), 1)
    blocks = LONG_LEN // 128
    heads_grad = hg_ref[...]
    products = heads_grad.astype(jnp.float32) * mixed_ref[...].astype(jnp.float32)
    q_t = jnp.transpose(q_ref[...])
    hg_t = jnp.transpose(heads_grad)
    qg = []
    kg_t = []
    vg_t = []
    for sub in range(2):
        own = (lane >= 64) == (sub == 1)
        rows_t = slice(64 * sub, 64 * sub + 64)
        masked = jnp.where(own, heads_grad, 0)
        delta = jnp.sum(jnp.where(own, products, 0.0), axis=1, keepdims=True)
        grads = [
            dot_nt(masked[block * 128 : block * 128 + 128], v_ref[block * 128 : block * 128 + 128, :])
            for block in range(SHORT_DEV)
        ]
        probs = short_ref[sub]
        part = probs.astype(jnp.float32) * (jnp.concatenate(grads, axis=0) - delta[:short_tok])
        same = part[:128]
        for block in range(1, SHORT_DEV):
            same = same + part[block * 128 : block * 128 + 128]
        part = part.astype(jnp.bfloat16)
        qg_parts = []
        kg_parts = []
        vg_parts = []
        for block in range(SHORT_DEV):
            rows = slice(block * 128, block * 128 + 128)
            qg_parts.append(dot_nn(part[rows], k_ref[rows, :]))
            kg_parts.append(dot_nn(q_t[rows_t, rows], part[rows]))
            vg_parts.append(dot_nn(hg_t[rows_t, rows], probs[rows]))
        above = jnp.zeros((128, 128), jnp.float32)
        below = above
        far_above = above
        far_below = above
        for start in range(0, LONG_LEN, block_rows):
            places = slice(start, start + block_rows)
            rows = slice(short_tok + start, short_tok + start + block_rows)
            part = long_ref[sub, places, :].astype(jnp.float32) * (
                dot_nt(masked[rows], v_ref[short_tok:, :]) - delta[rows]
            )
            for block in range(start // 128, (start + block_rows) // 128):
                for other in range(blocks):
                    first = block * 128 - start
                    piece = part[first : first + 128, other * 128 : other * 128 + 128]
                    if other == block:
                        same = same + piece
                    elif other == block + 1:
                        above = above + piece
                    elif other == block - 1:
                        below = below + piece
                    elif other > block:
                        far_above = far_above + piece
                    else:
                        far_below = far_below + piece
            part = part.astype(jnp.bfloat16)
            sg_ref[places, :] = part
            qg_parts.append(dot_nn(part, k_ref[short_tok:, :]))
        kg_parts.append(dot_nn(q_t[rows_t, short_tok:], sg_ref[...]))
        vg_parts.append(dot_nn(hg_t[rows_t, short_tok:], long_ref[sub]))
        qg.append(jnp.concatenate(qg_parts, axis=0))
        kg_t.append(jnp.concatenate(kg_parts, axis=1))
        vg_t.append(jnp.concatenate(vg_parts, axis=1))
        tiles_ref[sub, :, 0:128] = same
        tiles_ref[sub, :, 128:256] = above
        tiles_ref[sub, :, 256:384] = below
        far_ref[sub, 0:1, :] = jnp.sum(far_above, axis=0, keepdims=True)
        far_ref[sub, 1:2, :] = jnp.sum(far_below, axis=0, keepdims=True)
    qg_ref[...] = (jnp.where(lane < 64, qg[0], qg[1]) * 0.125).astype(jnp.bfloat16)
    kg_ref[...] = jnp.transpose(jnp.concatenate(kg_t, axis=0).astype(jnp.bfloat16))
    vg_ref[...] = jnp.transpose(jnp.concatenate(vg_t, axis=0).astype(jnp.bfloat16))


def attend_back(heads_grad, query_rows, key_rows, value_rows, mixed, long_probs, short_probs):
    tok_count, own = query_rows.shape
    pairs = own // 128
    short_tok = SHORT_DEV * SHORT_LEN
    rows_spec = pl.BlockSpec((tok_count, 128), lambda pair: (0, pair))
    flops = 10 * pairs * 2 * (512 * 512 + short_tok * 128) * 64
    return pl.pallas_call(
        partial(attend_back_kernel, LONG_LEN),
        grid=(pairs,),
        out_shape=[hbm_out((tok_count, own), jnp.bfloat16)] * 3
        + [
            hbm_out((pairs * 2, 128, 384), jnp.float32),
            hbm_out((pairs * 2, 2, 128), jnp.float32),
        ],
        in_specs=[rows_spec] * 5
        + [
            pl.BlockSpec((2, LONG_LEN, LONG_LEN), lambda pair: (pair, 0, 0)),
            pl.BlockSpec((2, short_tok, SHORT_LEN), lambda pair: (pair, 0, 0)),
        ],
        out_specs=[rows_spec] * 3
        + [
            pl.BlockSpec((2, 128, 384), lambda pair: (pair, 0, 0)),
            pl.BlockSpec((2, 2, 128), lambda pair: (pair, 0, 0)),
        ],
        scratch_shapes=[pltpu.VMEM((LONG_LEN, LONG_LEN), jnp.bfloat16)],
        compiler_params=params(24),
        cost_estimate=pl.CostEstimate(flops=flops, bytes_accessed=12000000, transcendentals=0),
        name="attend_back",
    )(
        in_hbm(heads_grad),
        in_hbm(query_rows),
        in_hbm(key_rows),
        in_hbm(value_rows),
        in_hbm(mixed),
        in_hbm(long_probs),
        in_hbm(short_probs),
    )


def table_kernel(tiles_ref, far_ref, out_ref):
    for head in range(tiles_ref.shape[0]):
        tile = jnp.concatenate(
            [
                tiles_ref[head, :, 0:256],
                jnp.zeros((128, 128), jnp.float32),
                tiles_ref[head, :, 256:384],
            ],
            axis=1,
        )
        span = 64
        while span:
            tile = tile[:span] + pltpu.roll(tile[span:], 512 - span, 1)
            span //= 2
        out_ref[head : head + 1, 0:512] = tile
        out_ref[head : head + 1, 512:640] = far_ref[head, 0:1, :]
        out_ref[head : head + 1, 640:768] = far_ref[head, 1:2, :]


def table_diagonals(tiles, far):
    heads = tiles.shape[0]
    return pl.pallas_call(
        table_kernel,
        out_shape=jax.ShapeDtypeStruct((heads, 768), jnp.float32),
        compiler_params=params(16),
        cost_estimate=pl.CostEstimate(flops=heads * 128 * 512 * 14, bytes_accessed=1300000, transcendentals=0),
        name="table",
    )(in_hbm(tiles), in_hbm(far))


def table_from(diag, bucket_count):
    lane = jnp.arange(768, dtype=jnp.int32)
    offset = jnp.where(lane < 256, lane, lane - 512)
    offset = jnp.where(lane >= 640, -256, jnp.where(lane >= 512, 256, offset))
    hot = (diagonal_buckets(offset)[:, None] == jnp.arange(bucket_count)[None, :]).astype(jnp.float32)
    return lax.dot_general(
        hot, diag, (((0,), (1,)), ((), ())), precision=highest, preferred_element_type=jnp.float32
    )


def dispatch_rows(send_ref, slot_row, half_rows):
    slots = send_ref.shape[0]
    tok_count = slot_row.shape[1]
    for base in range(0, slots, 256):
        span = min(256, slots - base)
        place = lax.broadcasted_iota(jnp.int32, (span, tok_count), 0) + base
        hot = jnp.where(place == slot_row, 1.0, 0.0).astype(jnp.bfloat16)
        send_ref[base : base + span, :] = dot_nn(hot, half_rows).astype(jnp.bfloat16)


def half_lanes(core, half):
    return pl.ds(pl.multiple_of(core * half, half), half)


def route_kernel(
    capacity, where_ref, routes_ref, grad_hbm, row_ref, col_ref, send_ref, grad_ref, in_sem
):
    tok_count = routes_ref.shape[1]
    slots, half = send_ref.shape
    experts = slots // capacity
    copy = pltpu.make_async_copy(
        grad_hbm.at[:, half_lanes(where_ref[0], half)], grad_ref, in_sem
    )
    copy.start()
    routes = routes_ref[...]
    expert = lax.broadcasted_iota(jnp.int32, (experts, tok_count), 0)
    lane = lax.broadcasted_iota(jnp.int32, (1, tok_count), 1)
    hot = jnp.where(expert == routes, 1.0, 0.0)
    total = hot
    step = 1
    while step < tok_count:
        total = total + jnp.where(lane >= step, pltpu.roll(total, step, 1), 0.0)
        step *= 2
    before = jnp.sum(hot * total, axis=0, keepdims=True).astype(jnp.int32) - 1
    slot = jnp.where(before < capacity, routes * capacity + before, slots)
    row_ref[...] = slot
    wide = jnp.broadcast_to(slot.astype(jnp.float32), (128, tok_count))
    col_ref[...] = jnp.transpose(wide).astype(jnp.int32)
    copy.wait()
    dispatch_rows(send_ref, slot, grad_ref[...])


def route(where, routes, out_grad, experts, capacity):
    tok_count, width = out_grad.shape
    slots = experts * capacity
    return pl.pallas_call(
        partial(route_kernel, capacity),
        out_shape=[
            hbm_out((1, tok_count), jnp.int32),
            hbm_out((tok_count, 128), jnp.int32),
            jax.ShapeDtypeStruct((slots, width // 2), jnp.bfloat16),
        ],
        in_specs=[
            pl.BlockSpec(memory_space=pltpu.SMEM),
            pl.BlockSpec((1, tok_count), lambda: (0, 0)),
            pl.BlockSpec(memory_space=pltpu.HBM),
        ],
        scratch_shapes=[
            pltpu.VMEM((tok_count, width // 2), jnp.bfloat16),
            pltpu.SemaphoreType.DMA,
        ],
        compiler_params=params(),
        cost_estimate=pl.CostEstimate(
            flops=slots * tok_count * width, bytes_accessed=4000000, transcendentals=0
        ),
        name="route",
    )(where, routes.reshape(1, tok_count), in_hbm(out_grad))


def second_kernel(
    where_ref, tokens_ref, own_ref, other_ref, gain_ref, row_ref, residual_ref, send_ref, second_ref
):
    step = pl.program_id(0)
    tile = tokens_ref.shape[0]
    half = send_ref.shape[1]
    residual = tokens_ref[...].astype(jnp.float32) + (
        own_ref[...].astype(jnp.float32) + other_ref[...].astype(jnp.float32)
    )
    residual_ref[...] = residual
    second_ref[pl.ds(pl.multiple_of(step * tile, tile), tile), :] = (
        residual * inverse_rms(residual) * gain_ref[...]
    ).astype(jnp.bfloat16)

    @pl.when(step == pl.num_programs(0) - 1)
    def _():
        dispatch_rows(send_ref, row_ref[...], second_ref[:, half_lanes(where_ref[0], half)])


def second_rows(where, tokens, own, other, gain, slot_row, slots):
    tok_count, width = tokens.shape
    tile = 256
    rows = pl.BlockSpec((tile, width), lambda step: (step, 0))
    return pl.pallas_call(
        second_kernel,
        grid=(tok_count // tile,),
        out_shape=[
            hbm_out((tok_count, width), jnp.float32),
            jax.ShapeDtypeStruct((slots, width // 2), jnp.bfloat16),
        ],
        in_specs=[
            pl.BlockSpec(memory_space=pltpu.SMEM),
            rows,
            rows,
            rows,
            pl.BlockSpec((1, width), lambda step: (0, 0)),
            pl.BlockSpec((1, tok_count), lambda step: (0, 0)),
        ],
        out_specs=[rows, pl.BlockSpec((slots, width // 2), lambda step: (0, 0))],
        scratch_shapes=[pltpu.VMEM((tok_count, width), jnp.bfloat16)],
        compiler_params=params(),
        cost_estimate=pl.CostEstimate(
            flops=slots * tok_count * width, bytes_accessed=13000000, transcendentals=0
        ),
        name="second",
    )(where, in_hbm(tokens), own, other, gain.astype(jnp.float32)[None], in_hbm(slot_row))


def hidden_grad_kernel(where_ref, own_ref, other_ref, outer_ref, out_ref, whole_ref):
    half = own_ref.shape[1]
    core = where_ref[0]
    whole_ref[:, half_lanes(core, half)] = own_ref[...]
    whole_ref[:, half_lanes(1 - core, half)] = other_ref[...]
    out_ref[...] = dot_nt(whole_ref[...], outer_ref[...]).astype(jnp.bfloat16)


def hidden_grad_of(where, own, other, outer):
    slots, half = own.shape
    hidden = outer.shape[0]
    tile = 256
    rows = pl.BlockSpec((tile, half), lambda step: (step, 0))
    return pl.pallas_call(
        hidden_grad_kernel,
        grid=(slots // tile,),
        out_shape=hbm_out((slots, hidden), jnp.bfloat16),
        in_specs=[pl.BlockSpec(memory_space=pltpu.SMEM), rows, rows] + vmem(1),
        out_specs=pl.BlockSpec((tile, hidden), lambda step: (step, 0)),
        scratch_shapes=[pltpu.VMEM((tile, 2 * half), jnp.bfloat16)],
        compiler_params=params(),
        cost_estimate=pl.CostEstimate(
            flops=4 * slots * half * hidden, bytes_accessed=12000000, transcendentals=0
        ),
        name="hidden_grad",
    )(where, own, other, outer)


def gate_of(rows, router, index):
    experts = router.shape[1]
    logits = dot_nn(rows, router)
    exp_logit = jnp.exp(logits - jnp.max(logits, axis=1, keepdims=True))
    probs = exp_logit * (1.0 / jnp.sum(exp_logit, axis=1, keepdims=True))
    hit = jnp.where(lax.broadcasted_iota(jnp.int32, (1, experts), 1) == index, 1.0, 0.0)
    return probs, hit, jnp.sum(probs * hit, axis=1, keepdims=True)


def expert_kernel(
    where_ref,
    own_ref,
    other_ref,
    hg_ref,
    inner_ref,
    router_ref,
    hidden_ref,
    pre_grad_ref,
    keep_ref,
    send_ref,
    logit_ref,
    arrived_ref,
    whole_ref,
):
    core = where_ref[0]
    tile, half = own_ref.shape
    own_lanes = half_lanes(core, half)
    other_lanes = half_lanes(1 - core, half)
    arrived_ref[:, own_lanes] = own_ref[...]
    arrived_ref[:, other_lanes] = other_ref[...]
    arrived = arrived_ref[...]
    probs, hit, gate = gate_of(arrived, router_ref[...], where_ref[1])
    curve = 0.7978845608028654
    gate_grad = jnp.zeros((tile, 1), jnp.float32)
    back = jnp.zeros((tile, 2 * half), jnp.float32)
    chunk = 512
    for start in range(0, hg_ref.shape[1], chunk):
        cols = slice(start, start + chunk)
        pre = dot_nn(arrived, inner_ref[:, cols])
        hg = hg_ref[:, cols].astype(jnp.float32)
        square = pre * pre
        bend = jnp.tanh(pre * (curve + (curve * 0.044715) * square))
        grown = 0.5 + 0.5 * bend
        hidden = (pre * grown).astype(jnp.bfloat16)
        hidden_ref[:, cols] = hidden
        gate_grad = gate_grad + jnp.sum(hidden.astype(jnp.float32) * hg, axis=1, keepdims=True)
        slope = grown + (pre * (curve + (3 * curve * 0.044715) * square)) * (0.5 - 0.5 * bend * bend)
        pre_grad = (slope * (gate * hg)).astype(jnp.bfloat16)
        pre_grad_ref[:, cols] = pre_grad
        back = back + dot_nt(pre_grad, inner_ref[:, cols])
    logit = (probs * (gate_grad * (hit - gate))).astype(jnp.bfloat16)
    logit_ref[...] = logit
    whole_ref[...] = back + dot_nt(logit, router_ref[...])
    send_ref[...] = whole_ref[:, other_lanes].astype(jnp.bfloat16)
    keep_ref[...] = whole_ref[:, own_lanes]


def expert(where, own, other, hidden_grad, inner, router):
    slots, half = own.shape
    width, hidden = inner.shape
    experts = router.shape[1]
    tile = 256
    halves = pl.BlockSpec((tile, half), lambda step: (step, 0))
    units = pl.BlockSpec((tile, hidden), lambda step: (step, 0))
    return pl.pallas_call(
        expert_kernel,
        grid=(slots // tile,),
        out_shape=[
            hbm_out((slots, hidden), jnp.bfloat16),
            hbm_out((slots, hidden), jnp.bfloat16),
            jax.ShapeDtypeStruct((slots, half), jnp.float32),
            jax.ShapeDtypeStruct((slots, half), jnp.bfloat16),
            hbm_out((slots, experts), jnp.bfloat16),
        ],
        in_specs=[pl.BlockSpec(memory_space=pltpu.SMEM), halves, halves, units] + vmem(2),
        out_specs=[
            units,
            units,
            halves,
            halves,
            pl.BlockSpec((tile, experts), lambda step: (step, 0)),
        ],
        scratch_shapes=[
            pltpu.VMEM((tile, width), jnp.bfloat16),
            pltpu.VMEM((tile, width), jnp.float32),
        ],
        compiler_params=params(),
        cost_estimate=pl.CostEstimate(
            flops=4 * slots * width * hidden, bytes_accessed=20000000, transcendentals=slots * hidden
        ),
        name="expert",
    )(where, own, other, in_hbm(hidden_grad), inner, router)


def expert_out_kernel(where_ref, hidden_ref, outer_ref, keep_ref, send_ref, whole_ref):
    core = where_ref[0]
    half = keep_ref.shape[1]
    whole_ref[...] = dot_nn(hidden_ref[...], outer_ref[...])
    send_ref[...] = whole_ref[:, half_lanes(1 - core, half)].astype(jnp.bfloat16)
    keep_ref[...] = whole_ref[:, half_lanes(core, half)]


def expert_out_of(where, hidden, outer):
    slots, units = hidden.shape
    width = outer.shape[1]
    half = width // 2
    tile = 256
    halves = pl.BlockSpec((tile, half), lambda step: (step, 0))
    return pl.pallas_call(
        expert_out_kernel,
        grid=(slots // tile,),
        out_shape=[
            jax.ShapeDtypeStruct((slots, half), jnp.float32),
            jax.ShapeDtypeStruct((slots, half), jnp.bfloat16),
        ],
        in_specs=[
            pl.BlockSpec(memory_space=pltpu.SMEM),
            pl.BlockSpec((tile, units), lambda step: (step, 0)),
        ]
        + vmem(1),
        out_specs=[halves, halves],
        scratch_shapes=[pltpu.VMEM((tile, width), jnp.float32)],
        compiler_params=params(),
        cost_estimate=pl.CostEstimate(
            flops=2 * slots * width * units, bytes_accessed=9000000, transcendentals=0
        ),
        name="expert_out",
    )(where, in_hbm(hidden), outer)


def expert_grads_kernel(
    where_ref,
    own_hbm,
    other_hbm,
    grad_own_hbm,
    grad_other_hbm,
    hidden_ref,
    pre_grad_ref,
    router_ref,
    logit_ref,
    router_out_ref,
    inner_grad_ref,
    outer_grad_ref,
    arrived_ref,
    gated_ref,
    sems,
):
    core = where_ref[0]
    half = own_hbm.shape[1]
    own_lanes = half_lanes(core, half)
    other_lanes = half_lanes(1 - core, half)

    @pl.when(pl.program_id(0) == 0)
    def _():
        copies = [
            pltpu.make_async_copy(own_hbm, arrived_ref.at[:, own_lanes], sems.at[0]),
            pltpu.make_async_copy(other_hbm, arrived_ref.at[:, other_lanes], sems.at[1]),
            pltpu.make_async_copy(grad_own_hbm, gated_ref.at[:, own_lanes], sems.at[2]),
            pltpu.make_async_copy(grad_other_hbm, gated_ref.at[:, other_lanes], sems.at[3]),
        ]
        for copy in copies:
            copy.start()
        for copy in copies:
            copy.wait()
        gate = gate_of(arrived_ref[...], router_ref[...], where_ref[1])[2]
        gated_ref[...] = (gate * gated_ref[...].astype(jnp.float32)).astype(jnp.bfloat16)
        router_out_ref[...] = contract_rows(logit_ref[...], arrived_ref[...])

    outer_grad_ref[...] = contract_rows(hidden_ref[...], gated_ref[...])
    inner_grad_ref[...] = contract_rows(arrived_ref[...], pre_grad_ref[...])


def expert_grads(where, own, other, grad_own, grad_other, hidden, pre_grad, router, logit_grad):
    slots, half = own.shape
    units = hidden.shape[1]
    width, experts = router.shape
    tile = 256
    hbm = pl.BlockSpec(memory_space=pltpu.HBM)
    whole = lambda shape: pl.BlockSpec(shape, lambda step: (0, 0))
    cols = pl.BlockSpec((slots, tile), lambda step: (0, step))
    return pl.pallas_call(
        expert_grads_kernel,
        grid=(units // tile,),
        out_shape=[
            hbm_out((experts, width), jnp.float32),
            hbm_out((width, units), jnp.float32),
            hbm_out((units, width), jnp.float32),
        ],
        in_specs=[
            pl.BlockSpec(memory_space=pltpu.SMEM),
            hbm,
            hbm,
            hbm,
            hbm,
            cols,
            cols,
            whole(router.shape),
            whole(logit_grad.shape),
        ],
        out_specs=[
            whole((experts, width)),
            pl.BlockSpec((width, tile), lambda step: (0, step)),
            pl.BlockSpec((tile, width), lambda step: (step, 0)),
        ],
        scratch_shapes=[
            pltpu.VMEM((slots, width), jnp.bfloat16),
            pltpu.VMEM((slots, width), jnp.bfloat16),
            pltpu.SemaphoreType.DMA((4,)),
        ],
        compiler_params=params(24),
        cost_estimate=pl.CostEstimate(
            flops=4 * slots * width * units, bytes_accessed=22000000, transcendentals=0
        ),
        name="expert_grads",
    )(
        where,
        in_hbm(own),
        in_hbm(other),
        in_hbm(grad_own),
        in_hbm(grad_other),
        in_hbm(hidden),
        in_hbm(pre_grad),
        router,
        in_hbm(logit_grad),
    )


def residual_back_kernel(
    where_ref,
    col_ref,
    own_ref,
    other_ref,
    residual_ref,
    grad_ref,
    gain_ref,
    wo_ref,
    out_ref,
    attn_ref,
    heads_ref,
    gain_out_ref,
    whole_ref,
):
    core = where_ref[0]
    slots, half = own_ref.shape
    tile = residual_ref.shape[0]
    place = lax.broadcasted_iota(jnp.int32, (tile, slots), 1)
    hot = jnp.where(place == col_ref[:, :1], 1.0, 0.0).astype(jnp.bfloat16)
    whole_ref[:, half_lanes(core, half)] = dot_nn(hot, own_ref[...])
    whole_ref[:, half_lanes(1 - core, half)] = dot_nn(hot, other_ref[...])
    ybar = whole_ref[...]
    values = residual_ref[...]
    scale = inverse_rms(values)
    scaled = values * scale
    pulled = ybar * gain_ref[...]

    @pl.when(pl.program_id(0) == 0)
    def _():
        gain_out_ref[...] = jnp.zeros_like(gain_out_ref)

    gain_out_ref[...] += jnp.sum(ybar * scaled, axis=0, keepdims=True)
    back = scale * (pulled - scaled * jnp.mean(pulled * scaled, axis=1, keepdims=True))
    out = back + grad_ref[...].astype(jnp.float32)
    out_ref[...] = out
    attn = out.astype(jnp.bfloat16)
    attn_ref[...] = attn
    heads_ref[...] = dot_nt(attn, wo_ref[...]).astype(jnp.bfloat16)


def residual_back(where, slot_col, own, other, residual, out_grad, gain, w_out):
    tok_count, width = residual.shape
    slots, half = own.shape
    heads_width = w_out.shape[0]
    tile = 256
    rows = pl.BlockSpec((tile, width), lambda step: (step, 0))
    whole = lambda shape: pl.BlockSpec(shape, lambda step: (0, 0))
    return pl.pallas_call(
        residual_back_kernel,
        grid=(tok_count // tile,),
        out_shape=[
            hbm_out((tok_count, width), jnp.float32),
            hbm_out((tok_count, width), jnp.bfloat16),
            hbm_out((tok_count, heads_width), jnp.bfloat16),
            hbm_out((1, width), jnp.float32),
        ],
        in_specs=[
            pl.BlockSpec(memory_space=pltpu.SMEM),
            pl.BlockSpec((tile, 128), lambda step: (step, 0)),
            whole(own.shape),
            whole(other.shape),
            rows,
            rows,
            whole((1, width)),
        ]
        + vmem(1),
        out_specs=[
            rows,
            rows,
            pl.BlockSpec((tile, heads_width), lambda step: (step, 0)),
            whole((1, width)),
        ],
        scratch_shapes=[pltpu.VMEM((tile, width), jnp.float32)],
        compiler_params=params(),
        cost_estimate=pl.CostEstimate(
            flops=tok_count * width * (2 * slots + 2 * heads_width),
            bytes_accessed=14000000,
            transcendentals=0,
        ),
        name="residual_back",
    )(
        where,
        in_hbm(slot_col),
        own,
        other,
        in_hbm(residual),
        in_hbm(out_grad),
        gain.astype(jnp.float32)[None],
        w_out,
    )


def output_kernel(
    capacity, where_ref, col_ref, returned_ref, residual_ref, gain_ref, router_ref, out_ref
):
    slots, half = returned_ref.shape
    tile = residual_ref.shape[0]
    experts = router_ref.shape[1]
    col = col_ref[:, :1]
    place = lax.broadcasted_iota(jnp.int32, (tile, slots), 1)
    hot = jnp.where(place == col, 1.0, 0.0).astype(jnp.bfloat16)
    token_out = dot_nn(hot, returned_ref[...])
    residual = residual_ref[...]
    second = (residual * inverse_rms(residual) * gain_ref[...]).astype(jnp.bfloat16)
    logits = dot_nn(second, router_ref[...])
    exp_logit = jnp.exp(logits - jnp.max(logits, axis=1, keepdims=True))
    first = lax.broadcasted_iota(jnp.int32, (1, experts), 1) * capacity
    hit = jnp.where((col >= first) & (col < first + capacity), exp_logit, 0.0)
    gate = jnp.sum(hit, axis=1, keepdims=True) / jnp.sum(exp_logit, axis=1, keepdims=True)
    own = residual_ref[:, half_lanes(where_ref[0], half)]
    out_ref[...] = (own + gate * token_out).astype(jnp.bfloat16)


def output_of(where, slot_col, returned, residual, gain, router, capacity):
    tok_count, width = residual.shape
    slots, half = returned.shape
    tile = 256
    whole = lambda shape: pl.BlockSpec(shape, lambda step: (0, 0))
    return pl.pallas_call(
        partial(output_kernel, capacity),
        grid=(tok_count // tile,),
        out_shape=jax.ShapeDtypeStruct((tok_count, half), jnp.bfloat16),
        in_specs=[
            pl.BlockSpec(memory_space=pltpu.SMEM),
            pl.BlockSpec((tile, 128), lambda step: (step, 0)),
            whole(returned.shape),
            pl.BlockSpec((tile, width), lambda step: (step, 0)),
            whole((1, width)),
            whole(router.shape),
        ],
        out_specs=pl.BlockSpec((tile, half), lambda step: (step, 0)),
        compiler_params=params(),
        cost_estimate=pl.CostEstimate(
            flops=2 * tok_count * half * slots, bytes_accessed=6000000, transcendentals=0
        ),
        name="output",
    )(
        where, in_hbm(slot_col), in_hbm(returned), in_hbm(residual), gain.astype(jnp.float32)[None], router
    )


def normed_back_kernel(qg_ref, kg_ref, vg_ref, wq_ref, wk_ref, wv_ref, out_ref):
    out_ref[...] = (
        dot_nt(qg_ref[...], wq_ref[...])
        + dot_nt(kg_ref[...], wk_ref[...])
        + dot_nt(vg_ref[...], wv_ref[...])
    ).astype(jnp.bfloat16)


def normed_back(qg, kg, vg, w_query, w_key, w_value):
    tok_count, own = qg.shape
    width = w_query.shape[0]
    tile = 256
    rows = pl.BlockSpec((tile, own), lambda step: (step, 0))
    whole = pl.BlockSpec((width, own), lambda step: (0, 0))
    return pl.pallas_call(
        normed_back_kernel,
        grid=(tok_count // tile,),
        out_shape=jax.ShapeDtypeStruct((tok_count, width), jnp.bfloat16),
        in_specs=[rows] * 3 + [whole] * 3,
        out_specs=pl.BlockSpec((tile, width), lambda step: (step, 0)),
        compiler_params=params(),
        cost_estimate=pl.CostEstimate(
            flops=6 * tok_count * own * width, bytes_accessed=6000000, transcendentals=0
        ),
        name="normed_back",
    )(*(in_hbm(array) for array in (qg, kg, vg, w_query, w_key, w_value)))


def input_back_kernel(tokens_ref, own_ref, other_ref, gain_ref, residual_ref, out_ref):
    ybar = own_ref[...].astype(jnp.float32) + other_ref[...].astype(jnp.float32)
    values = tokens_ref[...].astype(jnp.float32)
    scale = inverse_rms(values)
    scaled = values * scale
    pulled = ybar * gain_ref[...]
    out_ref[...] = residual_ref[...] + scale * (
        pulled - scaled * jnp.mean(pulled * scaled, axis=1, keepdims=True)
    )


def input_back(tokens, own, other, gain, residual_grad):
    tok_count, width = tokens.shape
    tile = 256
    rows = pl.BlockSpec((tile, width), lambda step: (step, 0))
    return pl.pallas_call(
        input_back_kernel,
        grid=(tok_count // tile,),
        out_shape=jax.ShapeDtypeStruct((tok_count, width), jnp.float32),
        in_specs=[rows, rows, rows, pl.BlockSpec((1, width), lambda step: (0, 0)), rows],
        out_specs=rows,
        compiler_params=params(),
        cost_estimate=pl.CostEstimate(
            flops=10 * tok_count * width, bytes_accessed=11000000, transcendentals=0
        ),
        name="input_back",
    )(in_hbm(tokens), own, other, gain.astype(jnp.float32)[None], in_hbm(residual_grad))


def weights_kernel(
    normed_hbm,
    qg_hbm,
    kg_hbm,
    vg_hbm,
    mixed_hbm,
    attn_hbm,
    wq_hbm,
    wk_hbm,
    wv_hbm,
    gain_ref,
    stack_ref,
    gain_out_ref,
    normed_ref,
    qg_ref,
    kg_ref,
    vg_ref,
    mixed_ref,
    attn_ref,
    wq_ref,
    wk_ref,
    wv_ref,
    sems,
):
    width = normed_ref.shape[1]
    own = mixed_ref.shape[1]
    tile = 256
    sources = [mixed_hbm, attn_hbm, normed_hbm, qg_hbm, wq_hbm, kg_hbm, wk_hbm, vg_hbm, wv_hbm]
    targets = [mixed_ref, attn_ref, normed_ref, qg_ref, wq_ref, kg_ref, wk_ref, vg_ref, wv_ref]
    copies = start_copies(
        [(source, target, sems.at[index]) for index, (source, target) in enumerate(zip(sources, targets))]
    )
    copies[0].wait()
    copies[1].wait()
    for start in range(0, own, 128):
        grad = contract_rows(mixed_ref[:, start : start + 128], attn_ref[...]).astype(jnp.bfloat16)
        for part in range(width // own):
            base = 3 * width + part * own + start
            stack_ref[base : base + 128, :] = grad[:, part * own : part * own + own]
    copies[2].wait()
    total = jnp.zeros((width, 1), jnp.float32)
    for index, (grad_ref, w_ref) in enumerate(((qg_ref, wq_ref), (kg_ref, wk_ref), (vg_ref, wv_ref))):
        copies[3 + 2 * index].wait()
        copies[4 + 2 * index].wait()
        sums = []
        for start in range(0, width, tile):
            rows = slice(start, start + tile)
            grad = contract_rows(normed_ref[:, rows], grad_ref[...])
            sums.append(jnp.sum(grad * w_ref[rows, :].astype(jnp.float32), axis=1, keepdims=True))
            stack_ref[index * width + start : index * width + start + tile, :] = grad.astype(jnp.bfloat16)
        total = total + jnp.concatenate(sums, axis=0)
    wide = jnp.transpose(jnp.broadcast_to(total, (width, 128)))
    gain_out_ref[...] = wide[:8, :] / gain_ref[...]


def weight_grads(normed, qg, kg, vg, mixed, attn_grad, w_query, w_key, w_value, gain):
    tok_count, width = normed.shape
    own = qg.shape[1]
    arrays = (normed, qg, kg, vg, mixed, attn_grad, w_query, w_key, w_value)
    return pl.pallas_call(
        weights_kernel,
        out_shape=[
            jax.ShapeDtypeStruct((4 * width, own), jnp.bfloat16),
            jax.ShapeDtypeStruct((8, width), jnp.float32),
        ],
        in_specs=[pl.BlockSpec(memory_space=pltpu.HBM)] * 9 + vmem(1),
        out_specs=vmem(2),
        scratch_shapes=[pltpu.VMEM(array.shape, jnp.bfloat16) for array in arrays]
        + [pltpu.SemaphoreType.DMA((9,))],
        compiler_params=params(),
        cost_estimate=pl.CostEstimate(
            flops=8 * tok_count * width * own, bytes_accessed=12000000, transcendentals=0
        ),
        name="weight_grads",
    )(*(in_hbm(array) for array in arrays), gain.astype(jnp.float32)[None])


def split_kernel(count, bits_ref, *refs):
    for part in range(count):
        whole = refs[part]
        span = whole.shape[0] // 2
        mine = bits_ref[part]
        refs[count + part][...] = whole[pl.ds((1 - mine) * span, span)]
        refs[2 * count + part][...] = whole[pl.ds(mine * span, span)]


def split(bits, parts):
    count = len(parts)
    halves = [jax.ShapeDtypeStruct((p.shape[0] // 2,) + p.shape[1:], p.dtype) for p in parts]
    out = pl.pallas_call(
        partial(split_kernel, count),
        out_shape=halves + halves,
        in_specs=[pl.BlockSpec(memory_space=pltpu.SMEM)] + vmem(count),
        out_specs=vmem(2 * count),
        compiler_params=params(16),
        name="split",
    )(bits, *parts)
    return out[:count], out[count:]


def fold_kernel(count, bits_ref, *refs):
    kept, got, sent, keep = (refs[count * k : count * (k + 1)] for k in range(4))
    for part in range(count):
        span = kept[part].shape[0] // 2
        mine = bits_ref[part]
        for ref, start in ((sent[part], (1 - mine) * span), (keep[part], mine * span)):
            rows = pl.ds(start, span)
            ref[...] = (
                kept[part][rows].astype(jnp.float32) + got[part][rows].astype(jnp.float32)
            ).astype(jnp.bfloat16)


def fold(bits, kept, got):
    count = len(kept)
    halves = [jax.ShapeDtypeStruct((p.shape[0] // 2,) + p.shape[1:], p.dtype) for p in kept]
    out = pl.pallas_call(
        partial(fold_kernel, count),
        out_shape=halves + halves,
        in_specs=[pl.BlockSpec(memory_space=pltpu.SMEM)] + vmem(2 * count),
        out_specs=vmem(2 * count),
        compiler_params=params(16),
        name="fold",
    )(bits, *kept, *got)
    return out[:count], out[count:]


def join_kernel(count, bits_ref, *refs):
    own, got, out = (refs[count * k : count * (k + 1)] for k in range(3))
    for part in range(count):
        span = own[part].shape[0]
        mine = bits_ref[part]
        out[part][pl.ds(mine * span, span)] = own[part][...]
        out[part][pl.ds((1 - mine) * span, span)] = got[part][...]


def join(bits, own, got):
    count = len(own)
    return pl.pallas_call(
        partial(join_kernel, count),
        out_shape=[jax.ShapeDtypeStruct((p.shape[0] * 2,) + p.shape[1:], p.dtype) for p in own],
        in_specs=[pl.BlockSpec(memory_space=pltpu.SMEM)] + vmem(2 * count),
        out_specs=vmem(count),
        compiler_params=params(16),
        name="join",
    )(bits, *own, *got)


def pack_kernel(count, *refs):
    kept, got = refs[:count], refs[count : 2 * count]
    span = kept[0].shape[0]
    for part in range(count):
        refs[-1][part * span : (part + 1) * span] = (
            kept[part][...].astype(jnp.float32) + got[part][...].astype(jnp.float32)
        ).astype(jnp.bfloat16)


def pack(kept, got):
    count = len(kept)
    shape = kept[0].shape
    return pl.pallas_call(
        partial(pack_kernel, count),
        out_shape=jax.ShapeDtypeStruct((count * shape[0],) + shape[1:], jnp.bfloat16),
        in_specs=vmem(2 * count),
        out_specs=vmem(1)[0],
        compiler_params=params(16),
        name="pack",
    )(*kept, *got)


def unpack_kernel(own_ref, got_ref, *out):
    span = out[0].shape[0]
    for part, ref in enumerate(out):
        rows = slice(part * span, (part + 1) * span)
        ref[...] = (own_ref[rows].astype(jnp.float32) + got_ref[rows].astype(jnp.float32)).astype(
            jnp.bfloat16
        )


def unpack(own, got, count):
    shape = (own.shape[0] // count,) + own.shape[1:]
    return pl.pallas_call(
        unpack_kernel,
        out_shape=[jax.ShapeDtypeStruct(shape, jnp.bfloat16)] * count,
        in_specs=vmem(2),
        out_specs=vmem(count),
        compiler_params=params(16),
        name="unpack",
    )(own, got)


def finish_kernel(count, bits_ref, *refs):
    own, got = refs[:count], refs[count : 2 * count]
    query_ref, key_ref, value_ref, out_ref, whole_ref = refs[2 * count :]
    span = own[0].shape[0]
    rows = 2 * span * own[0].shape[1]
    width, lanes = query_ref.shape
    for part in range(count):
        mine = bits_ref[part]
        whole_ref[pl.ds(mine * span, span)] = own[part][...].astype(jnp.float32)
        whole_ref[pl.ds((1 - mine) * span, span)] = got[part][...].astype(jnp.float32)
        flat = whole_ref[...].reshape(rows, lanes)
        for index, ref in enumerate((query_ref, key_ref, value_ref)):
            first = max(index * width, part * rows)
            last = min((index + 1) * width, (part + 1) * rows)
            if first < last:
                ref[first - index * width : last - index * width, :] = flat[
                    first - part * rows : last - part * rows
                ]
        for index in range(width // lanes):
            base = 3 * width + index * lanes
            first = max(base, part * rows)
            last = min(base + lanes, (part + 1) * rows)
            if first < last:
                out_ref[first - base : last - base, index * lanes : (index + 1) * lanes] = flat[
                    first - part * rows : last - part * rows
                ]


def finish(bits, own, got, width):
    count = len(own)
    span, rows, lanes = own[0].shape
    return pl.pallas_call(
        partial(finish_kernel, count),
        out_shape=[jax.ShapeDtypeStruct((width, lanes), jnp.float32)] * 3
        + [jax.ShapeDtypeStruct((lanes, width), jnp.float32)],
        in_specs=[pl.BlockSpec(memory_space=pltpu.SMEM)] + vmem(2 * count),
        out_specs=vmem(4),
        scratch_shapes=[pltpu.VMEM((2 * span, rows, lanes), jnp.float32)],
        compiler_params=params(24),
        name="finish",
    )(bits, *own, *got)


def swap_heads(rows):
    return lax.ppermute(rows, "heads", [(0, 1), (1, 0)])


def trade(rows, bit):
    count = lax.axis_size("seq")
    return lax.ppermute(rows, "seq", [(i, i ^ (1 << bit)) for i in range(count)])


def together(*groups):
    return lax.optimization_barrier(groups)


def contract_rows(left, right):
    return lax.dot_general(
        left, right, (((0,), (0,)), ((), ())), preferred_element_type=jnp.float32
    )


def on_device(
    tokens,
    gain_attn,
    w_query,
    w_key,
    w_value,
    w_out,
    bias_table,
    gain_ffn,
    w_router,
    w_inner,
    w_outer,
    routes,
    seq_lengths,
    out_grad,
):
    tok_count, width = tokens.shape
    bucket_count = bias_table.shape[0]
    experts = w_router.shape[1]
    capacity = max(2, 5 * tok_count // (4 * experts))
    senders = lax.axis_size("seq")
    bits = list(range(senders.bit_length() - 1))
    slots = experts * capacity
    half = width // 2
    own = w_query.shape[1]
    where = jnp.stack([lax.axis_index("heads"), lax.axis_index("seq")]).astype(jnp.int32)

    def exchange(rows):
        return lax.all_to_all(
            rows.reshape(senders, capacity, half), "seq", split_axis=0, concat_axis=0, tiled=True
        ).reshape(slots, half)

    def summed(keep, send):
        return (keep + swap_heads(send).astype(jnp.float32)).astype(jnp.bfloat16)

    slot_row, slot_col, grad_sent = route(where, routes, out_grad, experts, capacity)
    grad_sent, tokens = together(grad_sent, tokens)
    grad_own = exchange(grad_sent)
    attn_part, normed, query_rows, key_rows, value_rows, mixed, long_probs, short_probs = attend(
        seq_lengths, tokens, gain_attn, w_query, w_key, w_value, w_out, bias_table
    )
    residual, second_sent = second_rows(
        where, tokens, attn_part, swap_heads(attn_part), gain_ffn, slot_row, slots
    )
    second_sent, grad_own = together(second_sent, grad_own)
    arrived_own = exchange(second_sent)

    inner = w_inner[0]
    outer = w_outer[0]
    grad_other = swap_heads(grad_own)
    hidden_grad = hidden_grad_of(where, grad_own, grad_other, outer)
    arrived_own, hidden_grad = together(arrived_own, hidden_grad)
    arrived_other = swap_heads(arrived_own)
    hidden, pre_grad, keep, send, logit_grad = expert(
        where, arrived_own, arrived_other, hidden_grad, inner, w_router
    )
    back_sum, hidden = together(summed(keep, send), hidden)
    back_own = exchange(back_sum)
    out_keep, out_send = expert_out_of(where, hidden, outer)
    out_send, pre_grad = together(out_send, pre_grad)
    out_sum = summed(out_keep, out_send)
    router_part, inner_grad, outer_grad = expert_grads(
        where, arrived_own, arrived_other, grad_own, grad_other, hidden, pre_grad, w_router, logit_grad
    )
    back_own, out_sum, inner_grad = together(back_own, out_sum, inner_grad)
    back_other, out_sum = together(swap_heads(back_own), out_sum)
    returned = exchange(out_sum)

    residual_grad, attn_grad, heads_grad, gain_two_part = residual_back(
        where, slot_col, back_own, back_other, residual, out_grad, gain_ffn, w_out
    )
    query_grad, key_grad, value_grad, tiles, far = attend_back(
        heads_grad, query_rows, key_rows, value_rows, mixed, long_probs, short_probs
    )
    query_grad, returned = together(query_grad, returned)
    stack, gain_one_part = weight_grads(
        normed, query_grad, key_grad, value_grad, mixed, attn_grad, w_query, w_key, w_value, gain_attn
    )
    stack, query_grad, tiles = together(stack, query_grad, tiles)

    depth = len(bits) - 1
    turns = [bits[k * depth // 3 : depth] + bits[: k * depth // 3] for k in range(3)]
    place = lax.axis_index("seq")
    mine = [jnp.stack([(place >> turn[k]) & 1 for turn in turns]).astype(jnp.int32) for k in range(depth)]
    rows = stack.shape[0] // 3
    parts = [
        stack[k * rows : (k + 1) * rows].reshape(senders, rows // senders, own) for k in range(3)
    ]

    def trades(arrays, k):
        return [trade(array, turn[k]) for array, turn in zip(arrays, turns)]

    pair_part = jnp.concatenate([router_part, gain_one_part[:1]], axis=0)
    sent, kept = split(mine[0], parts)
    waiting = swap_heads(pair_part)
    for k in range(depth):
        got = trades(sent, k)
        if k == 0:
            output = output_of(where, slot_col, returned, residual, gain_ffn, w_router, capacity)
            got, output, tiles = together(got, output, tiles)
        elif k == 1:
            table_grad = table_from(table_diagonals(tiles, far), bucket_count)
            table_row = jnp.pad(table_grad.reshape(1, -1), ((0, 0), (0, width - table_grad.size)))
            small = jnp.concatenate([pair_part + waiting, gain_two_part, table_row], axis=0)
            got, small = together(got, small)
        else:
            if k > 2:
                small = small + waiting
            waiting = trade(small, bits[k - 2])
        if k + 1 < depth:
            sent, kept = fold(mine[k + 1], kept, got)
    packed = pack(kept, got)
    packed, query_grad, small, waiting = together(packed, query_grad, small, waiting)
    got = trade(packed, bits[-1])
    normed_part = normed_back(query_grad, key_grad, value_grad, w_query, w_key, w_value)
    small = small + waiting
    waiting = trade(small, bits[depth - 2])
    got, normed_part = together(got, normed_part)
    normed_other = swap_heads(normed_part)
    summed_parts = unpack(packed, got, 3)
    left = bits[depth - 1 :]
    for k in reversed(range(1, depth)):
        got = trades(summed_parts, k)
        if left:
            got, small, waiting = together(got, small, waiting)
            small = small + waiting
            waiting = trade(small, left.pop(0))
        summed_parts = join(mine[k], summed_parts, got)
    summed_parts, small, waiting = together(summed_parts, small, waiting)
    got = trades(summed_parts, 0)
    small = small + waiting
    for bit in left:
        small = small + trade(small, bit)
    input_grad = input_back(tokens, normed_part, normed_other, gain_attn, residual_grad)
    got, input_grad, small = together(got, input_grad, small)
    query_w_grad, key_w_grad, value_w_grad, out_w_grad = finish(mine[0], summed_parts, got, width)
    return (
        output,
        input_grad,
        small[experts],
        query_w_grad,
        key_w_grad,
        value_w_grad,
        out_w_grad,
        small[experts + 2, : table_grad.size].reshape(table_grad.shape),
        small[experts + 1],
        small[:experts].T,
        inner_grad[None],
        outer_grad[None],
    )


def solution(mesh):
    in_specs = (
        P("seq", None),
        P(),
        P(None, "heads"),
        P(None, "heads"),
        P(None, "heads"),
        P("heads", None),
        P(None, "heads"),
        P(),
        P(),
        P("seq", None, "heads"),
        P("seq", "heads", None),
        P("seq", None),
        P("seq"),
        P("seq", None),
    )
    out_specs = (
        P("seq", "heads"),
        P("seq", None),
        P(),
        P(None, "heads"),
        P(None, "heads"),
        P(None, "heads"),
        P("heads", None),
        P(None, "heads"),
        P(),
        P(),
        P("seq", None, "heads"),
        P("seq", "heads", None),
    )
    return jax.shard_map(
        on_device, mesh=mesh, in_specs=in_specs, out_specs=out_specs, check_vma=False
    )
```

```python
from functools import partial

import jax
import jax.numpy as jnp
from jax import lax
from jax.experimental import pallas as pl
from jax.experimental.pallas import tpu as pltpu
from jax.sharding import PartitionSpec as P

SHORT_LEN = 128
LONG_LEN = 512
SHORT_DEV = 4
LONG_DEV = 1


epsilon = 1e-06
highest = lax.Precision.HIGHEST
far_limits = (12, 16, 23, 32, 46, 64, 91)


def vmem(count):
    return [pl.BlockSpec(memory_space=pltpu.VMEM)] * count


def params(mib=16):
    return pltpu.CompilerParams(vmem_limit_bytes=mib * 1024 * 1024)


def dot_nn(left, right):
    return jnp.dot(left, right, preferred_element_type=jnp.float32)


def dot_nt(left, right):
    return lax.dot_general(
        left, right, (((1,), (1,)), ((), ())), preferred_element_type=jnp.float32
    )


def inverse_rms(values):
    return lax.rsqrt(jnp.mean(values * values, axis=-1, keepdims=True) + epsilon)


def diagonal_buckets(offset):
    distance = jnp.abs(offset)
    far_bucket = jnp.full(offset.shape, 8, jnp.int32)
    for limit in far_limits:
        far_bucket = far_bucket + (distance >= limit).astype(jnp.int32)
    return jnp.where(distance < 8, distance, far_bucket) + jnp.where(offset > 0, 16, 0)


def hbm_out(shape, dtype):
    return pltpu.HBM(shape, dtype)


def in_hbm(array):
    return pltpu.with_memory_space_constraint(array, pltpu.HBM)


def start_copies(pairs):
    copies = [pltpu.make_async_copy(*triple) for triple in pairs]
    for copy in copies:
        copy.start()
    return copies


def attend_kernel(
    block_rows,
    lengths_ref,
    tokens_hbm,
    gain_ref,
    wq_hbm,
    wk_hbm,
    wv_hbm,
    wo_hbm,
    table_ref,
    part_hbm,
    normed_hbm,
    q_hbm,
    k_hbm,
    v_hbm,
    mixed_hbm,
    long_hbm,
    short_hbm,
    tokens_ref,
    wq_ref,
    wk_ref,
    wv_ref,
    wo_ref,
    part_ref,
    normed_ref,
    q_ref,
    k_ref,
    v_ref,
    mixed_ref,
    long_ref,
    short_ref,
    diag_ref,
    in_sems,
    out_sems,
):
    tok_count, width = tokens_ref.shape
    pairs = wq_ref.shape[1] // 128
    short_tok = SHORT_DEV * SHORT_LEN
    tile = 256
    steps = tok_count // tile
    tiles_in = []
    for step in range(steps):
        rows = slice(step * tile, step * tile + tile)
        tiles_in.append((tokens_hbm.at[rows], tokens_ref.at[rows], in_sems.at[step]))
    weights = [(wq_hbm, wq_ref), (wk_hbm, wk_ref), (wv_hbm, wv_ref), (wo_hbm, wo_ref)]
    triples = [tiles_in[0]]
    triples += [(src, dst, in_sems.at[steps + index]) for index, (src, dst) in enumerate(weights[:3])]
    triples += tiles_in[1:]
    triples += [(weights[3][0], weights[3][1], in_sems.at[steps + 3])]
    copies = start_copies(triples)
    tile_copies = [copies[0]] + copies[4 : 3 + steps]
    weight_copies = copies[1:4] + copies[3 + steps :]
    outs = []

    offset = lax.broadcasted_iota(jnp.int32, (table_ref.shape[1], 512), 1) - 256
    hot = jnp.where(
        diagonal_buckets(offset)
        == lax.broadcasted_iota(jnp.int32, (table_ref.shape[1], 512), 0),
        1.0,
        0.0,
    )
    diag_ref[...] = dot_nn(table_ref[...], hot.astype(jnp.bfloat16))
    gain = gain_ref[...]
    for step in range(steps):
        rows = slice(step * tile, step * tile + tile)
        tile_copies[step].wait()
        values = tokens_ref[rows, :].astype(jnp.float32)
        normed = (values * inverse_rms(values) * gain).astype(jnp.bfloat16)
        normed_ref[rows, :] = normed
        if step == 0:
            for copy in weight_copies[:3]:
                copy.wait()
        q_ref[rows, :] = dot_nn(normed, wq_ref[...]).astype(jnp.bfloat16) * jnp.bfloat16(0.125)
        k_ref[rows, :] = dot_nn(normed, wk_ref[...]).astype(jnp.bfloat16)
        v_ref[rows, :] = dot_nn(normed, wv_ref[...]).astype(jnp.bfloat16)
    outs += start_copies(
        [
            (normed_ref, normed_hbm, out_sems.at[0]),
            (q_ref, q_hbm, out_sems.at[1]),
            (k_ref, k_hbm, out_sems.at[2]),
            (v_ref, v_hbm, out_sems.at[3]),
        ]
    )
    lane = lax.broadcasted_iota(jnp.int32, (1, 128), 1)
    key_place = lax.broadcasted_iota(jnp.int32, (1, LONG_LEN), 1)
    live_long = key_place < lengths_ref[SHORT_DEV]

    def softmax(scores):
        weights = jnp.exp(scores - jnp.max(scores, axis=1, keepdims=True))
        return (weights * (1.0 / jnp.sum(weights, axis=1, keepdims=True))).astype(jnp.bfloat16)

    def one_pair(pair):
        lanes = slice(pair * 128, pair * 128 + 128)
        tiles = []
        for sub in range(2):
            row = diag_ref[pair * 2 + sub : pair * 2 + sub + 1, :]
            spread = pltpu.roll(
                jnp.broadcast_to(row, (128, 512)), 256, 1, stride=1, stride_axis=0
            )
            tiles.append(
                (
                    spread[:, 0:128],
                    spread[:, 128:256],
                    spread[:, 384:512],
                    jnp.broadcast_to(row[:, 511:512], (128, 128)),
                    jnp.broadcast_to(row[:, 0:1], (128, 128)),
                )
            )
        out = []
        for sub in range(2):
            scores = []
            for block in range(SHORT_DEV):
                rows = slice(block * 128, block * 128 + 128)
                masked = jnp.where((lane >= 64) == (sub == 1), q_ref[rows, lanes], 0)
                live = key_place[:, :128] < lengths_ref[block]
                scores.append(
                    jnp.where(
                        live, dot_nt(masked, k_ref[rows, lanes]) + tiles[sub][0], -1000000000.0
                    )
                )
            probs = softmax(jnp.concatenate(scores, axis=0))
            short_ref[pair * 2 + sub] = probs
            mixed = []
            for block in range(SHORT_DEV):
                rows = slice(block * 128, block * 128 + 128)
                mixed.append(dot_nn(probs[rows], v_ref[rows, lanes]))
            out.append(jnp.concatenate(mixed, axis=0))
        mixed_ref[:short_tok, lanes] = jnp.where(lane < 64, out[0], out[1]).astype(jnp.bfloat16)
        keys = k_ref[short_tok:, lanes]
        values = v_ref[short_tok:, lanes]
        for start in range(0, LONG_LEN, block_rows):
            places = slice(start, start + block_rows)
            rows = slice(short_tok + start, short_tok + start + block_rows)
            queries = q_ref[rows, lanes]
            out = []
            for sub in range(2):
                masked = jnp.where((lane >= 64) == (sub == 1), queries, 0)
                same, above, below, far_above, far_below = tiles[sub]
                bias = jnp.concatenate(
                    [
                        jnp.concatenate(
                            [
                                same
                                if other == block
                                else above
                                if other == block + 1
                                else below
                                if other == block - 1
                                else far_above
                                if other > block
                                else far_below
                                for other in range(LONG_LEN // 128)
                            ],
                            axis=1,
                        )
                        for block in range(start // 128, (start + block_rows) // 128)
                    ],
                    axis=0,
                )
                scores = jnp.where(live_long, dot_nt(masked, keys) + bias, -1000000000.0)
                probs = softmax(scores)
                long_ref[pair * 2 + sub, places, :] = probs
                out.append(dot_nn(probs, values))
            mixed_ref[rows, lanes] = jnp.where(lane < 64, out[0], out[1]).astype(jnp.bfloat16)

    for pair in range(pairs):
        one_pair(pair)
        both = slice(pair * 2, pair * 2 + 2)
        outs += start_copies(
            [
                (long_ref.at[both], long_hbm.at[both], out_sems.at[4 + 2 * pair]),
                (short_ref.at[both], short_hbm.at[both], out_sems.at[5 + 2 * pair]),
            ]
        )
    weight_copies[3].wait()
    base = 4 + 2 * pairs
    outs += start_copies([(mixed_ref, mixed_hbm, out_sems.at[base])])
    for step in range(steps):
        rows = slice(step * tile, step * tile + tile)
        part_ref[rows, :] = dot_nn(mixed_ref[rows, :], wo_ref[...]).astype(part_ref.dtype)
        outs += start_copies([(part_ref.at[rows], part_hbm.at[rows], out_sems.at[base + 1 + step])])
    for copy in outs:
        copy.wait()


def attend(lengths, tokens, gain, w_query, w_key, w_value, w_out, table, block_rows=512):
    tok_count, width = tokens.shape
    own = w_query.shape[1]
    heads = own // 64
    heads_pad = -(-heads // 8) * 8
    table = jnp.pad(table.T, ((0, heads_pad - heads), (0, 0)))
    short_tok = SHORT_DEV * SHORT_LEN
    flops = 2 * tok_count * width * own * 4 + 4 * heads * (512 * 512 + short_tok * 128) * 64
    hbm = pl.BlockSpec(memory_space=pltpu.HBM)
    out_shapes = [
        ((tok_count, width), jnp.bfloat16),
        ((tok_count, width), jnp.bfloat16),
        ((tok_count, own), jnp.bfloat16),
        ((tok_count, own), jnp.bfloat16),
        ((tok_count, own), jnp.bfloat16),
        ((tok_count, own), jnp.bfloat16),
        ((heads, LONG_LEN, LONG_LEN), jnp.bfloat16),
        ((heads, short_tok, SHORT_LEN), jnp.bfloat16),
    ]
    steps = tok_count // 256
    return pl.pallas_call(
        partial(attend_kernel, block_rows),
        out_shape=[jax.ShapeDtypeStruct(*out_shapes[0])]
        + [hbm_out(shape, dtype) for shape, dtype in out_shapes[1:]],
        in_specs=[pl.BlockSpec(memory_space=pltpu.SMEM), hbm]
        + vmem(1)
        + [hbm] * 4
        + vmem(1),
        out_specs=[hbm] * 8,
        scratch_shapes=[pltpu.VMEM(tokens.shape, jnp.bfloat16)]
        + [pltpu.VMEM(w.shape, jnp.bfloat16) for w in (w_query, w_key, w_value, w_out)]
        + [pltpu.VMEM(shape, dtype) for shape, dtype in out_shapes]
        + [
            pltpu.VMEM((heads_pad, 512), jnp.float32),
            pltpu.SemaphoreType.DMA((steps + 4,)),
            pltpu.SemaphoreType.DMA((5 + 2 * (heads // 2) + steps,)),
        ],
        compiler_params=params(24),
        cost_estimate=pl.CostEstimate(
            flops=flops, bytes_accessed=16000000, transcendentals=heads * 512 * 640
        ),
        name="attend",
    )(
        lengths,
        in_hbm(tokens),
        gain.astype(jnp.float32)[None],
        in_hbm(w_query),
        in_hbm(w_key),
        in_hbm(w_value),
        in_hbm(w_out),
        table,
    )


def attend_back_pair(
    pair, hg_ref, q_ref, k_ref, v_ref, mixed_ref, long_ref, short_ref, qg_ref, kg_ref, vg_ref, tiles_ref,
    far_ref, sg_ref,
):
    short_tok = SHORT_DEV * SHORT_LEN
    lane = lax.broadcasted_iota(jnp.int32, (1, 128), 1)
    lanes = slice(pair * 128, pair * 128 + 128)
    blocks = LONG_LEN // 128
    heads_grad = hg_ref[:, lanes]
    products = heads_grad.astype(jnp.float32) * mixed_ref[:, lanes].astype(jnp.float32)
    q_t = jnp.transpose(q_ref[:, lanes])
    hg_t = jnp.transpose(heads_grad)
    qg = []
    kg_t = []
    vg_t = []
    for sub in range(2):
        head = pair * 2 + sub
        own = (lane >= 64) == (sub == 1)
        rows_t = slice(64 * sub, 64 * sub + 64)
        masked = jnp.where(own, heads_grad, 0)
        delta = jnp.sum(jnp.where(own, products, 0.0), axis=1, keepdims=True)
        grads = [
            dot_nt(masked[block * 128 : block * 128 + 128], v_ref[block * 128 : block * 128 + 128, lanes])
            for block in range(SHORT_DEV)
        ]
        probs = short_ref[head]
        part = probs.astype(jnp.float32) * (jnp.concatenate(grads, axis=0) - delta[:short_tok])
        same = part[:128]
        for block in range(1, SHORT_DEV):
            same = same + part[block * 128 : block * 128 + 128]
        part = part.astype(jnp.bfloat16)
        qg_parts = []
        kg_parts = []
        vg_parts = []
        for block in range(SHORT_DEV):
            rows = slice(block * 128, block * 128 + 128)
            qg_parts.append(dot_nn(part[rows], k_ref[rows, lanes]))
            kg_parts.append(dot_nn(q_t[rows_t, rows], part[rows]))
            vg_parts.append(dot_nn(hg_t[rows_t, rows], probs[rows]))
        above = jnp.zeros((128, 128), jnp.float32)
        below = above
        far_above = above
        far_below = above
        probs = long_ref[head]
        part = probs.astype(jnp.float32) * (
            dot_nt(masked[short_tok:], v_ref[short_tok:, lanes]) - delta[short_tok:]
        )
        for block in range(blocks):
            for other in range(blocks):
                piece = part[block * 128 : block * 128 + 128, other * 128 : other * 128 + 128]
                if other == block:
                    same = same + piece
                elif other == block + 1:
                    above = above + piece
                elif other == block - 1:
                    below = below + piece
                elif other > block:
                    far_above = far_above + piece
                else:
                    far_below = far_below + piece
        sg_ref[...] = part.astype(jnp.bfloat16)
        qg_parts.append(dot_nn(sg_ref[...], k_ref[short_tok:, lanes]))
        kg_parts.append(dot_nn(q_t[rows_t, short_tok:], sg_ref[...]))
        vg_parts.append(dot_nn(hg_t[rows_t, short_tok:], probs))
        qg.append(jnp.concatenate(qg_parts, axis=0))
        kg_t.append(jnp.concatenate(kg_parts, axis=1))
        vg_t.append(jnp.concatenate(vg_parts, axis=1))
        tiles_ref[head, :, 0:128] = same
        tiles_ref[head, :, 128:256] = above
        tiles_ref[head, :, 256:384] = below
        far_ref[head, 0:1, :] = jnp.sum(far_above, axis=0, keepdims=True)
        far_ref[head, 1:2, :] = jnp.sum(far_below, axis=0, keepdims=True)
    qg_ref[:, lanes] = (jnp.where(lane < 64, qg[0], qg[1]) * 0.125).astype(jnp.bfloat16)
    kg_ref[:, lanes] = jnp.transpose(jnp.concatenate(kg_t, axis=0).astype(jnp.bfloat16))
    vg_ref[:, lanes] = jnp.transpose(jnp.concatenate(vg_t, axis=0).astype(jnp.bfloat16))


def diagonals(tiles):
    tile = jnp.concatenate(
        [tiles[:, 0:256], jnp.zeros((128, 128), jnp.float32), tiles[:, 256:384]], axis=1
    )
    span = 64
    while span:
        tile = tile[:span] + pltpu.roll(tile[span:], 512 - span, 1)
        span //= 2
    return tile


def table_from(diag, bucket_count):
    lane = jnp.arange(768, dtype=jnp.int32)
    offset = jnp.where(lane < 256, lane, lane - 512)
    offset = jnp.where(lane >= 640, -256, jnp.where(lane >= 512, 256, offset))
    hot = (diagonal_buckets(offset)[:, None] == jnp.arange(bucket_count)[None, :]).astype(jnp.float32)
    return lax.dot_general(
        hot, diag, (((0,), (1,)), ((), ())), precision=highest, preferred_element_type=jnp.float32
    )


def dispatch_rows(send_ref, slot_row, half_rows):
    slots = send_ref.shape[0]
    tok_count = slot_row.shape[1]
    for base in range(0, slots, 256):
        span = min(256, slots - base)
        place = lax.broadcasted_iota(jnp.int32, (span, tok_count), 0) + base
        hot = jnp.where(place == slot_row, 1.0, 0.0).astype(jnp.bfloat16)
        send_ref[base : base + span, :] = dot_nn(hot, half_rows).astype(jnp.bfloat16)


def half_lanes(core, half):
    return pl.ds(pl.multiple_of(core * half, half), half)


def route_kernel(
    capacity, where_ref, routes_ref, grad_hbm, row_hbm, col_hbm, send_ref, grad_ref, row_ref, col_ref, in_sem,
    out_sems,
):
    tok_count = routes_ref.shape[1]
    slots, half = send_ref.shape
    experts = slots // capacity
    copy = pltpu.make_async_copy(
        grad_hbm.at[:, half_lanes(where_ref[0], half)], grad_ref, in_sem
    )
    copy.start()
    routes = routes_ref[...]
    expert = lax.broadcasted_iota(jnp.int32, (experts, tok_count), 0)
    lane = lax.broadcasted_iota(jnp.int32, (1, tok_count), 1)
    hot = jnp.where(expert == routes, 1.0, 0.0)
    total = hot
    step = 1
    while step < tok_count:
        total = total + jnp.where(lane >= step, pltpu.roll(total, step, 1), 0.0)
        step *= 2
    before = jnp.sum(hot * total, axis=0, keepdims=True).astype(jnp.int32) - 1
    slot = jnp.where(before < capacity, routes * capacity + before, slots)
    row_ref[...] = slot
    wide = jnp.broadcast_to(slot.astype(jnp.float32), (128, tok_count))
    col_ref[...] = jnp.transpose(wide).astype(jnp.int32)
    outs = start_copies([(row_ref, row_hbm, out_sems.at[0]), (col_ref, col_hbm, out_sems.at[1])])
    copy.wait()
    dispatch_rows(send_ref, slot, grad_ref[...])
    for copy in outs:
        copy.wait()


def route(where, routes, out_grad, experts, capacity):
    tok_count, width = out_grad.shape
    slots = experts * capacity
    return pl.pallas_call(
        partial(route_kernel, capacity),
        out_shape=[
            hbm_out((1, tok_count), jnp.int32),
            hbm_out((tok_count, 128), jnp.int32),
            jax.ShapeDtypeStruct((slots, width // 2), jnp.bfloat16),
        ],
        in_specs=[
            pl.BlockSpec(memory_space=pltpu.SMEM),
            pl.BlockSpec((1, tok_count), lambda: (0, 0)),
            pl.BlockSpec(memory_space=pltpu.HBM),
        ],
        out_specs=[pl.BlockSpec(memory_space=pltpu.HBM)] * 2 + vmem(1),
        scratch_shapes=[
            pltpu.VMEM((tok_count, width // 2), jnp.bfloat16),
            pltpu.VMEM((1, tok_count), jnp.int32),
            pltpu.VMEM((tok_count, 128), jnp.int32),
            pltpu.SemaphoreType.DMA,
            pltpu.SemaphoreType.DMA((2,)),
        ],
        compiler_params=params(),
        cost_estimate=pl.CostEstimate(
            flops=slots * tok_count * width, bytes_accessed=4000000, transcendentals=0
        ),
        name="route",
    )(where, routes.reshape(1, tok_count), in_hbm(out_grad))


def second_kernel(
    where_ref, tokens_hbm, own_ref, other_ref, gain_ref, row_hbm, residual_hbm, send_ref, tokens_ref,
    row_ref, residual_ref, second_ref, in_sems, out_sems,
):
    tile = 256
    tok_count = tokens_ref.shape[0]
    half = send_ref.shape[1]
    tiles_rows = [slice(start, start + tile) for start in range(0, tok_count, tile)]
    copies = start_copies(
        [
            (tokens_hbm.at[rows], tokens_ref.at[rows], in_sems.at[step])
            for step, rows in enumerate(tiles_rows)
        ]
        + [(row_hbm, row_ref, in_sems.at[len(tiles_rows)])]
    )
    outs = []
    gain = gain_ref[...]
    for step, rows in enumerate(tiles_rows):
        attn = own_ref[rows, :].astype(jnp.float32) + other_ref[rows, :].astype(jnp.float32)
        copies[step].wait()
        residual = tokens_ref[rows, :].astype(jnp.float32) + attn
        residual_ref[rows, :] = residual
        outs += start_copies([(residual_ref.at[rows], residual_hbm.at[rows], out_sems.at[step])])
        second_ref[rows, :] = (residual * inverse_rms(residual) * gain).astype(jnp.bfloat16)
    copies[-1].wait()
    dispatch_rows(send_ref, row_ref[...], second_ref[:, half_lanes(where_ref[0], half)])
    for copy in outs:
        copy.wait()


def second_rows(where, tokens, own, other, gain, slot_row, slots):
    tok_count, width = tokens.shape
    steps = tok_count // 256
    hbm = pl.BlockSpec(memory_space=pltpu.HBM)
    return pl.pallas_call(
        second_kernel,
        out_shape=[
            hbm_out((tok_count, width), jnp.float32),
            jax.ShapeDtypeStruct((slots, width // 2), jnp.bfloat16),
        ],
        in_specs=[pl.BlockSpec(memory_space=pltpu.SMEM), hbm] + vmem(3) + [hbm],
        out_specs=[hbm] + vmem(1),
        scratch_shapes=[
            pltpu.VMEM((tok_count, width), jnp.bfloat16),
            pltpu.VMEM((1, tok_count), jnp.int32),
            pltpu.VMEM((tok_count, width), jnp.float32),
            pltpu.VMEM((tok_count, width), jnp.bfloat16),
            pltpu.SemaphoreType.DMA((steps + 1,)),
            pltpu.SemaphoreType.DMA((steps,)),
        ],
        compiler_params=params(),
        cost_estimate=pl.CostEstimate(
            flops=slots * tok_count * width, bytes_accessed=13000000, transcendentals=0
        ),
        name="second",
    )(where, in_hbm(tokens), own, other, gain.astype(jnp.float32)[None], in_hbm(slot_row))


def hidden_grad_kernel(where_ref, own_ref, other_ref, outer_ref, out_ref, whole_ref):
    half = own_ref.shape[1]
    core = where_ref[0]
    whole_ref[:, half_lanes(core, half)] = own_ref[...]
    whole_ref[:, half_lanes(1 - core, half)] = other_ref[...]
    out_ref[...] = dot_nt(whole_ref[...], outer_ref[...]).astype(jnp.bfloat16)


def hidden_grad_of(where, own, other, outer):
    slots, half = own.shape
    hidden = outer.shape[0]
    tile = 256
    rows = pl.BlockSpec((tile, half), lambda step: (step, 0))
    return pl.pallas_call(
        hidden_grad_kernel,
        grid=(slots // tile,),
        out_shape=hbm_out((slots, hidden), jnp.bfloat16),
        in_specs=[pl.BlockSpec(memory_space=pltpu.SMEM), rows, rows] + vmem(1),
        out_specs=pl.BlockSpec((tile, hidden), lambda step: (step, 0)),
        scratch_shapes=[pltpu.VMEM((tile, 2 * half), jnp.bfloat16)],
        compiler_params=params(),
        cost_estimate=pl.CostEstimate(
            flops=4 * slots * half * hidden, bytes_accessed=12000000, transcendentals=0
        ),
        name="hidden_grad",
    )(where, own, other, outer)


def gate_of(rows, router, index):
    experts = router.shape[1]
    logits = dot_nn(rows, router)
    exp_logit = jnp.exp(logits - jnp.max(logits, axis=1, keepdims=True))
    probs = exp_logit * (1.0 / jnp.sum(exp_logit, axis=1, keepdims=True))
    hit = jnp.where(lax.broadcasted_iota(jnp.int32, (1, experts), 1) == index, 1.0, 0.0)
    return probs, hit, jnp.sum(probs * hit, axis=1, keepdims=True)


def expert_kernel(
    where_ref,
    own_ref,
    other_ref,
    hg_ref,
    inner_ref,
    router_ref,
    hidden_ref,
    pre_grad_ref,
    keep_ref,
    send_ref,
    router_out_ref,
    arrived_ref,
    whole_ref,
):
    core = where_ref[0]
    tile, half = own_ref.shape
    own_lanes = half_lanes(core, half)
    other_lanes = half_lanes(1 - core, half)
    arrived_ref[:, own_lanes] = own_ref[...]
    arrived_ref[:, other_lanes] = other_ref[...]
    arrived = arrived_ref[...]
    probs, hit, gate = gate_of(arrived, router_ref[...], where_ref[1])
    curve = 0.7978845608028654
    gate_grad = jnp.zeros((tile, 1), jnp.float32)
    back = jnp.zeros((tile, 2 * half), jnp.float32)
    chunk = 512
    for start in range(0, hg_ref.shape[1], chunk):
        cols = slice(start, start + chunk)
        pre = dot_nn(arrived, inner_ref[:, cols])
        hg = hg_ref[:, cols].astype(jnp.float32)
        square = pre * pre
        bend = jnp.tanh(pre * (curve + (curve * 0.044715) * square))
        grown = 0.5 + 0.5 * bend
        hidden = (pre * grown).astype(jnp.bfloat16)
        hidden_ref[:, cols] = hidden
        gate_grad = gate_grad + jnp.sum(hidden.astype(jnp.float32) * hg, axis=1, keepdims=True)
        slope = grown + (pre * (curve + (3 * curve * 0.044715) * square)) * (0.5 - 0.5 * bend * bend)
        pre_grad = (slope * (gate * hg)).astype(jnp.bfloat16)
        pre_grad_ref[:, cols] = pre_grad
        back = back + dot_nt(pre_grad, inner_ref[:, cols])
    logit = (probs * (gate_grad * (hit - gate))).astype(jnp.bfloat16)

    @pl.when(pl.program_id(0) == 0)
    def _():
        router_out_ref[...] = jnp.zeros_like(router_out_ref)

    router_out_ref[...] += contract_rows(logit, arrived)
    whole_ref[...] = back + dot_nt(logit, router_ref[...])
    send_ref[...] = whole_ref[:, other_lanes].astype(jnp.bfloat16)
    keep_ref[...] = whole_ref[:, own_lanes]


def expert(where, own, other, hidden_grad, inner, router):
    slots, half = own.shape
    width, hidden = inner.shape
    experts = router.shape[1]
    tile = 256
    halves = pl.BlockSpec((tile, half), lambda step: (step, 0))
    units = pl.BlockSpec((tile, hidden), lambda step: (step, 0))
    return pl.pallas_call(
        expert_kernel,
        grid=(slots // tile,),
        out_shape=[
            hbm_out((slots, hidden), jnp.bfloat16),
            hbm_out((slots, hidden), jnp.bfloat16),
            jax.ShapeDtypeStruct((slots, half), jnp.float32),
            jax.ShapeDtypeStruct((slots, half), jnp.bfloat16),
            hbm_out((experts, width), jnp.float32),
        ],
        in_specs=[pl.BlockSpec(memory_space=pltpu.SMEM), halves, halves, units] + vmem(2),
        out_specs=[
            units,
            units,
            halves,
            halves,
            pl.BlockSpec((experts, width), lambda step: (0, 0)),
        ],
        scratch_shapes=[
            pltpu.VMEM((tile, width), jnp.bfloat16),
            pltpu.VMEM((tile, width), jnp.float32),
        ],
        compiler_params=params(),
        cost_estimate=pl.CostEstimate(
            flops=4 * slots * width * hidden, bytes_accessed=20000000, transcendentals=slots * hidden
        ),
        name="expert",
    )(where, own, other, in_hbm(hidden_grad), inner, router)


def expert_out_kernel(where_ref, hidden_ref, outer_ref, keep_ref, send_ref, whole_ref):
    core = where_ref[0]
    half = keep_ref.shape[1]
    whole_ref[...] = dot_nn(hidden_ref[...], outer_ref[...])
    send_ref[...] = whole_ref[:, half_lanes(1 - core, half)].astype(jnp.bfloat16)
    keep_ref[...] = whole_ref[:, half_lanes(core, half)]


def expert_out_of(where, hidden, outer):
    slots, units = hidden.shape
    width = outer.shape[1]
    half = width // 2
    tile = 256
    halves = pl.BlockSpec((tile, half), lambda step: (step, 0))
    return pl.pallas_call(
        expert_out_kernel,
        grid=(slots // tile,),
        out_shape=[
            jax.ShapeDtypeStruct((slots, half), jnp.float32),
            jax.ShapeDtypeStruct((slots, half), jnp.bfloat16),
        ],
        in_specs=[
            pl.BlockSpec(memory_space=pltpu.SMEM),
            pl.BlockSpec((tile, units), lambda step: (step, 0)),
        ]
        + vmem(1),
        out_specs=[halves, halves],
        scratch_shapes=[pltpu.VMEM((tile, width), jnp.float32)],
        compiler_params=params(),
        cost_estimate=pl.CostEstimate(
            flops=2 * slots * width * units, bytes_accessed=9000000, transcendentals=0
        ),
        name="expert_out",
    )(where, in_hbm(hidden), outer)


def expert_grads_kernel(
    where_ref,
    own_hbm,
    other_hbm,
    grad_own_hbm,
    grad_other_hbm,
    hidden_ref,
    pre_grad_ref,
    router_ref,
    inner_grad_ref,
    outer_grad_ref,
    arrived_ref,
    gated_ref,
    sems,
):
    core = where_ref[0]
    half = own_hbm.shape[1]
    own_lanes = half_lanes(core, half)
    other_lanes = half_lanes(1 - core, half)

    @pl.when(pl.program_id(0) == 0)
    def _():
        copies = [
            pltpu.make_async_copy(own_hbm, arrived_ref.at[:, own_lanes], sems.at[0]),
            pltpu.make_async_copy(other_hbm, arrived_ref.at[:, other_lanes], sems.at[1]),
            pltpu.make_async_copy(grad_own_hbm, gated_ref.at[:, own_lanes], sems.at[2]),
            pltpu.make_async_copy(grad_other_hbm, gated_ref.at[:, other_lanes], sems.at[3]),
        ]
        for copy in copies:
            copy.start()
        for copy in copies:
            copy.wait()
        gate = gate_of(arrived_ref[...], router_ref[...], where_ref[1])[2]
        gated_ref[...] = (gate * gated_ref[...].astype(jnp.float32)).astype(jnp.bfloat16)

    outer_grad_ref[...] = contract_rows(hidden_ref[...], gated_ref[...])
    inner_grad_ref[...] = contract_rows(arrived_ref[...], pre_grad_ref[...])


def expert_grads(where, own, other, grad_own, grad_other, hidden, pre_grad, router):
    slots, half = own.shape
    units = hidden.shape[1]
    width = router.shape[0]
    tile = 256
    hbm = pl.BlockSpec(memory_space=pltpu.HBM)
    whole = lambda shape: pl.BlockSpec(shape, lambda step: (0, 0))
    cols = pl.BlockSpec((slots, tile), lambda step: (0, step))
    return pl.pallas_call(
        expert_grads_kernel,
        grid=(units // tile,),
        out_shape=[
            hbm_out((width, units), jnp.float32),
            hbm_out((units, width), jnp.float32),
        ],
        in_specs=[
            pl.BlockSpec(memory_space=pltpu.SMEM),
            hbm,
            hbm,
            hbm,
            hbm,
            cols,
            cols,
            whole(router.shape),
        ],
        out_specs=[
            pl.BlockSpec((width, tile), lambda step: (0, step)),
            pl.BlockSpec((tile, width), lambda step: (step, 0)),
        ],
        scratch_shapes=[
            pltpu.VMEM((slots, width), jnp.bfloat16),
            pltpu.VMEM((slots, width), jnp.bfloat16),
            pltpu.SemaphoreType.DMA((4,)),
        ],
        compiler_params=params(24),
        cost_estimate=pl.CostEstimate(
            flops=4 * slots * width * units, bytes_accessed=22000000, transcendentals=0
        ),
        name="expert_grads",
    )(
        where,
        in_hbm(own),
        in_hbm(other),
        in_hbm(grad_own),
        in_hbm(grad_other),
        in_hbm(hidden),
        in_hbm(pre_grad),
        router,
    )


def output_kernel(
    capacity, where_ref, col_ref, returned_ref, residual_ref, gain_ref, router_ref, out_ref
):
    slots, half = returned_ref.shape
    tile = residual_ref.shape[0]
    experts = router_ref.shape[1]
    col = col_ref[:, :1]
    place = lax.broadcasted_iota(jnp.int32, (tile, slots), 1)
    hot = jnp.where(place == col, 1.0, 0.0).astype(jnp.bfloat16)
    token_out = dot_nn(hot, returned_ref[...])
    residual = residual_ref[...]
    second = (residual * inverse_rms(residual) * gain_ref[...]).astype(jnp.bfloat16)
    logits = dot_nn(second, router_ref[...])
    exp_logit = jnp.exp(logits - jnp.max(logits, axis=1, keepdims=True))
    first = lax.broadcasted_iota(jnp.int32, (1, experts), 1) * capacity
    hit = jnp.where((col >= first) & (col < first + capacity), exp_logit, 0.0)
    gate = jnp.sum(hit, axis=1, keepdims=True) / jnp.sum(exp_logit, axis=1, keepdims=True)
    own = residual_ref[:, half_lanes(where_ref[0], half)]
    out_ref[...] = (own + gate * token_out).astype(jnp.bfloat16)


def output_of(where, slot_col, returned, residual, gain, router, capacity):
    tok_count, width = residual.shape
    slots, half = returned.shape
    tile = 256
    whole = lambda shape: pl.BlockSpec(shape, lambda step: (0, 0))
    return pl.pallas_call(
        partial(output_kernel, capacity),
        grid=(tok_count // tile,),
        out_shape=jax.ShapeDtypeStruct((tok_count, half), jnp.bfloat16),
        in_specs=[
            pl.BlockSpec(memory_space=pltpu.SMEM),
            pl.BlockSpec((tile, 128), lambda step: (step, 0)),
            whole(returned.shape),
            pl.BlockSpec((tile, width), lambda step: (step, 0)),
            whole((1, width)),
            whole(router.shape),
        ],
        out_specs=pl.BlockSpec((tile, half), lambda step: (step, 0)),
        compiler_params=params(),
        cost_estimate=pl.CostEstimate(
            flops=2 * tok_count * half * slots, bytes_accessed=6000000, transcendentals=0
        ),
        name="output",
    )(
        where, in_hbm(slot_col), in_hbm(returned), in_hbm(residual), gain.astype(jnp.float32)[None], router
    )


def normed_back_kernel(qg_ref, kg_ref, vg_ref, wq_ref, wk_ref, wv_ref, out_ref):
    out_ref[...] = (
        dot_nt(qg_ref[...], wq_ref[...])
        + dot_nt(kg_ref[...], wk_ref[...])
        + dot_nt(vg_ref[...], wv_ref[...])
    ).astype(jnp.bfloat16)


def normed_back(qg, kg, vg, w_query, w_key, w_value):
    tok_count, own = qg.shape
    width = w_query.shape[0]
    tile = 256
    rows = pl.BlockSpec((tile, own), lambda step: (step, 0))
    whole = pl.BlockSpec((width, own), lambda step: (0, 0))
    return pl.pallas_call(
        normed_back_kernel,
        grid=(tok_count // tile,),
        out_shape=jax.ShapeDtypeStruct((tok_count, width), jnp.bfloat16),
        in_specs=[rows] * 3 + [whole] * 3,
        out_specs=pl.BlockSpec((tile, width), lambda step: (step, 0)),
        compiler_params=params(),
        cost_estimate=pl.CostEstimate(
            flops=6 * tok_count * own * width, bytes_accessed=6000000, transcendentals=0
        ),
        name="normed_back",
    )(*(in_hbm(array) for array in (qg, kg, vg, w_query, w_key, w_value)))


def input_back_kernel(tokens_ref, own_ref, other_ref, gain_ref, residual_ref, out_ref):
    ybar = own_ref[...].astype(jnp.float32) + other_ref[...].astype(jnp.float32)
    values = tokens_ref[...].astype(jnp.float32)
    scale = inverse_rms(values)
    scaled = values * scale
    pulled = ybar * gain_ref[...]
    out_ref[...] = residual_ref[...] + scale * (
        pulled - scaled * jnp.mean(pulled * scaled, axis=1, keepdims=True)
    )


def input_back(tokens, own, other, gain, residual_grad):
    tok_count, width = tokens.shape
    tile = 256
    rows = pl.BlockSpec((tile, width), lambda step: (step, 0))
    return pl.pallas_call(
        input_back_kernel,
        grid=(tok_count // tile,),
        out_shape=jax.ShapeDtypeStruct((tok_count, width), jnp.float32),
        in_specs=[rows, rows, rows, pl.BlockSpec((1, width), lambda step: (0, 0)), rows],
        out_specs=rows,
        compiler_params=params(),
        cost_estimate=pl.CostEstimate(
            flops=10 * tok_count * width, bytes_accessed=11000000, transcendentals=0
        ),
        name="input_back",
    )(in_hbm(tokens), own, other, gain.astype(jnp.float32)[None], in_hbm(residual_grad))


def back_kernel(
    bits_ref,
    where_ref,
    col_hbm,
    own_hbm,
    other_hbm,
    residual_hbm,
    grad_hbm,
    wo_hbm,
    q_hbm,
    k_hbm,
    v_hbm,
    mixed_hbm,
    long_hbm,
    short_hbm,
    normed_hbm,
    wq_hbm,
    wk_hbm,
    wv_hbm,
    gain_one_ref,
    gain_two_ref,
    router_ref,
    out_hbm,
    qg_hbm,
    kg_hbm,
    vg_hbm,
    sent_a,
    sent_b,
    sent_c,
    kept_a,
    kept_b,
    kept_c,
    col_ref,
    own_ref,
    other_ref,
    residual_ref,
    grad_ref,
    wo_ref,
    q_ref,
    k_ref,
    v_ref,
    mixed_ref,
    long_ref,
    short_ref,
    normed_ref,
    wq_ref,
    wk_ref,
    wv_ref,
    attn_ref,
    heads_ref,
    qg_ref,
    kg_ref,
    vg_ref,
    sg_ref,
    tiles_ref,
    far_ref,
    stack_ref,
    small_ref,
    packed_ref,
    whole_ref,
    in_sems,
    out_sems,
):
    tok_count, width = residual_ref.shape
    slots, half = own_ref.shape
    own = mixed_ref.shape[1]
    experts = router_ref.shape[0]
    pairs = own // 128
    tile = 256
    steps = tok_count // tile
    core = where_ref[0]
    tiles_rows = [slice(step * tile, step * tile + tile) for step in range(steps)]

    first = [(own_hbm, own_ref), (other_hbm, other_ref), (col_hbm, col_ref)]
    first += [(residual_hbm.at[tiles_rows[0]], residual_ref.at[tiles_rows[0]])]
    first += [(grad_hbm.at[tiles_rows[0]], grad_ref.at[tiles_rows[0]]), (wo_hbm, wo_ref)]
    later = []
    for rows in tiles_rows[1:]:
        later.append((residual_hbm.at[rows], residual_ref.at[rows]))
        later.append((grad_hbm.at[rows], grad_ref.at[rows]))
    attention = [(q_hbm, q_ref), (k_hbm, k_ref), (v_hbm, v_ref), (mixed_hbm, mixed_ref), (short_hbm, short_ref)]
    for pair in range(pairs):
        both = slice(pair * 2, pair * 2 + 2)
        attention.append((long_hbm.at[both], long_ref.at[both]))
    weights = [(normed_hbm, normed_ref), (wq_hbm, wq_ref), (wk_hbm, wk_ref), (wv_hbm, wv_ref)]
    copies = start_copies(
        [
            (source, target, in_sems.at[index])
            for index, (source, target) in enumerate(first + later + attention + weights)
        ]
    )
    outs = []

    for copy in copies[: len(first)]:
        copy.wait()
    gain_two = gain_two_ref[...]
    gain_two_grad = jnp.zeros((1, width), jnp.float32)
    place = lax.broadcasted_iota(jnp.int32, (tile, slots), 1)
    for step, rows in enumerate(tiles_rows):
        if step > 0:
            for copy in copies[len(first) + 2 * step - 2 : len(first) + 2 * step]:
                copy.wait()
        hot = jnp.where(place == col_ref[rows, :1], 1.0, 0.0).astype(jnp.bfloat16)
        whole_ref[:, half_lanes(core, half)] = dot_nn(hot, own_ref[...])
        whole_ref[:, half_lanes(1 - core, half)] = dot_nn(hot, other_ref[...])
        ybar = whole_ref[...]
        values = residual_ref[rows, :]
        scale = inverse_rms(values)
        scaled = values * scale
        pulled = ybar * gain_two
        gain_two_grad = gain_two_grad + jnp.sum(ybar * scaled, axis=0, keepdims=True)
        back = scale * (pulled - scaled * jnp.mean(pulled * scaled, axis=1, keepdims=True))
        out = back + grad_ref[rows, :].astype(jnp.float32)
        residual_ref[rows, :] = out
        attn = out.astype(jnp.bfloat16)
        attn_ref[rows, :] = attn
        heads_ref[rows, :] = dot_nt(attn, wo_ref[...]).astype(jnp.bfloat16)
        outs += start_copies([(residual_ref.at[rows], out_hbm.at[rows], out_sems.at[step])])

    base = len(first) + len(later)
    for copy in copies[base : base + 5]:
        copy.wait()
    for pair in range(pairs):
        copies[base + 5 + pair].wait()
        attend_back_pair(
            pair, heads_ref, q_ref, k_ref, v_ref, mixed_ref, long_ref, short_ref, qg_ref, kg_ref, vg_ref,
            tiles_ref, far_ref, sg_ref,
        )
    outs += start_copies(
        [
            (qg_ref, qg_hbm, out_sems.at[steps]),
            (kg_ref, kg_hbm, out_sems.at[steps + 1]),
            (vg_ref, vg_hbm, out_sems.at[steps + 2]),
        ]
    )

    for start in range(0, own, 128):
        grad = contract_rows(mixed_ref[:, start : start + 128], attn_ref[...]).astype(jnp.bfloat16)
        for part in range(width // own):
            at = 3 * width + part * own + start
            stack_ref[at : at + 128, :] = grad[:, part * own : part * own + own]
    small_ref[0:experts, :] = router_ref[...]
    small_ref[experts + 1 : experts + 2, :] = gain_two_grad
    for head in range(2 * pairs):
        row = experts + 2 + head
        small_ref[row : row + 1, 0:512] = diagonals(tiles_ref[head])
        small_ref[row : row + 1, 512:640] = far_ref[head, 0:1, :]
        small_ref[row : row + 1, 640:768] = far_ref[head, 1:2, :]
    for copy in copies[base + 5 + pairs :]:
        copy.wait()
    total = jnp.zeros((width, 1), jnp.float32)
    rows = stack_ref.shape[0] // 3
    span = rows // 2

    def send_part(part, sent, kept):
        mine = bits_ref[part]
        sent_rows = pl.ds(pl.multiple_of(part * rows + (1 - mine) * span, span), span)
        kept_rows = pl.ds(pl.multiple_of(part * rows + mine * span, span), span)
        return start_copies(
            [
                (stack_ref.at[sent_rows], sent.at[:span], out_sems.at[steps + 4 + 2 * part]),
                (stack_ref.at[kept_rows], kept, out_sems.at[steps + 5 + 2 * part]),
            ]
        )

    for index, (grads_ref, w_ref) in enumerate(((qg_ref, wq_ref), (kg_ref, wk_ref), (vg_ref, wv_ref))):
        sums = []
        for start in range(0, width, tile):
            piece = slice(start, start + tile)
            grad = contract_rows(normed_ref[:, piece], grads_ref[...])
            sums.append(jnp.sum(grad * w_ref[piece, :].astype(jnp.float32), axis=1, keepdims=True))
            stack_ref[index * width + start : index * width + start + tile, :] = grad.astype(jnp.bfloat16)
        total = total + jnp.concatenate(sums, axis=0)
        if index > 0:
            outs += send_part(index - 1, (sent_a, sent_b)[index - 1], (kept_a, kept_b)[index - 1])
    outs += send_part(2, sent_c, kept_c)
    wide = jnp.transpose(jnp.broadcast_to(total, (width, 128)))
    small_ref[experts : experts + 1, :] = wide[:1, :] / gain_one_ref[...]
    small = small_ref[...]
    packed_ref[...] = jnp.concatenate([small[:, :own], small[:, own:]], axis=0).astype(jnp.bfloat16)
    outs += start_copies([(packed_ref, sent_a.at[span:], out_sems.at[steps + 3])])
    for copy in outs:
        copy.wait()


def back_pass(
    bits, where, slot_col, back_own, back_other, residual, out_grad, w_out, query_rows, key_rows,
    value_rows, mixed, long_probs, short_probs, normed, w_query, w_key, w_value, gain_one, gain_two,
    router_part,
):
    tok_count, width = normed.shape
    own = mixed.shape[1]
    slots, half = back_own.shape
    heads = long_probs.shape[0]
    count = router_part.shape[0] + 2 + heads
    span = 4 * width // 6
    tile = 256
    steps = tok_count // tile
    half_rows = hbm_out((span, own), jnp.bfloat16)
    pinned = (residual, out_grad, w_out, query_rows, key_rows, value_rows, mixed, long_probs, short_probs, normed,
              w_query, w_key, w_value)
    hbm = pl.BlockSpec(memory_space=pltpu.HBM)
    smem = pl.BlockSpec(memory_space=pltpu.SMEM)

    def scratch(array):
        return pltpu.VMEM(array.shape, array.dtype)

    flops = 2 * tok_count * width * (slots + 5 * own) + 10 * heads * (512 * 512 + 512 * 128) * 64
    out = pl.pallas_call(
        back_kernel,
        out_shape=[
            hbm_out((tok_count, width), jnp.float32),
            hbm_out((tok_count, own), jnp.bfloat16),
            hbm_out((tok_count, own), jnp.bfloat16),
            hbm_out((tok_count, own), jnp.bfloat16),
            hbm_out((span + 2 * count, own), jnp.bfloat16),
        ]
        + [half_rows] * 5,
        in_specs=[smem, smem] + [hbm] * 16 + vmem(3),
        out_specs=[hbm] * 10,
        scratch_shapes=[scratch(slot_col), scratch(back_own), scratch(back_other)]
        + [scratch(array) for array in pinned]
        + [
            pltpu.VMEM((tok_count, width), jnp.bfloat16),
            pltpu.VMEM((tok_count, own), jnp.bfloat16),
            pltpu.VMEM((tok_count, own), jnp.bfloat16),
            pltpu.VMEM((tok_count, own), jnp.bfloat16),
            pltpu.VMEM((tok_count, own), jnp.bfloat16),
            pltpu.VMEM((LONG_LEN, LONG_LEN), jnp.bfloat16),
            pltpu.VMEM((heads, 128, 384), jnp.float32),
            pltpu.VMEM((heads, 2, 128), jnp.float32),
            pltpu.VMEM((4 * width, own), jnp.bfloat16),
            pltpu.VMEM((count, width), jnp.float32),
            pltpu.VMEM((2 * count, own), jnp.bfloat16),
            pltpu.VMEM((tile, width), jnp.float32),
            pltpu.SemaphoreType.DMA((2 * steps + 4 + 5 + heads // 2 + 4,)),
            pltpu.SemaphoreType.DMA((steps + 10,)),
        ],
        compiler_params=params(30),
        cost_estimate=pl.CostEstimate(flops=flops, bytes_accessed=25000000, transcendentals=0),
        name="back",
    )(
        bits,
        where,
        in_hbm(slot_col),
        in_hbm(back_own),
        in_hbm(back_other),
        *(in_hbm(array) for array in pinned),
        gain_one.astype(jnp.float32)[None],
        gain_two.astype(jnp.float32)[None],
        router_part,
    )
    return out[0], out[1], out[2], out[3], out[4:7], out[7:]


def added(left, right):
    return (left.astype(jnp.float32) + right.astype(jnp.float32)).astype(jnp.bfloat16)


def fold_kernel(bits_ref, *refs):
    kept, got, sent, keep = refs[0:3], refs[3:6], refs[7:10], refs[10:13]
    before = refs[6]
    for part in range(3):
        span = kept[part].shape[0] // 2
        mine = bits_ref[part]
        for ref, start in ((sent[part], (1 - mine) * span), (keep[part], mine * span)):
            rows = pl.ds(pl.multiple_of(start, span), span)
            ref[:span, :] = added(kept[part][rows, :], got[part][rows, :])
    rows = kept[0].shape[0]
    sent[0][rows // 2 :, :] = added(before[rows:, :], got[0][rows:, :])


def fold(bits, kept, got, before):
    rows, lanes = kept[0].shape
    extra = before.shape[0] - rows
    half = jax.ShapeDtypeStruct((rows // 2, lanes), jnp.bfloat16)
    out = pl.pallas_call(
        fold_kernel,
        out_shape=[jax.ShapeDtypeStruct((rows // 2 + extra, lanes), jnp.bfloat16)] + [half] * 5,
        in_specs=[pl.BlockSpec(memory_space=pltpu.SMEM)] + vmem(7),
        out_specs=vmem(6),
        compiler_params=params(16),
        name="fold",
    )(bits, *kept, *got, before)
    return out[:3], out[3:]


def pack_kernel(*refs):
    kept, got, before, out = refs[0:3], refs[3:6], refs[6], refs[7]
    rows = kept[0].shape[0]
    for part in range(3):
        out[part * rows : (part + 1) * rows, :] = added(kept[part][...], got[part][:rows, :])
    out[3 * rows :, :] = added(before[rows:, :], got[0][rows:, :])


def pack(kept, got, before):
    rows, lanes = kept[0].shape
    return pl.pallas_call(
        pack_kernel,
        out_shape=jax.ShapeDtypeStruct((2 * rows + before.shape[0], lanes), jnp.bfloat16),
        in_specs=vmem(7),
        out_specs=vmem(1)[0],
        compiler_params=params(16),
        name="pack",
    )(*kept, *got, before)


def unpack_kernel(own_ref, got_ref, *out):
    rows = out[0].shape[0]
    for part in range(3):
        piece = slice(part * rows, (part + 1) * rows)
        out[part][...] = added(own_ref[piece, :], got_ref[piece, :])
    out[3][...] = own_ref[3 * rows :, :].astype(jnp.float32) + got_ref[3 * rows :, :].astype(jnp.float32)


def unpack(own, got, rows):
    lanes = own.shape[1]
    out = pl.pallas_call(
        unpack_kernel,
        out_shape=[jax.ShapeDtypeStruct((rows, lanes), jnp.bfloat16)] * 3
        + [jax.ShapeDtypeStruct((own.shape[0] - 3 * rows, lanes), jnp.float32)],
        in_specs=vmem(2),
        out_specs=vmem(4),
        compiler_params=params(16),
        name="unpack",
    )(own, got)
    return out[:3], out[3]


def join_kernel(bits_ref, *refs):
    own, got, out = refs[0:3], refs[3:6], refs[6:9]
    for part in range(3):
        span = own[part].shape[0]
        mine = bits_ref[part]
        out[part][pl.ds(pl.multiple_of(mine * span, span), span), :] = own[part][...]
        out[part][pl.ds(pl.multiple_of((1 - mine) * span, span), span), :] = got[part][...]


def join(bits, own, got):
    return pl.pallas_call(
        join_kernel,
        out_shape=[jax.ShapeDtypeStruct((p.shape[0] * 2, p.shape[1]), p.dtype) for p in own],
        in_specs=[pl.BlockSpec(memory_space=pltpu.SMEM)] + vmem(6),
        out_specs=vmem(3),
        compiler_params=params(16),
        name="join",
    )(bits, *own, *got)


def finish_kernel(bits_ref, *refs):
    own, got = refs[0:3], refs[3:6]
    query_ref, key_ref, value_ref, out_ref, whole_ref = refs[6:]
    span = own[0].shape[0]
    rows = 2 * span
    width, lanes = query_ref.shape
    for part in range(3):
        mine = bits_ref[part]
        whole_ref[pl.ds(pl.multiple_of(mine * span, span), span), :] = own[part][...].astype(jnp.float32)
        whole_ref[pl.ds(pl.multiple_of((1 - mine) * span, span), span), :] = got[part][...].astype(
            jnp.float32
        )
        for index, ref in enumerate((query_ref, key_ref, value_ref)):
            first = max(index * width, part * rows)
            last = min((index + 1) * width, (part + 1) * rows)
            if first < last:
                ref[first - index * width : last - index * width, :] = whole_ref[
                    first - part * rows : last - part * rows, :
                ]
        for index in range(width // lanes):
            base = 3 * width + index * lanes
            first = max(base, part * rows)
            last = min(base + lanes, (part + 1) * rows)
            if first < last:
                out_ref[first - base : last - base, index * lanes : (index + 1) * lanes] = whole_ref[
                    first - part * rows : last - part * rows, :
                ]


def finish(bits, own, got, width):
    span, lanes = own[0].shape
    return pl.pallas_call(
        finish_kernel,
        out_shape=[jax.ShapeDtypeStruct((width, lanes), jnp.float32)] * 3
        + [jax.ShapeDtypeStruct((lanes, width), jnp.float32)],
        in_specs=[pl.BlockSpec(memory_space=pltpu.SMEM)] + vmem(6),
        out_specs=vmem(4),
        scratch_shapes=[pltpu.VMEM((2 * span, lanes), jnp.float32)],
        compiler_params=params(24),
        name="finish",
    )(bits, *own, *got)


def swap_heads(rows):
    return lax.ppermute(rows, "heads", [(0, 1), (1, 0)])


def trade(rows, bit):
    count = lax.axis_size("seq")
    return lax.ppermute(rows, "seq", [(i, i ^ (1 << bit)) for i in range(count)])


def together(*groups):
    return lax.optimization_barrier(groups)


def contract_rows(left, right):
    return lax.dot_general(
        left, right, (((0,), (0,)), ((), ())), preferred_element_type=jnp.float32
    )


def on_device(
    tokens,
    gain_attn,
    w_query,
    w_key,
    w_value,
    w_out,
    bias_table,
    gain_ffn,
    w_router,
    w_inner,
    w_outer,
    routes,
    seq_lengths,
    out_grad,
):
    tok_count, width = tokens.shape
    bucket_count = bias_table.shape[0]
    experts = w_router.shape[1]
    capacity = max(2, 5 * tok_count // (4 * experts))
    senders = lax.axis_size("seq")
    bits = list(range(senders.bit_length() - 1))
    slots = experts * capacity
    half = width // 2
    own = w_query.shape[1]
    where = jnp.stack([lax.axis_index("heads"), lax.axis_index("seq")]).astype(jnp.int32)

    def exchange(rows):
        return lax.all_to_all(
            rows.reshape(senders, capacity, half), "seq", split_axis=0, concat_axis=0, tiled=True
        ).reshape(slots, half)

    def summed(keep, send):
        return (keep + swap_heads(send).astype(jnp.float32)).astype(jnp.bfloat16)

    slot_row, slot_col, grad_sent = route(where, routes, out_grad, experts, capacity)
    grad_sent, tokens = together(grad_sent, tokens)
    grad_own = exchange(grad_sent)
    attn_part, normed, query_rows, key_rows, value_rows, mixed, long_probs, short_probs = attend(
        seq_lengths, tokens, gain_attn, w_query, w_key, w_value, w_out, bias_table
    )
    residual, second_sent = second_rows(
        where, tokens, attn_part, swap_heads(attn_part), gain_ffn, slot_row, slots
    )
    second_sent, grad_own = together(second_sent, grad_own)
    arrived_own = exchange(second_sent)

    inner = w_inner[0]
    outer = w_outer[0]
    grad_other = swap_heads(grad_own)
    hidden_grad = hidden_grad_of(where, grad_own, grad_other, outer)
    arrived_own, hidden_grad = together(arrived_own, hidden_grad)
    arrived_other = swap_heads(arrived_own)
    hidden, pre_grad, keep, send, router_part = expert(
        where, arrived_own, arrived_other, hidden_grad, inner, w_router
    )
    back_sum, hidden = together(summed(keep, send), hidden)
    back_own = exchange(back_sum)
    out_keep, out_send = expert_out_of(where, hidden, outer)
    out_sum = summed(out_keep, out_send)
    back_own, out_sum = together(back_own, out_sum)
    back_other, out_sum = together(swap_heads(back_own), out_sum)
    returned = exchange(out_sum)

    depth = len(bits) - 1
    turns = [bits[k * depth // 3 : depth] + bits[: k * depth // 3] for k in range(3)]
    place = lax.axis_index("seq")
    mine = [jnp.stack([(place >> turn[k]) & 1 for turn in turns]).astype(jnp.int32) for k in range(depth)]
    residual_grad, query_grad, key_grad, value_grad, sent, kept = back_pass(
        mine[0], where, slot_col, back_own, back_other, residual, out_grad, w_out, query_rows, key_rows,
        value_rows, mixed, long_probs, short_probs, normed, w_query, w_key, w_value, gain_attn, gain_ffn,
        router_part,
    )

    def trades(arrays, k):
        return [trade(array, turn[k]) for array, turn in zip(arrays, turns)]

    for k in range(depth):
        got = trades(sent, k)
        if k == 0:
            output = output_of(where, slot_col, returned, residual, gain_ffn, w_router, capacity)
            got, output, query_grad = together(got, output, query_grad)
        if k == 1:
            normed_part = normed_back(query_grad, key_grad, value_grad, w_query, w_key, w_value)
            got, normed_part = together(got, normed_part)
        if k + 1 < depth:
            sent, kept = fold(mine[k + 1], kept, got, sent[0])
    normed_other = swap_heads(normed_part)
    packed = pack(kept, got, sent[0])
    packed, normed_other, pre_grad = together(packed, normed_other, pre_grad)
    got = trade(packed, bits[-1])
    inner_grad, outer_grad = expert_grads(
        where, arrived_own, arrived_other, grad_own, grad_other, hidden, pre_grad, w_router
    )
    got, inner_grad = together(got, inner_grad)
    summed_parts, small = unpack(packed, got, kept[0].shape[0])
    small = jnp.concatenate([small[: small.shape[0] // 2], small[small.shape[0] // 2 :]], axis=1)
    small_other = swap_heads(small)
    for k in reversed(range(1, depth)):
        got = trades(summed_parts, k)
        if k == 1:
            both = small[: experts + 1] + small_other[: experts + 1]
            router_grad = both[:experts].T
            table_grad = table_from(small[experts + 2 :], bucket_count)
            got, both, router_grad, table_grad = together(got, both, router_grad, table_grad)
        summed_parts = join(mine[k], summed_parts, got)
    got = trades(summed_parts, 0)
    input_grad = input_back(tokens, normed_part, normed_other, gain_attn, residual_grad)
    got, input_grad = together(got, input_grad)
    query_w_grad, key_w_grad, value_w_grad, out_w_grad = finish(mine[0], summed_parts, got, width)
    return (
        output,
        input_grad,
        both[experts],
        query_w_grad,
        key_w_grad,
        value_w_grad,
        out_w_grad,
        table_grad,
        small[experts + 1],
        router_grad,
        inner_grad[None],
        outer_grad[None],
    )


def solution(mesh):
    in_specs = (
        P("seq", None),
        P(),
        P(None, "heads"),
        P(None, "heads"),
        P(None, "heads"),
        P("heads", None),
        P(None, "heads"),
        P(),
        P(),
        P("seq", None, "heads"),
        P("seq", "heads", None),
        P("seq", None),
        P("seq"),
        P("seq", None),
    )
    out_specs = (
        P("seq", "heads"),
        P("seq", None),
        P(),
        P(None, "heads"),
        P(None, "heads"),
        P(None, "heads"),
        P("heads", None),
        P(None, "heads"),
        P(),
        P(),
        P("seq", None, "heads"),
        P("seq", "heads", None),
    )
    return jax.shard_map(
        on_device, mesh=mesh, in_specs=in_specs, out_specs=out_specs, check_vma=False
    )
```

```python
from functools import partial

import jax
import jax.numpy as jnp
from jax import lax
from jax.experimental import pallas as pl
from jax.experimental.pallas import tpu as pltpu
from jax.sharding import PartitionSpec as P

SHORT_LEN = 128
LONG_LEN = 512
SHORT_DEV = 4
LONG_DEV = 1


epsilon = 1e-06
highest = lax.Precision.HIGHEST
far_limits = (12, 16, 23, 32, 46, 64, 91)


def vmem(count):
    return [pl.BlockSpec(memory_space=pltpu.VMEM)] * count


def params(mib=16):
    return pltpu.CompilerParams(vmem_limit_bytes=mib * 1024 * 1024)


def dot_nn(left, right):
    return jnp.dot(left, right, preferred_element_type=jnp.float32)


def dot_nt(left, right):
    return lax.dot_general(
        left, right, (((1,), (1,)), ((), ())), preferred_element_type=jnp.float32
    )


def inverse_rms(values):
    return lax.rsqrt(jnp.mean(values * values, axis=-1, keepdims=True) + epsilon)


def diagonal_buckets(offset):
    distance = jnp.abs(offset)
    far_bucket = jnp.full(offset.shape, 8, jnp.int32)
    for limit in far_limits:
        far_bucket = far_bucket + (distance >= limit).astype(jnp.int32)
    return jnp.where(distance < 8, distance, far_bucket) + jnp.where(offset > 0, 16, 0)


def hbm_out(shape, dtype):
    return pltpu.HBM(shape, dtype)


def in_hbm(array):
    return pltpu.with_memory_space_constraint(array, pltpu.HBM)


def start_copies(pairs):
    copies = [pltpu.make_async_copy(*triple) for triple in pairs]
    for copy in copies:
        copy.start()
    return copies


def attend_kernel(
    block_rows,
    lengths_ref,
    tokens_hbm,
    gain_ref,
    wq_hbm,
    wk_hbm,
    wv_hbm,
    wo_hbm,
    table_ref,
    part_hbm,
    normed_hbm,
    q_hbm,
    k_hbm,
    v_hbm,
    mixed_hbm,
    long_hbm,
    short_hbm,
    tokens_ref,
    wq_ref,
    wk_ref,
    wv_ref,
    wo_ref,
    part_ref,
    normed_ref,
    q_ref,
    k_ref,
    v_ref,
    mixed_ref,
    long_ref,
    short_ref,
    diag_ref,
    in_sems,
    out_sems,
):
    tok_count, width = tokens_ref.shape
    pairs = wq_ref.shape[1] // 128
    short_tok = SHORT_DEV * SHORT_LEN
    tile = 256
    steps = tok_count // tile
    tiles_in = []
    for step in range(steps):
        rows = slice(step * tile, step * tile + tile)
        tiles_in.append((tokens_hbm.at[rows], tokens_ref.at[rows], in_sems.at[step]))
    weights = [(wq_hbm, wq_ref), (wk_hbm, wk_ref), (wv_hbm, wv_ref), (wo_hbm, wo_ref)]
    triples = [tiles_in[0]]
    triples += [(src, dst, in_sems.at[steps + index]) for index, (src, dst) in enumerate(weights[:3])]
    triples += tiles_in[1:]
    triples += [(weights[3][0], weights[3][1], in_sems.at[steps + 3])]
    copies = start_copies(triples)
    tile_copies = [copies[0]] + copies[4 : 3 + steps]
    weight_copies = copies[1:4] + copies[3 + steps :]
    outs = []

    offset = lax.broadcasted_iota(jnp.int32, (table_ref.shape[1], 512), 1) - 256
    hot = jnp.where(
        diagonal_buckets(offset)
        == lax.broadcasted_iota(jnp.int32, (table_ref.shape[1], 512), 0),
        1.0,
        0.0,
    )
    diag_ref[...] = dot_nn(table_ref[...], hot.astype(jnp.bfloat16))
    gain = gain_ref[...]
    for step in range(steps):
        rows = slice(step * tile, step * tile + tile)
        tile_copies[step].wait()
        values = tokens_ref[rows, :].astype(jnp.float32)
        normed = (values * inverse_rms(values) * gain).astype(jnp.bfloat16)
        normed_ref[rows, :] = normed
        if step == 0:
            for copy in weight_copies[:3]:
                copy.wait()
        q_ref[rows, :] = dot_nn(normed, wq_ref[...]).astype(jnp.bfloat16) * jnp.bfloat16(0.125)
        k_ref[rows, :] = dot_nn(normed, wk_ref[...]).astype(jnp.bfloat16)
        v_ref[rows, :] = dot_nn(normed, wv_ref[...]).astype(jnp.bfloat16)
    outs += start_copies(
        [
            (normed_ref, normed_hbm, out_sems.at[0]),
            (q_ref, q_hbm, out_sems.at[1]),
            (k_ref, k_hbm, out_sems.at[2]),
            (v_ref, v_hbm, out_sems.at[3]),
        ]
    )
    lane = lax.broadcasted_iota(jnp.int32, (1, 128), 1)
    key_place = lax.broadcasted_iota(jnp.int32, (1, LONG_LEN), 1)
    live_long = key_place < lengths_ref[SHORT_DEV]

    def softmax(scores):
        weights = jnp.exp(scores - jnp.max(scores, axis=1, keepdims=True))
        return (weights * (1.0 / jnp.sum(weights, axis=1, keepdims=True))).astype(jnp.bfloat16)

    def one_pair(pair):
        lanes = slice(pair * 128, pair * 128 + 128)
        tiles = []
        for sub in range(2):
            row = diag_ref[pair * 2 + sub : pair * 2 + sub + 1, :]
            spread = pltpu.roll(
                jnp.broadcast_to(row, (128, 512)), 256, 1, stride=1, stride_axis=0
            )
            tiles.append(
                (
                    spread[:, 0:128],
                    spread[:, 128:256],
                    spread[:, 384:512],
                    jnp.broadcast_to(row[:, 511:512], (128, 128)),
                    jnp.broadcast_to(row[:, 0:1], (128, 128)),
                )
            )
        out = []
        for sub in range(2):
            scores = []
            for block in range(SHORT_DEV):
                rows = slice(block * 128, block * 128 + 128)
                masked = jnp.where((lane >= 64) == (sub == 1), q_ref[rows, lanes], 0)
                live = key_place[:, :128] < lengths_ref[block]
                scores.append(
                    jnp.where(
                        live, dot_nt(masked, k_ref[rows, lanes]) + tiles[sub][0], -1000000000.0
                    )
                )
            probs = softmax(jnp.concatenate(scores, axis=0))
            short_ref[pair * 2 + sub] = probs
            mixed = []
            for block in range(SHORT_DEV):
                rows = slice(block * 128, block * 128 + 128)
                mixed.append(dot_nn(probs[rows], v_ref[rows, lanes]))
            out.append(jnp.concatenate(mixed, axis=0))
        mixed_ref[:short_tok, lanes] = jnp.where(lane < 64, out[0], out[1]).astype(jnp.bfloat16)
        keys = k_ref[short_tok:, lanes]
        values = v_ref[short_tok:, lanes]
        for start in range(0, LONG_LEN, block_rows):
            places = slice(start, start + block_rows)
            rows = slice(short_tok + start, short_tok + start + block_rows)
            queries = q_ref[rows, lanes]
            out = []
            for sub in range(2):
                masked = jnp.where((lane >= 64) == (sub == 1), queries, 0)
                same, above, below, far_above, far_below = tiles[sub]
                bias = jnp.concatenate(
                    [
                        jnp.concatenate(
                            [
                                same
                                if other == block
                                else above
                                if other == block + 1
                                else below
                                if other == block - 1
                                else far_above
                                if other > block
                                else far_below
                                for other in range(LONG_LEN // 128)
                            ],
                            axis=1,
                        )
                        for block in range(start // 128, (start + block_rows) // 128)
                    ],
                    axis=0,
                )
                scores = jnp.where(live_long, dot_nt(masked, keys) + bias, -1000000000.0)
                probs = softmax(scores)
                long_ref[pair * 2 + sub, places, :] = probs
                out.append(dot_nn(probs, values))
            mixed_ref[rows, lanes] = jnp.where(lane < 64, out[0], out[1]).astype(jnp.bfloat16)

    for pair in range(pairs):
        one_pair(pair)
        both = slice(pair * 2, pair * 2 + 2)
        outs += start_copies(
            [
                (long_ref.at[both], long_hbm.at[both], out_sems.at[4 + 2 * pair]),
                (short_ref.at[both], short_hbm.at[both], out_sems.at[5 + 2 * pair]),
            ]
        )
    weight_copies[3].wait()
    base = 4 + 2 * pairs
    outs += start_copies([(mixed_ref, mixed_hbm, out_sems.at[base])])
    for step in range(steps):
        rows = slice(step * tile, step * tile + tile)
        part_ref[rows, :] = dot_nn(mixed_ref[rows, :], wo_ref[...]).astype(part_ref.dtype)
        outs += start_copies([(part_ref.at[rows], part_hbm.at[rows], out_sems.at[base + 1 + step])])
    for copy in outs:
        copy.wait()


def attend(lengths, tokens, gain, w_query, w_key, w_value, w_out, table, block_rows=512):
    tok_count, width = tokens.shape
    own = w_query.shape[1]
    heads = own // 64
    heads_pad = -(-heads // 8) * 8
    table = jnp.pad(table.T, ((0, heads_pad - heads), (0, 0)))
    short_tok = SHORT_DEV * SHORT_LEN
    flops = 2 * tok_count * width * own * 4 + 4 * heads * (512 * 512 + short_tok * 128) * 64
    hbm = pl.BlockSpec(memory_space=pltpu.HBM)
    out_shapes = [
        ((tok_count, width), jnp.bfloat16),
        ((tok_count, width), jnp.bfloat16),
        ((tok_count, own), jnp.bfloat16),
        ((tok_count, own), jnp.bfloat16),
        ((tok_count, own), jnp.bfloat16),
        ((tok_count, own), jnp.bfloat16),
        ((heads, LONG_LEN, LONG_LEN), jnp.bfloat16),
        ((heads, short_tok, SHORT_LEN), jnp.bfloat16),
    ]
    steps = tok_count // 256
    return pl.pallas_call(
        partial(attend_kernel, block_rows),
        out_shape=[jax.ShapeDtypeStruct(*out_shapes[0])]
        + [hbm_out(shape, dtype) for shape, dtype in out_shapes[1:]],
        in_specs=[pl.BlockSpec(memory_space=pltpu.SMEM), hbm]
        + vmem(1)
        + [hbm] * 4
        + vmem(1),
        out_specs=[hbm] * 8,
        scratch_shapes=[pltpu.VMEM(tokens.shape, jnp.bfloat16)]
        + [pltpu.VMEM(w.shape, jnp.bfloat16) for w in (w_query, w_key, w_value, w_out)]
        + [pltpu.VMEM(shape, dtype) for shape, dtype in out_shapes]
        + [
            pltpu.VMEM((heads_pad, 512), jnp.float32),
            pltpu.SemaphoreType.DMA((steps + 4,)),
            pltpu.SemaphoreType.DMA((5 + 2 * (heads // 2) + steps,)),
        ],
        compiler_params=params(24),
        cost_estimate=pl.CostEstimate(
            flops=flops, bytes_accessed=16000000, transcendentals=heads * 512 * 640
        ),
        name="attend",
    )(
        lengths,
        in_hbm(tokens),
        gain.astype(jnp.float32)[None],
        in_hbm(w_query),
        in_hbm(w_key),
        in_hbm(w_value),
        in_hbm(w_out),
        table,
    )


def attend_back_pair(
    pair, hg_ref, q_ref, k_ref, v_ref, mixed_ref, long_ref, short_ref, grads_ref, tiles_ref, far_ref, sg_ref,
):
    short_tok = SHORT_DEV * SHORT_LEN
    lane = lax.broadcasted_iota(jnp.int32, (1, 128), 1)
    lanes = pl.ds(pl.multiple_of(pair * 128, 128), 128)
    blocks = LONG_LEN // 128
    heads_grad = hg_ref[:, lanes]
    products = heads_grad.astype(jnp.float32) * mixed_ref[:, lanes].astype(jnp.float32)
    q_t = jnp.transpose(q_ref[:, lanes])
    hg_t = jnp.transpose(heads_grad)
    qg = []
    kg_t = []
    vg_t = []
    for sub in range(2):
        head = pair * 2 + sub
        own = (lane >= 64) == (sub == 1)
        rows_t = slice(64 * sub, 64 * sub + 64)
        masked = jnp.where(own, heads_grad, 0)
        delta = jnp.sum(jnp.where(own, products, 0.0), axis=1, keepdims=True)
        grads = [
            dot_nt(masked[block * 128 : block * 128 + 128], v_ref[block * 128 : block * 128 + 128, lanes])
            for block in range(SHORT_DEV)
        ]
        probs = short_ref[head]
        part = probs.astype(jnp.float32) * (jnp.concatenate(grads, axis=0) - delta[:short_tok])
        same = part[:128]
        for block in range(1, SHORT_DEV):
            same = same + part[block * 128 : block * 128 + 128]
        part = part.astype(jnp.bfloat16)
        qg_parts = []
        kg_parts = []
        vg_parts = []
        for block in range(SHORT_DEV):
            rows = slice(block * 128, block * 128 + 128)
            qg_parts.append(dot_nn(part[rows], k_ref[rows, lanes]))
            kg_parts.append(dot_nn(q_t[rows_t, rows], part[rows]))
            vg_parts.append(dot_nn(hg_t[rows_t, rows], probs[rows]))
        above = jnp.zeros((128, 128), jnp.float32)
        below = above
        far_above = above
        far_below = above
        probs = long_ref[head]
        part = probs.astype(jnp.float32) * (
            dot_nt(masked[short_tok:], v_ref[short_tok:, lanes]) - delta[short_tok:]
        )
        for block in range(blocks):
            for other in range(blocks):
                piece = part[block * 128 : block * 128 + 128, other * 128 : other * 128 + 128]
                if other == block:
                    same = same + piece
                elif other == block + 1:
                    above = above + piece
                elif other == block - 1:
                    below = below + piece
                elif other > block:
                    far_above = far_above + piece
                else:
                    far_below = far_below + piece
        sg_ref[...] = part.astype(jnp.bfloat16)
        qg_parts.append(dot_nn(sg_ref[...], k_ref[short_tok:, lanes]))
        kg_parts.append(dot_nn(q_t[rows_t, short_tok:], sg_ref[...]))
        vg_parts.append(dot_nn(hg_t[rows_t, short_tok:], probs))
        qg.append(jnp.concatenate(qg_parts, axis=0))
        kg_t.append(jnp.concatenate(kg_parts, axis=1))
        vg_t.append(jnp.concatenate(vg_parts, axis=1))
        tiles_ref[head, :, 0:128] = same
        tiles_ref[head, :, 128:256] = above
        tiles_ref[head, :, 256:384] = below
        far_ref[head, 0:1, :] = jnp.sum(far_above, axis=0, keepdims=True)
        far_ref[head, 1:2, :] = jnp.sum(far_below, axis=0, keepdims=True)
    width = q_ref.shape[1]
    grads_ref[:, lanes] = (jnp.where(lane < 64, qg[0], qg[1]) * 0.125).astype(jnp.bfloat16)
    for index, whole in ((1, kg_t), (2, vg_t)):
        place = pl.ds(pl.multiple_of(index * width + pair * 128, 128), 128)
        grads_ref[:, place] = jnp.transpose(jnp.concatenate(whole, axis=0).astype(jnp.bfloat16))


def diagonals(tiles):
    tile = jnp.concatenate(
        [tiles[:, 0:256], jnp.zeros((128, 128), jnp.float32), tiles[:, 256:384]], axis=1
    )
    span = 64
    while span:
        tile = tile[:span] + pltpu.roll(tile[span:], 512 - span, 1)
        span //= 2
    return tile


def table_from(diag, bucket_count):
    lane = jnp.arange(768, dtype=jnp.int32)
    offset = jnp.where(lane < 256, lane, lane - 512)
    offset = jnp.where(lane >= 640, -256, jnp.where(lane >= 512, 256, offset))
    hot = (diagonal_buckets(offset)[:, None] == jnp.arange(bucket_count)[None, :]).astype(jnp.float32)
    return lax.dot_general(
        hot, diag, (((0,), (1,)), ((), ())), precision=highest, preferred_element_type=jnp.float32
    )


def dispatch_rows(send_ref, slot_row, half_rows):
    slots = send_ref.shape[0]
    tok_count = slot_row.shape[1]
    span = 256

    def one_block(block, carry):
        base = pl.multiple_of(block * span, span)
        place = lax.broadcasted_iota(jnp.int32, (span, tok_count), 0) + base
        hot = jnp.where(place == slot_row, 1.0, 0.0).astype(jnp.bfloat16)
        send_ref[pl.ds(base, span), :] = dot_nn(hot, half_rows).astype(jnp.bfloat16)
        return carry

    lax.fori_loop(0, slots // span, one_block, 0)


def half_lanes(core, half):
    return pl.ds(pl.multiple_of(core * half, half), half)


def route_kernel(
    capacity, where_ref, routes_ref, grad_hbm, row_hbm, col_hbm, send_ref, grad_ref, row_ref, col_ref, in_sem,
    out_sems,
):
    tok_count = routes_ref.shape[1]
    slots, half = send_ref.shape
    experts = slots // capacity
    copy = pltpu.make_async_copy(
        grad_hbm.at[:, half_lanes(where_ref[0], half)], grad_ref, in_sem
    )
    copy.start()
    routes = routes_ref[...]
    expert = lax.broadcasted_iota(jnp.int32, (experts, tok_count), 0)
    lane = lax.broadcasted_iota(jnp.int32, (1, tok_count), 1)
    hot = jnp.where(expert == routes, 1.0, 0.0)
    total = hot
    step = 1
    while step < tok_count:
        total = total + jnp.where(lane >= step, pltpu.roll(total, step, 1), 0.0)
        step *= 2
    before = jnp.sum(hot * total, axis=0, keepdims=True).astype(jnp.int32) - 1
    slot = jnp.where(before < capacity, routes * capacity + before, slots)
    row_ref[...] = slot
    wide = jnp.broadcast_to(slot.astype(jnp.float32), (128, tok_count))
    col_ref[...] = jnp.transpose(wide).astype(jnp.int32)
    outs = start_copies([(row_ref, row_hbm, out_sems.at[0]), (col_ref, col_hbm, out_sems.at[1])])
    copy.wait()
    dispatch_rows(send_ref, slot, grad_ref[...])
    for copy in outs:
        copy.wait()


def route(where, routes, out_grad, experts, capacity):
    tok_count, width = out_grad.shape
    slots = experts * capacity
    return pl.pallas_call(
        partial(route_kernel, capacity),
        out_shape=[
            hbm_out((1, tok_count), jnp.int32),
            hbm_out((tok_count, 128), jnp.int32),
            jax.ShapeDtypeStruct((slots, width // 2), jnp.bfloat16),
        ],
        in_specs=[
            pl.BlockSpec(memory_space=pltpu.SMEM),
            pl.BlockSpec((1, tok_count), lambda: (0, 0)),
            pl.BlockSpec(memory_space=pltpu.HBM),
        ],
        out_specs=[pl.BlockSpec(memory_space=pltpu.HBM)] * 2 + vmem(1),
        scratch_shapes=[
            pltpu.VMEM((tok_count, width // 2), jnp.bfloat16),
            pltpu.VMEM((1, tok_count), jnp.int32),
            pltpu.VMEM((tok_count, 128), jnp.int32),
            pltpu.SemaphoreType.DMA,
            pltpu.SemaphoreType.DMA((2,)),
        ],
        compiler_params=params(),
        cost_estimate=pl.CostEstimate(
            flops=slots * tok_count * width, bytes_accessed=4000000, transcendentals=0
        ),
        name="route",
    )(where, routes.reshape(1, tok_count), in_hbm(out_grad))


def second_kernel(
    where_ref, tokens_hbm, own_ref, other_ref, gain_ref, row_hbm, residual_hbm, send_ref, tokens_ref,
    row_ref, residual_ref, second_ref, in_sems, out_sems,
):
    tile = 256
    tok_count = tokens_ref.shape[0]
    half = send_ref.shape[1]
    tiles_rows = [slice(start, start + tile) for start in range(0, tok_count, tile)]
    copies = start_copies(
        [
            (tokens_hbm.at[rows], tokens_ref.at[rows], in_sems.at[step])
            for step, rows in enumerate(tiles_rows)
        ]
        + [(row_hbm, row_ref, in_sems.at[len(tiles_rows)])]
    )
    outs = []
    gain = gain_ref[...]
    for step, rows in enumerate(tiles_rows):
        attn = own_ref[rows, :].astype(jnp.float32) + other_ref[rows, :].astype(jnp.float32)
        copies[step].wait()
        residual = tokens_ref[rows, :].astype(jnp.float32) + attn
        residual_ref[rows, :] = residual
        outs += start_copies([(residual_ref.at[rows], residual_hbm.at[rows], out_sems.at[step])])
        second_ref[rows, :] = (residual * inverse_rms(residual) * gain).astype(jnp.bfloat16)
    copies[-1].wait()
    dispatch_rows(send_ref, row_ref[...], second_ref[:, half_lanes(where_ref[0], half)])
    for copy in outs:
        copy.wait()


def second_rows(where, tokens, own, other, gain, slot_row, slots):
    tok_count, width = tokens.shape
    steps = tok_count // 256
    hbm = pl.BlockSpec(memory_space=pltpu.HBM)
    return pl.pallas_call(
        second_kernel,
        out_shape=[
            hbm_out((tok_count, width), jnp.float32),
            jax.ShapeDtypeStruct((slots, width // 2), jnp.bfloat16),
        ],
        in_specs=[pl.BlockSpec(memory_space=pltpu.SMEM), hbm] + vmem(3) + [hbm],
        out_specs=[hbm] + vmem(1),
        scratch_shapes=[
            pltpu.VMEM((tok_count, width), jnp.bfloat16),
            pltpu.VMEM((1, tok_count), jnp.int32),
            pltpu.VMEM((tok_count, width), jnp.float32),
            pltpu.VMEM((tok_count, width), jnp.bfloat16),
            pltpu.SemaphoreType.DMA((steps + 1,)),
            pltpu.SemaphoreType.DMA((steps,)),
        ],
        compiler_params=params(),
        cost_estimate=pl.CostEstimate(
            flops=slots * tok_count * width, bytes_accessed=13000000, transcendentals=0
        ),
        name="second",
    )(where, in_hbm(tokens), own, other, gain.astype(jnp.float32)[None], in_hbm(slot_row))


def hidden_grad_kernel(where_ref, own_ref, other_ref, outer_ref, out_ref, whole_ref):
    half = own_ref.shape[1]
    core = where_ref[0]
    whole_ref[:, half_lanes(core, half)] = own_ref[...]
    whole_ref[:, half_lanes(1 - core, half)] = other_ref[...]
    out_ref[...] = dot_nt(whole_ref[...], outer_ref[...]).astype(jnp.bfloat16)


def hidden_grad_of(where, own, other, outer):
    slots, half = own.shape
    hidden = outer.shape[0]
    tile = 256
    rows = pl.BlockSpec((tile, half), lambda step: (step, 0))
    return pl.pallas_call(
        hidden_grad_kernel,
        grid=(slots // tile,),
        out_shape=hbm_out((slots, hidden), jnp.bfloat16),
        in_specs=[pl.BlockSpec(memory_space=pltpu.SMEM), rows, rows] + vmem(1),
        out_specs=pl.BlockSpec((tile, hidden), lambda step: (step, 0)),
        scratch_shapes=[pltpu.VMEM((tile, 2 * half), jnp.bfloat16)],
        compiler_params=params(),
        cost_estimate=pl.CostEstimate(
            flops=4 * slots * half * hidden, bytes_accessed=12000000, transcendentals=0
        ),
        name="hidden_grad",
    )(where, own, other, outer)


def gate_of(rows, router, index):
    experts = router.shape[1]
    logits = dot_nn(rows, router)
    exp_logit = jnp.exp(logits - jnp.max(logits, axis=1, keepdims=True))
    probs = exp_logit * (1.0 / jnp.sum(exp_logit, axis=1, keepdims=True))
    hit = jnp.where(lax.broadcasted_iota(jnp.int32, (1, experts), 1) == index, 1.0, 0.0)
    return probs, hit, jnp.sum(probs * hit, axis=1, keepdims=True)


def expert_kernel(
    where_ref,
    own_ref,
    other_ref,
    hg_ref,
    inner_ref,
    router_ref,
    hidden_ref,
    pre_grad_ref,
    keep_ref,
    send_ref,
    router_out_ref,
    arrived_ref,
    whole_ref,
):
    core = where_ref[0]
    tile, half = own_ref.shape
    own_lanes = half_lanes(core, half)
    other_lanes = half_lanes(1 - core, half)
    arrived_ref[:, own_lanes] = own_ref[...]
    arrived_ref[:, other_lanes] = other_ref[...]
    arrived = arrived_ref[...]
    probs, hit, gate = gate_of(arrived, router_ref[...], where_ref[1])
    curve = 0.7978845608028654
    gate_grad = jnp.zeros((tile, 1), jnp.float32)
    back = jnp.zeros((tile, 2 * half), jnp.float32)
    chunk = 512
    for start in range(0, hg_ref.shape[1], chunk):
        cols = slice(start, start + chunk)
        pre = dot_nn(arrived, inner_ref[:, cols])
        hg = hg_ref[:, cols].astype(jnp.float32)
        square = pre * pre
        bend = jnp.tanh(pre * (curve + (curve * 0.044715) * square))
        grown = 0.5 + 0.5 * bend
        hidden = (pre * grown).astype(jnp.bfloat16)
        hidden_ref[:, cols] = hidden
        gate_grad = gate_grad + jnp.sum(hidden.astype(jnp.float32) * hg, axis=1, keepdims=True)
        slope = grown + (pre * (curve + (3 * curve * 0.044715) * square)) * (0.5 - 0.5 * bend * bend)
        pre_grad = (slope * (gate * hg)).astype(jnp.bfloat16)
        pre_grad_ref[:, cols] = pre_grad
        back = back + dot_nt(pre_grad, inner_ref[:, cols])
    logit = (probs * (gate_grad * (hit - gate))).astype(jnp.bfloat16)

    @pl.when(pl.program_id(0) == 0)
    def _():
        router_out_ref[...] = jnp.zeros_like(router_out_ref)

    router_out_ref[...] += contract_rows(logit, arrived)
    whole_ref[...] = back + dot_nt(logit, router_ref[...])
    send_ref[...] = whole_ref[:, other_lanes].astype(jnp.bfloat16)
    keep_ref[...] = whole_ref[:, own_lanes]


def expert(where, own, other, hidden_grad, inner, router):
    slots, half = own.shape
    width, hidden = inner.shape
    experts = router.shape[1]
    tile = 256
    halves = pl.BlockSpec((tile, half), lambda step: (step, 0))
    units = pl.BlockSpec((tile, hidden), lambda step: (step, 0))
    return pl.pallas_call(
        expert_kernel,
        grid=(slots // tile,),
        out_shape=[
            hbm_out((slots, hidden), jnp.bfloat16),
            hbm_out((slots, hidden), jnp.bfloat16),
            jax.ShapeDtypeStruct((slots, half), jnp.float32),
            jax.ShapeDtypeStruct((slots, half), jnp.bfloat16),
            hbm_out((experts, width), jnp.float32),
        ],
        in_specs=[
            pl.BlockSpec(memory_space=pltpu.SMEM),
            halves,
            halves,
            units,
            pl.BlockSpec(inner.shape, lambda step: (0, 0), pipeline_mode=pl.Buffered(1)),
        ]
        + vmem(1),
        out_specs=[
            units,
            units,
            halves,
            halves,
            pl.BlockSpec((experts, width), lambda step: (0, 0)),
        ],
        scratch_shapes=[
            pltpu.VMEM((tile, width), jnp.bfloat16),
            pltpu.VMEM((tile, width), jnp.float32),
        ],
        compiler_params=params(),
        cost_estimate=pl.CostEstimate(
            flops=4 * slots * width * hidden, bytes_accessed=20000000, transcendentals=slots * hidden
        ),
        name="expert",
    )(where, own, other, in_hbm(hidden_grad), in_hbm(inner), router)


def expert_out_kernel(where_ref, hidden_ref, outer_ref, keep_ref, send_ref, whole_ref):
    core = where_ref[0]
    half = keep_ref.shape[1]
    whole_ref[...] = dot_nn(hidden_ref[...], outer_ref[...])
    send_ref[...] = whole_ref[:, half_lanes(1 - core, half)].astype(jnp.bfloat16)
    keep_ref[...] = whole_ref[:, half_lanes(core, half)]


def expert_out_of(where, hidden, outer):
    slots, units = hidden.shape
    width = outer.shape[1]
    half = width // 2
    tile = 256
    halves = pl.BlockSpec((tile, half), lambda step: (step, 0))
    return pl.pallas_call(
        expert_out_kernel,
        grid=(slots // tile,),
        out_shape=[
            jax.ShapeDtypeStruct((slots, half), jnp.float32),
            jax.ShapeDtypeStruct((slots, half), jnp.bfloat16),
        ],
        in_specs=[
            pl.BlockSpec(memory_space=pltpu.SMEM),
            pl.BlockSpec((tile, units), lambda step: (step, 0)),
        ]
        + vmem(1),
        out_specs=[halves, halves],
        scratch_shapes=[pltpu.VMEM((tile, width), jnp.float32)],
        compiler_params=params(),
        cost_estimate=pl.CostEstimate(
            flops=2 * slots * width * units, bytes_accessed=9000000, transcendentals=0
        ),
        name="expert_out",
    )(where, in_hbm(hidden), outer)


def expert_grads_kernel(
    where_ref,
    own_hbm,
    other_hbm,
    grad_own_hbm,
    grad_other_hbm,
    hidden_ref,
    pre_grad_ref,
    router_ref,
    inner_grad_ref,
    outer_grad_ref,
    arrived_ref,
    gated_ref,
    sems,
):
    core = where_ref[0]
    half = own_hbm.shape[1]
    own_lanes = half_lanes(core, half)
    other_lanes = half_lanes(1 - core, half)

    @pl.when(pl.program_id(0) == 0)
    def _():
        copies = [
            pltpu.make_async_copy(own_hbm, arrived_ref.at[:, own_lanes], sems.at[0]),
            pltpu.make_async_copy(other_hbm, arrived_ref.at[:, other_lanes], sems.at[1]),
            pltpu.make_async_copy(grad_own_hbm, gated_ref.at[:, own_lanes], sems.at[2]),
            pltpu.make_async_copy(grad_other_hbm, gated_ref.at[:, other_lanes], sems.at[3]),
        ]
        for copy in copies:
            copy.start()
        for copy in copies:
            copy.wait()
        gate = gate_of(arrived_ref[...], router_ref[...], where_ref[1])[2]
        gated_ref[...] = (gate * gated_ref[...].astype(jnp.float32)).astype(jnp.bfloat16)

    outer_grad_ref[...] = contract_rows(hidden_ref[...], gated_ref[...])
    inner_grad_ref[...] = contract_rows(arrived_ref[...], pre_grad_ref[...])


def expert_grads(where, own, other, grad_own, grad_other, hidden, pre_grad, router):
    slots, half = own.shape
    units = hidden.shape[1]
    width = router.shape[0]
    tile = 256
    hbm = pl.BlockSpec(memory_space=pltpu.HBM)
    whole = lambda shape: pl.BlockSpec(shape, lambda step: (0, 0))
    cols = pl.BlockSpec((slots, tile), lambda step: (0, step))
    return pl.pallas_call(
        expert_grads_kernel,
        grid=(units // tile,),
        out_shape=[
            hbm_out((width, units), jnp.float32),
            hbm_out((units, width), jnp.float32),
        ],
        in_specs=[
            pl.BlockSpec(memory_space=pltpu.SMEM),
            hbm,
            hbm,
            hbm,
            hbm,
            cols,
            cols,
            whole(router.shape),
        ],
        out_specs=[
            pl.BlockSpec((width, tile), lambda step: (0, step)),
            pl.BlockSpec((tile, width), lambda step: (step, 0)),
        ],
        scratch_shapes=[
            pltpu.VMEM((slots, width), jnp.bfloat16),
            pltpu.VMEM((slots, width), jnp.bfloat16),
            pltpu.SemaphoreType.DMA((4,)),
        ],
        compiler_params=params(24),
        cost_estimate=pl.CostEstimate(
            flops=4 * slots * width * units, bytes_accessed=22000000, transcendentals=0
        ),
        name="expert_grads",
    )(
        where,
        in_hbm(own),
        in_hbm(other),
        in_hbm(grad_own),
        in_hbm(grad_other),
        in_hbm(hidden),
        in_hbm(pre_grad),
        router,
    )


def output_kernel(
    capacity, where_ref, col_ref, returned_ref, residual_ref, gain_ref, router_ref, out_ref
):
    slots, half = returned_ref.shape
    tile = residual_ref.shape[0]
    experts = router_ref.shape[1]
    col = col_ref[:, :1]
    place = lax.broadcasted_iota(jnp.int32, (tile, slots), 1)
    hot = jnp.where(place == col, 1.0, 0.0).astype(jnp.bfloat16)
    token_out = dot_nn(hot, returned_ref[...])
    residual = residual_ref[...]
    second = (residual * inverse_rms(residual) * gain_ref[...]).astype(jnp.bfloat16)
    logits = dot_nn(second, router_ref[...])
    exp_logit = jnp.exp(logits - jnp.max(logits, axis=1, keepdims=True))
    first = lax.broadcasted_iota(jnp.int32, (1, experts), 1) * capacity
    hit = jnp.where((col >= first) & (col < first + capacity), exp_logit, 0.0)
    gate = jnp.sum(hit, axis=1, keepdims=True) / jnp.sum(exp_logit, axis=1, keepdims=True)
    own = residual_ref[:, half_lanes(where_ref[0], half)]
    out_ref[...] = (own + gate * token_out).astype(jnp.bfloat16)


def output_of(where, slot_col, returned, residual, gain, router, capacity):
    tok_count, width = residual.shape
    slots, half = returned.shape
    tile = 256
    whole = lambda shape: pl.BlockSpec(shape, lambda step: (0, 0))
    return pl.pallas_call(
        partial(output_kernel, capacity),
        grid=(tok_count // tile,),
        out_shape=jax.ShapeDtypeStruct((tok_count, half), jnp.bfloat16),
        in_specs=[
            pl.BlockSpec(memory_space=pltpu.SMEM),
            pl.BlockSpec((tile, 128), lambda step: (step, 0)),
            whole(returned.shape),
            pl.BlockSpec((tile, width), lambda step: (step, 0)),
            whole((1, width)),
            whole(router.shape),
        ],
        out_specs=pl.BlockSpec((tile, half), lambda step: (step, 0)),
        compiler_params=params(),
        cost_estimate=pl.CostEstimate(
            flops=2 * tok_count * half * slots, bytes_accessed=6000000, transcendentals=0
        ),
        name="output",
    )(
        where, in_hbm(slot_col), in_hbm(returned), in_hbm(residual), gain.astype(jnp.float32)[None], router
    )


def normed_back_kernel(grads_ref, wq_ref, wk_ref, wv_ref, out_ref):
    own = wq_ref.shape[1]
    out_ref[...] = (
        dot_nt(grads_ref[:, :own], wq_ref[...])
        + dot_nt(grads_ref[:, own : 2 * own], wk_ref[...])
        + dot_nt(grads_ref[:, 2 * own :], wv_ref[...])
    ).astype(jnp.bfloat16)


def normed_back(grads, w_query, w_key, w_value):
    tok_count = grads.shape[0]
    width, own = w_query.shape
    tile = 256
    whole = pl.BlockSpec((width, own), lambda step: (0, 0))
    return pl.pallas_call(
        normed_back_kernel,
        grid=(tok_count // tile,),
        out_shape=jax.ShapeDtypeStruct((tok_count, width), jnp.bfloat16),
        in_specs=[pl.BlockSpec((tile, 3 * own), lambda step: (step, 0))] + [whole] * 3,
        out_specs=pl.BlockSpec((tile, width), lambda step: (step, 0)),
        compiler_params=params(),
        cost_estimate=pl.CostEstimate(
            flops=6 * tok_count * own * width, bytes_accessed=6000000, transcendentals=0
        ),
        name="normed_back",
    )(*(in_hbm(array) for array in (grads, w_query, w_key, w_value)))


def input_back_kernel(tokens_ref, own_ref, other_ref, gain_ref, residual_ref, out_ref):
    ybar = own_ref[...].astype(jnp.float32) + other_ref[...].astype(jnp.float32)
    values = tokens_ref[...].astype(jnp.float32)
    scale = inverse_rms(values)
    scaled = values * scale
    pulled = ybar * gain_ref[...]
    out_ref[...] = residual_ref[...] + scale * (
        pulled - scaled * jnp.mean(pulled * scaled, axis=1, keepdims=True)
    )


def input_back(tokens, own, other, gain, residual_grad):
    tok_count, width = tokens.shape
    tile = 256
    rows = pl.BlockSpec((tile, width), lambda step: (step, 0))
    return pl.pallas_call(
        input_back_kernel,
        grid=(tok_count // tile,),
        out_shape=jax.ShapeDtypeStruct((tok_count, width), jnp.float32),
        in_specs=[rows, rows, rows, pl.BlockSpec((1, width), lambda step: (0, 0)), rows],
        out_specs=rows,
        compiler_params=params(),
        cost_estimate=pl.CostEstimate(
            flops=10 * tok_count * width, bytes_accessed=11000000, transcendentals=0
        ),
        name="input_back",
    )(in_hbm(tokens), own, other, gain.astype(jnp.float32)[None], in_hbm(residual_grad))


def back_kernel(
    bits_ref,
    where_ref,
    col_hbm,
    own_hbm,
    other_hbm,
    residual_hbm,
    grad_hbm,
    wo_hbm,
    q_hbm,
    k_hbm,
    v_hbm,
    mixed_hbm,
    long_hbm,
    short_hbm,
    normed_hbm,
    wq_hbm,
    wk_hbm,
    wv_hbm,
    gain_one_ref,
    gain_two_ref,
    router_ref,
    out_hbm,
    grads_hbm,
    sent_a,
    sent_b,
    sent_c,
    kept_a,
    kept_b,
    kept_c,
    col_ref,
    back_ref,
    residual_ref,
    grad_ref,
    wo_ref,
    q_ref,
    k_ref,
    v_ref,
    mixed_ref,
    long_ref,
    short_ref,
    normed_ref,
    wq_ref,
    wk_ref,
    wv_ref,
    attn_ref,
    heads_ref,
    grads_ref,
    sg_ref,
    tiles_ref,
    far_ref,
    stack_ref,
    small_ref,
    packed_ref,
    in_sems,
    out_sems,
):
    tok_count, width = residual_ref.shape
    slots, half = own_hbm.shape
    own = mixed_ref.shape[1]
    experts = router_ref.shape[0]
    pairs = own // 128
    tile = 256
    steps = tok_count // tile
    core = where_ref[0]
    tiles_rows = [slice(step * tile, step * tile + tile) for step in range(steps)]

    first = [
        (own_hbm, back_ref.at[:, half_lanes(core, half)]),
        (other_hbm, back_ref.at[:, half_lanes(1 - core, half)]),
        (col_hbm, col_ref),
    ]
    first += [(residual_hbm.at[tiles_rows[0]], residual_ref.at[tiles_rows[0]])]
    first += [(grad_hbm.at[tiles_rows[0]], grad_ref.at[tiles_rows[0]]), (wo_hbm, wo_ref)]
    later = []
    for rows in tiles_rows[1:]:
        later.append((residual_hbm.at[rows], residual_ref.at[rows]))
        later.append((grad_hbm.at[rows], grad_ref.at[rows]))
    attention = [(q_hbm, q_ref), (k_hbm, k_ref), (v_hbm, v_ref), (mixed_hbm, mixed_ref), (short_hbm, short_ref)]
    for pair in range(pairs):
        both = slice(pair * 2, pair * 2 + 2)
        attention.append((long_hbm.at[both], long_ref.at[both]))
    weights = [(normed_hbm, normed_ref), (wq_hbm, wq_ref), (wk_hbm, wk_ref), (wv_hbm, wv_ref)]
    copies = start_copies(
        [
            (source, target, in_sems.at[index])
            for index, (source, target) in enumerate(first + later + attention + weights)
        ]
    )
    outs = []

    for copy in copies[: len(first)]:
        copy.wait()
    gain_two = gain_two_ref[...]
    gain_two_grad = jnp.zeros((1, width), jnp.float32)
    place = lax.broadcasted_iota(jnp.int32, (tile, slots), 1)
    for step, rows in enumerate(tiles_rows):
        if step > 0:
            for copy in copies[len(first) + 2 * step - 2 : len(first) + 2 * step]:
                copy.wait()
        hot = jnp.where(place == col_ref[rows, :1], 1.0, 0.0).astype(jnp.bfloat16)
        ybar = dot_nn(hot, back_ref[...])
        values = residual_ref[rows, :]
        scale = inverse_rms(values)
        scaled = values * scale
        pulled = ybar * gain_two
        gain_two_grad = gain_two_grad + jnp.sum(ybar * scaled, axis=0, keepdims=True)
        back = scale * (pulled - scaled * jnp.mean(pulled * scaled, axis=1, keepdims=True))
        out = back + grad_ref[rows, :].astype(jnp.float32)
        residual_ref[rows, :] = out
        attn = out.astype(jnp.bfloat16)
        attn_ref[rows, :] = attn
        heads_ref[rows, :] = dot_nt(attn, wo_ref[...]).astype(jnp.bfloat16)
        outs += start_copies([(residual_ref.at[rows], out_hbm.at[rows], out_sems.at[step])])

    base = len(first) + len(later)
    for copy in copies[base : base + 5]:
        copy.wait()

    def one_pair(pair, carry):
        both = pl.ds(pair * 2, 2)
        pltpu.make_async_copy(long_hbm.at[both], long_ref.at[both], in_sems.at[base + 5 + pair]).wait()
        attend_back_pair(
            pair, heads_ref, q_ref, k_ref, v_ref, mixed_ref, long_ref, short_ref, grads_ref, tiles_ref, far_ref,
            sg_ref,
        )
        return carry

    lax.fori_loop(0, pairs, one_pair, 0)
    outs += start_copies([(grads_ref, grads_hbm, out_sems.at[steps])])

    for start in range(0, own, 128):
        grad = contract_rows(mixed_ref[:, start : start + 128], attn_ref[...]).astype(jnp.bfloat16)
        for part in range(width // own):
            at = 3 * width + part * own + start
            stack_ref[at : at + 128, :] = grad[:, part * own : part * own + own]
    small_ref[0:experts, :] = router_ref[...]
    small_ref[experts + 1 : experts + 2, :] = gain_two_grad
    for head in range(2 * pairs):
        row = experts + 2 + head
        small_ref[row : row + 1, 0:512] = diagonals(tiles_ref[head])
        small_ref[row : row + 1, 512:640] = far_ref[head, 0:1, :]
        small_ref[row : row + 1, 640:768] = far_ref[head, 1:2, :]
    for copy in copies[base + 5 + pairs :]:
        copy.wait()
    totals = []
    rows = stack_ref.shape[0] // 3
    span = rows // 2

    def send_part(part, sent, kept):
        mine = bits_ref[part]
        sent_rows = pl.ds(pl.multiple_of(part * rows + (1 - mine) * span, span), span)
        kept_rows = pl.ds(pl.multiple_of(part * rows + mine * span, span), span)
        return start_copies(
            [
                (stack_ref.at[sent_rows], sent.at[:span], out_sems.at[steps + 4 + 2 * part]),
                (stack_ref.at[kept_rows], kept, out_sems.at[steps + 5 + 2 * part]),
            ]
        )

    for start in range(0, width, tile):
        piece = slice(start, start + tile)
        grad = contract_rows(normed_ref[:, piece], grads_ref[...])
        for index, w_ref in enumerate((wq_ref, wk_ref, wv_ref)):
            part = grad[:, index * own : index * own + own]
            totals.append(jnp.sum(part * w_ref[piece, :].astype(jnp.float32), axis=1, keepdims=True))
            stack_ref[index * width + start : index * width + start + tile, :] = part.astype(jnp.bfloat16)
    for part, (sent, kept) in enumerate(((sent_a, kept_a), (sent_b, kept_b))):
        outs += send_part(part, sent, kept)
    outs += send_part(2, sent_c, kept_c)
    total = jnp.concatenate([sum(totals[3 * k : 3 * k + 3]) for k in range(width // tile)], axis=0)
    wide = jnp.transpose(jnp.broadcast_to(total, (width, 128)))
    small_ref[experts : experts + 1, :] = wide[:1, :] / gain_one_ref[...]
    small = small_ref[...]
    packed_ref[...] = jnp.concatenate([small[:, :own], small[:, own:]], axis=0).astype(jnp.bfloat16)
    outs += start_copies([(packed_ref, sent_a.at[span:], out_sems.at[steps + 3])])
    for copy in outs:
        copy.wait()


def back_pass(
    bits, where, slot_col, back_own, back_other, residual, out_grad, w_out, query_rows, key_rows,
    value_rows, mixed, long_probs, short_probs, normed, w_query, w_key, w_value, gain_one, gain_two,
    router_part,
):
    tok_count, width = normed.shape
    own = mixed.shape[1]
    slots, half = back_own.shape
    heads = long_probs.shape[0]
    count = router_part.shape[0] + 2 + heads
    span = 4 * width // 6
    tile = 256
    steps = tok_count // tile
    half_rows = hbm_out((span, own), jnp.bfloat16)
    pinned = (residual, out_grad, w_out, query_rows, key_rows, value_rows, mixed, long_probs, short_probs, normed,
              w_query, w_key, w_value)
    hbm = pl.BlockSpec(memory_space=pltpu.HBM)
    smem = pl.BlockSpec(memory_space=pltpu.SMEM)

    def scratch(array):
        return pltpu.VMEM(array.shape, array.dtype)

    flops = 2 * tok_count * width * (slots + 5 * own) + 10 * heads * (512 * 512 + 512 * 128) * 64
    out = pl.pallas_call(
        back_kernel,
        out_shape=[
            hbm_out((tok_count, width), jnp.float32),
            hbm_out((tok_count, 3 * own), jnp.bfloat16),
            hbm_out((span + 2 * count, own), jnp.bfloat16),
        ]
        + [half_rows] * 5,
        in_specs=[smem, smem] + [hbm] * 16 + vmem(3),
        out_specs=[hbm] * 8,
        scratch_shapes=[scratch(slot_col), pltpu.VMEM((slots, width), jnp.bfloat16)]
        + [scratch(array) for array in pinned]
        + [
            pltpu.VMEM((tok_count, width), jnp.bfloat16),
            pltpu.VMEM((tok_count, own), jnp.bfloat16),
            pltpu.VMEM((tok_count, 3 * own), jnp.bfloat16),
            pltpu.VMEM((LONG_LEN, LONG_LEN), jnp.bfloat16),
            pltpu.VMEM((heads, 128, 384), jnp.float32),
            pltpu.VMEM((heads, 2, 128), jnp.float32),
            pltpu.VMEM((4 * width, own), jnp.bfloat16),
            pltpu.VMEM((count, width), jnp.float32),
            pltpu.VMEM((2 * count, own), jnp.bfloat16),
            pltpu.SemaphoreType.DMA((2 * steps + 4 + 5 + heads // 2 + 4,)),
            pltpu.SemaphoreType.DMA((steps + 10,)),
        ],
        compiler_params=params(30),
        cost_estimate=pl.CostEstimate(flops=flops, bytes_accessed=25000000, transcendentals=0),
        name="back",
    )(
        bits,
        where,
        in_hbm(slot_col),
        in_hbm(back_own),
        in_hbm(back_other),
        *(in_hbm(array) for array in pinned),
        gain_one.astype(jnp.float32)[None],
        gain_two.astype(jnp.float32)[None],
        router_part,
    )
    return out[0], out[1], out[2:5], out[5:]


def added(left, right):
    return (left.astype(jnp.float32) + right.astype(jnp.float32)).astype(jnp.bfloat16)


def fold_kernel(bits_ref, *refs):
    kept, got, sent, keep = refs[0:3], refs[3:6], refs[7:10], refs[10:13]
    before = refs[6]
    for part in range(3):
        span = kept[part].shape[0] // 2
        mine = bits_ref[part]
        for ref, start in ((sent[part], (1 - mine) * span), (keep[part], mine * span)):
            rows = pl.ds(pl.multiple_of(start, span), span)
            ref[:span, :] = added(kept[part][rows, :], got[part][rows, :])
    rows = kept[0].shape[0]
    sent[0][rows // 2 :, :] = added(before[rows:, :], got[0][rows:, :])


def fold(bits, kept, got, before):
    rows, lanes = kept[0].shape
    extra = before.shape[0] - rows
    half = jax.ShapeDtypeStruct((rows // 2, lanes), jnp.bfloat16)
    out = pl.pallas_call(
        fold_kernel,
        out_shape=[jax.ShapeDtypeStruct((rows // 2 + extra, lanes), jnp.bfloat16)] + [half] * 5,
        in_specs=[pl.BlockSpec(memory_space=pltpu.SMEM)] + vmem(7),
        out_specs=vmem(6),
        compiler_params=params(16),
        name="fold",
    )(bits, *kept, *got, before)
    return out[:3], out[3:]


def pack_kernel(*refs):
    kept, got, before, out = refs[0:3], refs[3:6], refs[6], refs[7]
    rows = kept[0].shape[0]
    for part in range(3):
        out[part * rows : (part + 1) * rows, :] = added(kept[part][...], got[part][:rows, :])
    out[3 * rows :, :] = added(before[rows:, :], got[0][rows:, :])


def pack(kept, got, before):
    rows, lanes = kept[0].shape
    return pl.pallas_call(
        pack_kernel,
        out_shape=jax.ShapeDtypeStruct((2 * rows + before.shape[0], lanes), jnp.bfloat16),
        in_specs=vmem(7),
        out_specs=vmem(1)[0],
        compiler_params=params(16),
        name="pack",
    )(*kept, *got, before)


def unpack_kernel(own_ref, got_ref, *out):
    rows = out[0].shape[0]
    for part in range(3):
        piece = slice(part * rows, (part + 1) * rows)
        out[part][...] = added(own_ref[piece, :], got_ref[piece, :])
    out[3][...] = own_ref[3 * rows :, :].astype(jnp.float32) + got_ref[3 * rows :, :].astype(jnp.float32)


def unpack(own, got, rows):
    lanes = own.shape[1]
    out = pl.pallas_call(
        unpack_kernel,
        out_shape=[jax.ShapeDtypeStruct((rows, lanes), jnp.bfloat16)] * 3
        + [jax.ShapeDtypeStruct((own.shape[0] - 3 * rows, lanes), jnp.float32)],
        in_specs=vmem(2),
        out_specs=vmem(4),
        compiler_params=params(16),
        name="unpack",
    )(own, got)
    return out[:3], out[3]


def join_kernel(bits_ref, *refs):
    own, got, out = refs[0:3], refs[3:6], refs[6:9]
    for part in range(3):
        span = own[part].shape[0]
        mine = bits_ref[part]
        out[part][pl.ds(pl.multiple_of(mine * span, span), span), :] = own[part][...]
        out[part][pl.ds(pl.multiple_of((1 - mine) * span, span), span), :] = got[part][...]


def join(bits, own, got):
    return pl.pallas_call(
        join_kernel,
        out_shape=[jax.ShapeDtypeStruct((p.shape[0] * 2, p.shape[1]), p.dtype) for p in own],
        in_specs=[pl.BlockSpec(memory_space=pltpu.SMEM)] + vmem(6),
        out_specs=vmem(3),
        compiler_params=params(16),
        name="join",
    )(bits, *own, *got)


def finish_kernel(bits_ref, *refs):
    own, got = refs[0:3], refs[3:6]
    query_ref, key_ref, value_ref, out_ref, whole_ref = refs[6:]
    span = own[0].shape[0]
    rows = 2 * span
    width, lanes = query_ref.shape
    for part in range(3):
        mine = bits_ref[part]
        whole_ref[pl.ds(pl.multiple_of(mine * span, span), span), :] = own[part][...].astype(jnp.float32)
        whole_ref[pl.ds(pl.multiple_of((1 - mine) * span, span), span), :] = got[part][...].astype(
            jnp.float32
        )
        for index, ref in enumerate((query_ref, key_ref, value_ref)):
            first = max(index * width, part * rows)
            last = min((index + 1) * width, (part + 1) * rows)
            if first < last:
                ref[first - index * width : last - index * width, :] = whole_ref[
                    first - part * rows : last - part * rows, :
                ]
        for index in range(width // lanes):
            base = 3 * width + index * lanes
            first = max(base, part * rows)
            last = min(base + lanes, (part + 1) * rows)
            if first < last:
                out_ref[first - base : last - base, index * lanes : (index + 1) * lanes] = whole_ref[
                    first - part * rows : last - part * rows, :
                ]


def finish(bits, own, got, width):
    span, lanes = own[0].shape
    return pl.pallas_call(
        finish_kernel,
        out_shape=[jax.ShapeDtypeStruct((width, lanes), jnp.float32)] * 3
        + [jax.ShapeDtypeStruct((lanes, width), jnp.float32)],
        in_specs=[pl.BlockSpec(memory_space=pltpu.SMEM)] + vmem(6),
        out_specs=vmem(4),
        scratch_shapes=[pltpu.VMEM((2 * span, lanes), jnp.float32)],
        compiler_params=params(24),
        name="finish",
    )(bits, *own, *got)


def swap_heads(rows):
    return lax.ppermute(rows, "heads", [(0, 1), (1, 0)])


def trade(rows, bit):
    count = lax.axis_size("seq")
    return lax.ppermute(rows, "seq", [(i, i ^ (1 << bit)) for i in range(count)])


def together(*groups):
    return lax.optimization_barrier(groups)


def contract_rows(left, right):
    return lax.dot_general(
        left, right, (((0,), (0,)), ((), ())), preferred_element_type=jnp.float32
    )


def on_device(
    tokens,
    gain_attn,
    w_query,
    w_key,
    w_value,
    w_out,
    bias_table,
    gain_ffn,
    w_router,
    w_inner,
    w_outer,
    routes,
    seq_lengths,
    out_grad,
):
    tok_count, width = tokens.shape
    bucket_count = bias_table.shape[0]
    experts = w_router.shape[1]
    capacity = max(2, 5 * tok_count // (4 * experts))
    senders = lax.axis_size("seq")
    bits = list(range(senders.bit_length() - 1))
    slots = experts * capacity
    half = width // 2
    own = w_query.shape[1]
    where = jnp.stack([lax.axis_index("heads"), lax.axis_index("seq")]).astype(jnp.int32)

    def exchange(rows):
        return lax.all_to_all(
            rows.reshape(senders, capacity, half), "seq", split_axis=0, concat_axis=0, tiled=True
        ).reshape(slots, half)

    def summed(keep, send):
        return (keep + swap_heads(send).astype(jnp.float32)).astype(jnp.bfloat16)

    slot_row, slot_col, grad_sent = route(where, routes, out_grad, experts, capacity)
    grad_sent, tokens = together(grad_sent, tokens)
    grad_own = exchange(grad_sent)
    attn_part, normed, query_rows, key_rows, value_rows, mixed, long_probs, short_probs = attend(
        seq_lengths, tokens, gain_attn, w_query, w_key, w_value, w_out, bias_table
    )
    residual, second_sent = second_rows(
        where, tokens, attn_part, swap_heads(attn_part), gain_ffn, slot_row, slots
    )
    second_sent, grad_own = together(second_sent, grad_own)
    arrived_own = exchange(second_sent)

    inner = w_inner[0]
    outer = w_outer[0]
    grad_other = swap_heads(grad_own)
    hidden_grad = hidden_grad_of(where, grad_own, grad_other, outer)
    arrived_own, hidden_grad = together(arrived_own, hidden_grad)
    arrived_other = swap_heads(arrived_own)
    hidden, pre_grad, keep, send, router_part = expert(
        where, arrived_own, arrived_other, hidden_grad, inner, w_router
    )
    back_sum, hidden = together(summed(keep, send), hidden)
    back_own = exchange(back_sum)
    out_keep, out_send = expert_out_of(where, hidden, outer)
    out_sum = summed(out_keep, out_send)
    back_own, out_sum = together(back_own, out_sum)
    back_other, out_sum = together(swap_heads(back_own), out_sum)
    returned = exchange(out_sum)

    depth = len(bits) - 1
    turns = [bits[k * depth // 3 : depth] + bits[: k * depth // 3] for k in range(3)]
    place = lax.axis_index("seq")
    mine = [jnp.stack([(place >> turn[k]) & 1 for turn in turns]).astype(jnp.int32) for k in range(depth)]
    residual_grad, head_grads, sent, kept = back_pass(
        mine[0], where, slot_col, back_own, back_other, residual, out_grad, w_out, query_rows, key_rows,
        value_rows, mixed, long_probs, short_probs, normed, w_query, w_key, w_value, gain_attn, gain_ffn,
        router_part,
    )

    def trades(arrays, k):
        return [trade(array, turn[k]) for array, turn in zip(arrays, turns)]

    for k in range(depth):
        got = trades(sent, k)
        if k == 0:
            output = output_of(where, slot_col, returned, residual, gain_ffn, w_router, capacity)
            got, output, head_grads = together(got, output, head_grads)
        if k == 1:
            normed_part = normed_back(head_grads, w_query, w_key, w_value)
            got, normed_part = together(got, normed_part)
        if k + 1 < depth:
            sent, kept = fold(mine[k + 1], kept, got, sent[0])
    normed_other = swap_heads(normed_part)
    packed = pack(kept, got, sent[0])
    packed, normed_other, pre_grad = together(packed, normed_other, pre_grad)
    got = trade(packed, bits[-1])
    inner_grad, outer_grad = expert_grads(
        where, arrived_own, arrived_other, grad_own, grad_other, hidden, pre_grad, w_router
    )
    got, inner_grad = together(got, inner_grad)
    summed_parts, small = unpack(packed, got, kept[0].shape[0])
    small = jnp.concatenate([small[: small.shape[0] // 2], small[small.shape[0] // 2 :]], axis=1)
    small_other = swap_heads(small)
    for k in reversed(range(1, depth)):
        got = trades(summed_parts, k)
        if k == 1:
            both = small[: experts + 1] + small_other[: experts + 1]
            router_grad = both[:experts].T
            table_grad = table_from(small[experts + 2 :], bucket_count)
            got, both, router_grad, table_grad = together(got, both, router_grad, table_grad)
        summed_parts = join(mine[k], summed_parts, got)
    got = trades(summed_parts, 0)
    input_grad = input_back(tokens, normed_part, normed_other, gain_attn, residual_grad)
    got, input_grad = together(got, input_grad)
    query_w_grad, key_w_grad, value_w_grad, out_w_grad = finish(mine[0], summed_parts, got, width)
    return (
        output,
        input_grad,
        both[experts],
        query_w_grad,
        key_w_grad,
        value_w_grad,
        out_w_grad,
        table_grad,
        small[experts + 1],
        router_grad,
        inner_grad[None],
        outer_grad[None],
    )


def solution(mesh):
    in_specs = (
        P("seq", None),
        P(),
        P(None, "heads"),
        P(None, "heads"),
        P(None, "heads"),
        P("heads", None),
        P(None, "heads"),
        P(),
        P(),
        P("seq", None, "heads"),
        P("seq", "heads", None),
        P("seq", None),
        P("seq"),
        P("seq", None),
    )
    out_specs = (
        P("seq", "heads"),
        P("seq", None),
        P(),
        P(None, "heads"),
        P(None, "heads"),
        P(None, "heads"),
        P("heads", None),
        P(None, "heads"),
        P(),
        P(),
        P("seq", None, "heads"),
        P("seq", "heads", None),
    )
    return jax.shard_map(
        on_device, mesh=mesh, in_specs=in_specs, out_specs=out_specs, check_vma=False
    )
```

```python
from functools import partial

import jax
import jax.numpy as jnp
from jax import lax
from jax.experimental import pallas as pl
from jax.experimental.pallas import tpu as pltpu
from jax.sharding import PartitionSpec as P

SHORT_LEN = 128
LONG_LEN = 512
SHORT_DEV = 4
LONG_DEV = 1


epsilon = 1e-06
highest = lax.Precision.HIGHEST
far_limits = (12, 16, 23, 32, 46, 64, 91)


def vmem(count):
    return [pl.BlockSpec(memory_space=pltpu.VMEM)] * count


def params(mib=16):
    return pltpu.CompilerParams(vmem_limit_bytes=mib * 1024 * 1024)


def dot_nn(left, right):
    return jnp.dot(left, right, preferred_element_type=jnp.float32)


def dot_nt(left, right):
    return lax.dot_general(
        left, right, (((1,), (1,)), ((), ())), preferred_element_type=jnp.float32
    )


def inverse_rms(values):
    return lax.rsqrt(jnp.mean(values * values, axis=-1, keepdims=True) + epsilon)


def diagonal_buckets(offset):
    distance = jnp.abs(offset)
    far_bucket = jnp.full(offset.shape, 8, jnp.int32)
    for limit in far_limits:
        far_bucket = far_bucket + (distance >= limit).astype(jnp.int32)
    return jnp.where(distance < 8, distance, far_bucket) + jnp.where(offset > 0, 16, 0)


def hbm_out(shape, dtype):
    return pltpu.HBM(shape, dtype)


def in_hbm(array):
    return pltpu.with_memory_space_constraint(array, pltpu.HBM)


def start_copies(pairs):
    copies = [pltpu.make_async_copy(*triple) for triple in pairs]
    for copy in copies:
        copy.start()
    return copies


def attend_kernel(
    block_rows,
    lengths_ref,
    tokens_hbm,
    gain_ref,
    wq_hbm,
    wk_hbm,
    wv_hbm,
    wo_hbm,
    table_ref,
    part_hbm,
    normed_hbm,
    q_hbm,
    k_hbm,
    v_hbm,
    mixed_hbm,
    long_hbm,
    short_hbm,
    tokens_ref,
    wq_ref,
    wk_ref,
    wv_ref,
    wo_ref,
    part_ref,
    normed_ref,
    q_ref,
    k_ref,
    v_ref,
    mixed_ref,
    long_ref,
    short_ref,
    diag_ref,
    in_sems,
    out_sems,
):
    tok_count, width = tokens_ref.shape
    pairs = wq_ref.shape[1] // 128
    short_tok = SHORT_DEV * SHORT_LEN
    tile = 256
    steps = tok_count // tile
    tiles_in = []
    for step in range(steps):
        rows = slice(step * tile, step * tile + tile)
        tiles_in.append((tokens_hbm.at[rows], tokens_ref.at[rows], in_sems.at[step]))
    weights = [(wq_hbm, wq_ref), (wk_hbm, wk_ref), (wv_hbm, wv_ref), (wo_hbm, wo_ref)]
    triples = [tiles_in[0]]
    triples += [(src, dst, in_sems.at[steps + index]) for index, (src, dst) in enumerate(weights[:3])]
    triples += tiles_in[1:]
    triples += [(weights[3][0], weights[3][1], in_sems.at[steps + 3])]
    copies = start_copies(triples)
    weight_copies = copies[1:4] + copies[3 + steps :]
    outs = []

    offset = lax.broadcasted_iota(jnp.int32, (table_ref.shape[1], 512), 1) - 256
    hot = jnp.where(
        diagonal_buckets(offset)
        == lax.broadcasted_iota(jnp.int32, (table_ref.shape[1], 512), 0),
        1.0,
        0.0,
    )
    diag_ref[...] = dot_nn(table_ref[...], hot.astype(jnp.bfloat16))
    gain = gain_ref[...]
    for copy in weight_copies[:3]:
        copy.wait()

    def project(step, carry):
        rows = pl.ds(pl.multiple_of(step * tile, tile), tile)
        pltpu.make_async_copy(tokens_hbm.at[rows], tokens_ref.at[rows], in_sems.at[step]).wait()
        values = tokens_ref[rows, :].astype(jnp.float32)
        normed = (values * inverse_rms(values) * gain).astype(jnp.bfloat16)
        normed_ref[rows, :] = normed
        q_ref[rows, :] = dot_nn(normed, wq_ref[...]).astype(jnp.bfloat16) * jnp.bfloat16(0.125)
        k_ref[rows, :] = dot_nn(normed, wk_ref[...]).astype(jnp.bfloat16)
        v_ref[rows, :] = dot_nn(normed, wv_ref[...]).astype(jnp.bfloat16)
        return carry

    lax.fori_loop(0, steps, project, 0)
    outs += start_copies(
        [
            (normed_ref, normed_hbm, out_sems.at[0]),
            (q_ref, q_hbm, out_sems.at[1]),
            (k_ref, k_hbm, out_sems.at[2]),
            (v_ref, v_hbm, out_sems.at[3]),
        ]
    )
    lane = lax.broadcasted_iota(jnp.int32, (1, 128), 1)
    key_place = lax.broadcasted_iota(jnp.int32, (1, LONG_LEN), 1)
    live_long = key_place < lengths_ref[SHORT_DEV]

    def softmax(scores):
        weights = jnp.exp(scores - jnp.max(scores, axis=1, keepdims=True))
        return (weights * (1.0 / jnp.sum(weights, axis=1, keepdims=True))).astype(jnp.bfloat16)

    def one_pair(pair):
        lanes = slice(pair * 128, pair * 128 + 128)
        tiles = []
        for sub in range(2):
            row = diag_ref[pair * 2 + sub : pair * 2 + sub + 1, :]
            spread = pltpu.roll(
                jnp.broadcast_to(row, (128, 512)), 256, 1, stride=1, stride_axis=0
            )
            tiles.append(
                (
                    spread[:, 0:128],
                    spread[:, 128:256],
                    spread[:, 384:512],
                    jnp.broadcast_to(row[:, 511:512], (128, 128)),
                    jnp.broadcast_to(row[:, 0:1], (128, 128)),
                )
            )
        out = []
        for sub in range(2):
            scores = []
            for block in range(SHORT_DEV):
                rows = slice(block * 128, block * 128 + 128)
                masked = jnp.where((lane >= 64) == (sub == 1), q_ref[rows, lanes], 0)
                live = key_place[:, :128] < lengths_ref[block]
                scores.append(
                    jnp.where(
                        live, dot_nt(masked, k_ref[rows, lanes]) + tiles[sub][0], -1000000000.0
                    )
                )
            probs = softmax(jnp.concatenate(scores, axis=0))
            short_ref[pair * 2 + sub] = probs
            mixed = []
            for block in range(SHORT_DEV):
                rows = slice(block * 128, block * 128 + 128)
                mixed.append(dot_nn(probs[rows], v_ref[rows, lanes]))
            out.append(jnp.concatenate(mixed, axis=0))
        mixed_ref[:short_tok, lanes] = jnp.where(lane < 64, out[0], out[1]).astype(jnp.bfloat16)
        keys = k_ref[short_tok:, lanes]
        values = v_ref[short_tok:, lanes]
        for start in range(0, LONG_LEN, block_rows):
            places = slice(start, start + block_rows)
            rows = slice(short_tok + start, short_tok + start + block_rows)
            queries = q_ref[rows, lanes]
            out = []
            for sub in range(2):
                masked = jnp.where((lane >= 64) == (sub == 1), queries, 0)
                same, above, below, far_above, far_below = tiles[sub]
                bias = jnp.concatenate(
                    [
                        jnp.concatenate(
                            [
                                same
                                if other == block
                                else above
                                if other == block + 1
                                else below
                                if other == block - 1
                                else far_above
                                if other > block
                                else far_below
                                for other in range(LONG_LEN // 128)
                            ],
                            axis=1,
                        )
                        for block in range(start // 128, (start + block_rows) // 128)
                    ],
                    axis=0,
                )
                scores = jnp.where(live_long, dot_nt(masked, keys) + bias, -1000000000.0)
                probs = softmax(scores)
                long_ref[pair * 2 + sub, places, :] = probs
                out.append(dot_nn(probs, values))
            mixed_ref[rows, lanes] = jnp.where(lane < 64, out[0], out[1]).astype(jnp.bfloat16)

    for pair in range(pairs):
        one_pair(pair)
        both = slice(pair * 2, pair * 2 + 2)
        outs += start_copies(
            [
                (long_ref.at[both], long_hbm.at[both], out_sems.at[4 + 2 * pair]),
                (short_ref.at[both], short_hbm.at[both], out_sems.at[5 + 2 * pair]),
            ]
        )
    weight_copies[3].wait()
    base = 4 + 2 * pairs
    outs += start_copies([(mixed_ref, mixed_hbm, out_sems.at[base])])

    def part_copy(step):
        rows = pl.ds(pl.multiple_of(step * tile, tile), tile)
        return pltpu.make_async_copy(part_ref.at[rows], part_hbm.at[rows], out_sems.at[base + 1 + step])

    def project_out(step, carry):
        rows = pl.ds(pl.multiple_of(step * tile, tile), tile)
        part_ref[rows, :] = dot_nn(mixed_ref[rows, :], wo_ref[...]).astype(part_ref.dtype)
        part_copy(step).start()
        return carry

    lax.fori_loop(0, steps, project_out, 0)
    outs += [part_copy(step) for step in range(steps)]
    for copy in outs:
        copy.wait()


def attend(lengths, tokens, gain, w_query, w_key, w_value, w_out, table, block_rows=512):
    tok_count, width = tokens.shape
    own = w_query.shape[1]
    heads = own // 64
    heads_pad = -(-heads // 8) * 8
    table = jnp.pad(table.T, ((0, heads_pad - heads), (0, 0)))
    short_tok = SHORT_DEV * SHORT_LEN
    flops = 2 * tok_count * width * own * 4 + 4 * heads * (512 * 512 + short_tok * 128) * 64
    hbm = pl.BlockSpec(memory_space=pltpu.HBM)
    out_shapes = [
        ((tok_count, width), jnp.bfloat16),
        ((tok_count, width), jnp.bfloat16),
        ((tok_count, own), jnp.bfloat16),
        ((tok_count, own), jnp.bfloat16),
        ((tok_count, own), jnp.bfloat16),
        ((tok_count, own), jnp.bfloat16),
        ((heads, LONG_LEN, LONG_LEN), jnp.bfloat16),
        ((heads, short_tok, SHORT_LEN), jnp.bfloat16),
    ]
    steps = tok_count // 256
    return pl.pallas_call(
        partial(attend_kernel, block_rows),
        out_shape=[jax.ShapeDtypeStruct(*out_shapes[0])]
        + [hbm_out(shape, dtype) for shape, dtype in out_shapes[1:]],
        in_specs=[pl.BlockSpec(memory_space=pltpu.SMEM), hbm]
        + vmem(1)
        + [hbm] * 4
        + vmem(1),
        out_specs=[hbm] * 8,
        scratch_shapes=[pltpu.VMEM(tokens.shape, jnp.bfloat16)]
        + [pltpu.VMEM(w.shape, jnp.bfloat16) for w in (w_query, w_key, w_value, w_out)]
        + [pltpu.VMEM(shape, dtype) for shape, dtype in out_shapes]
        + [
            pltpu.VMEM((heads_pad, 512), jnp.float32),
            pltpu.SemaphoreType.DMA((steps + 4,)),
            pltpu.SemaphoreType.DMA((5 + 2 * (heads // 2) + steps,)),
        ],
        compiler_params=params(24),
        cost_estimate=pl.CostEstimate(
            flops=flops, bytes_accessed=16000000, transcendentals=heads * 512 * 640
        ),
        name="attend",
    )(
        lengths,
        in_hbm(tokens),
        gain.astype(jnp.float32)[None],
        in_hbm(w_query),
        in_hbm(w_key),
        in_hbm(w_value),
        in_hbm(w_out),
        table,
    )


def attend_back_pair(
    pair, hg_ref, q_ref, k_ref, v_ref, mixed_ref, long_ref, short_ref, grads_ref, tiles_ref, far_ref, sg_ref,
):
    short_tok = SHORT_DEV * SHORT_LEN
    lane = lax.broadcasted_iota(jnp.int32, (1, 128), 1)
    lanes = pl.ds(pl.multiple_of(pair * 128, 128), 128)
    blocks = LONG_LEN // 128
    heads_grad = hg_ref[:, lanes]
    products = heads_grad.astype(jnp.float32) * mixed_ref[:, lanes].astype(jnp.float32)
    q_t = jnp.transpose(q_ref[:, lanes])
    hg_t = jnp.transpose(heads_grad)
    qg = []
    kg_t = []
    vg_t = []
    for sub in range(2):
        head = pair * 2 + sub
        own = (lane >= 64) == (sub == 1)
        rows_t = slice(64 * sub, 64 * sub + 64)
        masked = jnp.where(own, heads_grad, 0)
        delta = jnp.sum(jnp.where(own, products, 0.0), axis=1, keepdims=True)
        grads = [
            dot_nt(masked[block * 128 : block * 128 + 128], v_ref[block * 128 : block * 128 + 128, lanes])
            for block in range(SHORT_DEV)
        ]
        probs = short_ref[head]
        part = probs.astype(jnp.float32) * (jnp.concatenate(grads, axis=0) - delta[:short_tok])
        same = part[:128]
        for block in range(1, SHORT_DEV):
            same = same + part[block * 128 : block * 128 + 128]
        part = part.astype(jnp.bfloat16)
        qg_parts = []
        kg_parts = []
        vg_parts = []
        for block in range(SHORT_DEV):
            rows = slice(block * 128, block * 128 + 128)
            qg_parts.append(dot_nn(part[rows], k_ref[rows, lanes]))
            kg_parts.append(dot_nn(q_t[rows_t, rows], part[rows]))
            vg_parts.append(dot_nn(hg_t[rows_t, rows], probs[rows]))
        above = jnp.zeros((128, 128), jnp.float32)
        below = above
        far_above = above
        far_below = above
        probs = long_ref[head]
        part = probs.astype(jnp.float32) * (
            dot_nt(masked[short_tok:], v_ref[short_tok:, lanes]) - delta[short_tok:]
        )
        for block in range(blocks):
            for other in range(blocks):
                piece = part[block * 128 : block * 128 + 128, other * 128 : other * 128 + 128]
                if other == block:
                    same = same + piece
                elif other == block + 1:
                    above = above + piece
                elif other == block - 1:
                    below = below + piece
                elif other > block:
                    far_above = far_above + piece
                else:
                    far_below = far_below + piece
        sg_ref[...] = part.astype(jnp.bfloat16)
        qg_parts.append(dot_nn(sg_ref[...], k_ref[short_tok:, lanes]))
        kg_parts.append(dot_nn(q_t[rows_t, short_tok:], sg_ref[...]))
        vg_parts.append(dot_nn(hg_t[rows_t, short_tok:], probs))
        qg.append(jnp.concatenate(qg_parts, axis=0))
        kg_t.append(jnp.concatenate(kg_parts, axis=1))
        vg_t.append(jnp.concatenate(vg_parts, axis=1))
        tiles_ref[head, :, 0:128] = same
        tiles_ref[head, :, 128:256] = above
        tiles_ref[head, :, 256:384] = below
        far_ref[head, 0:1, :] = jnp.sum(far_above, axis=0, keepdims=True)
        far_ref[head, 1:2, :] = jnp.sum(far_below, axis=0, keepdims=True)
    width = q_ref.shape[1]
    grads_ref[:, lanes] = (jnp.where(lane < 64, qg[0], qg[1]) * 0.125).astype(jnp.bfloat16)
    for index, whole in ((1, kg_t), (2, vg_t)):
        place = pl.ds(pl.multiple_of(index * width + pair * 128, 128), 128)
        grads_ref[:, place] = jnp.transpose(jnp.concatenate(whole, axis=0).astype(jnp.bfloat16))


def diagonals(tiles):
    tile = jnp.concatenate(
        [tiles[:, 0:256], jnp.zeros((128, 128), jnp.float32), tiles[:, 256:384]], axis=1
    )
    span = 64
    while span:
        tile = tile[:span] + pltpu.roll(tile[span:], 512 - span, 1)
        span //= 2
    return tile


def table_from(diag, bucket_count):
    lane = jnp.arange(768, dtype=jnp.int32)
    offset = jnp.where(lane < 256, lane, lane - 512)
    offset = jnp.where(lane >= 640, -256, jnp.where(lane >= 512, 256, offset))
    hot = (diagonal_buckets(offset)[:, None] == jnp.arange(bucket_count)[None, :]).astype(jnp.float32)
    return lax.dot_general(
        hot, diag, (((0,), (1,)), ((), ())), precision=highest, preferred_element_type=jnp.float32
    )


def dispatch_rows(send_ref, slot_row, half_rows):
    slots = send_ref.shape[0]
    tok_count = slot_row.shape[1]
    span = 256
    for base in range(0, slots, span):
        place = lax.broadcasted_iota(jnp.int32, (span, tok_count), 0) + base
        hot = jnp.where(place == slot_row, 1.0, 0.0).astype(jnp.bfloat16)
        send_ref[base : base + span, :] = dot_nn(hot, half_rows).astype(jnp.bfloat16)


def half_lanes(core, half):
    return pl.ds(pl.multiple_of(core * half, half), half)


def route_kernel(
    capacity, where_ref, routes_hbm, grad_hbm, row_hbm, col_hbm, send_ref, routes_ref, grad_ref, row_ref,
    col_ref, in_sems, out_sems,
):
    tok_count = routes_ref.shape[1]
    slots, half = send_ref.shape
    experts = slots // capacity
    fetch, copy = start_copies(
        [
            (routes_hbm, routes_ref, in_sems.at[0]),
            (grad_hbm.at[:, half_lanes(where_ref[0], half)], grad_ref, in_sems.at[1]),
        ]
    )
    fetch.wait()
    routes = routes_ref[...]
    expert = lax.broadcasted_iota(jnp.int32, (experts, tok_count), 0)
    lane = lax.broadcasted_iota(jnp.int32, (1, tok_count), 1)
    hot = jnp.where(expert == routes, 1.0, 0.0)
    total = hot
    step = 1
    while step < tok_count:
        total = total + jnp.where(lane >= step, pltpu.roll(total, step, 1), 0.0)
        step *= 2
    before = jnp.sum(hot * total, axis=0, keepdims=True).astype(jnp.int32) - 1
    slot = jnp.where(before < capacity, routes * capacity + before, slots)
    row_ref[...] = slot
    wide = jnp.broadcast_to(slot.astype(jnp.float32), (128, tok_count))
    col_ref[...] = jnp.transpose(wide).astype(jnp.int32)
    outs = start_copies([(row_ref, row_hbm, out_sems.at[0]), (col_ref, col_hbm, out_sems.at[1])])
    copy.wait()
    dispatch_rows(send_ref, slot, grad_ref[...])
    for copy in outs:
        copy.wait()


def route(where, routes, out_grad, experts, capacity):
    tok_count, width = out_grad.shape
    slots = experts * capacity
    return pl.pallas_call(
        partial(route_kernel, capacity),
        out_shape=[
            hbm_out((1, tok_count), jnp.int32),
            hbm_out((tok_count, 128), jnp.int32),
            jax.ShapeDtypeStruct((slots, width // 2), jnp.bfloat16),
        ],
        in_specs=[
            pl.BlockSpec(memory_space=pltpu.SMEM),
            pl.BlockSpec(memory_space=pltpu.HBM),
            pl.BlockSpec(memory_space=pltpu.HBM),
        ],
        out_specs=[pl.BlockSpec(memory_space=pltpu.HBM)] * 2 + vmem(1),
        scratch_shapes=[
            pltpu.VMEM((1, tok_count), jnp.int32),
            pltpu.VMEM((tok_count, width // 2), jnp.bfloat16),
            pltpu.VMEM((1, tok_count), jnp.int32),
            pltpu.VMEM((tok_count, 128), jnp.int32),
            pltpu.SemaphoreType.DMA((2,)),
            pltpu.SemaphoreType.DMA((2,)),
        ],
        compiler_params=params(),
        cost_estimate=pl.CostEstimate(
            flops=slots * tok_count * width, bytes_accessed=4000000, transcendentals=0
        ),
        name="route",
    )(where, in_hbm(routes.reshape(1, tok_count)), in_hbm(out_grad))


def second_kernel(
    where_ref, tokens_hbm, own_ref, other_ref, gain_ref, row_hbm, residual_hbm, send_ref, tokens_ref,
    row_ref, residual_ref, second_ref, in_sems, out_sems,
):
    tile = 256
    tok_count = tokens_ref.shape[0]
    half = send_ref.shape[1]
    tiles_rows = [slice(start, start + tile) for start in range(0, tok_count, tile)]
    copies = start_copies(
        [
            (tokens_hbm.at[rows], tokens_ref.at[rows], in_sems.at[step])
            for step, rows in enumerate(tiles_rows)
        ]
        + [(row_hbm, row_ref, in_sems.at[len(tiles_rows)])]
    )
    outs = []
    gain = gain_ref[...]
    for step, rows in enumerate(tiles_rows):
        attn = own_ref[rows, :].astype(jnp.float32) + other_ref[rows, :].astype(jnp.float32)
        copies[step].wait()
        residual = tokens_ref[rows, :].astype(jnp.float32) + attn
        residual_ref[rows, :] = residual
        outs += start_copies([(residual_ref.at[rows], residual_hbm.at[rows], out_sems.at[step])])
        second_ref[rows, :] = (residual * inverse_rms(residual) * gain).astype(jnp.bfloat16)
    copies[-1].wait()
    dispatch_rows(send_ref, row_ref[...], second_ref[:, half_lanes(where_ref[0], half)])
    for copy in outs:
        copy.wait()


def second_rows(where, tokens, own, other, gain, slot_row, slots):
    tok_count, width = tokens.shape
    steps = tok_count // 256
    hbm = pl.BlockSpec(memory_space=pltpu.HBM)
    return pl.pallas_call(
        second_kernel,
        out_shape=[
            hbm_out((tok_count, width), jnp.float32),
            jax.ShapeDtypeStruct((slots, width // 2), jnp.bfloat16),
        ],
        in_specs=[pl.BlockSpec(memory_space=pltpu.SMEM), hbm] + vmem(3) + [hbm],
        out_specs=[hbm] + vmem(1),
        scratch_shapes=[
            pltpu.VMEM((tok_count, width), jnp.bfloat16),
            pltpu.VMEM((1, tok_count), jnp.int32),
            pltpu.VMEM((tok_count, width), jnp.float32),
            pltpu.VMEM((tok_count, width), jnp.bfloat16),
            pltpu.SemaphoreType.DMA((steps + 1,)),
            pltpu.SemaphoreType.DMA((steps,)),
        ],
        compiler_params=params(),
        cost_estimate=pl.CostEstimate(
            flops=slots * tok_count * width, bytes_accessed=13000000, transcendentals=0
        ),
        name="second",
    )(where, in_hbm(tokens), own, other, gain.astype(jnp.float32)[None], in_hbm(slot_row))


def hidden_grad_kernel(where_ref, own_ref, other_ref, outer_ref, out_ref, whole_ref):
    half = own_ref.shape[1]
    core = where_ref[0]
    whole_ref[:, half_lanes(core, half)] = own_ref[...]
    whole_ref[:, half_lanes(1 - core, half)] = other_ref[...]
    out_ref[...] = dot_nt(whole_ref[...], outer_ref[...]).astype(jnp.bfloat16)


def hidden_grad_of(where, own, other, outer):
    slots, half = own.shape
    hidden = outer.shape[0]
    tile = 256
    rows = pl.BlockSpec((tile, half), lambda step: (step, 0))
    return pl.pallas_call(
        hidden_grad_kernel,
        grid=(slots // tile,),
        out_shape=hbm_out((slots, hidden), jnp.bfloat16),
        in_specs=[pl.BlockSpec(memory_space=pltpu.SMEM), rows, rows] + vmem(1),
        out_specs=pl.BlockSpec((tile, hidden), lambda step: (step, 0)),
        scratch_shapes=[pltpu.VMEM((tile, 2 * half), jnp.bfloat16)],
        compiler_params=params(),
        cost_estimate=pl.CostEstimate(
            flops=4 * slots * half * hidden, bytes_accessed=12000000, transcendentals=0
        ),
        name="hidden_grad",
    )(where, own, other, outer)


def gate_of(rows, router, index):
    experts = router.shape[1]
    logits = dot_nn(rows, router)
    exp_logit = jnp.exp(logits - jnp.max(logits, axis=1, keepdims=True))
    probs = exp_logit * (1.0 / jnp.sum(exp_logit, axis=1, keepdims=True))
    hit = jnp.where(lax.broadcasted_iota(jnp.int32, (1, experts), 1) == index, 1.0, 0.0)
    return probs, hit, jnp.sum(probs * hit, axis=1, keepdims=True)


def expert_kernel(
    where_ref,
    own_ref,
    other_ref,
    hg_ref,
    inner_ref,
    router_ref,
    hidden_ref,
    pre_grad_ref,
    keep_ref,
    send_ref,
    logit_ref,
    arrived_ref,
    whole_ref,
):
    core = where_ref[0]
    tile, half = own_ref.shape
    own_lanes = half_lanes(core, half)
    other_lanes = half_lanes(1 - core, half)
    arrived_ref[:, own_lanes] = own_ref[...]
    arrived_ref[:, other_lanes] = other_ref[...]
    arrived = arrived_ref[...]
    probs, hit, gate = gate_of(arrived, router_ref[...], where_ref[1])
    curve = 0.7978845608028654
    gate_grad = jnp.zeros((tile, 1), jnp.float32)
    back = jnp.zeros((tile, 2 * half), jnp.float32)
    chunk = 512
    for start in range(0, hg_ref.shape[1], chunk):
        cols = slice(start, start + chunk)
        pre = dot_nn(arrived, inner_ref[:, cols])
        square = pre * pre
        share = 0.5 + 0.5 * jnp.tanh(pre * (curve + (curve * 0.044715) * square))
        hidden_ref[:, cols] = (pre * share).astype(jnp.bfloat16)
        passed = share * hg_ref[:, cols].astype(jnp.float32)
        gate_grad = gate_grad + jnp.sum(pre * passed, axis=1, keepdims=True)
        bend = pre * (2.0 * curve + (6.0 * curve * 0.044715) * square)
        pre_grad = ((gate * passed) * (1.0 + (1.0 - share) * bend)).astype(jnp.bfloat16)
        pre_grad_ref[:, cols] = pre_grad
        back = back + dot_nt(pre_grad, inner_ref[:, cols])
    logit = (probs * (gate_grad * (hit - gate))).astype(jnp.bfloat16)
    logit_ref[...] = logit
    whole_ref[...] = back + dot_nt(logit, router_ref[...])
    send_ref[...] = whole_ref[:, other_lanes].astype(jnp.bfloat16)
    keep_ref[...] = whole_ref[:, own_lanes]


def expert(where, own, other, hidden_grad, inner, router):
    slots, half = own.shape
    width, hidden = inner.shape
    experts = router.shape[1]
    tile = 256
    halves = pl.BlockSpec((tile, half), lambda step: (step, 0))
    units = pl.BlockSpec((tile, hidden), lambda step: (step, 0))
    return pl.pallas_call(
        expert_kernel,
        grid=(slots // tile,),
        out_shape=[
            hbm_out((slots, hidden), jnp.bfloat16),
            hbm_out((slots, hidden), jnp.bfloat16),
            jax.ShapeDtypeStruct((slots, half), jnp.float32),
            jax.ShapeDtypeStruct((slots, half), jnp.bfloat16),
            hbm_out((slots, experts), jnp.bfloat16),
        ],
        in_specs=[
            pl.BlockSpec(memory_space=pltpu.SMEM),
            halves,
            halves,
            units,
            pl.BlockSpec(inner.shape, lambda step: (0, 0), pipeline_mode=pl.Buffered(1)),
        ]
        + vmem(1),
        out_specs=[
            units,
            units,
            halves,
            halves,
            pl.BlockSpec((tile, experts), lambda step: (step, 0)),
        ],
        scratch_shapes=[
            pltpu.VMEM((tile, width), jnp.bfloat16),
            pltpu.VMEM((tile, width), jnp.float32),
        ],
        compiler_params=params(),
        cost_estimate=pl.CostEstimate(
            flops=4 * slots * width * hidden, bytes_accessed=20000000, transcendentals=slots * hidden
        ),
        name="expert",
    )(where, own, other, in_hbm(hidden_grad), in_hbm(inner), router)


def expert_out_kernel(
    where_ref, hidden_ref, own_ref, other_ref, logit_ref, outer_ref, keep_ref, send_ref, router_ref, whole_ref
):
    core = where_ref[0]
    half = keep_ref.shape[1]
    own_lanes = half_lanes(core, half)
    other_lanes = half_lanes(1 - core, half)
    whole_ref[...] = dot_nn(hidden_ref[...], outer_ref[...])
    send_ref[...] = whole_ref[:, other_lanes].astype(jnp.bfloat16)
    keep_ref[...] = whole_ref[:, own_lanes]

    @pl.when(pl.program_id(0) == 0)
    def _():
        router_ref[...] = jnp.zeros_like(router_ref)

    router_ref[:, own_lanes] += contract_rows(logit_ref[...], own_ref[...])
    router_ref[:, other_lanes] += contract_rows(logit_ref[...], other_ref[...])


def expert_out_of(where, hidden, own, other, logit_grad, outer):
    slots, units = hidden.shape
    width = outer.shape[1]
    experts = logit_grad.shape[1]
    half = width // 2
    tile = 256
    halves = pl.BlockSpec((tile, half), lambda step: (step, 0))
    return pl.pallas_call(
        expert_out_kernel,
        grid=(slots // tile,),
        out_shape=[
            jax.ShapeDtypeStruct((slots, half), jnp.float32),
            jax.ShapeDtypeStruct((slots, half), jnp.bfloat16),
            hbm_out((experts, width), jnp.float32),
        ],
        in_specs=[
            pl.BlockSpec(memory_space=pltpu.SMEM),
            pl.BlockSpec((tile, units), lambda step: (step, 0)),
            halves,
            halves,
            pl.BlockSpec((tile, experts), lambda step: (step, 0)),
        ]
        + vmem(1),
        out_specs=[halves, halves, pl.BlockSpec((experts, width), lambda step: (0, 0))],
        scratch_shapes=[pltpu.VMEM((tile, width), jnp.float32)],
        compiler_params=params(),
        cost_estimate=pl.CostEstimate(
            flops=2 * slots * width * units, bytes_accessed=9000000, transcendentals=0
        ),
        name="expert_out",
    )(where, in_hbm(hidden), in_hbm(own), in_hbm(other), in_hbm(logit_grad), outer)


def expert_grads_kernel(
    where_ref,
    own_hbm,
    other_hbm,
    grad_own_hbm,
    grad_other_hbm,
    hidden_ref,
    pre_grad_ref,
    router_ref,
    inner_grad_ref,
    outer_grad_ref,
    arrived_ref,
    gated_ref,
    sems,
):
    core = where_ref[0]
    half = own_hbm.shape[1]
    own_lanes = half_lanes(core, half)
    other_lanes = half_lanes(1 - core, half)

    @pl.when(pl.program_id(0) == 0)
    def _():
        copies = [
            pltpu.make_async_copy(own_hbm, arrived_ref.at[:, own_lanes], sems.at[0]),
            pltpu.make_async_copy(other_hbm, arrived_ref.at[:, other_lanes], sems.at[1]),
            pltpu.make_async_copy(grad_own_hbm, gated_ref.at[:, own_lanes], sems.at[2]),
            pltpu.make_async_copy(grad_other_hbm, gated_ref.at[:, other_lanes], sems.at[3]),
        ]
        for copy in copies:
            copy.start()
        for copy in copies:
            copy.wait()
        gate = gate_of(arrived_ref[...], router_ref[...], where_ref[1])[2]
        gated_ref[...] = (gate * gated_ref[...].astype(jnp.float32)).astype(jnp.bfloat16)

    outer_grad_ref[...] = contract_rows(hidden_ref[...], gated_ref[...])
    inner_grad_ref[...] = contract_rows(arrived_ref[...], pre_grad_ref[...])


def expert_grads(where, own, other, grad_own, grad_other, hidden, pre_grad, router):
    slots, half = own.shape
    units = hidden.shape[1]
    width = router.shape[0]
    tile = 256
    hbm = pl.BlockSpec(memory_space=pltpu.HBM)
    whole = lambda shape: pl.BlockSpec(shape, lambda step: (0, 0))
    cols = pl.BlockSpec((slots, tile), lambda step: (0, step))
    return pl.pallas_call(
        expert_grads_kernel,
        grid=(units // tile,),
        out_shape=[
            hbm_out((width, units), jnp.float32),
            hbm_out((units, width), jnp.float32),
        ],
        in_specs=[
            pl.BlockSpec(memory_space=pltpu.SMEM),
            hbm,
            hbm,
            hbm,
            hbm,
            cols,
            cols,
            whole(router.shape),
        ],
        out_specs=[
            pl.BlockSpec((width, tile), lambda step: (0, step)),
            pl.BlockSpec((tile, width), lambda step: (step, 0)),
        ],
        scratch_shapes=[
            pltpu.VMEM((slots, width), jnp.bfloat16),
            pltpu.VMEM((slots, width), jnp.bfloat16),
            pltpu.SemaphoreType.DMA((4,)),
        ],
        compiler_params=params(24),
        cost_estimate=pl.CostEstimate(
            flops=4 * slots * width * units, bytes_accessed=22000000, transcendentals=0
        ),
        name="expert_grads",
    )(
        where,
        in_hbm(own),
        in_hbm(other),
        in_hbm(grad_own),
        in_hbm(grad_other),
        in_hbm(hidden),
        in_hbm(pre_grad),
        router,
    )


def output_kernel(
    capacity, where_ref, col_ref, returned_ref, residual_ref, gain_ref, router_ref, out_ref
):
    slots, half = returned_ref.shape
    tile = residual_ref.shape[0]
    experts = router_ref.shape[1]
    col = col_ref[:, :1]
    place = lax.broadcasted_iota(jnp.int32, (tile, slots), 1)
    hot = jnp.where(place == col, 1.0, 0.0).astype(jnp.bfloat16)
    token_out = dot_nn(hot, returned_ref[...])
    residual = residual_ref[...]
    second = (residual * inverse_rms(residual) * gain_ref[...]).astype(jnp.bfloat16)
    logits = dot_nn(second, router_ref[...])
    exp_logit = jnp.exp(logits - jnp.max(logits, axis=1, keepdims=True))
    first = lax.broadcasted_iota(jnp.int32, (1, experts), 1) * capacity
    hit = jnp.where((col >= first) & (col < first + capacity), exp_logit, 0.0)
    gate = jnp.sum(hit, axis=1, keepdims=True) / jnp.sum(exp_logit, axis=1, keepdims=True)
    own = residual_ref[:, half_lanes(where_ref[0], half)]
    out_ref[...] = (own + gate * token_out).astype(jnp.bfloat16)


def output_of(where, slot_col, returned, residual, gain, router, capacity):
    tok_count, width = residual.shape
    slots, half = returned.shape
    tile = 256
    whole = lambda shape: pl.BlockSpec(shape, lambda step: (0, 0))
    return pl.pallas_call(
        partial(output_kernel, capacity),
        grid=(tok_count // tile,),
        out_shape=jax.ShapeDtypeStruct((tok_count, half), jnp.bfloat16),
        in_specs=[
            pl.BlockSpec(memory_space=pltpu.SMEM),
            pl.BlockSpec((tile, 128), lambda step: (step, 0)),
            whole(returned.shape),
            pl.BlockSpec((tile, width), lambda step: (step, 0)),
            whole((1, width)),
            whole(router.shape),
        ],
        out_specs=pl.BlockSpec((tile, half), lambda step: (step, 0)),
        compiler_params=params(),
        cost_estimate=pl.CostEstimate(
            flops=2 * tok_count * half * slots, bytes_accessed=6000000, transcendentals=0
        ),
        name="output",
    )(
        where, in_hbm(slot_col), in_hbm(returned), in_hbm(residual), gain.astype(jnp.float32)[None], router
    )


def normed_back_kernel(grads_ref, wq_ref, wk_ref, wv_ref, out_ref):
    own = wq_ref.shape[1]
    out_ref[...] = (
        dot_nt(grads_ref[:, :own], wq_ref[...])
        + dot_nt(grads_ref[:, own : 2 * own], wk_ref[...])
        + dot_nt(grads_ref[:, 2 * own :], wv_ref[...])
    ).astype(jnp.bfloat16)


def normed_back(grads, w_query, w_key, w_value):
    tok_count = grads.shape[0]
    width, own = w_query.shape
    tile = 256
    whole = pl.BlockSpec((width, own), lambda step: (0, 0))
    return pl.pallas_call(
        normed_back_kernel,
        grid=(tok_count // tile,),
        out_shape=jax.ShapeDtypeStruct((tok_count, width), jnp.bfloat16),
        in_specs=[pl.BlockSpec((tile, 3 * own), lambda step: (step, 0))] + [whole] * 3,
        out_specs=pl.BlockSpec((tile, width), lambda step: (step, 0)),
        compiler_params=params(),
        cost_estimate=pl.CostEstimate(
            flops=6 * tok_count * own * width, bytes_accessed=6000000, transcendentals=0
        ),
        name="normed_back",
    )(*(in_hbm(array) for array in (grads, w_query, w_key, w_value)))


def input_back_kernel(tokens_ref, own_ref, other_ref, gain_ref, residual_ref, out_ref):
    ybar = own_ref[...].astype(jnp.float32) + other_ref[...].astype(jnp.float32)
    values = tokens_ref[...].astype(jnp.float32)
    scale = inverse_rms(values)
    scaled = values * scale
    pulled = ybar * gain_ref[...]
    out_ref[...] = residual_ref[...] + scale * (
        pulled - scaled * jnp.mean(pulled * scaled, axis=1, keepdims=True)
    )


def input_back(tokens, own, other, gain, residual_grad):
    tok_count, width = tokens.shape
    tile = 256
    rows = pl.BlockSpec((tile, width), lambda step: (step, 0))
    return pl.pallas_call(
        input_back_kernel,
        grid=(tok_count // tile,),
        out_shape=jax.ShapeDtypeStruct((tok_count, width), jnp.float32),
        in_specs=[rows, rows, rows, pl.BlockSpec((1, width), lambda step: (0, 0)), rows],
        out_specs=rows,
        compiler_params=params(),
        cost_estimate=pl.CostEstimate(
            flops=10 * tok_count * width, bytes_accessed=11000000, transcendentals=0
        ),
        name="input_back",
    )(in_hbm(tokens), own, other, gain.astype(jnp.float32)[None], in_hbm(residual_grad))


def back_kernel(
    bits_ref,
    where_ref,
    col_hbm,
    own_hbm,
    other_hbm,
    residual_hbm,
    grad_hbm,
    wo_hbm,
    q_hbm,
    k_hbm,
    v_hbm,
    mixed_hbm,
    long_hbm,
    short_hbm,
    normed_hbm,
    wq_hbm,
    wk_hbm,
    wv_hbm,
    gain_one_ref,
    gain_two_ref,
    router_ref,
    out_hbm,
    grads_hbm,
    sent_a,
    sent_b,
    sent_c,
    kept_a,
    kept_b,
    kept_c,
    col_ref,
    back_ref,
    residual_ref,
    grad_ref,
    wo_ref,
    q_ref,
    k_ref,
    v_ref,
    mixed_ref,
    long_ref,
    short_ref,
    normed_ref,
    wq_ref,
    wk_ref,
    wv_ref,
    attn_ref,
    heads_ref,
    grads_ref,
    sg_ref,
    tiles_ref,
    far_ref,
    stack_ref,
    small_ref,
    packed_ref,
    total_ref,
    in_sems,
    out_sems,
):
    tok_count, width = residual_ref.shape
    slots, half = own_hbm.shape
    own = mixed_ref.shape[1]
    experts = router_ref.shape[0]
    pairs = own // 128
    tile = 256
    steps = tok_count // tile
    core = where_ref[0]
    first = [
        (own_hbm, back_ref.at[:, half_lanes(core, half)]),
        (other_hbm, back_ref.at[:, half_lanes(1 - core, half)]),
        (col_hbm, col_ref),
        (wo_hbm, wo_ref),
    ]
    tiles = []
    for start in range(0, tok_count, tile):
        rows = slice(start, start + tile)
        tiles.append((residual_hbm.at[rows], residual_ref.at[rows]))
        tiles.append((grad_hbm.at[rows], grad_ref.at[rows]))
    attention = [(q_hbm, q_ref), (k_hbm, k_ref), (v_hbm, v_ref), (mixed_hbm, mixed_ref), (short_hbm, short_ref)]
    for pair in range(pairs):
        both = slice(pair * 2, pair * 2 + 2)
        attention.append((long_hbm.at[both], long_ref.at[both]))
    weights = [(normed_hbm, normed_ref), (wq_hbm, wq_ref), (wk_hbm, wk_ref), (wv_hbm, wv_ref)]
    copies = start_copies(
        [
            (source, target, in_sems.at[index])
            for index, (source, target) in enumerate(first + tiles + attention + weights)
        ]
    )
    base = len(first) + len(tiles)
    outs = []

    for copy in copies[: len(first)]:
        copy.wait()
    gain_two = gain_two_ref[...]
    place = lax.broadcasted_iota(jnp.int32, (tile, slots), 1)

    def tile_out(step):
        rows = pl.ds(pl.multiple_of(step * tile, tile), tile)
        return pltpu.make_async_copy(residual_ref.at[rows], out_hbm.at[rows], out_sems.at[step])

    def one_tile(step, gain_two_grad):
        rows = pl.ds(pl.multiple_of(step * tile, tile), tile)
        at = len(first) + 2 * step
        pltpu.make_async_copy(residual_hbm.at[rows], residual_ref.at[rows], in_sems.at[at]).wait()
        pltpu.make_async_copy(grad_hbm.at[rows], grad_ref.at[rows], in_sems.at[at + 1]).wait()
        hot = jnp.where(place == col_ref[rows, :][:, :1], 1.0, 0.0).astype(jnp.bfloat16)
        ybar = dot_nn(hot, back_ref[...])
        values = residual_ref[rows, :]
        scale = inverse_rms(values)
        scaled = values * scale
        pulled = ybar * gain_two
        back = scale * (pulled - scaled * jnp.mean(pulled * scaled, axis=1, keepdims=True))
        out = back + grad_ref[rows, :].astype(jnp.float32)
        residual_ref[rows, :] = out
        attn = out.astype(jnp.bfloat16)
        attn_ref[rows, :] = attn
        heads_ref[rows, :] = dot_nt(attn, wo_ref[...]).astype(jnp.bfloat16)
        tile_out(step).start()
        return gain_two_grad + jnp.sum(ybar * scaled, axis=0, keepdims=True)

    gain_two_grad = lax.fori_loop(0, steps, one_tile, jnp.zeros((1, width), jnp.float32), unroll=2)
    outs += [tile_out(step) for step in range(steps)]

    for copy in copies[base : base + 5]:
        copy.wait()

    def one_pair(pair, carry):
        both = pl.ds(pair * 2, 2)
        pltpu.make_async_copy(long_hbm.at[both], long_ref.at[both], in_sems.at[base + 5 + pair]).wait()
        attend_back_pair(
            pair, heads_ref, q_ref, k_ref, v_ref, mixed_ref, long_ref, short_ref, grads_ref, tiles_ref, far_ref,
            sg_ref,
        )
        return carry

    lax.fori_loop(0, pairs, one_pair, 0, unroll=True)
    outs += start_copies([(grads_ref, grads_hbm, out_sems.at[steps])])

    def out_rows(block, carry):
        start = pl.multiple_of(block * 128, 128)
        grad = contract_rows(mixed_ref[:, pl.ds(start, 128)], attn_ref[...]).astype(jnp.bfloat16)
        for part in range(width // own):
            at = pl.multiple_of(3 * width + part * own + start, 128)
            stack_ref[pl.ds(at, 128), :] = grad[:, part * own : part * own + own]
        return carry

    lax.fori_loop(0, own // 128, out_rows, 0, unroll=True)
    small_ref[0:experts, :] = router_ref[...]
    small_ref[experts + 1 : experts + 2, :] = gain_two_grad
    for head in range(2 * pairs):
        row = experts + 2 + head
        small_ref[row : row + 1, 0:512] = diagonals(tiles_ref[head])
        small_ref[row : row + 1, 512:640] = far_ref[head, 0:1, :]
        small_ref[row : row + 1, 640:768] = far_ref[head, 1:2, :]
    for copy in copies[base + 5 + pairs :]:
        copy.wait()
    rows = stack_ref.shape[0] // 3
    span = rows // 2

    def send_part(part, sent, kept):
        mine = bits_ref[part]
        sent_rows = pl.ds(pl.multiple_of(part * rows + (1 - mine) * span, span), span)
        kept_rows = pl.ds(pl.multiple_of(part * rows + mine * span, span), span)
        return start_copies(
            [
                (stack_ref.at[sent_rows], sent.at[:span], out_sems.at[steps + 4 + 2 * part]),
                (stack_ref.at[kept_rows], kept, out_sems.at[steps + 5 + 2 * part]),
            ]
        )

    def head_rows(block, carry):
        start = pl.multiple_of(block * tile, tile)
        piece = pl.ds(start, tile)
        grad = contract_rows(normed_ref[:, piece], grads_ref[...])
        total = jnp.zeros((tile, 1), jnp.float32)
        for index, w_ref in enumerate((wq_ref, wk_ref, wv_ref)):
            part = grad[:, index * own : index * own + own]
            total = total + jnp.sum(part * w_ref[piece, :].astype(jnp.float32), axis=1, keepdims=True)
            stack_ref[pl.ds(pl.multiple_of(index * width + start, tile), tile), :] = part.astype(jnp.bfloat16)
        total_ref[piece, :] = jnp.broadcast_to(total, (tile, 128))
        return carry

    lax.fori_loop(0, width // tile, head_rows, 0, unroll=True)
    for part, (sent, kept) in enumerate(((sent_a, kept_a), (sent_b, kept_b))):
        outs += send_part(part, sent, kept)
    outs += send_part(2, sent_c, kept_c)
    wide = jnp.transpose(total_ref[...])
    small_ref[experts : experts + 1, :] = wide[:1, :] / gain_one_ref[...]
    small = small_ref[...]
    packed_ref[...] = jnp.concatenate([small[:, :own], small[:, own:]], axis=0).astype(jnp.bfloat16)
    outs += start_copies([(packed_ref, sent_a.at[span:], out_sems.at[steps + 3])])
    for copy in outs:
        copy.wait()


def back_pass(
    bits, where, slot_col, back_own, back_other, residual, out_grad, w_out, query_rows, key_rows,
    value_rows, mixed, long_probs, short_probs, normed, w_query, w_key, w_value, gain_one, gain_two,
    router_part,
):
    tok_count, width = normed.shape
    own = mixed.shape[1]
    slots, half = back_own.shape
    heads = long_probs.shape[0]
    count = router_part.shape[0] + 2 + heads
    span = 4 * width // 6
    tile = 256
    steps = tok_count // tile
    half_rows = hbm_out((span, own), jnp.bfloat16)
    pinned = (residual, out_grad, w_out, query_rows, key_rows, value_rows, mixed, long_probs, short_probs, normed,
              w_query, w_key, w_value)
    hbm = pl.BlockSpec(memory_space=pltpu.HBM)
    smem = pl.BlockSpec(memory_space=pltpu.SMEM)

    def scratch(array):
        return pltpu.VMEM(array.shape, array.dtype)

    flops = 2 * tok_count * width * (slots + 5 * own) + 10 * heads * (512 * 512 + 512 * 128) * 64
    out = pl.pallas_call(
        back_kernel,
        out_shape=[
            hbm_out((tok_count, width), jnp.float32),
            hbm_out((tok_count, 3 * own), jnp.bfloat16),
            hbm_out((span + 2 * count, own), jnp.bfloat16),
        ]
        + [half_rows] * 5,
        in_specs=[smem, smem] + [hbm] * 16 + vmem(3),
        out_specs=[hbm] * 8,
        scratch_shapes=[scratch(slot_col), pltpu.VMEM((slots, width), jnp.bfloat16)]
        + [scratch(array) for array in pinned]
        + [
            pltpu.VMEM((tok_count, width), jnp.bfloat16),
            pltpu.VMEM((tok_count, own), jnp.bfloat16),
            pltpu.VMEM((tok_count, 3 * own), jnp.bfloat16),
            pltpu.VMEM((LONG_LEN, LONG_LEN), jnp.bfloat16),
            pltpu.VMEM((heads, 128, 384), jnp.float32),
            pltpu.VMEM((heads, 2, 128), jnp.float32),
            pltpu.VMEM((4 * width, own), jnp.bfloat16),
            pltpu.VMEM((count, width), jnp.float32),
            pltpu.VMEM((2 * count, own), jnp.bfloat16),
            pltpu.VMEM((width, 128), jnp.float32),
            pltpu.SemaphoreType.DMA((2 * steps + 4 + 5 + heads // 2 + 4,)),
            pltpu.SemaphoreType.DMA((steps + 10,)),
        ],
        compiler_params=params(30),
        cost_estimate=pl.CostEstimate(flops=flops, bytes_accessed=25000000, transcendentals=0),
        name="back",
    )(
        bits,
        where,
        in_hbm(slot_col),
        in_hbm(back_own),
        in_hbm(back_other),
        *(in_hbm(array) for array in pinned),
        gain_one.astype(jnp.float32)[None],
        gain_two.astype(jnp.float32)[None],
        router_part,
    )
    return out[0], out[1], out[2:5], out[5:]


def added(left, right):
    return (left.astype(jnp.float32) + right.astype(jnp.float32)).astype(jnp.bfloat16)


def fold_kernel(bits_ref, *refs):
    kept, got, sent, keep = refs[0:3], refs[3:6], refs[7:10], refs[10:13]
    before = refs[6]
    for part in range(3):
        span = kept[part].shape[0] // 2
        mine = bits_ref[part]
        for ref, start in ((sent[part], (1 - mine) * span), (keep[part], mine * span)):
            rows = pl.ds(pl.multiple_of(start, span), span)
            ref[:span, :] = added(kept[part][rows, :], got[part][rows, :])
    rows = kept[0].shape[0]
    sent[0][rows // 2 :, :] = added(before[rows:, :], got[0][rows:, :])


def fold(bits, kept, got, before):
    rows, lanes = kept[0].shape
    extra = before.shape[0] - rows
    half = jax.ShapeDtypeStruct((rows // 2, lanes), jnp.bfloat16)
    out = pl.pallas_call(
        fold_kernel,
        out_shape=[jax.ShapeDtypeStruct((rows // 2 + extra, lanes), jnp.bfloat16)] + [half] * 5,
        in_specs=[pl.BlockSpec(memory_space=pltpu.SMEM)] + vmem(7),
        out_specs=vmem(6),
        compiler_params=params(16),
        name="fold",
    )(bits, *kept, *got, before)
    return out[:3], out[3:]


def pack_kernel(*refs):
    kept, got, before, out = refs[0:3], refs[3:6], refs[6], refs[7]
    rows = kept[0].shape[0]
    for part in range(3):
        out[part * rows : (part + 1) * rows, :] = added(kept[part][...], got[part][:rows, :])
    out[3 * rows :, :] = added(before[rows:, :], got[0][rows:, :])


def pack(kept, got, before):
    rows, lanes = kept[0].shape
    return pl.pallas_call(
        pack_kernel,
        out_shape=jax.ShapeDtypeStruct((2 * rows + before.shape[0], lanes), jnp.bfloat16),
        in_specs=vmem(7),
        out_specs=vmem(1)[0],
        compiler_params=params(16),
        name="pack",
    )(*kept, *got, before)


def unpack_kernel(own_ref, got_ref, *out):
    rows = out[0].shape[0]
    for part in range(3):
        piece = slice(part * rows, (part + 1) * rows)
        out[part][...] = added(own_ref[piece, :], got_ref[piece, :])
    out[3][...] = own_ref[3 * rows :, :].astype(jnp.float32) + got_ref[3 * rows :, :].astype(jnp.float32)


def unpack(own, got, rows):
    lanes = own.shape[1]
    out = pl.pallas_call(
        unpack_kernel,
        out_shape=[jax.ShapeDtypeStruct((rows, lanes), jnp.bfloat16)] * 3
        + [jax.ShapeDtypeStruct((own.shape[0] - 3 * rows, lanes), jnp.float32)],
        in_specs=vmem(2),
        out_specs=vmem(4),
        compiler_params=params(16),
        name="unpack",
    )(own, got)
    return out[:3], out[3]


def join_kernel(bits_ref, *refs):
    own, got, out = refs[0:3], refs[3:6], refs[6:9]
    for part in range(3):
        span = own[part].shape[0]
        mine = bits_ref[part]
        out[part][pl.ds(pl.multiple_of(mine * span, span), span), :] = own[part][...]
        out[part][pl.ds(pl.multiple_of((1 - mine) * span, span), span), :] = got[part][...]


def join(bits, own, got):
    return pl.pallas_call(
        join_kernel,
        out_shape=[jax.ShapeDtypeStruct((p.shape[0] * 2, p.shape[1]), p.dtype) for p in own],
        in_specs=[pl.BlockSpec(memory_space=pltpu.SMEM)] + vmem(6),
        out_specs=vmem(3),
        compiler_params=params(16),
        name="join",
    )(bits, *own, *got)


def finish_kernel(bits_ref, *refs):
    own, got = refs[0:3], refs[3:6]
    results = refs[6:10]
    held, sems = refs[10:14], refs[14]
    span = own[0].shape[0]
    rows = 2 * span
    width, lanes = held[0].shape
    copies = []
    for part in range(3):
        mine = bits_ref[part]
        first = jnp.where(mine == 0, own[part][...], got[part][...])
        second = jnp.where(mine == 0, got[part][...], own[part][...])
        for base, piece in ((part * rows, first), (part * rows + span, second)):
            for index in range(3 + width // lanes):
                start = index * width if index < 3 else 3 * width + (index - 3) * lanes
                size = width if index < 3 else lanes
                low = max(start, base)
                high = min(start + size, base + span)
                if low < high:
                    values = piece[low - base : high - base, :].astype(jnp.float32)
                    if index < 3:
                        held[index][low - start : high - start, :] = values
                    else:
                        place = (index - 3) * lanes
                        held[3][low - start : high - start, place : place + lanes] = values
        for index in range(4):
            last = (index + 1) * width - 1
            if part * rows <= last < (part + 1) * rows:
                copies += start_copies([(held[index], results[index], sems.at[index])])
    for copy in copies:
        copy.wait()


def finish(bits, own, got, width):
    lanes = own[0].shape[1]
    shapes = [(width, lanes)] * 3 + [(lanes, width)]
    return pl.pallas_call(
        finish_kernel,
        out_shape=[hbm_out(shape, jnp.float32) for shape in shapes],
        in_specs=[pl.BlockSpec(memory_space=pltpu.SMEM)] + vmem(6),
        out_specs=[pl.BlockSpec(memory_space=pltpu.HBM)] * 4,
        scratch_shapes=[pltpu.VMEM(shape, jnp.float32) for shape in shapes]
        + [pltpu.SemaphoreType.DMA((4,))],
        compiler_params=params(24),
        name="finish",
    )(bits, *own, *got)


def swap_heads(rows):
    return lax.ppermute(rows, "heads", [(0, 1), (1, 0)])


def trade(rows, bit):
    count = lax.axis_size("seq")
    return lax.ppermute(rows, "seq", [(i, i ^ (1 << bit)) for i in range(count)])


def together(*groups):
    return lax.optimization_barrier(groups)


def contract_rows(left, right):
    return lax.dot_general(
        left, right, (((0,), (0,)), ((), ())), preferred_element_type=jnp.float32
    )


def on_device(
    tokens,
    gain_attn,
    w_query,
    w_key,
    w_value,
    w_out,
    bias_table,
    gain_ffn,
    w_router,
    w_inner,
    w_outer,
    routes,
    seq_lengths,
    out_grad,
):
    tok_count, width = tokens.shape
    bucket_count = bias_table.shape[0]
    experts = w_router.shape[1]
    capacity = max(2, 5 * tok_count // (4 * experts))
    senders = lax.axis_size("seq")
    bits = list(range(senders.bit_length() - 1))
    slots = experts * capacity
    half = width // 2
    own = w_query.shape[1]
    where = jnp.stack([lax.axis_index("heads"), lax.axis_index("seq")]).astype(jnp.int32)

    def exchange(rows):
        return lax.all_to_all(
            rows.reshape(senders, capacity, half), "seq", split_axis=0, concat_axis=0, tiled=True
        ).reshape(slots, half)

    def summed(keep, send):
        return (keep + swap_heads(send).astype(jnp.float32)).astype(jnp.bfloat16)

    slot_row, slot_col, grad_sent = route(where, routes, out_grad, experts, capacity)
    grad_sent, tokens = together(grad_sent, tokens)
    grad_own = exchange(grad_sent)
    attn_part, normed, query_rows, key_rows, value_rows, mixed, long_probs, short_probs = attend(
        seq_lengths, tokens, gain_attn, w_query, w_key, w_value, w_out, bias_table
    )
    residual, second_sent = second_rows(
        where, tokens, attn_part, swap_heads(attn_part), gain_ffn, slot_row, slots
    )
    second_sent, grad_own = together(second_sent, grad_own)
    arrived_own = exchange(second_sent)

    inner = w_inner[0]
    outer = w_outer[0]
    grad_other = swap_heads(grad_own)
    hidden_grad = hidden_grad_of(where, grad_own, grad_other, outer)
    arrived_own, hidden_grad = together(arrived_own, hidden_grad)
    arrived_other = swap_heads(arrived_own)
    hidden, pre_grad, keep, send, logit_grad = expert(
        where, arrived_own, arrived_other, hidden_grad, inner, w_router
    )
    back_sum, hidden = together(summed(keep, send), hidden)
    back_own = exchange(back_sum)
    out_keep, out_send, router_part = expert_out_of(
        where, hidden, arrived_own, arrived_other, logit_grad, outer
    )
    out_sum = summed(out_keep, out_send)
    corner, back_own, out_sum = together(out_sum[:16, :128], back_own, out_sum)
    back_other = swap_heads(back_own)
    out_sum = lax.dynamic_update_slice(out_sum, corner, (0, 0))
    returned = exchange(out_sum)

    depth = len(bits) - 1
    turns = [bits[k * depth // 3 : depth] + bits[: k * depth // 3] for k in range(3)]
    place = lax.axis_index("seq")
    mine = [jnp.stack([(place >> turn[k]) & 1 for turn in turns]).astype(jnp.int32) for k in range(depth)]
    residual_grad, head_grads, sent, kept = back_pass(
        mine[0], where, slot_col, back_own, back_other, residual, out_grad, w_out, query_rows, key_rows,
        value_rows, mixed, long_probs, short_probs, normed, w_query, w_key, w_value, gain_attn, gain_ffn,
        router_part,
    )

    def trades(arrays, k):
        return [trade(array, turn[k]) for array, turn in zip(arrays, turns)]

    for k in range(depth):
        got = trades(sent, k)
        if k == 0:
            output = output_of(where, slot_col, returned, residual, gain_ffn, w_router, capacity)
            got, output, head_grads = together(got, output, head_grads)
        if k == 1:
            normed_part = normed_back(head_grads, w_query, w_key, w_value)
            got, normed_part = together(got, normed_part)
        if k + 1 < depth:
            sent, kept = fold(mine[k + 1], kept, got, sent[0])
    normed_other = swap_heads(normed_part)
    packed = pack(kept, got, sent[0])
    packed, normed_other, pre_grad = together(packed, normed_other, pre_grad)
    got = trade(packed, bits[-1])
    inner_grad, outer_grad = expert_grads(
        where, arrived_own, arrived_other, grad_own, grad_other, hidden, pre_grad, w_router
    )
    got, inner_grad = together(got, inner_grad)
    summed_parts, small = unpack(packed, got, kept[0].shape[0])
    small = jnp.concatenate([small[: small.shape[0] // 2], small[small.shape[0] // 2 :]], axis=1)
    small_other = swap_heads(small)
    for k in reversed(range(1, depth)):
        got = trades(summed_parts, k)
        if k == 1:
            both = small[: experts + 1] + small_other[: experts + 1]
            router_grad = both[:experts].T
            table_grad = table_from(small[experts + 2 :], bucket_count)
            got, both, router_grad, table_grad = together(got, both, router_grad, table_grad)
        summed_parts = join(mine[k], summed_parts, got)
    got = trades(summed_parts, 0)
    input_grad = input_back(tokens, normed_part, normed_other, gain_attn, residual_grad)
    got, input_grad = together(got, input_grad)
    query_w_grad, key_w_grad, value_w_grad, out_w_grad = finish(mine[0], summed_parts, got, width)
    return (
        output,
        input_grad,
        both[experts],
        query_w_grad,
        key_w_grad,
        value_w_grad,
        out_w_grad,
        table_grad,
        small[experts + 1],
        router_grad,
        inner_grad[None],
        outer_grad[None],
    )


def solution(mesh):
    in_specs = (
        P("seq", None),
        P(),
        P(None, "heads"),
        P(None, "heads"),
        P(None, "heads"),
        P("heads", None),
        P(None, "heads"),
        P(),
        P(),
        P("seq", None, "heads"),
        P("seq", "heads", None),
        P("seq", None),
        P("seq"),
        P("seq", None),
    )
    out_specs = (
        P("seq", "heads"),
        P("seq", None),
        P(),
        P(None, "heads"),
        P(None, "heads"),
        P(None, "heads"),
        P("heads", None),
        P(None, "heads"),
        P(),
        P(),
        P("seq", None, "heads"),
        P("seq", "heads", None),
    )
    return jax.shard_map(
        on_device, mesh=mesh, in_specs=in_specs, out_specs=out_specs, check_vma=False
    )
```

```python
from functools import partial

import jax
import jax.numpy as jnp
from jax import lax
from jax.experimental import pallas as pl
from jax.experimental.pallas import tpu as pltpu
from jax.sharding import PartitionSpec as P

SHORT_LEN = 128
LONG_LEN = 512
SHORT_DEV = 4
LONG_DEV = 1


epsilon = 1e-06
highest = lax.Precision.HIGHEST
far_limits = (12, 16, 23, 32, 46, 64, 91)


def vmem(count):
    return [pl.BlockSpec(memory_space=pltpu.VMEM)] * count


def params(mib=16):
    return pltpu.CompilerParams(vmem_limit_bytes=mib * 1024 * 1024)


def dot_nn(left, right):
    return jnp.dot(left, right, preferred_element_type=jnp.float32)


def dot_nt(left, right):
    return lax.dot_general(
        left, right, (((1,), (1,)), ((), ())), preferred_element_type=jnp.float32
    )


def inverse_rms(values):
    return lax.rsqrt(jnp.mean(values * values, axis=-1, keepdims=True) + epsilon)


def diagonal_buckets(offset):
    distance = jnp.abs(offset)
    far_bucket = jnp.full(offset.shape, 8, jnp.int32)
    for limit in far_limits:
        far_bucket = far_bucket + (distance >= limit).astype(jnp.int32)
    return jnp.where(distance < 8, distance, far_bucket) + jnp.where(offset > 0, 16, 0)


def hbm_out(shape, dtype):
    return pltpu.HBM(shape, dtype)


def in_hbm(array):
    return pltpu.with_memory_space_constraint(array, pltpu.HBM)


def start_copies(pairs):
    copies = [pltpu.make_async_copy(*triple) for triple in pairs]
    for copy in copies:
        copy.start()
    return copies


def attend_kernel(
    block_rows,
    lengths_ref,
    tokens_hbm,
    gain_ref,
    wq_hbm,
    wk_hbm,
    wv_hbm,
    wo_hbm,
    table_ref,
    part_hbm,
    normed_hbm,
    q_hbm,
    k_hbm,
    v_hbm,
    mixed_hbm,
    long_hbm,
    short_hbm,
    tokens_ref,
    joint_ref,
    wo_ref,
    part_ref,
    normed_ref,
    q_ref,
    k_ref,
    v_ref,
    mixed_ref,
    long_ref,
    short_ref,
    diag_ref,
    in_sems,
    out_sems,
):
    tok_count, width = tokens_ref.shape
    own = q_ref.shape[1]
    pairs = own // 128
    short_tok = SHORT_DEV * SHORT_LEN
    tile = 256
    steps = tok_count // tile
    tiles_in = []
    for step in range(steps):
        rows = slice(step * tile, step * tile + tile)
        tiles_in.append((tokens_hbm.at[rows], tokens_ref.at[rows], in_sems.at[step]))
    weights = [
        (source, joint_ref.at[:, index * own : index * own + own])
        for index, source in enumerate((wq_hbm, wk_hbm, wv_hbm))
    ]
    weights.append((wo_hbm, wo_ref))
    copies = start_copies(
        tiles_in + [(src, dst, in_sems.at[steps + index]) for index, (src, dst) in enumerate(weights)]
    )
    weight_copies = copies[steps:]
    outs = []

    offset = lax.broadcasted_iota(jnp.int32, (table_ref.shape[1], 512), 1) - 256
    hot = jnp.where(
        diagonal_buckets(offset)
        == lax.broadcasted_iota(jnp.int32, (table_ref.shape[1], 512), 0),
        1.0,
        0.0,
    )
    diag_ref[...] = dot_nn(table_ref[...], hot.astype(jnp.bfloat16))
    gain = gain_ref[...]

    def normalize(step, carry):
        rows = pl.ds(pl.multiple_of(step * tile, tile), tile)
        pltpu.make_async_copy(tokens_hbm.at[rows], tokens_ref.at[rows], in_sems.at[step]).wait()
        values = tokens_ref[rows, :].astype(jnp.float32)
        normed_ref[rows, :] = (values * inverse_rms(values) * gain).astype(jnp.bfloat16)
        return carry

    lax.fori_loop(0, steps, normalize, 0)
    outs += start_copies([(normed_ref, normed_hbm, out_sems.at[0])])
    for copy in weight_copies[:3]:
        copy.wait()

    def project(step, carry):
        rows = pl.ds(pl.multiple_of(step * tile, tile), tile)
        joint = dot_nn(normed_ref[rows, :], joint_ref[...]).astype(jnp.bfloat16)
        q_ref[rows, :] = joint[:, :own] * jnp.bfloat16(0.125)
        k_ref[rows, :] = joint[:, own : 2 * own]
        v_ref[rows, :] = joint[:, 2 * own :]
        return carry

    lax.fori_loop(0, steps, project, 0)
    outs += start_copies(
        [
            (q_ref, q_hbm, out_sems.at[1]),
            (k_ref, k_hbm, out_sems.at[2]),
            (v_ref, v_hbm, out_sems.at[3]),
        ]
    )
    lane = lax.broadcasted_iota(jnp.int32, (1, 128), 1)
    key_place = lax.broadcasted_iota(jnp.int32, (1, LONG_LEN), 1)
    live_long = key_place < lengths_ref[SHORT_DEV]

    def softmax(scores):
        weights = jnp.exp(scores - jnp.max(scores, axis=1, keepdims=True))
        return (weights * (1.0 / jnp.sum(weights, axis=1, keepdims=True))).astype(jnp.bfloat16)

    def one_pair(pair):
        lanes = slice(pair * 128, pair * 128 + 128)
        tiles = []
        for sub in range(2):
            row = diag_ref[pair * 2 + sub : pair * 2 + sub + 1, :]
            spread = pltpu.roll(
                jnp.broadcast_to(row, (128, 512)), 256, 1, stride=1, stride_axis=0
            )
            tiles.append(
                (
                    spread[:, 0:128],
                    spread[:, 128:256],
                    spread[:, 384:512],
                    jnp.broadcast_to(row[:, 511:512], (128, 128)),
                    jnp.broadcast_to(row[:, 0:1], (128, 128)),
                )
            )
        out = []
        for sub in range(2):
            scores = []
            for block in range(SHORT_DEV):
                rows = slice(block * 128, block * 128 + 128)
                masked = jnp.where((lane >= 64) == (sub == 1), q_ref[rows, lanes], 0)
                live = key_place[:, :128] < lengths_ref[block]
                scores.append(
                    jnp.where(
                        live, dot_nt(masked, k_ref[rows, lanes]) + tiles[sub][0], -1000000000.0
                    )
                )
            probs = softmax(jnp.concatenate(scores, axis=0))
            short_ref[pair * 2 + sub] = probs
            mixed = []
            for block in range(SHORT_DEV):
                rows = slice(block * 128, block * 128 + 128)
                mixed.append(dot_nn(probs[rows], v_ref[rows, lanes]))
            out.append(jnp.concatenate(mixed, axis=0))
        mixed_ref[:short_tok, lanes] = jnp.where(lane < 64, out[0], out[1]).astype(jnp.bfloat16)
        keys = k_ref[short_tok:, lanes]
        values = v_ref[short_tok:, lanes]
        for start in range(0, LONG_LEN, block_rows):
            places = slice(start, start + block_rows)
            rows = slice(short_tok + start, short_tok + start + block_rows)
            queries = q_ref[rows, lanes]
            out = []
            for sub in range(2):
                masked = jnp.where((lane >= 64) == (sub == 1), queries, 0)
                same, above, below, far_above, far_below = tiles[sub]
                bias = jnp.concatenate(
                    [
                        jnp.concatenate(
                            [
                                same
                                if other == block
                                else above
                                if other == block + 1
                                else below
                                if other == block - 1
                                else far_above
                                if other > block
                                else far_below
                                for other in range(LONG_LEN // 128)
                            ],
                            axis=1,
                        )
                        for block in range(start // 128, (start + block_rows) // 128)
                    ],
                    axis=0,
                )
                scores = jnp.where(live_long, dot_nt(masked, keys) + bias, -1000000000.0)
                probs = softmax(scores)
                long_ref[pair * 2 + sub, places, :] = probs
                out.append(dot_nn(probs, values))
            mixed_ref[rows, lanes] = jnp.where(lane < 64, out[0], out[1]).astype(jnp.bfloat16)

    for pair in range(pairs):
        one_pair(pair)
        both = slice(pair * 2, pair * 2 + 2)
        outs += start_copies(
            [
                (long_ref.at[both], long_hbm.at[both], out_sems.at[4 + 2 * pair]),
                (short_ref.at[both], short_hbm.at[both], out_sems.at[5 + 2 * pair]),
            ]
        )
    weight_copies[3].wait()
    base = 4 + 2 * pairs
    outs += start_copies([(mixed_ref, mixed_hbm, out_sems.at[base])])

    def part_copy(step):
        rows = pl.ds(pl.multiple_of(step * tile, tile), tile)
        return pltpu.make_async_copy(part_ref.at[rows], part_hbm.at[rows], out_sems.at[base + 1 + step])

    def project_out(step, carry):
        rows = pl.ds(pl.multiple_of(step * tile, tile), tile)
        part_ref[rows, :] = dot_nn(mixed_ref[rows, :], wo_ref[...]).astype(part_ref.dtype)
        part_copy(step).start()
        return carry

    lax.fori_loop(0, steps, project_out, 0)
    outs += [part_copy(step) for step in range(steps)]
    for copy in outs:
        copy.wait()


def attend(lengths, tokens, gain, w_query, w_key, w_value, w_out, table, block_rows=512):
    tok_count, width = tokens.shape
    own = w_query.shape[1]
    heads = own // 64
    heads_pad = -(-heads // 8) * 8
    table = jnp.pad(table.T, ((0, heads_pad - heads), (0, 0)))
    short_tok = SHORT_DEV * SHORT_LEN
    flops = 2 * tok_count * width * own * 4 + 4 * heads * (512 * 512 + short_tok * 128) * 64
    hbm = pl.BlockSpec(memory_space=pltpu.HBM)
    out_shapes = [
        ((tok_count, width), jnp.bfloat16),
        ((tok_count, width), jnp.bfloat16),
        ((tok_count, own), jnp.bfloat16),
        ((tok_count, own), jnp.bfloat16),
        ((tok_count, own), jnp.bfloat16),
        ((tok_count, own), jnp.bfloat16),
        ((heads, LONG_LEN, LONG_LEN), jnp.bfloat16),
        ((heads, short_tok, SHORT_LEN), jnp.bfloat16),
    ]
    steps = tok_count // 256
    return pl.pallas_call(
        partial(attend_kernel, block_rows),
        out_shape=[jax.ShapeDtypeStruct(*out_shapes[0])]
        + [hbm_out(shape, dtype) for shape, dtype in out_shapes[1:]],
        in_specs=[pl.BlockSpec(memory_space=pltpu.SMEM), hbm]
        + vmem(1)
        + [hbm] * 4
        + vmem(1),
        out_specs=[hbm] * 8,
        scratch_shapes=[pltpu.VMEM(tokens.shape, jnp.bfloat16)]
        + [pltpu.VMEM((width, 3 * own), jnp.bfloat16), pltpu.VMEM(w_out.shape, jnp.bfloat16)]
        + [pltpu.VMEM(shape, dtype) for shape, dtype in out_shapes]
        + [
            pltpu.VMEM((heads_pad, 512), jnp.float32),
            pltpu.SemaphoreType.DMA((steps + 4,)),
            pltpu.SemaphoreType.DMA((5 + 2 * (heads // 2) + steps,)),
        ],
        compiler_params=params(24),
        cost_estimate=pl.CostEstimate(
            flops=flops, bytes_accessed=16000000, transcendentals=heads * 512 * 640
        ),
        name="attend",
    )(
        lengths,
        in_hbm(tokens),
        gain.astype(jnp.float32)[None],
        in_hbm(w_query),
        in_hbm(w_key),
        in_hbm(w_value),
        in_hbm(w_out),
        table,
    )


def attend_back_pair(
    pair, hg_ref, q_ref, k_ref, v_ref, mixed_ref, long_ref, short_ref, grads_ref, tiles_ref, far_ref, sg_ref,
):
    short_tok = SHORT_DEV * SHORT_LEN
    lane = lax.broadcasted_iota(jnp.int32, (1, 128), 1)
    lanes = pl.ds(pl.multiple_of(pair * 128, 128), 128)
    blocks = LONG_LEN // 128
    heads_grad = hg_ref[:, lanes]
    products = heads_grad.astype(jnp.float32) * mixed_ref[:, lanes].astype(jnp.float32)
    q_t = jnp.transpose(q_ref[:, lanes])
    hg_t = jnp.transpose(heads_grad)
    qg = []
    kg_t = []
    vg_t = []
    for sub in range(2):
        head = pair * 2 + sub
        own = (lane >= 64) == (sub == 1)
        rows_t = slice(64 * sub, 64 * sub + 64)
        masked = jnp.where(own, heads_grad, 0)
        delta = jnp.sum(jnp.where(own, products, 0.0), axis=1, keepdims=True)
        grads = [
            dot_nt(masked[block * 128 : block * 128 + 128], v_ref[block * 128 : block * 128 + 128, lanes])
            for block in range(SHORT_DEV)
        ]
        probs = short_ref[head]
        part = probs.astype(jnp.float32) * (jnp.concatenate(grads, axis=0) - delta[:short_tok])
        same = part[:128]
        for block in range(1, SHORT_DEV):
            same = same + part[block * 128 : block * 128 + 128]
        part = part.astype(jnp.bfloat16)
        qg_parts = []
        kg_parts = []
        vg_parts = []
        for block in range(SHORT_DEV):
            rows = slice(block * 128, block * 128 + 128)
            qg_parts.append(dot_nn(part[rows], k_ref[rows, lanes]))
            kg_parts.append(dot_nn(q_t[rows_t, rows], part[rows]))
            vg_parts.append(dot_nn(hg_t[rows_t, rows], probs[rows]))
        above = jnp.zeros((128, 128), jnp.float32)
        below = above
        far_above = above
        far_below = above
        probs = long_ref[head]
        part = probs.astype(jnp.float32) * (
            dot_nt(masked[short_tok:], v_ref[short_tok:, lanes]) - delta[short_tok:]
        )
        for block in range(blocks):
            for other in range(blocks):
                piece = part[block * 128 : block * 128 + 128, other * 128 : other * 128 + 128]
                if other == block:
                    same = same + piece
                elif other == block + 1:
                    above = above + piece
                elif other == block - 1:
                    below = below + piece
                elif other > block:
                    far_above = far_above + piece
                else:
                    far_below = far_below + piece
        sg_ref[...] = part.astype(jnp.bfloat16)
        qg_parts.append(dot_nn(sg_ref[...], k_ref[short_tok:, lanes]))
        kg_parts.append(dot_nn(q_t[rows_t, short_tok:], sg_ref[...]))
        vg_parts.append(dot_nn(hg_t[rows_t, short_tok:], probs))
        qg.append(jnp.concatenate(qg_parts, axis=0))
        kg_t.append(jnp.concatenate(kg_parts, axis=1))
        vg_t.append(jnp.concatenate(vg_parts, axis=1))
        tiles_ref[head, :, 0:128] = same
        tiles_ref[head, :, 128:256] = above
        tiles_ref[head, :, 256:384] = below
        far_ref[head, 0:1, :] = jnp.sum(far_above, axis=0, keepdims=True)
        far_ref[head, 1:2, :] = jnp.sum(far_below, axis=0, keepdims=True)
    width = q_ref.shape[1]
    grads_ref[:, lanes] = (jnp.where(lane < 64, qg[0], qg[1]) * 0.125).astype(jnp.bfloat16)
    for index, whole in ((1, kg_t), (2, vg_t)):
        place = pl.ds(pl.multiple_of(index * width + pair * 128, 128), 128)
        grads_ref[:, place] = jnp.transpose(jnp.concatenate(whole, axis=0).astype(jnp.bfloat16))


def diagonals(tiles):
    tile = jnp.concatenate(
        [tiles[:, 0:256], jnp.zeros((128, 128), jnp.float32), tiles[:, 256:384]], axis=1
    )
    span = 64
    while span:
        tile = tile[:span] + pltpu.roll(tile[span:], 512 - span, 1)
        span //= 2
    return tile


def table_from(diag, bucket_count):
    lane = jnp.arange(768, dtype=jnp.int32)
    offset = jnp.where(lane < 256, lane, lane - 512)
    offset = jnp.where(lane >= 640, -256, jnp.where(lane >= 512, 256, offset))
    hot = (diagonal_buckets(offset)[:, None] == jnp.arange(bucket_count)[None, :]).astype(jnp.float32)
    return lax.dot_general(
        hot, diag, (((0,), (1,)), ((), ())), precision=highest, preferred_element_type=jnp.float32
    )


def dispatch_rows(send_ref, slot_row, half_rows):
    slots = send_ref.shape[0]
    tok_count = slot_row.shape[1]
    span = 256
    for base in range(0, slots, span):
        place = lax.broadcasted_iota(jnp.int32, (span, tok_count), 0) + base
        hot = jnp.where(place == slot_row, 1.0, 0.0).astype(jnp.bfloat16)
        send_ref[base : base + span, :] = dot_nn(hot, half_rows).astype(jnp.bfloat16)


def half_lanes(core, half):
    return pl.ds(pl.multiple_of(core * half, half), half)


def route_kernel(
    capacity, where_ref, routes_hbm, grad_hbm, row_hbm, col_hbm, send_ref, routes_ref, grad_ref, row_ref,
    col_ref, in_sems, out_sems,
):
    tok_count = routes_ref.shape[1]
    slots, half = send_ref.shape
    experts = slots // capacity
    fetch, copy = start_copies(
        [
            (routes_hbm, routes_ref, in_sems.at[0]),
            (grad_hbm.at[:, half_lanes(where_ref[0], half)], grad_ref, in_sems.at[1]),
        ]
    )
    fetch.wait()
    routes = routes_ref[...]
    expert = lax.broadcasted_iota(jnp.int32, (experts, tok_count), 0)
    lane = lax.broadcasted_iota(jnp.int32, (1, tok_count), 1)
    hot = jnp.where(expert == routes, 1.0, 0.0)
    total = hot
    step = 1
    while step < tok_count:
        total = total + jnp.where(lane >= step, pltpu.roll(total, step, 1), 0.0)
        step *= 2
    before = jnp.sum(hot * total, axis=0, keepdims=True).astype(jnp.int32) - 1
    slot = jnp.where(before < capacity, routes * capacity + before, slots)
    row_ref[...] = slot
    wide = jnp.broadcast_to(slot.astype(jnp.float32), (128, tok_count))
    col_ref[...] = jnp.transpose(wide).astype(jnp.int32)
    outs = start_copies([(row_ref, row_hbm, out_sems.at[0]), (col_ref, col_hbm, out_sems.at[1])])
    copy.wait()
    dispatch_rows(send_ref, slot, grad_ref[...])
    for copy in outs:
        copy.wait()


def route(where, routes, out_grad, experts, capacity):
    tok_count, width = out_grad.shape
    slots = experts * capacity
    return pl.pallas_call(
        partial(route_kernel, capacity),
        out_shape=[
            hbm_out((1, tok_count), jnp.int32),
            hbm_out((tok_count, 128), jnp.int32),
            jax.ShapeDtypeStruct((slots, width // 2), jnp.bfloat16),
        ],
        in_specs=[
            pl.BlockSpec(memory_space=pltpu.SMEM),
            pl.BlockSpec(memory_space=pltpu.HBM),
            pl.BlockSpec(memory_space=pltpu.HBM),
        ],
        out_specs=[pl.BlockSpec(memory_space=pltpu.HBM)] * 2 + vmem(1),
        scratch_shapes=[
            pltpu.VMEM((1, tok_count), jnp.int32),
            pltpu.VMEM((tok_count, width // 2), jnp.bfloat16),
            pltpu.VMEM((1, tok_count), jnp.int32),
            pltpu.VMEM((tok_count, 128), jnp.int32),
            pltpu.SemaphoreType.DMA((2,)),
            pltpu.SemaphoreType.DMA((2,)),
        ],
        compiler_params=params(),
        cost_estimate=pl.CostEstimate(
            flops=slots * tok_count * width, bytes_accessed=4000000, transcendentals=0
        ),
        name="route",
    )(where, in_hbm(routes.reshape(1, tok_count)), in_hbm(out_grad))


def second_kernel(
    where_ref, tokens_hbm, own_ref, other_ref, gain_ref, row_hbm, residual_hbm, send_ref, tokens_ref,
    row_ref, residual_ref, second_ref, in_sems, out_sems,
):
    tile = 256
    tok_count = tokens_ref.shape[0]
    half = send_ref.shape[1]
    tiles_rows = [slice(start, start + tile) for start in range(0, tok_count, tile)]
    copies = start_copies(
        [
            (tokens_hbm.at[rows], tokens_ref.at[rows], in_sems.at[step])
            for step, rows in enumerate(tiles_rows)
        ]
        + [(row_hbm, row_ref, in_sems.at[len(tiles_rows)])]
    )
    outs = []
    gain = gain_ref[...]
    for step, rows in enumerate(tiles_rows):
        attn = own_ref[rows, :].astype(jnp.float32) + other_ref[rows, :].astype(jnp.float32)
        copies[step].wait()
        residual = tokens_ref[rows, :].astype(jnp.float32) + attn
        residual_ref[rows, :] = residual
        outs += start_copies([(residual_ref.at[rows], residual_hbm.at[rows], out_sems.at[step])])
        second_ref[rows, :] = (residual * inverse_rms(residual) * gain).astype(jnp.bfloat16)
    copies[-1].wait()
    dispatch_rows(send_ref, row_ref[...], second_ref[:, half_lanes(where_ref[0], half)])
    for copy in outs:
        copy.wait()


def second_rows(where, tokens, own, other, gain, slot_row, slots):
    tok_count, width = tokens.shape
    steps = tok_count // 256
    hbm = pl.BlockSpec(memory_space=pltpu.HBM)
    return pl.pallas_call(
        second_kernel,
        out_shape=[
            hbm_out((tok_count, width), jnp.float32),
            jax.ShapeDtypeStruct((slots, width // 2), jnp.bfloat16),
        ],
        in_specs=[pl.BlockSpec(memory_space=pltpu.SMEM), hbm] + vmem(3) + [hbm],
        out_specs=[hbm] + vmem(1),
        scratch_shapes=[
            pltpu.VMEM((tok_count, width), jnp.bfloat16),
            pltpu.VMEM((1, tok_count), jnp.int32),
            pltpu.VMEM((tok_count, width), jnp.float32),
            pltpu.VMEM((tok_count, width), jnp.bfloat16),
            pltpu.SemaphoreType.DMA((steps + 1,)),
            pltpu.SemaphoreType.DMA((steps,)),
        ],
        compiler_params=params(),
        cost_estimate=pl.CostEstimate(
            flops=slots * tok_count * width, bytes_accessed=13000000, transcendentals=0
        ),
        name="second",
    )(where, in_hbm(tokens), own, other, gain.astype(jnp.float32)[None], in_hbm(slot_row))


def hidden_grad_kernel(where_ref, own_ref, other_ref, outer_ref, out_ref, whole_ref):
    half = own_ref.shape[1]
    core = where_ref[0]
    whole_ref[:, half_lanes(core, half)] = own_ref[...]
    whole_ref[:, half_lanes(1 - core, half)] = other_ref[...]
    out_ref[...] = dot_nt(whole_ref[...], outer_ref[...]).astype(jnp.bfloat16)


def hidden_grad_of(where, own, other, outer):
    slots, half = own.shape
    hidden = outer.shape[0]
    tile = 256
    rows = pl.BlockSpec((tile, half), lambda step: (step, 0))
    return pl.pallas_call(
        hidden_grad_kernel,
        grid=(slots // tile,),
        out_shape=hbm_out((slots, hidden), jnp.bfloat16),
        in_specs=[pl.BlockSpec(memory_space=pltpu.SMEM), rows, rows] + vmem(1),
        out_specs=pl.BlockSpec((tile, hidden), lambda step: (step, 0)),
        scratch_shapes=[pltpu.VMEM((tile, 2 * half), jnp.bfloat16)],
        compiler_params=params(),
        cost_estimate=pl.CostEstimate(
            flops=4 * slots * half * hidden, bytes_accessed=12000000, transcendentals=0
        ),
        name="hidden_grad",
    )(where, own, other, outer)


def gate_of(rows, router, index):
    experts = router.shape[1]
    logits = dot_nn(rows, router)
    exp_logit = jnp.exp(logits - jnp.max(logits, axis=1, keepdims=True))
    probs = exp_logit * (1.0 / jnp.sum(exp_logit, axis=1, keepdims=True))
    hit = jnp.where(lax.broadcasted_iota(jnp.int32, (1, experts), 1) == index, 1.0, 0.0)
    return probs, hit, jnp.sum(probs * hit, axis=1, keepdims=True)


def expert_kernel(
    where_ref,
    own_ref,
    other_ref,
    hg_ref,
    inner_ref,
    router_ref,
    hidden_ref,
    pre_grad_ref,
    keep_ref,
    send_ref,
    logit_ref,
    arrived_ref,
    whole_ref,
):
    core = where_ref[0]
    tile, half = own_ref.shape
    own_lanes = half_lanes(core, half)
    other_lanes = half_lanes(1 - core, half)
    arrived_ref[:, own_lanes] = own_ref[...]
    arrived_ref[:, other_lanes] = other_ref[...]
    arrived = arrived_ref[...]
    probs, hit, gate = gate_of(arrived, router_ref[...], where_ref[1])
    curve = 0.7978845608028654
    gate_grad = jnp.zeros((tile, 1), jnp.float32)
    back = jnp.zeros((tile, 2 * half), jnp.float32)
    chunk = 512
    for start in range(0, hg_ref.shape[1], chunk):
        cols = slice(start, start + chunk)
        pre = dot_nn(arrived, inner_ref[:, cols])
        square = pre * pre
        share = 0.5 + 0.5 * jnp.tanh(pre * (curve + (curve * 0.044715) * square))
        hidden_ref[:, cols] = (pre * share).astype(jnp.bfloat16)
        passed = share * hg_ref[:, cols].astype(jnp.float32)
        gate_grad = gate_grad + jnp.sum(pre * passed, axis=1, keepdims=True)
        bend = pre * (2.0 * curve + (6.0 * curve * 0.044715) * square)
        pre_grad = ((gate * passed) * (1.0 + (1.0 - share) * bend)).astype(jnp.bfloat16)
        pre_grad_ref[:, cols] = pre_grad
        back = back + dot_nt(pre_grad, inner_ref[:, cols])
    logit = (probs * (gate_grad * (hit - gate))).astype(jnp.bfloat16)
    logit_ref[...] = logit
    whole_ref[...] = back + dot_nt(logit, router_ref[...])
    send_ref[...] = whole_ref[:, other_lanes].astype(jnp.bfloat16)
    keep_ref[...] = whole_ref[:, own_lanes]


def expert(where, own, other, hidden_grad, inner, router):
    slots, half = own.shape
    width, hidden = inner.shape
    experts = router.shape[1]
    tile = 256
    halves = pl.BlockSpec((tile, half), lambda step: (step, 0))
    units = pl.BlockSpec((tile, hidden), lambda step: (step, 0))
    return pl.pallas_call(
        expert_kernel,
        grid=(slots // tile,),
        out_shape=[
            hbm_out((slots, hidden), jnp.bfloat16),
            hbm_out((slots, hidden), jnp.bfloat16),
            jax.ShapeDtypeStruct((slots, half), jnp.float32),
            jax.ShapeDtypeStruct((slots, half), jnp.bfloat16),
            hbm_out((slots, experts), jnp.bfloat16),
        ],
        in_specs=[
            pl.BlockSpec(memory_space=pltpu.SMEM),
            halves,
            halves,
            units,
            pl.BlockSpec(inner.shape, lambda step: (0, 0), pipeline_mode=pl.Buffered(1)),
        ]
        + vmem(1),
        out_specs=[
            units,
            units,
            halves,
            halves,
            pl.BlockSpec((tile, experts), lambda step: (step, 0)),
        ],
        scratch_shapes=[
            pltpu.VMEM((tile, width), jnp.bfloat16),
            pltpu.VMEM((tile, width), jnp.float32),
        ],
        compiler_params=params(),
        cost_estimate=pl.CostEstimate(
            flops=4 * slots * width * hidden, bytes_accessed=20000000, transcendentals=slots * hidden
        ),
        name="expert",
    )(where, own, other, in_hbm(hidden_grad), in_hbm(inner), router)


def expert_out_kernel(
    where_ref, hidden_ref, own_ref, other_ref, logit_ref, outer_ref, keep_ref, send_ref, router_ref, whole_ref
):
    core = where_ref[0]
    half = keep_ref.shape[1]
    own_lanes = half_lanes(core, half)
    other_lanes = half_lanes(1 - core, half)
    whole_ref[...] = dot_nn(hidden_ref[...], outer_ref[...])
    send_ref[...] = whole_ref[:, other_lanes].astype(jnp.bfloat16)
    keep_ref[...] = whole_ref[:, own_lanes]

    @pl.when(pl.program_id(0) == 0)
    def _():
        router_ref[...] = jnp.zeros_like(router_ref)

    router_ref[:, own_lanes] += contract_rows(logit_ref[...], own_ref[...])
    router_ref[:, other_lanes] += contract_rows(logit_ref[...], other_ref[...])


def expert_out_of(where, hidden, own, other, logit_grad, outer):
    slots, units = hidden.shape
    width = outer.shape[1]
    experts = logit_grad.shape[1]
    half = width // 2
    tile = 256
    halves = pl.BlockSpec((tile, half), lambda step: (step, 0))
    return pl.pallas_call(
        expert_out_kernel,
        grid=(slots // tile,),
        out_shape=[
            jax.ShapeDtypeStruct((slots, half), jnp.float32),
            jax.ShapeDtypeStruct((slots, half), jnp.bfloat16),
            hbm_out((experts, width), jnp.float32),
        ],
        in_specs=[
            pl.BlockSpec(memory_space=pltpu.SMEM),
            pl.BlockSpec((tile, units), lambda step: (step, 0)),
            halves,
            halves,
            pl.BlockSpec((tile, experts), lambda step: (step, 0)),
        ]
        + vmem(1),
        out_specs=[halves, halves, pl.BlockSpec((experts, width), lambda step: (0, 0))],
        scratch_shapes=[pltpu.VMEM((tile, width), jnp.float32)],
        compiler_params=params(),
        cost_estimate=pl.CostEstimate(
            flops=2 * slots * width * units, bytes_accessed=9000000, transcendentals=0
        ),
        name="expert_out",
    )(where, in_hbm(hidden), in_hbm(own), in_hbm(other), in_hbm(logit_grad), outer)


def expert_grads_kernel(
    where_ref,
    own_hbm,
    other_hbm,
    grad_own_hbm,
    grad_other_hbm,
    hidden_ref,
    pre_grad_ref,
    router_ref,
    inner_grad_ref,
    outer_grad_ref,
    arrived_ref,
    gated_ref,
    sems,
):
    core = where_ref[0]
    half = own_hbm.shape[1]
    own_lanes = half_lanes(core, half)
    other_lanes = half_lanes(1 - core, half)

    @pl.when(pl.program_id(0) == 0)
    def _():
        copies = [
            pltpu.make_async_copy(own_hbm, arrived_ref.at[:, own_lanes], sems.at[0]),
            pltpu.make_async_copy(other_hbm, arrived_ref.at[:, other_lanes], sems.at[1]),
            pltpu.make_async_copy(grad_own_hbm, gated_ref.at[:, own_lanes], sems.at[2]),
            pltpu.make_async_copy(grad_other_hbm, gated_ref.at[:, other_lanes], sems.at[3]),
        ]
        for copy in copies:
            copy.start()
        for copy in copies:
            copy.wait()
        gate = gate_of(arrived_ref[...], router_ref[...], where_ref[1])[2]
        gated_ref[...] = (gate * gated_ref[...].astype(jnp.float32)).astype(jnp.bfloat16)

    outer_grad_ref[...] = contract_rows(hidden_ref[...], gated_ref[...])
    inner_grad_ref[...] = contract_rows(arrived_ref[...], pre_grad_ref[...])


def expert_grads(where, own, other, grad_own, grad_other, hidden, pre_grad, router):
    slots, half = own.shape
    units = hidden.shape[1]
    width = router.shape[0]
    tile = 256
    hbm = pl.BlockSpec(memory_space=pltpu.HBM)
    whole = lambda shape: pl.BlockSpec(shape, lambda step: (0, 0))
    cols = pl.BlockSpec((slots, tile), lambda step: (0, step))
    return pl.pallas_call(
        expert_grads_kernel,
        grid=(units // tile,),
        out_shape=[
            hbm_out((width, units), jnp.float32),
            hbm_out((units, width), jnp.float32),
        ],
        in_specs=[
            pl.BlockSpec(memory_space=pltpu.SMEM),
            hbm,
            hbm,
            hbm,
            hbm,
            cols,
            cols,
            whole(router.shape),
        ],
        out_specs=[
            pl.BlockSpec((width, tile), lambda step: (0, step)),
            pl.BlockSpec((tile, width), lambda step: (step, 0)),
        ],
        scratch_shapes=[
            pltpu.VMEM((slots, width), jnp.bfloat16),
            pltpu.VMEM((slots, width), jnp.bfloat16),
            pltpu.SemaphoreType.DMA((4,)),
        ],
        compiler_params=params(24),
        cost_estimate=pl.CostEstimate(
            flops=4 * slots * width * units, bytes_accessed=22000000, transcendentals=0
        ),
        name="expert_grads",
    )(
        where,
        in_hbm(own),
        in_hbm(other),
        in_hbm(grad_own),
        in_hbm(grad_other),
        in_hbm(hidden),
        in_hbm(pre_grad),
        router,
    )


def output_kernel(
    capacity, where_ref, col_ref, returned_ref, residual_ref, gain_ref, router_ref, out_ref
):
    slots, half = returned_ref.shape
    tile = residual_ref.shape[0]
    experts = router_ref.shape[1]
    col = col_ref[:, :1]
    place = lax.broadcasted_iota(jnp.int32, (tile, slots), 1)
    hot = jnp.where(place == col, 1.0, 0.0).astype(jnp.bfloat16)
    token_out = dot_nn(hot, returned_ref[...])
    residual = residual_ref[...]
    second = (residual * inverse_rms(residual) * gain_ref[...]).astype(jnp.bfloat16)
    logits = dot_nn(second, router_ref[...])
    exp_logit = jnp.exp(logits - jnp.max(logits, axis=1, keepdims=True))
    first = lax.broadcasted_iota(jnp.int32, (1, experts), 1) * capacity
    hit = jnp.where((col >= first) & (col < first + capacity), exp_logit, 0.0)
    gate = jnp.sum(hit, axis=1, keepdims=True) / jnp.sum(exp_logit, axis=1, keepdims=True)
    own = residual_ref[:, half_lanes(where_ref[0], half)]
    out_ref[...] = (own + gate * token_out).astype(jnp.bfloat16)


def output_of(where, slot_col, returned, residual, gain, router, capacity):
    tok_count, width = residual.shape
    slots, half = returned.shape
    tile = 256
    whole = lambda shape: pl.BlockSpec(shape, lambda step: (0, 0))
    return pl.pallas_call(
        partial(output_kernel, capacity),
        grid=(tok_count // tile,),
        out_shape=jax.ShapeDtypeStruct((tok_count, half), jnp.bfloat16),
        in_specs=[
            pl.BlockSpec(memory_space=pltpu.SMEM),
            pl.BlockSpec((tile, 128), lambda step: (step, 0)),
            whole(returned.shape),
            pl.BlockSpec((tile, width), lambda step: (step, 0)),
            whole((1, width)),
            whole(router.shape),
        ],
        out_specs=pl.BlockSpec((tile, half), lambda step: (step, 0)),
        compiler_params=params(),
        cost_estimate=pl.CostEstimate(
            flops=2 * tok_count * half * slots, bytes_accessed=6000000, transcendentals=0
        ),
        name="output",
    )(
        where, in_hbm(slot_col), in_hbm(returned), in_hbm(residual), gain.astype(jnp.float32)[None], router
    )


def normed_back_kernel(grads_ref, wq_ref, wk_ref, wv_ref, out_ref):
    own = wq_ref.shape[1]
    out_ref[...] = (
        dot_nt(grads_ref[:, :own], wq_ref[...])
        + dot_nt(grads_ref[:, own : 2 * own], wk_ref[...])
        + dot_nt(grads_ref[:, 2 * own :], wv_ref[...])
    ).astype(jnp.bfloat16)


def normed_back(grads, w_query, w_key, w_value):
    tok_count = grads.shape[0]
    width, own = w_query.shape
    tile = 256
    whole = pl.BlockSpec((width, own), lambda step: (0, 0))
    return pl.pallas_call(
        normed_back_kernel,
        grid=(tok_count // tile,),
        out_shape=jax.ShapeDtypeStruct((tok_count, width), jnp.bfloat16),
        in_specs=[pl.BlockSpec((tile, 3 * own), lambda step: (step, 0))] + [whole] * 3,
        out_specs=pl.BlockSpec((tile, width), lambda step: (step, 0)),
        compiler_params=params(),
        cost_estimate=pl.CostEstimate(
            flops=6 * tok_count * own * width, bytes_accessed=6000000, transcendentals=0
        ),
        name="normed_back",
    )(*(in_hbm(array) for array in (grads, w_query, w_key, w_value)))


def input_back_kernel(tokens_ref, own_ref, other_ref, gain_ref, residual_ref, out_ref):
    ybar = own_ref[...].astype(jnp.float32) + other_ref[...].astype(jnp.float32)
    values = tokens_ref[...].astype(jnp.float32)
    scale = inverse_rms(values)
    scaled = values * scale
    pulled = ybar * gain_ref[...]
    out_ref[...] = residual_ref[...] + scale * (
        pulled - scaled * jnp.mean(pulled * scaled, axis=1, keepdims=True)
    )


def input_back(tokens, own, other, gain, residual_grad):
    tok_count, width = tokens.shape
    tile = 256
    rows = pl.BlockSpec((tile, width), lambda step: (step, 0))
    return pl.pallas_call(
        input_back_kernel,
        grid=(tok_count // tile,),
        out_shape=jax.ShapeDtypeStruct((tok_count, width), jnp.float32),
        in_specs=[rows, rows, rows, pl.BlockSpec((1, width), lambda step: (0, 0)), rows],
        out_specs=rows,
        compiler_params=params(),
        cost_estimate=pl.CostEstimate(
            flops=10 * tok_count * width, bytes_accessed=11000000, transcendentals=0
        ),
        name="input_back",
    )(in_hbm(tokens), own, other, gain.astype(jnp.float32)[None], in_hbm(residual_grad))


def back_kernel(
    bits_ref,
    where_ref,
    col_hbm,
    own_hbm,
    other_hbm,
    residual_hbm,
    grad_hbm,
    wo_hbm,
    q_hbm,
    k_hbm,
    v_hbm,
    mixed_hbm,
    long_hbm,
    short_hbm,
    normed_hbm,
    wq_hbm,
    wk_hbm,
    wv_hbm,
    gain_one_ref,
    gain_two_ref,
    router_ref,
    out_hbm,
    grads_hbm,
    sent_a,
    sent_b,
    sent_c,
    kept_a,
    kept_b,
    kept_c,
    col_ref,
    back_ref,
    residual_ref,
    grad_ref,
    wo_ref,
    q_ref,
    k_ref,
    v_ref,
    mixed_ref,
    long_ref,
    short_ref,
    normed_ref,
    wq_ref,
    wk_ref,
    wv_ref,
    attn_ref,
    heads_ref,
    grads_ref,
    sg_ref,
    tiles_ref,
    far_ref,
    stack_ref,
    small_ref,
    packed_ref,
    total_ref,
    in_sems,
    out_sems,
):
    tok_count, width = residual_ref.shape
    slots, half = own_hbm.shape
    own = mixed_ref.shape[1]
    experts = router_ref.shape[0]
    pairs = own // 128
    tile = 256
    steps = tok_count // tile
    core = where_ref[0]
    first = [
        (own_hbm, back_ref.at[:, half_lanes(core, half)]),
        (other_hbm, back_ref.at[:, half_lanes(1 - core, half)]),
        (col_hbm, col_ref),
        (wo_hbm, wo_ref),
    ]
    tiles = []
    for start in range(0, tok_count, tile):
        rows = slice(start, start + tile)
        tiles.append((residual_hbm.at[rows], residual_ref.at[rows]))
        tiles.append((grad_hbm.at[rows], grad_ref.at[rows]))
    attention = [(q_hbm, q_ref), (k_hbm, k_ref), (v_hbm, v_ref), (mixed_hbm, mixed_ref), (short_hbm, short_ref)]
    for pair in range(pairs):
        both = slice(pair * 2, pair * 2 + 2)
        attention.append((long_hbm.at[both], long_ref.at[both]))
    weights = [(normed_hbm, normed_ref), (wq_hbm, wq_ref), (wk_hbm, wk_ref), (wv_hbm, wv_ref)]
    copies = start_copies(
        [
            (source, target, in_sems.at[index])
            for index, (source, target) in enumerate(first + tiles + attention + weights)
        ]
    )
    base = len(first) + len(tiles)
    outs = []

    for copy in copies[: len(first)]:
        copy.wait()
    gain_two = gain_two_ref[...]
    place = lax.broadcasted_iota(jnp.int32, (tile, slots), 1)

    def tile_out(step):
        rows = pl.ds(pl.multiple_of(step * tile, tile), tile)
        return pltpu.make_async_copy(residual_ref.at[rows], out_hbm.at[rows], out_sems.at[step])

    def one_tile(step, gain_two_grad):
        rows = pl.ds(pl.multiple_of(step * tile, tile), tile)
        at = len(first) + 2 * step
        pltpu.make_async_copy(residual_hbm.at[rows], residual_ref.at[rows], in_sems.at[at]).wait()
        pltpu.make_async_copy(grad_hbm.at[rows], grad_ref.at[rows], in_sems.at[at + 1]).wait()
        hot = jnp.where(place == col_ref[rows, :][:, :1], 1.0, 0.0).astype(jnp.bfloat16)
        ybar = dot_nn(hot, back_ref[...])
        values = residual_ref[rows, :]
        scale = inverse_rms(values)
        scaled = values * scale
        pulled = ybar * gain_two
        back = scale * (pulled - scaled * jnp.mean(pulled * scaled, axis=1, keepdims=True))
        out = back + grad_ref[rows, :].astype(jnp.float32)
        residual_ref[rows, :] = out
        attn = out.astype(jnp.bfloat16)
        attn_ref[rows, :] = attn
        heads_ref[rows, :] = dot_nt(attn, wo_ref[...]).astype(jnp.bfloat16)
        tile_out(step).start()
        return gain_two_grad + jnp.sum(ybar * scaled, axis=0, keepdims=True)

    gain_two_grad = lax.fori_loop(0, steps, one_tile, jnp.zeros((1, width), jnp.float32), unroll=2)
    outs += [tile_out(step) for step in range(steps)]

    for copy in copies[base : base + 5]:
        copy.wait()

    def one_pair(pair, carry):
        both = pl.ds(pair * 2, 2)
        pltpu.make_async_copy(long_hbm.at[both], long_ref.at[both], in_sems.at[base + 5 + pair]).wait()
        attend_back_pair(
            pair, heads_ref, q_ref, k_ref, v_ref, mixed_ref, long_ref, short_ref, grads_ref, tiles_ref, far_ref,
            sg_ref,
        )
        return carry

    lax.fori_loop(0, pairs, one_pair, 0, unroll=True)
    outs += start_copies([(grads_ref, grads_hbm, out_sems.at[steps])])

    def out_rows(block, carry):
        start = pl.multiple_of(block * 128, 128)
        grad = contract_rows(mixed_ref[:, pl.ds(start, 128)], attn_ref[...]).astype(jnp.bfloat16)
        for part in range(width // own):
            at = pl.multiple_of(3 * width + part * own + start, 128)
            stack_ref[pl.ds(at, 128), :] = grad[:, part * own : part * own + own]
        return carry

    lax.fori_loop(0, own // 128, out_rows, 0, unroll=True)
    small_ref[0:experts, :] = router_ref[...]
    small_ref[experts + 1 : experts + 2, :] = gain_two_grad
    for head in range(2 * pairs):
        row = experts + 2 + head
        small_ref[row : row + 1, 0:512] = diagonals(tiles_ref[head])
        small_ref[row : row + 1, 512:640] = far_ref[head, 0:1, :]
        small_ref[row : row + 1, 640:768] = far_ref[head, 1:2, :]
    for copy in copies[base + 5 + pairs :]:
        copy.wait()
    rows = stack_ref.shape[0] // 3
    span = rows // 2

    def send_part(part, sent, kept):
        mine = bits_ref[part]
        sent_rows = pl.ds(pl.multiple_of(part * rows + (1 - mine) * span, span), span)
        kept_rows = pl.ds(pl.multiple_of(part * rows + mine * span, span), span)
        return start_copies(
            [
                (stack_ref.at[sent_rows], sent.at[:span], out_sems.at[steps + 4 + 2 * part]),
                (stack_ref.at[kept_rows], kept, out_sems.at[steps + 5 + 2 * part]),
            ]
        )

    def head_rows(block, carry):
        start = pl.multiple_of(block * tile, tile)
        piece = pl.ds(start, tile)
        grad = contract_rows(normed_ref[:, piece], grads_ref[...])
        total = jnp.zeros((tile, 1), jnp.float32)
        for index, w_ref in enumerate((wq_ref, wk_ref, wv_ref)):
            part = grad[:, index * own : index * own + own]
            total = total + jnp.sum(part * w_ref[piece, :].astype(jnp.float32), axis=1, keepdims=True)
            stack_ref[pl.ds(pl.multiple_of(index * width + start, tile), tile), :] = part.astype(jnp.bfloat16)
        total_ref[piece, :] = jnp.broadcast_to(total, (tile, 128))
        return carry

    lax.fori_loop(0, width // tile, head_rows, 0, unroll=True)
    for part, (sent, kept) in enumerate(((sent_a, kept_a), (sent_b, kept_b))):
        outs += send_part(part, sent, kept)
    outs += send_part(2, sent_c, kept_c)
    wide = jnp.transpose(total_ref[...])
    small_ref[experts : experts + 1, :] = wide[:1, :] / gain_one_ref[...]
    small = small_ref[...]
    packed_ref[...] = jnp.concatenate([small[:, :own], small[:, own:]], axis=0).astype(jnp.bfloat16)
    outs += start_copies([(packed_ref, sent_a.at[span:], out_sems.at[steps + 3])])
    for copy in outs:
        copy.wait()


def back_pass(
    bits, where, slot_col, back_own, back_other, residual, out_grad, w_out, query_rows, key_rows,
    value_rows, mixed, long_probs, short_probs, normed, w_query, w_key, w_value, gain_one, gain_two,
    router_part,
):
    tok_count, width = normed.shape
    own = mixed.shape[1]
    slots, half = back_own.shape
    heads = long_probs.shape[0]
    count = router_part.shape[0] + 2 + heads
    span = 4 * width // 6
    tile = 256
    steps = tok_count // tile
    half_rows = hbm_out((span, own), jnp.bfloat16)
    pinned = (residual, out_grad, w_out, query_rows, key_rows, value_rows, mixed, long_probs, short_probs, normed,
              w_query, w_key, w_value)
    hbm = pl.BlockSpec(memory_space=pltpu.HBM)
    smem = pl.BlockSpec(memory_space=pltpu.SMEM)

    def scratch(array):
        return pltpu.VMEM(array.shape, array.dtype)

    flops = 2 * tok_count * width * (slots + 5 * own) + 10 * heads * (512 * 512 + 512 * 128) * 64
    out = pl.pallas_call(
        back_kernel,
        out_shape=[
            hbm_out((tok_count, width), jnp.float32),
            hbm_out((tok_count, 3 * own), jnp.bfloat16),
            hbm_out((span + 2 * count, own), jnp.bfloat16),
        ]
        + [half_rows] * 5,
        in_specs=[smem, smem] + [hbm, hbm, pl.BlockSpec(memory_space=pl.ANY)] + [hbm] * 13 + vmem(3),
        out_specs=[hbm] * 8,
        scratch_shapes=[scratch(slot_col), pltpu.VMEM((slots, width), jnp.bfloat16)]
        + [scratch(array) for array in pinned]
        + [
            pltpu.VMEM((tok_count, width), jnp.bfloat16),
            pltpu.VMEM((tok_count, own), jnp.bfloat16),
            pltpu.VMEM((tok_count, 3 * own), jnp.bfloat16),
            pltpu.VMEM((LONG_LEN, LONG_LEN), jnp.bfloat16),
            pltpu.VMEM((heads, 128, 384), jnp.float32),
            pltpu.VMEM((heads, 2, 128), jnp.float32),
            pltpu.VMEM((4 * width, own), jnp.bfloat16),
            pltpu.VMEM((count, width), jnp.float32),
            pltpu.VMEM((2 * count, own), jnp.bfloat16),
            pltpu.VMEM((width, 128), jnp.float32),
            pltpu.SemaphoreType.DMA((2 * steps + 4 + 5 + heads // 2 + 4,)),
            pltpu.SemaphoreType.DMA((steps + 10,)),
        ],
        compiler_params=params(30),
        cost_estimate=pl.CostEstimate(flops=flops, bytes_accessed=25000000, transcendentals=0),
        name="back",
    )(
        bits,
        where,
        in_hbm(slot_col),
        in_hbm(back_own),
        back_other,
        *(in_hbm(array) for array in pinned),
        gain_one.astype(jnp.float32)[None],
        gain_two.astype(jnp.float32)[None],
        router_part,
    )
    return out[0], out[1], out[2:5], out[5:]


def added(left, right):
    return (left.astype(jnp.float32) + right.astype(jnp.float32)).astype(jnp.bfloat16)


def fold_kernel(bits_ref, *refs):
    kept, got, sent, keep = refs[0:3], refs[3:6], refs[7:10], refs[10:13]
    before = refs[6]
    for part in range(3):
        span = kept[part].shape[0] // 2
        mine = bits_ref[part]
        for ref, start in ((sent[part], (1 - mine) * span), (keep[part], mine * span)):
            rows = pl.ds(pl.multiple_of(start, span), span)
            ref[:span, :] = added(kept[part][rows, :], got[part][rows, :])
    rows = kept[0].shape[0]
    sent[0][rows // 2 :, :] = added(before[rows:, :], got[0][rows:, :])


def fold(bits, kept, got, before):
    rows, lanes = kept[0].shape
    extra = before.shape[0] - rows
    half = jax.ShapeDtypeStruct((rows // 2, lanes), jnp.bfloat16)
    out = pl.pallas_call(
        fold_kernel,
        out_shape=[jax.ShapeDtypeStruct((rows // 2 + extra, lanes), jnp.bfloat16)] + [half] * 5,
        in_specs=[pl.BlockSpec(memory_space=pltpu.SMEM)] + vmem(7),
        out_specs=vmem(6),
        compiler_params=params(16),
        name="fold",
    )(bits, *kept, *got, before)
    return out[:3], out[3:]


def pack_kernel(*refs):
    kept, got, before, out = refs[0:3], refs[3:6], refs[6], refs[7]
    rows = kept[0].shape[0]
    for part in range(3):
        out[part * rows : (part + 1) * rows, :] = added(kept[part][...], got[part][:rows, :])
    out[3 * rows :, :] = added(before[rows:, :], got[0][rows:, :])


def pack(kept, got, before):
    rows, lanes = kept[0].shape
    return pl.pallas_call(
        pack_kernel,
        out_shape=jax.ShapeDtypeStruct((2 * rows + before.shape[0], lanes), jnp.bfloat16),
        in_specs=vmem(7),
        out_specs=vmem(1)[0],
        compiler_params=params(16),
        name="pack",
    )(*kept, *got, before)


def unpack_kernel(own_ref, got_ref, *out):
    rows = out[0].shape[0]
    for part in range(3):
        piece = slice(part * rows, (part + 1) * rows)
        out[part][...] = added(own_ref[piece, :], got_ref[piece, :])
    out[3][...] = own_ref[3 * rows :, :].astype(jnp.float32) + got_ref[3 * rows :, :].astype(jnp.float32)


def unpack(own, got, rows):
    lanes = own.shape[1]
    out = pl.pallas_call(
        unpack_kernel,
        out_shape=[jax.ShapeDtypeStruct((rows, lanes), jnp.bfloat16)] * 3
        + [jax.ShapeDtypeStruct((own.shape[0] - 3 * rows, lanes), jnp.float32)],
        in_specs=vmem(2),
        out_specs=vmem(4),
        compiler_params=params(16),
        name="unpack",
    )(own, got)
    return out[:3], out[3]


def join_kernel(bits_ref, *refs):
    own, got, out = refs[0:3], refs[3:6], refs[6:9]
    for part in range(3):
        span = own[part].shape[0]
        mine = bits_ref[part]
        out[part][pl.ds(pl.multiple_of(mine * span, span), span), :] = own[part][...]
        out[part][pl.ds(pl.multiple_of((1 - mine) * span, span), span), :] = got[part][...]


def join(bits, own, got):
    return pl.pallas_call(
        join_kernel,
        out_shape=[jax.ShapeDtypeStruct((p.shape[0] * 2, p.shape[1]), p.dtype) for p in own],
        in_specs=[pl.BlockSpec(memory_space=pltpu.SMEM)] + vmem(6),
        out_specs=vmem(3),
        compiler_params=params(16),
        name="join",
    )(bits, *own, *got)


def finish_kernel(bits_ref, *refs):
    own, got = refs[0:3], refs[3:6]
    results = refs[6:10]
    held, sems = refs[10:14], refs[14]
    span = own[0].shape[0]
    rows = 2 * span
    width, lanes = held[0].shape
    copies = []
    for part in range(3):
        mine = bits_ref[part]
        first = jnp.where(mine == 0, own[part][...], got[part][...])
        second = jnp.where(mine == 0, got[part][...], own[part][...])
        for base, piece in ((part * rows, first), (part * rows + span, second)):
            for index in range(3 + width // lanes):
                start = index * width if index < 3 else 3 * width + (index - 3) * lanes
                size = width if index < 3 else lanes
                low = max(start, base)
                high = min(start + size, base + span)
                if low < high:
                    values = piece[low - base : high - base, :].astype(jnp.float32)
                    if index < 3:
                        held[index][low - start : high - start, :] = values
                    else:
                        place = (index - 3) * lanes
                        held[3][low - start : high - start, place : place + lanes] = values
        for index in range(4):
            last = (index + 1) * width - 1
            if part * rows <= last < (part + 1) * rows:
                copies += start_copies([(held[index], results[index], sems.at[index])])
    for copy in copies:
        copy.wait()


def finish(bits, own, got, width):
    lanes = own[0].shape[1]
    shapes = [(width, lanes)] * 3 + [(lanes, width)]
    return pl.pallas_call(
        finish_kernel,
        out_shape=[hbm_out(shape, jnp.float32) for shape in shapes],
        in_specs=[pl.BlockSpec(memory_space=pltpu.SMEM)] + vmem(6),
        out_specs=[pl.BlockSpec(memory_space=pltpu.HBM)] * 4,
        scratch_shapes=[pltpu.VMEM(shape, jnp.float32) for shape in shapes]
        + [pltpu.SemaphoreType.DMA((4,))],
        compiler_params=params(24),
        name="finish",
    )(bits, *own, *got)


def swap_heads(rows):
    return lax.ppermute(rows, "heads", [(0, 1), (1, 0)])


def trade(rows, bit):
    count = lax.axis_size("seq")
    return lax.ppermute(rows, "seq", [(i, i ^ (1 << bit)) for i in range(count)])


def together(*groups):
    return lax.optimization_barrier(groups)


def contract_rows(left, right):
    return lax.dot_general(
        left, right, (((0,), (0,)), ((), ())), preferred_element_type=jnp.float32
    )


def on_device(
    tokens,
    gain_attn,
    w_query,
    w_key,
    w_value,
    w_out,
    bias_table,
    gain_ffn,
    w_router,
    w_inner,
    w_outer,
    routes,
    seq_lengths,
    out_grad,
):
    tok_count, width = tokens.shape
    bucket_count = bias_table.shape[0]
    experts = w_router.shape[1]
    capacity = max(2, 5 * tok_count // (4 * experts))
    senders = lax.axis_size("seq")
    bits = list(range(senders.bit_length() - 1))
    slots = experts * capacity
    half = width // 2
    own = w_query.shape[1]
    where = jnp.stack([lax.axis_index("heads"), lax.axis_index("seq")]).astype(jnp.int32)

    def exchange(rows):
        return lax.all_to_all(
            rows.reshape(senders, capacity, half), "seq", split_axis=0, concat_axis=0, tiled=True
        ).reshape(slots, half)

    def summed(keep, send):
        return (keep + swap_heads(send).astype(jnp.float32)).astype(jnp.bfloat16)

    slot_row, slot_col, grad_sent = route(where, routes, out_grad, experts, capacity)
    grad_sent, tokens = together(grad_sent, tokens)
    grad_own = exchange(grad_sent)
    attn_part, normed, query_rows, key_rows, value_rows, mixed, long_probs, short_probs = attend(
        seq_lengths, tokens, gain_attn, w_query, w_key, w_value, w_out, bias_table
    )
    residual, second_sent = second_rows(
        where, tokens, attn_part, swap_heads(attn_part), gain_ffn, slot_row, slots
    )
    second_sent, grad_own = together(second_sent, grad_own)
    arrived_own = exchange(second_sent)

    inner = w_inner[0]
    outer = w_outer[0]
    grad_other = swap_heads(grad_own)
    hidden_grad = hidden_grad_of(where, grad_own, grad_other, outer)
    arrived_own, hidden_grad = together(arrived_own, hidden_grad)
    arrived_other = swap_heads(arrived_own)
    hidden, pre_grad, keep, send, logit_grad = expert(
        where, arrived_own, arrived_other, hidden_grad, inner, w_router
    )
    back_sum, hidden = together(summed(keep, send), hidden)
    back_own = exchange(back_sum)
    out_keep, out_send, router_part = expert_out_of(
        where, hidden, arrived_own, arrived_other, logit_grad, outer
    )
    out_sum = summed(out_keep, out_send)
    back_own, out_sum = together(back_own, out_sum)
    back_other = swap_heads(back_own)
    returned = exchange(out_sum)

    depth = len(bits) - 1
    turns = [bits[k * depth // 3 : depth] + bits[: k * depth // 3] for k in range(3)]
    place = lax.axis_index("seq")
    mine = [jnp.stack([(place >> turn[k]) & 1 for turn in turns]).astype(jnp.int32) for k in range(depth)]
    residual_grad, head_grads, sent, kept = back_pass(
        mine[0], where, slot_col, back_own, back_other, residual, out_grad, w_out, query_rows, key_rows,
        value_rows, mixed, long_probs, short_probs, normed, w_query, w_key, w_value, gain_attn, gain_ffn,
        router_part,
    )

    def trades(arrays, k):
        return [trade(array, turn[k]) for array, turn in zip(arrays, turns)]

    for k in range(depth):
        got = trades(sent, k)
        if k == 0:
            output = output_of(where, slot_col, returned, residual, gain_ffn, w_router, capacity)
            got, output, head_grads = together(got, output, head_grads)
        if k == 1:
            normed_part = normed_back(head_grads, w_query, w_key, w_value)
            got, normed_part = together(got, normed_part)
        if k + 1 < depth:
            sent, kept = fold(mine[k + 1], kept, got, sent[0])
    normed_other = swap_heads(normed_part)
    packed = pack(kept, got, sent[0])
    packed, normed_other, pre_grad = together(packed, normed_other, pre_grad)
    got = trade(packed, bits[-1])
    inner_grad, outer_grad = expert_grads(
        where, arrived_own, arrived_other, grad_own, grad_other, hidden, pre_grad, w_router
    )
    got, inner_grad = together(got, inner_grad)
    summed_parts, small = unpack(packed, got, kept[0].shape[0])
    small = jnp.concatenate([small[: small.shape[0] // 2], small[small.shape[0] // 2 :]], axis=1)
    small_other = swap_heads(small)
    for k in reversed(range(1, depth)):
        got = trades(summed_parts, k)
        if k == 1:
            both = small[: experts + 1] + small_other[: experts + 1]
            router_grad = both[:experts].T
            table_grad = table_from(small[experts + 2 :], bucket_count)
            got, both, router_grad, table_grad = together(got, both, router_grad, table_grad)
        summed_parts = join(mine[k], summed_parts, got)
    got = trades(summed_parts, 0)
    input_grad = input_back(tokens, normed_part, normed_other, gain_attn, residual_grad)
    got, input_grad = together(got, input_grad)
    query_w_grad, key_w_grad, value_w_grad, out_w_grad = finish(mine[0], summed_parts, got, width)
    return (
        output,
        input_grad,
        both[experts],
        query_w_grad,
        key_w_grad,
        value_w_grad,
        out_w_grad,
        table_grad,
        small[experts + 1],
        router_grad,
        inner_grad[None],
        outer_grad[None],
    )


def solution(mesh):
    in_specs = (
        P("seq", None),
        P(),
        P(None, "heads"),
        P(None, "heads"),
        P(None, "heads"),
        P("heads", None),
        P(None, "heads"),
        P(),
        P(),
        P("seq", None, "heads"),
        P("seq", "heads", None),
        P("seq", None),
        P("seq"),
        P("seq", None),
    )
    out_specs = (
        P("seq", "heads"),
        P("seq", None),
        P(),
        P(None, "heads"),
        P(None, "heads"),
        P(None, "heads"),
        P("heads", None),
        P(None, "heads"),
        P(),
        P(),
        P("seq", None, "heads"),
        P("seq", "heads", None),
    )
    return jax.shard_map(
        on_device, mesh=mesh, in_specs=in_specs, out_specs=out_specs, check_vma=False
    )
```

```python
from functools import partial

import jax
import jax.numpy as jnp
from jax import lax
from jax.experimental import pallas as pl
from jax.experimental.pallas import tpu as pltpu
from jax.sharding import PartitionSpec as P

SHORT_LEN = 128
LONG_LEN = 512
SHORT_DEV = 4
LONG_DEV = 1


epsilon = 1e-06
highest = lax.Precision.HIGHEST
far_limits = (12, 16, 23, 32, 46, 64, 91)


def vmem(count):
    return [pl.BlockSpec(memory_space=pltpu.VMEM)] * count


def params(mib=16):
    return pltpu.CompilerParams(vmem_limit_bytes=mib * 1024 * 1024)


def dot_nn(left, right):
    return jnp.dot(left, right, preferred_element_type=jnp.float32)


def dot_nt(left, right):
    return lax.dot_general(
        left, right, (((1,), (1,)), ((), ())), preferred_element_type=jnp.float32
    )


def inverse_rms(values):
    return lax.rsqrt(jnp.mean(values * values, axis=-1, keepdims=True) + epsilon)


def diagonal_buckets(offset):
    distance = jnp.abs(offset)
    far_bucket = jnp.full(offset.shape, 8, jnp.int32)
    for limit in far_limits:
        far_bucket = far_bucket + (distance >= limit).astype(jnp.int32)
    return jnp.where(distance < 8, distance, far_bucket) + jnp.where(offset > 0, 16, 0)


def hbm_out(shape, dtype):
    return pltpu.HBM(shape, dtype)


def in_hbm(array):
    return pltpu.with_memory_space_constraint(array, pltpu.HBM)


def start_copies(pairs):
    copies = [pltpu.make_async_copy(*triple) for triple in pairs]
    for copy in copies:
        copy.start()
    return copies


def attend_kernel(
    block_rows,
    lengths_ref,
    tokens_hbm,
    gain_ref,
    wq_hbm,
    wk_hbm,
    wv_hbm,
    wo_hbm,
    table_ref,
    part_hbm,
    normed_hbm,
    q_hbm,
    k_hbm,
    v_hbm,
    mixed_hbm,
    long_hbm,
    short_hbm,
    tokens_ref,
    joint_ref,
    wo_ref,
    part_ref,
    normed_ref,
    q_ref,
    k_ref,
    v_ref,
    mixed_ref,
    long_ref,
    short_ref,
    diag_ref,
    in_sems,
    out_sems,
):
    tok_count, width = tokens_ref.shape
    own = q_ref.shape[1]
    pairs = own // 128
    short_tok = SHORT_DEV * SHORT_LEN
    tile = 512
    steps = tok_count // tile
    tiles_in = []
    for step in range(steps):
        rows = slice(step * tile, step * tile + tile)
        tiles_in.append((tokens_hbm.at[rows], tokens_ref.at[rows], in_sems.at[step]))
    weights = [
        (source, joint_ref.at[:, index * own : index * own + own])
        for index, source in enumerate((wq_hbm, wk_hbm, wv_hbm))
    ]
    weights.append((wo_hbm, wo_ref))
    copies = start_copies(
        tiles_in + [(src, dst, in_sems.at[steps + index]) for index, (src, dst) in enumerate(weights)]
    )
    weight_copies = copies[steps:]
    outs = []

    offset = lax.broadcasted_iota(jnp.int32, (table_ref.shape[1], 512), 1) - 256
    hot = jnp.where(
        diagonal_buckets(offset)
        == lax.broadcasted_iota(jnp.int32, (table_ref.shape[1], 512), 0),
        1.0,
        0.0,
    )
    diag_ref[...] = dot_nn(table_ref[...], hot.astype(jnp.bfloat16))
    gain = gain_ref[...]

    def normalize(step, carry):
        rows = pl.ds(pl.multiple_of(step * tile, tile), tile)
        pltpu.make_async_copy(tokens_hbm.at[rows], tokens_ref.at[rows], in_sems.at[step]).wait()
        values = tokens_ref[rows, :].astype(jnp.float32)
        normed_ref[rows, :] = (values * inverse_rms(values) * gain).astype(jnp.bfloat16)
        return carry

    lax.fori_loop(0, steps, normalize, 0)
    outs += start_copies([(normed_ref, normed_hbm, out_sems.at[0])])
    for copy in weight_copies[:3]:
        copy.wait()

    def project(step, carry):
        rows = pl.ds(pl.multiple_of(step * tile, tile), tile)
        joint = dot_nn(normed_ref[rows, :], joint_ref[...]).astype(jnp.bfloat16)
        q_ref[rows, :] = joint[:, :own] * jnp.bfloat16(0.125)
        k_ref[rows, :] = joint[:, own : 2 * own]
        v_ref[rows, :] = joint[:, 2 * own :]
        return carry

    lax.fori_loop(0, steps, project, 0)
    outs += start_copies(
        [
            (q_ref, q_hbm, out_sems.at[1]),
            (k_ref, k_hbm, out_sems.at[2]),
            (v_ref, v_hbm, out_sems.at[3]),
        ]
    )
    lane = lax.broadcasted_iota(jnp.int32, (1, 128), 1)
    key_place = lax.broadcasted_iota(jnp.int32, (1, LONG_LEN), 1)
    live_long = key_place < lengths_ref[SHORT_DEV]

    def softmax(scores):
        weights = jnp.exp(scores - jnp.max(scores, axis=1, keepdims=True))
        return (weights * (1.0 / jnp.sum(weights, axis=1, keepdims=True))).astype(jnp.bfloat16)

    def one_pair(pair):
        lanes = slice(pair * 128, pair * 128 + 128)
        tiles = []
        for sub in range(2):
            row = diag_ref[pair * 2 + sub : pair * 2 + sub + 1, :]
            spread = pltpu.roll(
                jnp.broadcast_to(row, (128, 512)), 256, 1, stride=1, stride_axis=0
            )
            tiles.append(
                (
                    spread[:, 0:128],
                    spread[:, 128:256],
                    spread[:, 384:512],
                    jnp.broadcast_to(row[:, 511:512], (128, 128)),
                    jnp.broadcast_to(row[:, 0:1], (128, 128)),
                )
            )
        out = []
        for sub in range(2):
            scores = []
            for block in range(SHORT_DEV):
                rows = slice(block * 128, block * 128 + 128)
                masked = jnp.where((lane >= 64) == (sub == 1), q_ref[rows, lanes], 0)
                live = key_place[:, :128] < lengths_ref[block]
                scores.append(
                    jnp.where(
                        live, dot_nt(masked, k_ref[rows, lanes]) + tiles[sub][0], -1000000000.0
                    )
                )
            probs = softmax(jnp.concatenate(scores, axis=0))
            short_ref[pair * 2 + sub] = probs
            mixed = []
            for block in range(SHORT_DEV):
                rows = slice(block * 128, block * 128 + 128)
                mixed.append(dot_nn(probs[rows], v_ref[rows, lanes]))
            out.append(jnp.concatenate(mixed, axis=0))
        mixed_ref[:short_tok, lanes] = jnp.where(lane < 64, out[0], out[1]).astype(jnp.bfloat16)
        keys = k_ref[short_tok:, lanes]
        values = v_ref[short_tok:, lanes]
        for start in range(0, LONG_LEN, block_rows):
            places = slice(start, start + block_rows)
            rows = slice(short_tok + start, short_tok + start + block_rows)
            queries = q_ref[rows, lanes]
            out = []
            for sub in range(2):
                masked = jnp.where((lane >= 64) == (sub == 1), queries, 0)
                same, above, below, far_above, far_below = tiles[sub]
                bias = jnp.concatenate(
                    [
                        jnp.concatenate(
                            [
                                same
                                if other == block
                                else above
                                if other == block + 1
                                else below
                                if other == block - 1
                                else far_above
                                if other > block
                                else far_below
                                for other in range(LONG_LEN // 128)
                            ],
                            axis=1,
                        )
                        for block in range(start // 128, (start + block_rows) // 128)
                    ],
                    axis=0,
                )
                scores = jnp.where(live_long, dot_nt(masked, keys) + bias, -1000000000.0)
                probs = softmax(scores)
                long_ref[pair * 2 + sub, places, :] = probs
                out.append(dot_nn(probs, values))
            mixed_ref[rows, lanes] = jnp.where(lane < 64, out[0], out[1]).astype(jnp.bfloat16)

    for pair in range(pairs):
        one_pair(pair)
        both = slice(pair * 2, pair * 2 + 2)
        outs += start_copies(
            [
                (long_ref.at[both], long_hbm.at[both], out_sems.at[4 + 2 * pair]),
                (short_ref.at[both], short_hbm.at[both], out_sems.at[5 + 2 * pair]),
            ]
        )
    weight_copies[3].wait()
    base = 4 + 2 * pairs
    outs += start_copies([(mixed_ref, mixed_hbm, out_sems.at[base])])

    def part_copy(step):
        rows = pl.ds(pl.multiple_of(step * tile, tile), tile)
        return pltpu.make_async_copy(part_ref.at[rows], part_hbm.at[rows], out_sems.at[base + 1 + step])

    def project_out(step, carry):
        rows = pl.ds(pl.multiple_of(step * tile, tile), tile)
        part_ref[rows, :] = dot_nn(mixed_ref[rows, :], wo_ref[...]).astype(part_ref.dtype)
        part_copy(step).start()
        return carry

    lax.fori_loop(0, steps, project_out, 0)
    outs += [part_copy(step) for step in range(steps)]
    for copy in outs:
        copy.wait()


def attend(lengths, tokens, gain, w_query, w_key, w_value, w_out, table, block_rows=512):
    tok_count, width = tokens.shape
    own = w_query.shape[1]
    heads = own // 64
    heads_pad = -(-heads // 8) * 8
    table = jnp.pad(table.T, ((0, heads_pad - heads), (0, 0)))
    short_tok = SHORT_DEV * SHORT_LEN
    flops = 2 * tok_count * width * own * 4 + 4 * heads * (512 * 512 + short_tok * 128) * 64
    hbm = pl.BlockSpec(memory_space=pltpu.HBM)
    out_shapes = [
        ((tok_count, width), jnp.bfloat16),
        ((tok_count, width), jnp.bfloat16),
        ((tok_count, own), jnp.bfloat16),
        ((tok_count, own), jnp.bfloat16),
        ((tok_count, own), jnp.bfloat16),
        ((tok_count, own), jnp.bfloat16),
        ((heads, LONG_LEN, LONG_LEN), jnp.bfloat16),
        ((heads, short_tok, SHORT_LEN), jnp.bfloat16),
    ]
    steps = tok_count // 512
    return pl.pallas_call(
        partial(attend_kernel, block_rows),
        out_shape=[jax.ShapeDtypeStruct(*out_shapes[0])]
        + [hbm_out(shape, dtype) for shape, dtype in out_shapes[1:]],
        in_specs=[pl.BlockSpec(memory_space=pltpu.SMEM), hbm]
        + vmem(1)
        + [hbm] * 4
        + vmem(1),
        out_specs=[hbm] * 8,
        scratch_shapes=[pltpu.VMEM(tokens.shape, jnp.bfloat16)]
        + [pltpu.VMEM((width, 3 * own), jnp.bfloat16), pltpu.VMEM(w_out.shape, jnp.bfloat16)]
        + [pltpu.VMEM(shape, dtype) for shape, dtype in out_shapes]
        + [
            pltpu.VMEM((heads_pad, 512), jnp.float32),
            pltpu.SemaphoreType.DMA((steps + 4,)),
            pltpu.SemaphoreType.DMA((5 + 2 * (heads // 2) + steps,)),
        ],
        compiler_params=params(24),
        cost_estimate=pl.CostEstimate(
            flops=flops, bytes_accessed=16000000, transcendentals=heads * 512 * 640
        ),
        name="attend",
    )(
        lengths,
        in_hbm(tokens),
        gain.astype(jnp.float32)[None],
        in_hbm(w_query),
        in_hbm(w_key),
        in_hbm(w_value),
        in_hbm(w_out),
        table,
    )


def attend_back_pair(
    pair, hg_ref, q_ref, k_ref, v_ref, mixed_ref, long_ref, short_ref, grads_ref, tiles_ref, far_ref, sg_ref,
):
    short_tok = SHORT_DEV * SHORT_LEN
    lane = lax.broadcasted_iota(jnp.int32, (1, 128), 1)
    lanes = pl.ds(pl.multiple_of(pair * 128, 128), 128)
    blocks = LONG_LEN // 128
    heads_grad = hg_ref[:, lanes]
    products = heads_grad.astype(jnp.float32) * mixed_ref[:, lanes].astype(jnp.float32)
    q_t = jnp.transpose(q_ref[:, lanes])
    hg_t = jnp.transpose(heads_grad)
    qg = []
    kg_t = []
    vg_t = []
    for sub in range(2):
        head = pair * 2 + sub
        own = (lane >= 64) == (sub == 1)
        rows_t = slice(64 * sub, 64 * sub + 64)
        masked = jnp.where(own, heads_grad, 0)
        delta = jnp.sum(jnp.where(own, products, 0.0), axis=1, keepdims=True)
        grads = [
            dot_nt(masked[block * 128 : block * 128 + 128], v_ref[block * 128 : block * 128 + 128, lanes])
            for block in range(SHORT_DEV)
        ]
        probs = short_ref[head]
        part = probs.astype(jnp.float32) * (jnp.concatenate(grads, axis=0) - delta[:short_tok])
        same = part[:128]
        for block in range(1, SHORT_DEV):
            same = same + part[block * 128 : block * 128 + 128]
        part = part.astype(jnp.bfloat16)
        qg_parts = []
        kg_parts = []
        vg_parts = []
        for block in range(SHORT_DEV):
            rows = slice(block * 128, block * 128 + 128)
            qg_parts.append(dot_nn(part[rows], k_ref[rows, lanes]))
            kg_parts.append(dot_nn(q_t[rows_t, rows], part[rows]))
            vg_parts.append(dot_nn(hg_t[rows_t, rows], probs[rows]))
        above = jnp.zeros((128, 128), jnp.float32)
        below = above
        far_above = above
        far_below = above
        probs = long_ref[head]
        part = probs.astype(jnp.float32) * (
            dot_nt(masked[short_tok:], v_ref[short_tok:, lanes]) - delta[short_tok:]
        )
        for block in range(blocks):
            for other in range(blocks):
                piece = part[block * 128 : block * 128 + 128, other * 128 : other * 128 + 128]
                if other == block:
                    same = same + piece
                elif other == block + 1:
                    above = above + piece
                elif other == block - 1:
                    below = below + piece
                elif other > block:
                    far_above = far_above + piece
                else:
                    far_below = far_below + piece
        sg_ref[...] = part.astype(jnp.bfloat16)
        qg_parts.append(dot_nn(sg_ref[...], k_ref[short_tok:, lanes]))
        kg_parts.append(dot_nn(q_t[rows_t, short_tok:], sg_ref[...]))
        vg_parts.append(dot_nn(hg_t[rows_t, short_tok:], probs))
        qg.append(jnp.concatenate(qg_parts, axis=0))
        kg_t.append(jnp.concatenate(kg_parts, axis=1))
        vg_t.append(jnp.concatenate(vg_parts, axis=1))
        tiles_ref[head, :, 0:128] = same
        tiles_ref[head, :, 128:256] = above
        tiles_ref[head, :, 256:384] = below
        far_ref[head, 0:1, :] = jnp.sum(far_above, axis=0, keepdims=True)
        far_ref[head, 1:2, :] = jnp.sum(far_below, axis=0, keepdims=True)
    width = q_ref.shape[1]
    grads_ref[:, lanes] = (jnp.where(lane < 64, qg[0], qg[1]) * 0.125).astype(jnp.bfloat16)
    for index, whole in ((1, kg_t), (2, vg_t)):
        place = pl.ds(pl.multiple_of(index * width + pair * 128, 128), 128)
        grads_ref[:, place] = jnp.transpose(jnp.concatenate(whole, axis=0).astype(jnp.bfloat16))


def diagonals(tiles):
    tile = jnp.concatenate(
        [tiles[:, 0:256], jnp.zeros((128, 128), jnp.float32), tiles[:, 256:384]], axis=1
    )
    span = 64
    while span:
        tile = tile[:span] + pltpu.roll(tile[span:], 512 - span, 1)
        span //= 2
    return tile


def table_from(diag, bucket_count):
    lane = jnp.arange(768, dtype=jnp.int32)
    offset = jnp.where(lane < 256, lane, lane - 512)
    offset = jnp.where(lane >= 640, -256, jnp.where(lane >= 512, 256, offset))
    hot = (diagonal_buckets(offset)[:, None] == jnp.arange(bucket_count)[None, :]).astype(jnp.float32)
    return lax.dot_general(
        hot, diag, (((0,), (1,)), ((), ())), precision=highest, preferred_element_type=jnp.float32
    )


def dispatch_rows(send_ref, slot_row, half_rows):
    slots = send_ref.shape[0]
    tok_count = slot_row.shape[1]
    span = 640
    for base in range(0, slots, span):
        place = lax.broadcasted_iota(jnp.int32, (span, tok_count), 0) + base
        hot = jnp.where(place == slot_row, 1.0, 0.0).astype(jnp.bfloat16)
        send_ref[base : base + span, :] = dot_nn(hot, half_rows).astype(jnp.bfloat16)


def half_lanes(core, half):
    return pl.ds(pl.multiple_of(core * half, half), half)


def route_kernel(
    capacity, where_ref, routes_hbm, grad_hbm, row_hbm, col_hbm, send_ref, routes_ref, grad_ref, row_ref,
    col_ref, in_sems, out_sems,
):
    tok_count = routes_ref.shape[1]
    slots, half = send_ref.shape
    experts = slots // capacity
    fetch, copy = start_copies(
        [
            (routes_hbm, routes_ref, in_sems.at[0]),
            (grad_hbm.at[:, half_lanes(where_ref[0], half)], grad_ref, in_sems.at[1]),
        ]
    )
    fetch.wait()
    routes = routes_ref[...]
    expert = lax.broadcasted_iota(jnp.int32, (experts, tok_count), 0)
    lane = lax.broadcasted_iota(jnp.int32, (1, tok_count), 1)
    hot = jnp.where(expert == routes, 1.0, 0.0)
    total = hot
    step = 1
    while step < tok_count:
        total = total + jnp.where(lane >= step, pltpu.roll(total, step, 1), 0.0)
        step *= 2
    before = jnp.sum(hot * total, axis=0, keepdims=True).astype(jnp.int32) - 1
    slot = jnp.where(before < capacity, routes * capacity + before, slots)
    row_ref[...] = slot
    wide = jnp.broadcast_to(slot.astype(jnp.float32), (128, tok_count))
    col_ref[...] = jnp.transpose(wide).astype(jnp.int32)
    outs = start_copies([(row_ref, row_hbm, out_sems.at[0]), (col_ref, col_hbm, out_sems.at[1])])
    copy.wait()
    dispatch_rows(send_ref, slot, grad_ref[...])
    for copy in outs:
        copy.wait()


def route(where, routes, out_grad, experts, capacity):
    tok_count, width = out_grad.shape
    slots = experts * capacity
    return pl.pallas_call(
        partial(route_kernel, capacity),
        out_shape=[
            hbm_out((1, tok_count), jnp.int32),
            hbm_out((tok_count, 128), jnp.int32),
            jax.ShapeDtypeStruct((slots, width // 2), jnp.bfloat16),
        ],
        in_specs=[
            pl.BlockSpec(memory_space=pltpu.SMEM),
            pl.BlockSpec(memory_space=pltpu.HBM),
            pl.BlockSpec(memory_space=pltpu.HBM),
        ],
        out_specs=[pl.BlockSpec(memory_space=pltpu.HBM)] * 2 + vmem(1),
        scratch_shapes=[
            pltpu.VMEM((1, tok_count), jnp.int32),
            pltpu.VMEM((tok_count, width // 2), jnp.bfloat16),
            pltpu.VMEM((1, tok_count), jnp.int32),
            pltpu.VMEM((tok_count, 128), jnp.int32),
            pltpu.SemaphoreType.DMA((2,)),
            pltpu.SemaphoreType.DMA((2,)),
        ],
        compiler_params=params(),
        cost_estimate=pl.CostEstimate(
            flops=slots * tok_count * width, bytes_accessed=4000000, transcendentals=0
        ),
        name="route",
    )(where, in_hbm(routes.reshape(1, tok_count)), in_hbm(out_grad))


def second_kernel(
    where_ref, tokens_hbm, own_ref, other_ref, gain_ref, row_hbm, residual_hbm, send_ref, tokens_ref,
    row_ref, residual_ref, second_ref, in_sems, out_sems,
):
    tile = 256
    tok_count = tokens_ref.shape[0]
    half = send_ref.shape[1]
    tiles_rows = [slice(start, start + tile) for start in range(0, tok_count, tile)]
    copies = start_copies(
        [
            (tokens_hbm.at[rows], tokens_ref.at[rows], in_sems.at[step])
            for step, rows in enumerate(tiles_rows)
        ]
        + [(row_hbm, row_ref, in_sems.at[len(tiles_rows)])]
    )
    outs = []
    gain = gain_ref[...]
    for step, rows in enumerate(tiles_rows):
        attn = own_ref[rows, :].astype(jnp.float32) + other_ref[rows, :].astype(jnp.float32)
        copies[step].wait()
        residual = tokens_ref[rows, :].astype(jnp.float32) + attn
        residual_ref[rows, :] = residual
        outs += start_copies([(residual_ref.at[rows], residual_hbm.at[rows], out_sems.at[step])])
        second_ref[rows, :] = (residual * inverse_rms(residual) * gain).astype(jnp.bfloat16)
    copies[-1].wait()
    dispatch_rows(send_ref, row_ref[...], second_ref[:, half_lanes(where_ref[0], half)])
    for copy in outs:
        copy.wait()


def second_rows(where, tokens, own, other, gain, slot_row, slots):
    tok_count, width = tokens.shape
    steps = tok_count // 256
    hbm = pl.BlockSpec(memory_space=pltpu.HBM)
    return pl.pallas_call(
        second_kernel,
        out_shape=[
            hbm_out((tok_count, width), jnp.float32),
            jax.ShapeDtypeStruct((slots, width // 2), jnp.bfloat16),
        ],
        in_specs=[pl.BlockSpec(memory_space=pltpu.SMEM), hbm] + vmem(3) + [hbm],
        out_specs=[hbm] + vmem(1),
        scratch_shapes=[
            pltpu.VMEM((tok_count, width), jnp.bfloat16),
            pltpu.VMEM((1, tok_count), jnp.int32),
            pltpu.VMEM((tok_count, width), jnp.float32),
            pltpu.VMEM((tok_count, width), jnp.bfloat16),
            pltpu.SemaphoreType.DMA((steps + 1,)),
            pltpu.SemaphoreType.DMA((steps,)),
        ],
        compiler_params=params(),
        cost_estimate=pl.CostEstimate(
            flops=slots * tok_count * width, bytes_accessed=13000000, transcendentals=0
        ),
        name="second",
    )(where, in_hbm(tokens), own, other, gain.astype(jnp.float32)[None], in_hbm(slot_row))


def hidden_grad_kernel(where_ref, own_ref, other_ref, outer_ref, out_ref, whole_ref):
    half = own_ref.shape[1]
    core = where_ref[0]
    whole_ref[:, half_lanes(core, half)] = own_ref[...]
    whole_ref[:, half_lanes(1 - core, half)] = other_ref[...]
    out_ref[...] = dot_nt(whole_ref[...], outer_ref[...]).astype(jnp.bfloat16)


def hidden_grad_of(where, own, other, outer):
    slots, half = own.shape
    hidden = outer.shape[0]
    tile = 256
    rows = pl.BlockSpec((tile, half), lambda step: (step, 0))
    return pl.pallas_call(
        hidden_grad_kernel,
        grid=(slots // tile,),
        out_shape=hbm_out((slots, hidden), jnp.bfloat16),
        in_specs=[pl.BlockSpec(memory_space=pltpu.SMEM), rows, rows] + vmem(1),
        out_specs=pl.BlockSpec((tile, hidden), lambda step: (step, 0)),
        scratch_shapes=[pltpu.VMEM((tile, 2 * half), jnp.bfloat16)],
        compiler_params=params(),
        cost_estimate=pl.CostEstimate(
            flops=4 * slots * half * hidden, bytes_accessed=12000000, transcendentals=0
        ),
        name="hidden_grad",
    )(where, own, other, outer)


def gate_of(rows, router, index):
    experts = router.shape[1]
    logits = dot_nn(rows, router)
    exp_logit = jnp.exp(logits - jnp.max(logits, axis=1, keepdims=True))
    probs = exp_logit * (1.0 / jnp.sum(exp_logit, axis=1, keepdims=True))
    hit = jnp.where(lax.broadcasted_iota(jnp.int32, (1, experts), 1) == index, 1.0, 0.0)
    return probs, hit, jnp.sum(probs * hit, axis=1, keepdims=True)


def expert_kernel(
    where_ref,
    own_ref,
    other_ref,
    hg_ref,
    inner_ref,
    router_ref,
    hidden_ref,
    pre_grad_ref,
    keep_ref,
    send_ref,
    logit_ref,
    arrived_ref,
    whole_ref,
):
    core = where_ref[0]
    tile, half = own_ref.shape
    own_lanes = half_lanes(core, half)
    other_lanes = half_lanes(1 - core, half)
    arrived_ref[:, own_lanes] = own_ref[...]
    arrived_ref[:, other_lanes] = other_ref[...]
    arrived = arrived_ref[...]
    probs, hit, gate = gate_of(arrived, router_ref[...], where_ref[1])
    curve = 0.7978845608028654
    gate_grad = jnp.zeros((tile, 1), jnp.float32)
    back = jnp.zeros((tile, 2 * half), jnp.float32)
    chunk = 512
    for start in range(0, hg_ref.shape[1], chunk):
        cols = slice(start, start + chunk)
        pre = dot_nn(arrived, inner_ref[:, cols])
        square = pre * pre
        share = 0.5 + 0.5 * jnp.tanh(pre * (curve + (curve * 0.044715) * square))
        hidden_ref[:, cols] = (pre * share).astype(jnp.bfloat16)
        passed = share * hg_ref[:, cols].astype(jnp.float32)
        gate_grad = gate_grad + jnp.sum(pre * passed, axis=1, keepdims=True)
        bend = pre * (2.0 * curve + (6.0 * curve * 0.044715) * square)
        pre_grad = ((gate * passed) * (1.0 + (1.0 - share) * bend)).astype(jnp.bfloat16)
        pre_grad_ref[:, cols] = pre_grad
        back = back + dot_nt(pre_grad, inner_ref[:, cols])
    logit = (probs * (gate_grad * (hit - gate))).astype(jnp.bfloat16)
    logit_ref[...] = logit
    whole_ref[...] = back + dot_nt(logit, router_ref[...])
    send_ref[...] = whole_ref[:, other_lanes].astype(jnp.bfloat16)
    keep_ref[...] = whole_ref[:, own_lanes]


def expert(where, own, other, hidden_grad, inner, router):
    slots, half = own.shape
    width, hidden = inner.shape
    experts = router.shape[1]
    tile = 256
    halves = pl.BlockSpec((tile, half), lambda step: (step, 0))
    units = pl.BlockSpec((tile, hidden), lambda step: (step, 0))
    return pl.pallas_call(
        expert_kernel,
        grid=(slots // tile,),
        out_shape=[
            hbm_out((slots, hidden), jnp.bfloat16),
            hbm_out((slots, hidden), jnp.bfloat16),
            jax.ShapeDtypeStruct((slots, half), jnp.float32),
            jax.ShapeDtypeStruct((slots, half), jnp.bfloat16),
            hbm_out((slots, experts), jnp.bfloat16),
        ],
        in_specs=[
            pl.BlockSpec(memory_space=pltpu.SMEM),
            halves,
            halves,
            units,
            pl.BlockSpec(inner.shape, lambda step: (0, 0), pipeline_mode=pl.Buffered(1)),
        ]
        + vmem(1),
        out_specs=[
            units,
            units,
            halves,
            halves,
            pl.BlockSpec((tile, experts), lambda step: (step, 0)),
        ],
        scratch_shapes=[
            pltpu.VMEM((tile, width), jnp.bfloat16),
            pltpu.VMEM((tile, width), jnp.float32),
        ],
        compiler_params=params(),
        cost_estimate=pl.CostEstimate(
            flops=4 * slots * width * hidden, bytes_accessed=20000000, transcendentals=slots * hidden
        ),
        name="expert",
    )(where, own, other, in_hbm(hidden_grad), in_hbm(inner), router)


def expert_out_kernel(
    where_ref, hidden_ref, own_ref, other_ref, logit_ref, outer_ref, keep_ref, send_ref, router_ref, whole_ref
):
    core = where_ref[0]
    half = keep_ref.shape[1]
    own_lanes = half_lanes(core, half)
    other_lanes = half_lanes(1 - core, half)
    whole_ref[...] = dot_nn(hidden_ref[...], outer_ref[...])
    send_ref[...] = whole_ref[:, other_lanes].astype(jnp.bfloat16)
    keep_ref[...] = whole_ref[:, own_lanes]

    @pl.when(pl.program_id(0) == 0)
    def _():
        router_ref[...] = jnp.zeros_like(router_ref)

    router_ref[:, own_lanes] += contract_rows(logit_ref[...], own_ref[...])
    router_ref[:, other_lanes] += contract_rows(logit_ref[...], other_ref[...])


def expert_out_of(where, hidden, own, other, logit_grad, outer):
    slots, units = hidden.shape
    width = outer.shape[1]
    experts = logit_grad.shape[1]
    half = width // 2
    tile = 256
    halves = pl.BlockSpec((tile, half), lambda step: (step, 0))
    return pl.pallas_call(
        expert_out_kernel,
        grid=(slots // tile,),
        out_shape=[
            jax.ShapeDtypeStruct((slots, half), jnp.float32),
            jax.ShapeDtypeStruct((slots, half), jnp.bfloat16),
            hbm_out((experts, width), jnp.float32),
        ],
        in_specs=[
            pl.BlockSpec(memory_space=pltpu.SMEM),
            pl.BlockSpec((tile, units), lambda step: (step, 0)),
            halves,
            halves,
            pl.BlockSpec((tile, experts), lambda step: (step, 0)),
        ]
        + vmem(1),
        out_specs=[halves, halves, pl.BlockSpec((experts, width), lambda step: (0, 0))],
        scratch_shapes=[pltpu.VMEM((tile, width), jnp.float32)],
        compiler_params=params(),
        cost_estimate=pl.CostEstimate(
            flops=2 * slots * width * units, bytes_accessed=9000000, transcendentals=0
        ),
        name="expert_out",
    )(where, in_hbm(hidden), in_hbm(own), in_hbm(other), in_hbm(logit_grad), outer)


def expert_grads_kernel(
    where_ref,
    own_hbm,
    other_hbm,
    grad_own_hbm,
    grad_other_hbm,
    hidden_ref,
    pre_grad_ref,
    router_ref,
    inner_grad_ref,
    outer_grad_ref,
    arrived_ref,
    gated_ref,
    sems,
):
    core = where_ref[0]
    half = own_hbm.shape[1]
    own_lanes = half_lanes(core, half)
    other_lanes = half_lanes(1 - core, half)

    @pl.when(pl.program_id(0) == 0)
    def _():
        copies = [
            pltpu.make_async_copy(own_hbm, arrived_ref.at[:, own_lanes], sems.at[0]),
            pltpu.make_async_copy(other_hbm, arrived_ref.at[:, other_lanes], sems.at[1]),
            pltpu.make_async_copy(grad_own_hbm, gated_ref.at[:, own_lanes], sems.at[2]),
            pltpu.make_async_copy(grad_other_hbm, gated_ref.at[:, other_lanes], sems.at[3]),
        ]
        for copy in copies:
            copy.start()
        for copy in copies:
            copy.wait()
        gate = gate_of(arrived_ref[...], router_ref[...], where_ref[1])[2]
        gated_ref[...] = (gate * gated_ref[...].astype(jnp.float32)).astype(jnp.bfloat16)

    outer_grad_ref[...] = contract_rows(hidden_ref[...], gated_ref[...])
    inner_grad_ref[...] = contract_rows(arrived_ref[...], pre_grad_ref[...])


def expert_grads(where, own, other, grad_own, grad_other, hidden, pre_grad, router):
    slots, half = own.shape
    units = hidden.shape[1]
    width = router.shape[0]
    tile = 256
    hbm = pl.BlockSpec(memory_space=pltpu.HBM)
    whole = lambda shape: pl.BlockSpec(shape, lambda step: (0, 0))
    cols = pl.BlockSpec((slots, tile), lambda step: (0, step))
    return pl.pallas_call(
        expert_grads_kernel,
        grid=(units // tile,),
        out_shape=[
            hbm_out((width, units), jnp.float32),
            hbm_out((units, width), jnp.float32),
        ],
        in_specs=[
            pl.BlockSpec(memory_space=pltpu.SMEM),
            hbm,
            hbm,
            hbm,
            hbm,
            cols,
            cols,
            whole(router.shape),
        ],
        out_specs=[
            pl.BlockSpec((width, tile), lambda step: (0, step)),
            pl.BlockSpec((tile, width), lambda step: (step, 0)),
        ],
        scratch_shapes=[
            pltpu.VMEM((slots, width), jnp.bfloat16),
            pltpu.VMEM((slots, width), jnp.bfloat16),
            pltpu.SemaphoreType.DMA((4,)),
        ],
        compiler_params=params(24),
        cost_estimate=pl.CostEstimate(
            flops=4 * slots * width * units, bytes_accessed=22000000, transcendentals=0
        ),
        name="expert_grads",
    )(
        where,
        in_hbm(own),
        in_hbm(other),
        in_hbm(grad_own),
        in_hbm(grad_other),
        in_hbm(hidden),
        in_hbm(pre_grad),
        router,
    )


def output_kernel(
    capacity, where_ref, col_ref, returned_ref, residual_ref, gain_ref, router_ref, out_ref
):
    slots, half = returned_ref.shape
    tile = residual_ref.shape[0]
    experts = router_ref.shape[1]
    col = col_ref[:, :1]
    place = lax.broadcasted_iota(jnp.int32, (tile, slots), 1)
    hot = jnp.where(place == col, 1.0, 0.0).astype(jnp.bfloat16)
    token_out = dot_nn(hot, returned_ref[...])
    residual = residual_ref[...]
    second = (residual * inverse_rms(residual) * gain_ref[...]).astype(jnp.bfloat16)
    logits = dot_nn(second, router_ref[...])
    exp_logit = jnp.exp(logits - jnp.max(logits, axis=1, keepdims=True))
    first = lax.broadcasted_iota(jnp.int32, (1, experts), 1) * capacity
    hit = jnp.where((col >= first) & (col < first + capacity), exp_logit, 0.0)
    gate = jnp.sum(hit, axis=1, keepdims=True) / jnp.sum(exp_logit, axis=1, keepdims=True)
    own = residual_ref[:, half_lanes(where_ref[0], half)]
    out_ref[...] = (own + gate * token_out).astype(jnp.bfloat16)


def output_of(where, slot_col, returned, residual, gain, router, capacity):
    tok_count, width = residual.shape
    slots, half = returned.shape
    tile = 256
    whole = lambda shape: pl.BlockSpec(shape, lambda step: (0, 0))
    return pl.pallas_call(
        partial(output_kernel, capacity),
        grid=(tok_count // tile,),
        out_shape=jax.ShapeDtypeStruct((tok_count, half), jnp.bfloat16),
        in_specs=[
            pl.BlockSpec(memory_space=pltpu.SMEM),
            pl.BlockSpec((tile, 128), lambda step: (step, 0)),
            whole(returned.shape),
            pl.BlockSpec((tile, width), lambda step: (step, 0)),
            whole((1, width)),
            whole(router.shape),
        ],
        out_specs=pl.BlockSpec((tile, half), lambda step: (step, 0)),
        compiler_params=params(),
        cost_estimate=pl.CostEstimate(
            flops=2 * tok_count * half * slots, bytes_accessed=6000000, transcendentals=0
        ),
        name="output",
    )(
        where, in_hbm(slot_col), in_hbm(returned), in_hbm(residual), gain.astype(jnp.float32)[None], router
    )


def normed_back_kernel(grads_ref, wq_ref, wk_ref, wv_ref, out_ref):
    own = wq_ref.shape[1]
    out_ref[...] = (
        dot_nt(grads_ref[:, :own], wq_ref[...])
        + dot_nt(grads_ref[:, own : 2 * own], wk_ref[...])
        + dot_nt(grads_ref[:, 2 * own :], wv_ref[...])
    ).astype(jnp.bfloat16)


def normed_back(grads, w_query, w_key, w_value):
    tok_count = grads.shape[0]
    width, own = w_query.shape
    tile = 256
    whole = pl.BlockSpec((width, own), lambda step: (0, 0))
    return pl.pallas_call(
        normed_back_kernel,
        grid=(tok_count // tile,),
        out_shape=jax.ShapeDtypeStruct((tok_count, width), jnp.bfloat16),
        in_specs=[pl.BlockSpec((tile, 3 * own), lambda step: (step, 0))] + [whole] * 3,
        out_specs=pl.BlockSpec((tile, width), lambda step: (step, 0)),
        compiler_params=params(),
        cost_estimate=pl.CostEstimate(
            flops=6 * tok_count * own * width, bytes_accessed=6000000, transcendentals=0
        ),
        name="normed_back",
    )(*(in_hbm(array) for array in (grads, w_query, w_key, w_value)))


def input_back_kernel(tokens_ref, own_ref, other_ref, gain_ref, residual_ref, out_ref):
    ybar = own_ref[...].astype(jnp.float32) + other_ref[...].astype(jnp.float32)
    values = tokens_ref[...].astype(jnp.float32)
    scale = inverse_rms(values)
    scaled = values * scale
    pulled = ybar * gain_ref[...]
    out_ref[...] = residual_ref[...] + scale * (
        pulled - scaled * jnp.mean(pulled * scaled, axis=1, keepdims=True)
    )


def input_back(tokens, own, other, gain, residual_grad):
    tok_count, width = tokens.shape
    tile = 256
    rows = pl.BlockSpec((tile, width), lambda step: (step, 0))
    return pl.pallas_call(
        input_back_kernel,
        grid=(tok_count // tile,),
        out_shape=jax.ShapeDtypeStruct((tok_count, width), jnp.float32),
        in_specs=[rows, rows, rows, pl.BlockSpec((1, width), lambda step: (0, 0)), rows],
        out_specs=rows,
        compiler_params=params(),
        cost_estimate=pl.CostEstimate(
            flops=10 * tok_count * width, bytes_accessed=11000000, transcendentals=0
        ),
        name="input_back",
    )(in_hbm(tokens), own, other, gain.astype(jnp.float32)[None], in_hbm(residual_grad))


def back_kernel(
    bits_ref,
    where_ref,
    col_hbm,
    own_hbm,
    other_hbm,
    residual_hbm,
    grad_hbm,
    wo_hbm,
    q_hbm,
    k_hbm,
    v_hbm,
    mixed_hbm,
    long_hbm,
    short_hbm,
    normed_hbm,
    wq_hbm,
    wk_hbm,
    wv_hbm,
    gain_one_ref,
    gain_two_ref,
    router_ref,
    out_hbm,
    grads_hbm,
    sent_a,
    sent_b,
    sent_c,
    kept_a,
    kept_b,
    kept_c,
    col_ref,
    back_ref,
    residual_ref,
    grad_ref,
    wo_ref,
    q_ref,
    k_ref,
    v_ref,
    mixed_ref,
    long_ref,
    short_ref,
    normed_ref,
    wq_ref,
    wk_ref,
    wv_ref,
    attn_ref,
    heads_ref,
    grads_ref,
    sg_ref,
    tiles_ref,
    far_ref,
    stack_ref,
    small_ref,
    packed_ref,
    total_ref,
    in_sems,
    out_sems,
):
    tok_count, width = residual_ref.shape
    slots, half = own_hbm.shape
    own = mixed_ref.shape[1]
    experts = router_ref.shape[0]
    pairs = own // 128
    tile = 512
    steps = tok_count // tile
    core = where_ref[0]
    first = [
        (own_hbm, back_ref.at[:, half_lanes(core, half)]),
        (other_hbm, back_ref.at[:, half_lanes(1 - core, half)]),
        (col_hbm, col_ref),
        (wo_hbm, wo_ref),
    ]
    tiles = []
    for start in range(0, tok_count, tile):
        rows = slice(start, start + tile)
        tiles.append((residual_hbm.at[rows], residual_ref.at[rows]))
        tiles.append((grad_hbm.at[rows], grad_ref.at[rows]))
    attention = [(q_hbm, q_ref), (k_hbm, k_ref), (v_hbm, v_ref), (mixed_hbm, mixed_ref), (short_hbm, short_ref)]
    for pair in range(pairs):
        both = slice(pair * 2, pair * 2 + 2)
        attention.append((long_hbm.at[both], long_ref.at[both]))
    weights = [(normed_hbm, normed_ref), (wq_hbm, wq_ref), (wk_hbm, wk_ref), (wv_hbm, wv_ref)]
    copies = start_copies(
        [
            (source, target, in_sems.at[index])
            for index, (source, target) in enumerate(first + tiles + attention + weights)
        ]
    )
    base = len(first) + len(tiles)
    outs = []

    for copy in copies[: len(first)]:
        copy.wait()
    gain_two = gain_two_ref[...]
    place = lax.broadcasted_iota(jnp.int32, (tile, slots), 1)

    def tile_out(step):
        rows = pl.ds(pl.multiple_of(step * tile, tile), tile)
        return pltpu.make_async_copy(residual_ref.at[rows], out_hbm.at[rows], out_sems.at[step])

    def one_tile(step, gain_two_grad):
        rows = pl.ds(pl.multiple_of(step * tile, tile), tile)
        at = len(first) + 2 * step
        pltpu.make_async_copy(residual_hbm.at[rows], residual_ref.at[rows], in_sems.at[at]).wait()
        pltpu.make_async_copy(grad_hbm.at[rows], grad_ref.at[rows], in_sems.at[at + 1]).wait()
        hot = jnp.where(place == col_ref[rows, :][:, :1], 1.0, 0.0).astype(jnp.bfloat16)
        ybar = dot_nn(hot, back_ref[...])
        values = residual_ref[rows, :]
        scale = inverse_rms(values)
        scaled = values * scale
        pulled = ybar * gain_two
        back = scale * (pulled - scaled * jnp.mean(pulled * scaled, axis=1, keepdims=True))
        out = back + grad_ref[rows, :].astype(jnp.float32)
        residual_ref[rows, :] = out
        attn = out.astype(jnp.bfloat16)
        attn_ref[rows, :] = attn
        heads_ref[rows, :] = dot_nt(attn, wo_ref[...]).astype(jnp.bfloat16)
        tile_out(step).start()
        return gain_two_grad + jnp.sum(ybar * scaled, axis=0, keepdims=True)

    gain_two_grad = lax.fori_loop(0, steps, one_tile, jnp.zeros((1, width), jnp.float32))
    outs += [tile_out(step) for step in range(steps)]

    for copy in copies[base : base + 5]:
        copy.wait()

    def one_pair(pair, carry):
        both = pl.ds(pair * 2, 2)
        pltpu.make_async_copy(long_hbm.at[both], long_ref.at[both], in_sems.at[base + 5 + pair]).wait()
        attend_back_pair(
            pair, heads_ref, q_ref, k_ref, v_ref, mixed_ref, long_ref, short_ref, grads_ref, tiles_ref, far_ref,
            sg_ref,
        )
        return carry

    lax.fori_loop(0, pairs, one_pair, 0, unroll=True)
    outs += start_copies([(grads_ref, grads_hbm, out_sems.at[steps])])

    def out_rows(block, carry):
        start = pl.multiple_of(block * 128, 128)
        grad = contract_rows(mixed_ref[:, pl.ds(start, 128)], attn_ref[...]).astype(jnp.bfloat16)
        for part in range(width // own):
            at = pl.multiple_of(3 * width + part * own + start, 128)
            stack_ref[pl.ds(at, 128), :] = grad[:, part * own : part * own + own]
        return carry

    lax.fori_loop(0, own // 128, out_rows, 0, unroll=True)
    small_ref[0:experts, :] = router_ref[...]
    small_ref[experts + 1 : experts + 2, :] = gain_two_grad
    for head in range(2 * pairs):
        row = experts + 2 + head
        small_ref[row : row + 1, 0:512] = diagonals(tiles_ref[head])
        small_ref[row : row + 1, 512:640] = far_ref[head, 0:1, :]
        small_ref[row : row + 1, 640:768] = far_ref[head, 1:2, :]
    for copy in copies[base + 5 + pairs :]:
        copy.wait()
    rows = stack_ref.shape[0] // 3
    span = rows // 2

    def send_part(part, sent, kept):
        mine = bits_ref[part]
        sent_rows = pl.ds(pl.multiple_of(part * rows + (1 - mine) * span, span), span)
        kept_rows = pl.ds(pl.multiple_of(part * rows + mine * span, span), span)
        return start_copies(
            [
                (stack_ref.at[sent_rows], sent.at[:span], out_sems.at[steps + 4 + 2 * part]),
                (stack_ref.at[kept_rows], kept, out_sems.at[steps + 5 + 2 * part]),
            ]
        )

    span_rows = 256

    def head_rows(block, carry):
        start = pl.multiple_of(block * span_rows, span_rows)
        piece = pl.ds(start, span_rows)
        grad = contract_rows(normed_ref[:, piece], grads_ref[...])
        total = jnp.zeros((span_rows, 1), jnp.float32)
        for index, w_ref in enumerate((wq_ref, wk_ref, wv_ref)):
            part = grad[:, index * own : index * own + own]
            total = total + jnp.sum(part * w_ref[piece, :].astype(jnp.float32), axis=1, keepdims=True)
            stack_ref[pl.ds(pl.multiple_of(index * width + start, span_rows), span_rows), :] = part.astype(jnp.bfloat16)
        total_ref[piece, :] = jnp.broadcast_to(total, (span_rows, 128))
        return carry

    lax.fori_loop(0, width // span_rows, head_rows, 0, unroll=True)
    for part, (sent, kept) in enumerate(((sent_a, kept_a), (sent_b, kept_b))):
        outs += send_part(part, sent, kept)
    outs += send_part(2, sent_c, kept_c)
    wide = jnp.transpose(total_ref[...])
    small_ref[experts : experts + 1, :] = wide[:1, :] / gain_one_ref[...]
    small = small_ref[...]
    packed_ref[...] = jnp.concatenate([small[:, :own], small[:, own:]], axis=0).astype(jnp.bfloat16)
    outs += start_copies([(packed_ref, sent_a.at[span:], out_sems.at[steps + 3])])
    for copy in outs:
        copy.wait()


def back_pass(
    bits, where, slot_col, back_own, back_other, residual, out_grad, w_out, query_rows, key_rows,
    value_rows, mixed, long_probs, short_probs, normed, w_query, w_key, w_value, gain_one, gain_two,
    router_part,
):
    tok_count, width = normed.shape
    own = mixed.shape[1]
    slots, half = back_own.shape
    heads = long_probs.shape[0]
    count = router_part.shape[0] + 2 + heads
    span = 4 * width // 6
    tile = 512
    steps = tok_count // tile
    half_rows = hbm_out((span, own), jnp.bfloat16)
    pinned = (residual, out_grad, w_out, query_rows, key_rows, value_rows, mixed, long_probs, short_probs, normed,
              w_query, w_key, w_value)
    hbm = pl.BlockSpec(memory_space=pltpu.HBM)
    smem = pl.BlockSpec(memory_space=pltpu.SMEM)

    def scratch(array):
        return pltpu.VMEM(array.shape, array.dtype)

    flops = 2 * tok_count * width * (slots + 5 * own) + 10 * heads * (512 * 512 + 512 * 128) * 64
    out = pl.pallas_call(
        back_kernel,
        out_shape=[
            hbm_out((tok_count, width), jnp.float32),
            hbm_out((tok_count, 3 * own), jnp.bfloat16),
            hbm_out((span + 2 * count, own), jnp.bfloat16),
        ]
        + [half_rows] * 5,
        in_specs=[smem, smem] + [hbm, hbm, pl.BlockSpec(memory_space=pl.ANY)] + [hbm] * 13 + vmem(3),
        out_specs=[hbm] * 8,
        scratch_shapes=[scratch(slot_col), pltpu.VMEM((slots, width), jnp.bfloat16)]
        + [scratch(array) for array in pinned]
        + [
            pltpu.VMEM((tok_count, width), jnp.bfloat16),
            pltpu.VMEM((tok_count, own), jnp.bfloat16),
            pltpu.VMEM((tok_count, 3 * own), jnp.bfloat16),
            pltpu.VMEM((LONG_LEN, LONG_LEN), jnp.bfloat16),
            pltpu.VMEM((heads, 128, 384), jnp.float32),
            pltpu.VMEM((heads, 2, 128), jnp.float32),
            pltpu.VMEM((4 * width, own), jnp.bfloat16),
            pltpu.VMEM((count, width), jnp.float32),
            pltpu.VMEM((2 * count, own), jnp.bfloat16),
            pltpu.VMEM((width, 128), jnp.float32),
            pltpu.SemaphoreType.DMA((2 * steps + 4 + 5 + heads // 2 + 4,)),
            pltpu.SemaphoreType.DMA((steps + 10,)),
        ],
        compiler_params=params(36),
        cost_estimate=pl.CostEstimate(flops=flops, bytes_accessed=25000000, transcendentals=0),
        name="back",
    )(
        bits,
        where,
        in_hbm(slot_col),
        in_hbm(back_own),
        back_other,
        *(in_hbm(array) for array in pinned),
        gain_one.astype(jnp.float32)[None],
        gain_two.astype(jnp.float32)[None],
        router_part,
    )
    return out[0], out[1], out[2:5], out[5:]


def added(left, right):
    return (left.astype(jnp.float32) + right.astype(jnp.float32)).astype(jnp.bfloat16)


def fold_kernel(bits_ref, *refs):
    kept, got, sent, keep = refs[0:3], refs[3:6], refs[7:10], refs[10:13]
    before = refs[6]
    for part in range(3):
        span = kept[part].shape[0] // 2
        mine = bits_ref[part]
        for ref, start in ((sent[part], (1 - mine) * span), (keep[part], mine * span)):
            rows = pl.ds(pl.multiple_of(start, span), span)
            ref[:span, :] = added(kept[part][rows, :], got[part][rows, :])
    rows = kept[0].shape[0]
    sent[0][rows // 2 :, :] = added(before[rows:, :], got[0][rows:, :])


def fold(bits, kept, got, before):
    rows, lanes = kept[0].shape
    extra = before.shape[0] - rows
    half = jax.ShapeDtypeStruct((rows // 2, lanes), jnp.bfloat16)
    out = pl.pallas_call(
        fold_kernel,
        out_shape=[jax.ShapeDtypeStruct((rows // 2 + extra, lanes), jnp.bfloat16)] + [half] * 5,
        in_specs=[pl.BlockSpec(memory_space=pltpu.SMEM)] + vmem(7),
        out_specs=vmem(6),
        compiler_params=params(16),
        name="fold",
    )(bits, *kept, *got, before)
    return out[:3], out[3:]


def pack_kernel(*refs):
    kept, got, before, out = refs[0:3], refs[3:6], refs[6], refs[7]
    rows = kept[0].shape[0]
    for part in range(3):
        out[part * rows : (part + 1) * rows, :] = added(kept[part][...], got[part][:rows, :])
    out[3 * rows :, :] = added(before[rows:, :], got[0][rows:, :])


def pack(kept, got, before):
    rows, lanes = kept[0].shape
    return pl.pallas_call(
        pack_kernel,
        out_shape=jax.ShapeDtypeStruct((2 * rows + before.shape[0], lanes), jnp.bfloat16),
        in_specs=vmem(7),
        out_specs=vmem(1)[0],
        compiler_params=params(16),
        name="pack",
    )(*kept, *got, before)


def unpack_kernel(own_ref, got_ref, *out):
    rows = out[0].shape[0]
    for part in range(3):
        piece = slice(part * rows, (part + 1) * rows)
        out[part][...] = added(own_ref[piece, :], got_ref[piece, :])
    out[3][...] = own_ref[3 * rows :, :].astype(jnp.float32) + got_ref[3 * rows :, :].astype(jnp.float32)


def unpack(own, got, rows):
    lanes = own.shape[1]
    out = pl.pallas_call(
        unpack_kernel,
        out_shape=[jax.ShapeDtypeStruct((rows, lanes), jnp.bfloat16)] * 3
        + [jax.ShapeDtypeStruct((own.shape[0] - 3 * rows, lanes), jnp.float32)],
        in_specs=vmem(2),
        out_specs=vmem(4),
        compiler_params=params(16),
        name="unpack",
    )(own, got)
    return out[:3], out[3]


def join_kernel(bits_ref, *refs):
    own, got, out = refs[0:3], refs[3:6], refs[6:9]
    for part in range(3):
        span = own[part].shape[0]
        mine = bits_ref[part]
        out[part][pl.ds(pl.multiple_of(mine * span, span), span), :] = own[part][...]
        out[part][pl.ds(pl.multiple_of((1 - mine) * span, span), span), :] = got[part][...]


def join(bits, own, got):
    return pl.pallas_call(
        join_kernel,
        out_shape=[jax.ShapeDtypeStruct((p.shape[0] * 2, p.shape[1]), p.dtype) for p in own],
        in_specs=[pl.BlockSpec(memory_space=pltpu.SMEM)] + vmem(6),
        out_specs=vmem(3),
        compiler_params=params(16),
        name="join",
    )(bits, *own, *got)


def finish_kernel(bits_ref, *refs):
    own, got = refs[0:3], refs[3:6]
    results = refs[6:10]
    held, sems = refs[10:14], refs[14]
    span = own[0].shape[0]
    rows = 2 * span
    width, lanes = held[0].shape
    copies = []
    for part in range(3):
        mine = bits_ref[part]
        first = jnp.where(mine == 0, own[part][...], got[part][...])
        second = jnp.where(mine == 0, got[part][...], own[part][...])
        for base, piece in ((part * rows, first), (part * rows + span, second)):
            for index in range(3 + width // lanes):
                start = index * width if index < 3 else 3 * width + (index - 3) * lanes
                size = width if index < 3 else lanes
                low = max(start, base)
                high = min(start + size, base + span)
                if low < high:
                    values = piece[low - base : high - base, :].astype(jnp.float32)
                    if index < 3:
                        held[index][low - start : high - start, :] = values
                    else:
                        place = (index - 3) * lanes
                        held[3][low - start : high - start, place : place + lanes] = values
        for index in range(4):
            last = (index + 1) * width - 1
            if part * rows <= last < (part + 1) * rows:
                copies += start_copies([(held[index], results[index], sems.at[index])])
    for copy in copies:
        copy.wait()


def finish(bits, own, got, width):
    lanes = own[0].shape[1]
    shapes = [(width, lanes)] * 3 + [(lanes, width)]
    return pl.pallas_call(
        finish_kernel,
        out_shape=[hbm_out(shape, jnp.float32) for shape in shapes],
        in_specs=[pl.BlockSpec(memory_space=pltpu.SMEM)] + vmem(6),
        out_specs=[pl.BlockSpec(memory_space=pltpu.HBM)] * 4,
        scratch_shapes=[pltpu.VMEM(shape, jnp.float32) for shape in shapes]
        + [pltpu.SemaphoreType.DMA((4,))],
        compiler_params=params(24),
        name="finish",
    )(bits, *own, *got)


def swap_heads(rows):
    return lax.ppermute(rows, "heads", [(0, 1), (1, 0)])


def trade(rows, bit):
    count = lax.axis_size("seq")
    return lax.ppermute(rows, "seq", [(i, i ^ (1 << bit)) for i in range(count)])


def together(*groups):
    return lax.optimization_barrier(groups)


def contract_rows(left, right):
    return lax.dot_general(
        left, right, (((0,), (0,)), ((), ())), preferred_element_type=jnp.float32
    )


def on_device(
    tokens,
    gain_attn,
    w_query,
    w_key,
    w_value,
    w_out,
    bias_table,
    gain_ffn,
    w_router,
    w_inner,
    w_outer,
    routes,
    seq_lengths,
    out_grad,
):
    tok_count, width = tokens.shape
    bucket_count = bias_table.shape[0]
    experts = w_router.shape[1]
    capacity = max(2, 5 * tok_count // (4 * experts))
    senders = lax.axis_size("seq")
    bits = list(range(senders.bit_length() - 1))
    slots = experts * capacity
    half = width // 2
    own = w_query.shape[1]
    where = jnp.stack([lax.axis_index("heads"), lax.axis_index("seq")]).astype(jnp.int32)

    def exchange(rows):
        return lax.all_to_all(
            rows.reshape(senders, capacity, half), "seq", split_axis=0, concat_axis=0, tiled=True
        ).reshape(slots, half)

    def summed(keep, send):
        return (keep + swap_heads(send).astype(jnp.float32)).astype(jnp.bfloat16)

    slot_row, slot_col, grad_sent = route(where, routes, out_grad, experts, capacity)
    grad_sent, tokens = together(grad_sent, tokens)
    grad_own = exchange(grad_sent)
    attn_part, normed, query_rows, key_rows, value_rows, mixed, long_probs, short_probs = attend(
        seq_lengths, tokens, gain_attn, w_query, w_key, w_value, w_out, bias_table
    )
    residual, second_sent = second_rows(
        where, tokens, attn_part, swap_heads(attn_part), gain_ffn, slot_row, slots
    )
    second_sent, grad_own = together(second_sent, grad_own)
    arrived_own = exchange(second_sent)

    inner = w_inner[0]
    outer = w_outer[0]
    grad_other = swap_heads(grad_own)
    hidden_grad = hidden_grad_of(where, grad_own, grad_other, outer)
    arrived_own, hidden_grad = together(arrived_own, hidden_grad)
    arrived_other = swap_heads(arrived_own)
    hidden, pre_grad, keep, send, logit_grad = expert(
        where, arrived_own, arrived_other, hidden_grad, inner, w_router
    )
    back_sum, hidden = together(summed(keep, send), hidden)
    back_own = exchange(back_sum)
    out_keep, out_send, router_part = expert_out_of(
        where, hidden, arrived_own, arrived_other, logit_grad, outer
    )
    out_sum = summed(out_keep, out_send)
    back_own, out_sum = together(back_own, out_sum)
    back_other = swap_heads(back_own)
    returned = exchange(out_sum)

    depth = len(bits) - 1
    turns = [bits[k * depth // 3 : depth] + bits[: k * depth // 3] for k in range(3)]
    place = lax.axis_index("seq")
    mine = [jnp.stack([(place >> turn[k]) & 1 for turn in turns]).astype(jnp.int32) for k in range(depth)]
    residual_grad, head_grads, sent, kept = back_pass(
        mine[0], where, slot_col, back_own, back_other, residual, out_grad, w_out, query_rows, key_rows,
        value_rows, mixed, long_probs, short_probs, normed, w_query, w_key, w_value, gain_attn, gain_ffn,
        router_part,
    )

    def trades(arrays, k):
        return [trade(array, turn[k]) for array, turn in zip(arrays, turns)]

    for k in range(depth):
        got = trades(sent, k)
        if k == 0:
            output = output_of(where, slot_col, returned, residual, gain_ffn, w_router, capacity)
            got, output, head_grads = together(got, output, head_grads)
        if k == 1:
            normed_part = normed_back(head_grads, w_query, w_key, w_value)
            got, normed_part = together(got, normed_part)
        if k + 1 < depth:
            sent, kept = fold(mine[k + 1], kept, got, sent[0])
    normed_other = swap_heads(normed_part)
    packed = pack(kept, got, sent[0])
    packed, normed_other, pre_grad = together(packed, normed_other, pre_grad)
    got = trade(packed, bits[-1])
    inner_grad, outer_grad = expert_grads(
        where, arrived_own, arrived_other, grad_own, grad_other, hidden, pre_grad, w_router
    )
    got, inner_grad = together(got, inner_grad)
    summed_parts, small = unpack(packed, got, kept[0].shape[0])
    small = jnp.concatenate([small[: small.shape[0] // 2], small[small.shape[0] // 2 :]], axis=1)
    small_other = swap_heads(small)
    for k in reversed(range(1, depth)):
        got = trades(summed_parts, k)
        if k == depth - 1:
            got, small = together(got, small)
        if k == 1:
            both = small[: experts + 1] + small_other[: experts + 1]
            router_grad = both[:experts].T
            table_grad = table_from(small[experts + 2 :], bucket_count)
            got, both, router_grad, table_grad = together(got, both, router_grad, table_grad)
        summed_parts = join(mine[k], summed_parts, got)
    got = trades(summed_parts, 0)
    input_grad = input_back(tokens, normed_part, normed_other, gain_attn, residual_grad)
    got, input_grad = together(got, input_grad)
    query_w_grad, key_w_grad, value_w_grad, out_w_grad = finish(mine[0], summed_parts, got, width)
    return (
        output,
        input_grad,
        both[experts],
        query_w_grad,
        key_w_grad,
        value_w_grad,
        out_w_grad,
        table_grad,
        small[experts + 1],
        router_grad,
        inner_grad[None],
        outer_grad[None],
    )


def solution(mesh):
    in_specs = (
        P("seq", None),
        P(),
        P(None, "heads"),
        P(None, "heads"),
        P(None, "heads"),
        P("heads", None),
        P(None, "heads"),
        P(),
        P(),
        P("seq", None, "heads"),
        P("seq", "heads", None),
        P("seq", None),
        P("seq"),
        P("seq", None),
    )
    out_specs = (
        P("seq", "heads"),
        P("seq", None),
        P(),
        P(None, "heads"),
        P(None, "heads"),
        P(None, "heads"),
        P("heads", None),
        P(None, "heads"),
        P(),
        P(),
        P("seq", None, "heads"),
        P("seq", "heads", None),
    )
    return jax.shard_map(
        on_device, mesh=mesh, in_specs=in_specs, out_specs=out_specs, check_vma=False
    )
```

```python
from functools import partial

import jax
import jax.numpy as jnp
from jax import lax
from jax.experimental import pallas as pl
from jax.experimental.pallas import tpu as pltpu
from jax.sharding import PartitionSpec as P

SHORT_LEN = 128
LONG_LEN = 512
SHORT_DEV = 4
LONG_DEV = 1


epsilon = 1e-06
highest = lax.Precision.HIGHEST
far_limits = (12, 16, 23, 32, 46, 64, 91)


def vmem(count):
    return [pl.BlockSpec(memory_space=pltpu.VMEM)] * count


def params(mib=16):
    return pltpu.CompilerParams(vmem_limit_bytes=mib * 1024 * 1024)


def dot_nn(left, right):
    return jnp.dot(left, right, preferred_element_type=jnp.float32)


def dot_nt(left, right):
    return lax.dot_general(
        left, right, (((1,), (1,)), ((), ())), preferred_element_type=jnp.float32
    )


def inverse_rms(values):
    return lax.rsqrt(jnp.mean(values * values, axis=-1, keepdims=True) + epsilon)


def diagonal_buckets(offset):
    distance = jnp.abs(offset)
    far_bucket = jnp.full(offset.shape, 8, jnp.int32)
    for limit in far_limits:
        far_bucket = far_bucket + (distance >= limit).astype(jnp.int32)
    return jnp.where(distance < 8, distance, far_bucket) + jnp.where(offset > 0, 16, 0)


def hbm_out(shape, dtype):
    return pltpu.HBM(shape, dtype)


def in_hbm(array):
    return pltpu.with_memory_space_constraint(array, pltpu.HBM)


def start_copies(pairs):
    copies = [pltpu.make_async_copy(*triple) for triple in pairs]
    for copy in copies:
        copy.start()
    return copies


def attend_kernel(
    block_rows,
    lengths_ref,
    tokens_hbm,
    gain_ref,
    wq_hbm,
    wk_hbm,
    wv_hbm,
    wo_hbm,
    table_ref,
    part_hbm,
    normed_hbm,
    q_hbm,
    k_hbm,
    v_hbm,
    mixed_hbm,
    long_hbm,
    short_hbm,
    tokens_ref,
    joint_ref,
    wo_ref,
    part_ref,
    normed_ref,
    q_ref,
    k_ref,
    v_ref,
    mixed_ref,
    long_ref,
    short_ref,
    diag_ref,
    in_sems,
    out_sems,
):
    tok_count, width = tokens_ref.shape
    own = q_ref.shape[1]
    pairs = own // 128
    short_tok = SHORT_DEV * SHORT_LEN
    tile = 512
    steps = tok_count // tile
    tiles_in = []
    for step in range(steps):
        rows = slice(step * tile, step * tile + tile)
        tiles_in.append((tokens_hbm.at[rows], tokens_ref.at[rows], in_sems.at[step]))
    weights = [
        (source, joint_ref.at[:, index * own : index * own + own])
        for index, source in enumerate((wq_hbm, wk_hbm, wv_hbm))
    ]
    weights.append((wo_hbm, wo_ref))
    copies = start_copies(
        tiles_in + [(src, dst, in_sems.at[steps + index]) for index, (src, dst) in enumerate(weights)]
    )
    weight_copies = copies[steps:]
    outs = []

    offset = lax.broadcasted_iota(jnp.int32, (table_ref.shape[1], 512), 1) - 256
    hot = jnp.where(
        diagonal_buckets(offset)
        == lax.broadcasted_iota(jnp.int32, (table_ref.shape[1], 512), 0),
        1.0,
        0.0,
    )
    diag_ref[...] = dot_nn(table_ref[...], hot.astype(jnp.bfloat16))
    gain = gain_ref[...]

    def normalize(step, carry):
        rows = pl.ds(pl.multiple_of(step * tile, tile), tile)
        pltpu.make_async_copy(tokens_hbm.at[rows], tokens_ref.at[rows], in_sems.at[step]).wait()
        values = tokens_ref[rows, :].astype(jnp.float32)
        normed_ref[rows, :] = (values * inverse_rms(values) * gain).astype(jnp.bfloat16)
        return carry

    lax.fori_loop(0, steps, normalize, 0)
    outs += start_copies([(normed_ref, normed_hbm, out_sems.at[0])])
    for copy in weight_copies[:3]:
        copy.wait()

    def project(step, carry):
        rows = pl.ds(pl.multiple_of(step * tile, tile), tile)
        joint = dot_nn(normed_ref[rows, :], joint_ref[...]).astype(jnp.bfloat16)
        q_ref[rows, :] = joint[:, :own] * jnp.bfloat16(0.125)
        k_ref[rows, :] = joint[:, own : 2 * own]
        v_ref[rows, :] = joint[:, 2 * own :]
        return carry

    lax.fori_loop(0, steps, project, 0)
    outs += start_copies(
        [
            (q_ref, q_hbm, out_sems.at[1]),
            (k_ref, k_hbm, out_sems.at[2]),
            (v_ref, v_hbm, out_sems.at[3]),
        ]
    )
    lane = lax.broadcasted_iota(jnp.int32, (1, 128), 1)
    key_place = lax.broadcasted_iota(jnp.int32, (1, LONG_LEN), 1)
    live_long = key_place < lengths_ref[SHORT_DEV]

    def softmax(scores):
        weights = jnp.exp(scores - jnp.max(scores, axis=1, keepdims=True))
        return (weights * (1.0 / jnp.sum(weights, axis=1, keepdims=True))).astype(jnp.bfloat16)

    def one_pair(pair):
        lanes = slice(pair * 128, pair * 128 + 128)
        tiles = []
        for sub in range(2):
            row = diag_ref[pair * 2 + sub : pair * 2 + sub + 1, :]
            spread = pltpu.roll(
                jnp.broadcast_to(row, (128, 512)), 256, 1, stride=1, stride_axis=0
            )
            tiles.append(
                (
                    spread[:, 0:128],
                    spread[:, 128:256],
                    spread[:, 384:512],
                    jnp.broadcast_to(row[:, 511:512], (128, 128)),
                    jnp.broadcast_to(row[:, 0:1], (128, 128)),
                )
            )
        out = []
        for sub in range(2):
            scores = []
            for block in range(SHORT_DEV):
                rows = slice(block * 128, block * 128 + 128)
                masked = jnp.where((lane >= 64) == (sub == 1), q_ref[rows, lanes], 0)
                live = key_place[:, :128] < lengths_ref[block]
                scores.append(
                    jnp.where(
                        live, dot_nt(masked, k_ref[rows, lanes]) + tiles[sub][0], -1000000000.0
                    )
                )
            probs = softmax(jnp.concatenate(scores, axis=0))
            short_ref[pair * 2 + sub] = probs
            mixed = []
            for block in range(SHORT_DEV):
                rows = slice(block * 128, block * 128 + 128)
                mixed.append(dot_nn(probs[rows], v_ref[rows, lanes]))
            out.append(jnp.concatenate(mixed, axis=0))
        mixed_ref[:short_tok, lanes] = jnp.where(lane < 64, out[0], out[1]).astype(jnp.bfloat16)
        keys = k_ref[short_tok:, lanes]
        values = v_ref[short_tok:, lanes]
        for start in range(0, LONG_LEN, block_rows):
            places = slice(start, start + block_rows)
            rows = slice(short_tok + start, short_tok + start + block_rows)
            queries = q_ref[rows, lanes]
            out = []
            for sub in range(2):
                masked = jnp.where((lane >= 64) == (sub == 1), queries, 0)
                same, above, below, far_above, far_below = tiles[sub]
                bias = jnp.concatenate(
                    [
                        jnp.concatenate(
                            [
                                same
                                if other == block
                                else above
                                if other == block + 1
                                else below
                                if other == block - 1
                                else far_above
                                if other > block
                                else far_below
                                for other in range(LONG_LEN // 128)
                            ],
                            axis=1,
                        )
                        for block in range(start // 128, (start + block_rows) // 128)
                    ],
                    axis=0,
                )
                scores = jnp.where(live_long, dot_nt(masked, keys) + bias, -1000000000.0)
                probs = softmax(scores)
                long_ref[pair * 2 + sub, places, :] = probs
                out.append(dot_nn(probs, values))
            mixed_ref[rows, lanes] = jnp.where(lane < 64, out[0], out[1]).astype(jnp.bfloat16)

    for pair in range(pairs):
        one_pair(pair)
        both = slice(pair * 2, pair * 2 + 2)
        outs += start_copies(
            [
                (long_ref.at[both], long_hbm.at[both], out_sems.at[4 + 2 * pair]),
                (short_ref.at[both], short_hbm.at[both], out_sems.at[5 + 2 * pair]),
            ]
        )
    weight_copies[3].wait()
    base = 4 + 2 * pairs
    outs += start_copies([(mixed_ref, mixed_hbm, out_sems.at[base])])

    def part_copy(step):
        rows = pl.ds(pl.multiple_of(step * tile, tile), tile)
        return pltpu.make_async_copy(part_ref.at[rows], part_hbm.at[rows], out_sems.at[base + 1 + step])

    def project_out(step, carry):
        rows = pl.ds(pl.multiple_of(step * tile, tile), tile)
        part_ref[rows, :] = dot_nn(mixed_ref[rows, :], wo_ref[...]).astype(part_ref.dtype)
        part_copy(step).start()
        return carry

    lax.fori_loop(0, steps, project_out, 0)
    outs += [part_copy(step) for step in range(steps)]
    for copy in outs:
        copy.wait()


def attend(lengths, tokens, gain, w_query, w_key, w_value, w_out, table, block_rows=512):
    tok_count, width = tokens.shape
    own = w_query.shape[1]
    heads = own // 64
    heads_pad = -(-heads // 8) * 8
    table = jnp.pad(table.T, ((0, heads_pad - heads), (0, 0)))
    short_tok = SHORT_DEV * SHORT_LEN
    flops = 2 * tok_count * width * own * 4 + 4 * heads * (512 * 512 + short_tok * 128) * 64
    hbm = pl.BlockSpec(memory_space=pltpu.HBM)
    out_shapes = [
        ((tok_count, width), jnp.bfloat16),
        ((tok_count, width), jnp.bfloat16),
        ((tok_count, own), jnp.bfloat16),
        ((tok_count, own), jnp.bfloat16),
        ((tok_count, own), jnp.bfloat16),
        ((tok_count, own), jnp.bfloat16),
        ((heads, LONG_LEN, LONG_LEN), jnp.bfloat16),
        ((heads, short_tok, SHORT_LEN), jnp.bfloat16),
    ]
    steps = tok_count // 512
    return pl.pallas_call(
        partial(attend_kernel, block_rows),
        out_shape=[jax.ShapeDtypeStruct(*out_shapes[0])]
        + [hbm_out(shape, dtype) for shape, dtype in out_shapes[1:]],
        in_specs=[pl.BlockSpec(memory_space=pltpu.SMEM), hbm]
        + vmem(1)
        + [hbm] * 4
        + vmem(1),
        out_specs=[hbm] * 8,
        scratch_shapes=[pltpu.VMEM(tokens.shape, jnp.bfloat16)]
        + [pltpu.VMEM((width, 3 * own), jnp.bfloat16), pltpu.VMEM(w_out.shape, jnp.bfloat16)]
        + [pltpu.VMEM(shape, dtype) for shape, dtype in out_shapes]
        + [
            pltpu.VMEM((heads_pad, 512), jnp.float32),
            pltpu.SemaphoreType.DMA((steps + 4,)),
            pltpu.SemaphoreType.DMA((5 + 2 * (heads // 2) + steps,)),
        ],
        compiler_params=params(24),
        cost_estimate=pl.CostEstimate(
            flops=flops, bytes_accessed=16000000, transcendentals=heads * 512 * 640
        ),
        name="attend",
    )(
        lengths,
        in_hbm(tokens),
        gain.astype(jnp.float32)[None],
        in_hbm(w_query),
        in_hbm(w_key),
        in_hbm(w_value),
        in_hbm(w_out),
        table,
    )


def attend_back_pair(
    pair, hg_ref, q_ref, k_ref, v_ref, mixed_ref, long_ref, short_ref, grads_ref, tiles_ref, far_ref, sg_ref,
):
    short_tok = SHORT_DEV * SHORT_LEN
    lane = lax.broadcasted_iota(jnp.int32, (1, 128), 1)
    lanes = pl.ds(pl.multiple_of(pair * 128, 128), 128)
    blocks = LONG_LEN // 128
    heads_grad = hg_ref[:, lanes]
    products = heads_grad.astype(jnp.float32) * mixed_ref[:, lanes].astype(jnp.float32)
    q_t = jnp.transpose(q_ref[:, lanes])
    hg_t = jnp.transpose(heads_grad)
    qg = []
    kg_t = []
    vg_t = []
    for sub in range(2):
        head = pair * 2 + sub
        own = (lane >= 64) == (sub == 1)
        rows_t = slice(64 * sub, 64 * sub + 64)
        masked = jnp.where(own, heads_grad, 0)
        delta = jnp.sum(jnp.where(own, products, 0.0), axis=1, keepdims=True)
        grads = [
            dot_nt(masked[block * 128 : block * 128 + 128], v_ref[block * 128 : block * 128 + 128, lanes])
            for block in range(SHORT_DEV)
        ]
        probs = short_ref[head]
        part = probs.astype(jnp.float32) * (jnp.concatenate(grads, axis=0) - delta[:short_tok])
        same = part[:128]
        for block in range(1, SHORT_DEV):
            same = same + part[block * 128 : block * 128 + 128]
        part = part.astype(jnp.bfloat16)
        qg_parts = []
        kg_parts = []
        vg_parts = []
        for block in range(SHORT_DEV):
            rows = slice(block * 128, block * 128 + 128)
            qg_parts.append(dot_nn(part[rows], k_ref[rows, lanes]))
            kg_parts.append(dot_nn(q_t[rows_t, rows], part[rows]))
            vg_parts.append(dot_nn(hg_t[rows_t, rows], probs[rows]))
        above = jnp.zeros((128, 128), jnp.float32)
        below = above
        far_above = above
        far_below = above
        probs = long_ref[head]
        part = probs.astype(jnp.float32) * (
            dot_nt(masked[short_tok:], v_ref[short_tok:, lanes]) - delta[short_tok:]
        )
        for block in range(blocks):
            for other in range(blocks):
                piece = part[block * 128 : block * 128 + 128, other * 128 : other * 128 + 128]
                if other == block:
                    same = same + piece
                elif other == block + 1:
                    above = above + piece
                elif other == block - 1:
                    below = below + piece
                elif other > block:
                    far_above = far_above + piece
                else:
                    far_below = far_below + piece
        sg_ref[...] = part.astype(jnp.bfloat16)
        qg_parts.append(dot_nn(sg_ref[...], k_ref[short_tok:, lanes]))
        kg_parts.append(dot_nn(q_t[rows_t, short_tok:], sg_ref[...]))
        vg_parts.append(dot_nn(hg_t[rows_t, short_tok:], probs))
        qg.append(jnp.concatenate(qg_parts, axis=0))
        kg_t.append(jnp.concatenate(kg_parts, axis=1))
        vg_t.append(jnp.concatenate(vg_parts, axis=1))
        tiles_ref[head, :, 0:128] = same
        tiles_ref[head, :, 128:256] = above
        tiles_ref[head, :, 256:384] = below
        far_ref[head, 0:1, :] = jnp.sum(far_above, axis=0, keepdims=True)
        far_ref[head, 1:2, :] = jnp.sum(far_below, axis=0, keepdims=True)
    width = q_ref.shape[1]
    grads_ref[:, lanes] = (jnp.where(lane < 64, qg[0], qg[1]) * 0.125).astype(jnp.bfloat16)
    for index, whole in ((1, kg_t), (2, vg_t)):
        place = pl.ds(pl.multiple_of(index * width + pair * 128, 128), 128)
        grads_ref[:, place] = jnp.transpose(jnp.concatenate(whole, axis=0).astype(jnp.bfloat16))


def diagonals(tiles):
    tile = jnp.concatenate(
        [tiles[:, 0:256], jnp.zeros((128, 128), jnp.float32), tiles[:, 256:384]], axis=1
    )
    span = 64
    while span:
        tile = tile[:span] + pltpu.roll(tile[span:], 512 - span, 1)
        span //= 2
    return tile


def table_from(diag, bucket_count):
    lane = jnp.arange(768, dtype=jnp.int32)
    offset = jnp.where(lane < 256, lane, lane - 512)
    offset = jnp.where(lane >= 640, -256, jnp.where(lane >= 512, 256, offset))
    hot = (diagonal_buckets(offset)[:, None] == jnp.arange(bucket_count)[None, :]).astype(jnp.float32)
    return lax.dot_general(
        hot, diag, (((0,), (1,)), ((), ())), precision=highest, preferred_element_type=jnp.float32
    )


def dispatch_rows(send_ref, slot_row, half_rows):
    slots = send_ref.shape[0]
    tok_count = slot_row.shape[1]
    span = slots
    for base in range(0, slots, span):
        place = lax.broadcasted_iota(jnp.int32, (span, tok_count), 0) + base
        hot = jnp.where(place == slot_row, 1.0, 0.0).astype(jnp.bfloat16)
        send_ref[base : base + span, :] = dot_nn(hot, half_rows).astype(jnp.bfloat16)


def half_lanes(core, half):
    return pl.ds(pl.multiple_of(core * half, half), half)


def route_kernel(
    capacity, where_ref, routes_hbm, grad_hbm, row_hbm, send_ref, routes_ref, grad_ref, row_ref, in_sems,
    out_sem,
):
    tok_count = routes_ref.shape[1]
    slots, half = send_ref.shape
    experts = slots // capacity
    fetch, copy = start_copies(
        [
            (routes_hbm, routes_ref, in_sems.at[0]),
            (grad_hbm.at[:, half_lanes(where_ref[0], half)], grad_ref, in_sems.at[1]),
        ]
    )
    fetch.wait()
    routes = routes_ref[...]
    expert = lax.broadcasted_iota(jnp.int32, (experts, tok_count), 0)
    lane = lax.broadcasted_iota(jnp.int32, (1, tok_count), 1)
    hot = jnp.where(expert == routes, 1.0, 0.0)
    total = hot
    step = 1
    while step < tok_count:
        total = total + jnp.where(lane >= step, pltpu.roll(total, step, 1), 0.0)
        step *= 2
    before = jnp.sum(hot * total, axis=0, keepdims=True).astype(jnp.int32) - 1
    slot = jnp.where(before < capacity, routes * capacity + before, slots)
    row_ref[...] = slot
    out = pltpu.make_async_copy(row_ref, row_hbm, out_sem)
    out.start()
    copy.wait()
    dispatch_rows(send_ref, slot, grad_ref[...])
    out.wait()


def route(where, routes, out_grad, experts, capacity):
    tok_count, width = out_grad.shape
    slots = experts * capacity
    return pl.pallas_call(
        partial(route_kernel, capacity),
        out_shape=[
            hbm_out((1, tok_count), jnp.int32),
            jax.ShapeDtypeStruct((slots, width // 2), jnp.bfloat16),
        ],
        in_specs=[
            pl.BlockSpec(memory_space=pltpu.SMEM),
            pl.BlockSpec(memory_space=pltpu.HBM),
            pl.BlockSpec(memory_space=pltpu.HBM),
        ],
        out_specs=[pl.BlockSpec(memory_space=pltpu.HBM)] + vmem(1),
        scratch_shapes=[
            pltpu.VMEM((1, tok_count), jnp.int32),
            pltpu.VMEM((tok_count, width // 2), jnp.bfloat16),
            pltpu.VMEM((1, tok_count), jnp.int32),
            pltpu.SemaphoreType.DMA((2,)),
            pltpu.SemaphoreType.DMA,
        ],
        compiler_params=params(28),
        cost_estimate=pl.CostEstimate(
            flops=slots * tok_count * width, bytes_accessed=4000000, transcendentals=0
        ),
        name="route",
    )(where, in_hbm(routes.reshape(1, tok_count)), in_hbm(out_grad))


def second_kernel(
    where_ref, tokens_hbm, own_ref, other_ref, gain_ref, row_hbm, residual_hbm, send_ref, tokens_ref,
    row_ref, residual_ref, second_ref, in_sems, out_sems,
):
    tile = 256
    tok_count = tokens_ref.shape[0]
    half = send_ref.shape[1]
    tiles_rows = [slice(start, start + tile) for start in range(0, tok_count, tile)]
    copies = start_copies(
        [
            (tokens_hbm.at[rows], tokens_ref.at[rows], in_sems.at[step])
            for step, rows in enumerate(tiles_rows)
        ]
        + [(row_hbm, row_ref, in_sems.at[len(tiles_rows)])]
    )
    outs = []
    gain = gain_ref[...]
    for step, rows in enumerate(tiles_rows):
        attn = own_ref[rows, :].astype(jnp.float32) + other_ref[rows, :].astype(jnp.float32)
        copies[step].wait()
        residual = tokens_ref[rows, :].astype(jnp.float32) + attn
        residual_ref[rows, :] = residual
        outs += start_copies([(residual_ref.at[rows], residual_hbm.at[rows], out_sems.at[step])])
        second_ref[rows, :] = (residual * inverse_rms(residual) * gain).astype(jnp.bfloat16)
    copies[-1].wait()
    dispatch_rows(send_ref, row_ref[...], second_ref[:, half_lanes(where_ref[0], half)])
    for copy in outs:
        copy.wait()


def second_rows(where, tokens, own, other, gain, slot_row, slots):
    tok_count, width = tokens.shape
    steps = tok_count // 256
    hbm = pl.BlockSpec(memory_space=pltpu.HBM)
    return pl.pallas_call(
        second_kernel,
        out_shape=[
            hbm_out((tok_count, width), jnp.float32),
            jax.ShapeDtypeStruct((slots, width // 2), jnp.bfloat16),
        ],
        in_specs=[pl.BlockSpec(memory_space=pltpu.SMEM), hbm] + vmem(3) + [hbm],
        out_specs=[hbm] + vmem(1),
        scratch_shapes=[
            pltpu.VMEM((tok_count, width), jnp.bfloat16),
            pltpu.VMEM((1, tok_count), jnp.int32),
            pltpu.VMEM((tok_count, width), jnp.float32),
            pltpu.VMEM((tok_count, width), jnp.bfloat16),
            pltpu.SemaphoreType.DMA((steps + 1,)),
            pltpu.SemaphoreType.DMA((steps,)),
        ],
        compiler_params=params(28),
        cost_estimate=pl.CostEstimate(
            flops=slots * tok_count * width, bytes_accessed=13000000, transcendentals=0
        ),
        name="second",
    )(where, in_hbm(tokens), own, other, gain.astype(jnp.float32)[None], in_hbm(slot_row))


def hidden_grad_kernel(where_ref, own_ref, other_ref, outer_ref, out_ref, whole_ref):
    half = own_ref.shape[1]
    core = where_ref[0]
    whole_ref[:, half_lanes(core, half)] = own_ref[...]
    whole_ref[:, half_lanes(1 - core, half)] = other_ref[...]
    out_ref[...] = dot_nt(whole_ref[...], outer_ref[...]).astype(jnp.bfloat16)


def hidden_grad_of(where, own, other, outer):
    slots, half = own.shape
    hidden = outer.shape[0]
    tile = 256
    rows = pl.BlockSpec((tile, half), lambda step: (step, 0))
    return pl.pallas_call(
        hidden_grad_kernel,
        grid=(slots // tile,),
        out_shape=hbm_out((slots, hidden), jnp.bfloat16),
        in_specs=[pl.BlockSpec(memory_space=pltpu.SMEM), rows, rows] + vmem(1),
        out_specs=pl.BlockSpec((tile, hidden), lambda step: (step, 0)),
        scratch_shapes=[pltpu.VMEM((tile, 2 * half), jnp.bfloat16)],
        compiler_params=params(),
        cost_estimate=pl.CostEstimate(
            flops=4 * slots * half * hidden, bytes_accessed=12000000, transcendentals=0
        ),
        name="hidden_grad",
    )(where, own, other, outer)


def gate_of(rows, router, index):
    experts = router.shape[1]
    logits = dot_nn(rows, router)
    exp_logit = jnp.exp(logits - jnp.max(logits, axis=1, keepdims=True))
    probs = exp_logit * (1.0 / jnp.sum(exp_logit, axis=1, keepdims=True))
    hit = jnp.where(lax.broadcasted_iota(jnp.int32, (1, experts), 1) == index, 1.0, 0.0)
    return probs, hit, jnp.sum(probs * hit, axis=1, keepdims=True)


def expert_kernel(
    where_ref,
    own_ref,
    other_ref,
    hg_ref,
    inner_ref,
    router_ref,
    hidden_ref,
    pre_grad_ref,
    keep_ref,
    send_ref,
    logit_ref,
    arrived_ref,
    whole_ref,
):
    core = where_ref[0]
    tile, half = own_ref.shape
    own_lanes = half_lanes(core, half)
    other_lanes = half_lanes(1 - core, half)
    arrived_ref[:, own_lanes] = own_ref[...]
    arrived_ref[:, other_lanes] = other_ref[...]
    arrived = arrived_ref[...]
    probs, hit, gate = gate_of(arrived, router_ref[...], where_ref[1])
    curve = 0.7978845608028654
    gate_grad = jnp.zeros((tile, 1), jnp.float32)
    back = jnp.zeros((tile, 2 * half), jnp.float32)
    chunk = 512
    for start in range(0, hg_ref.shape[1], chunk):
        cols = slice(start, start + chunk)
        pre = dot_nn(arrived, inner_ref[:, cols])
        square = pre * pre
        share = 0.5 + 0.5 * jnp.tanh(pre * (curve + (curve * 0.044715) * square))
        hidden_ref[:, cols] = (pre * share).astype(jnp.bfloat16)
        passed = share * hg_ref[:, cols].astype(jnp.float32)
        gate_grad = gate_grad + jnp.sum(pre * passed, axis=1, keepdims=True)
        bend = pre * (2.0 * curve + (6.0 * curve * 0.044715) * square)
        pre_grad = ((gate * passed) * (1.0 + (1.0 - share) * bend)).astype(jnp.bfloat16)
        pre_grad_ref[:, cols] = pre_grad
        back = back + dot_nt(pre_grad, inner_ref[:, cols])
    logit = (probs * (gate_grad * (hit - gate))).astype(jnp.bfloat16)
    logit_ref[...] = logit
    whole_ref[...] = back + dot_nt(logit, router_ref[...])
    send_ref[...] = whole_ref[:, other_lanes].astype(jnp.bfloat16)
    keep_ref[...] = whole_ref[:, own_lanes]


def expert(where, own, other, hidden_grad, inner, router):
    slots, half = own.shape
    width, hidden = inner.shape
    experts = router.shape[1]
    tile = 256
    halves = pl.BlockSpec((tile, half), lambda step: (step, 0))
    units = pl.BlockSpec((tile, hidden), lambda step: (step, 0))
    return pl.pallas_call(
        expert_kernel,
        grid=(slots // tile,),
        out_shape=[
            hbm_out((slots, hidden), jnp.bfloat16),
            hbm_out((slots, hidden), jnp.bfloat16),
            jax.ShapeDtypeStruct((slots, half), jnp.float32),
            jax.ShapeDtypeStruct((slots, half), jnp.bfloat16),
            hbm_out((slots, experts), jnp.bfloat16),
        ],
        in_specs=[
            pl.BlockSpec(memory_space=pltpu.SMEM),
            halves,
            halves,
            units,
            pl.BlockSpec(inner.shape, lambda step: (0, 0), pipeline_mode=pl.Buffered(1)),
        ]
        + vmem(1),
        out_specs=[
            units,
            units,
            halves,
            halves,
            pl.BlockSpec((tile, experts), lambda step: (step, 0)),
        ],
        scratch_shapes=[
            pltpu.VMEM((tile, width), jnp.bfloat16),
            pltpu.VMEM((tile, width), jnp.float32),
        ],
        compiler_params=params(),
        cost_estimate=pl.CostEstimate(
            flops=4 * slots * width * hidden, bytes_accessed=20000000, transcendentals=slots * hidden
        ),
        name="expert",
    )(where, own, other, in_hbm(hidden_grad), in_hbm(inner), router)


def expert_out_kernel(
    where_ref, hidden_ref, own_ref, other_ref, logit_ref, row_ref, outer_ref, keep_ref, send_ref, router_ref,
    col_ref, whole_ref,
):
    core = where_ref[0]
    half = keep_ref.shape[1]
    own_lanes = half_lanes(core, half)
    other_lanes = half_lanes(1 - core, half)
    whole_ref[...] = dot_nn(hidden_ref[...], outer_ref[...])
    send_ref[...] = whole_ref[:, other_lanes].astype(jnp.bfloat16)
    keep_ref[...] = whole_ref[:, own_lanes]

    @pl.when(pl.program_id(0) == 0)
    def _():
        router_ref[...] = jnp.zeros_like(router_ref)
        wide = jnp.broadcast_to(row_ref[...].astype(jnp.float32), (128, row_ref.shape[1]))
        col_ref[...] = jnp.transpose(wide).astype(jnp.int32)

    router_ref[:, own_lanes] += contract_rows(logit_ref[...], own_ref[...])
    router_ref[:, other_lanes] += contract_rows(logit_ref[...], other_ref[...])


def expert_out_of(where, hidden, own, other, logit_grad, slot_row, outer):
    slots, units = hidden.shape
    tok_count = slot_row.shape[1]
    width = outer.shape[1]
    experts = logit_grad.shape[1]
    half = width // 2
    tile = 256
    halves = pl.BlockSpec((tile, half), lambda step: (step, 0))
    return pl.pallas_call(
        expert_out_kernel,
        grid=(slots // tile,),
        out_shape=[
            jax.ShapeDtypeStruct((slots, half), jnp.float32),
            jax.ShapeDtypeStruct((slots, half), jnp.bfloat16),
            hbm_out((experts, width), jnp.float32),
            hbm_out((tok_count, 128), jnp.int32),
        ],
        in_specs=[
            pl.BlockSpec(memory_space=pltpu.SMEM),
            pl.BlockSpec((tile, units), lambda step: (step, 0)),
            halves,
            halves,
            pl.BlockSpec((tile, experts), lambda step: (step, 0)),
            pl.BlockSpec((1, tok_count), lambda step: (0, 0)),
        ]
        + vmem(1),
        out_specs=[
            halves,
            halves,
            pl.BlockSpec((experts, width), lambda step: (0, 0)),
            pl.BlockSpec((tok_count, 128), lambda step: (0, 0)),
        ],
        scratch_shapes=[pltpu.VMEM((tile, width), jnp.float32)],
        compiler_params=params(),
        cost_estimate=pl.CostEstimate(
            flops=2 * slots * width * units, bytes_accessed=9000000, transcendentals=0
        ),
        name="expert_out",
    )(
        where, in_hbm(hidden), in_hbm(own), in_hbm(other), in_hbm(logit_grad), in_hbm(slot_row), outer
    )


def expert_grads_kernel(
    where_ref,
    own_hbm,
    other_hbm,
    grad_own_hbm,
    grad_other_hbm,
    hidden_ref,
    pre_grad_ref,
    router_ref,
    inner_grad_ref,
    outer_grad_ref,
    arrived_ref,
    gated_ref,
    sems,
):
    core = where_ref[0]
    half = own_hbm.shape[1]
    own_lanes = half_lanes(core, half)
    other_lanes = half_lanes(1 - core, half)

    @pl.when(pl.program_id(0) == 0)
    def _():
        copies = [
            pltpu.make_async_copy(own_hbm, arrived_ref.at[:, own_lanes], sems.at[0]),
            pltpu.make_async_copy(other_hbm, arrived_ref.at[:, other_lanes], sems.at[1]),
            pltpu.make_async_copy(grad_own_hbm, gated_ref.at[:, own_lanes], sems.at[2]),
            pltpu.make_async_copy(grad_other_hbm, gated_ref.at[:, other_lanes], sems.at[3]),
        ]
        for copy in copies:
            copy.start()
        for copy in copies:
            copy.wait()
        gate = gate_of(arrived_ref[...], router_ref[...], where_ref[1])[2]
        gated_ref[...] = (gate * gated_ref[...].astype(jnp.float32)).astype(jnp.bfloat16)

    outer_grad_ref[...] = contract_rows(hidden_ref[...], gated_ref[...])
    inner_grad_ref[...] = contract_rows(arrived_ref[...], pre_grad_ref[...])


def expert_grads(where, own, other, grad_own, grad_other, hidden, pre_grad, router):
    slots, half = own.shape
    units = hidden.shape[1]
    width = router.shape[0]
    tile = 256
    hbm = pl.BlockSpec(memory_space=pltpu.HBM)
    whole = lambda shape: pl.BlockSpec(shape, lambda step: (0, 0))
    cols = pl.BlockSpec((slots, tile), lambda step: (0, step))
    return pl.pallas_call(
        expert_grads_kernel,
        grid=(units // tile,),
        out_shape=[
            hbm_out((width, units), jnp.float32),
            hbm_out((units, width), jnp.float32),
        ],
        in_specs=[
            pl.BlockSpec(memory_space=pltpu.SMEM),
            hbm,
            hbm,
            hbm,
            hbm,
            cols,
            cols,
            whole(router.shape),
        ],
        out_specs=[
            pl.BlockSpec((width, tile), lambda step: (0, step)),
            pl.BlockSpec((tile, width), lambda step: (step, 0)),
        ],
        scratch_shapes=[
            pltpu.VMEM((slots, width), jnp.bfloat16),
            pltpu.VMEM((slots, width), jnp.bfloat16),
            pltpu.SemaphoreType.DMA((4,)),
        ],
        compiler_params=params(24),
        cost_estimate=pl.CostEstimate(
            flops=4 * slots * width * units, bytes_accessed=22000000, transcendentals=0
        ),
        name="expert_grads",
    )(
        where,
        in_hbm(own),
        in_hbm(other),
        in_hbm(grad_own),
        in_hbm(grad_other),
        in_hbm(hidden),
        in_hbm(pre_grad),
        router,
    )


def output_kernel(
    capacity, where_ref, col_ref, returned_ref, residual_ref, gain_ref, router_ref, out_ref
):
    slots, half = returned_ref.shape
    tile = residual_ref.shape[0]
    experts = router_ref.shape[1]
    col = col_ref[:, :1]
    place = lax.broadcasted_iota(jnp.int32, (tile, slots), 1)
    hot = jnp.where(place == col, 1.0, 0.0).astype(jnp.bfloat16)
    token_out = dot_nn(hot, returned_ref[...])
    residual = residual_ref[...]
    second = (residual * inverse_rms(residual) * gain_ref[...]).astype(jnp.bfloat16)
    logits = dot_nn(second, router_ref[...])
    exp_logit = jnp.exp(logits - jnp.max(logits, axis=1, keepdims=True))
    first = lax.broadcasted_iota(jnp.int32, (1, experts), 1) * capacity
    hit = jnp.where((col >= first) & (col < first + capacity), exp_logit, 0.0)
    gate = jnp.sum(hit, axis=1, keepdims=True) / jnp.sum(exp_logit, axis=1, keepdims=True)
    own = residual_ref[:, half_lanes(where_ref[0], half)]
    out_ref[...] = (own + gate * token_out).astype(jnp.bfloat16)


def output_of(where, slot_col, returned, residual, gain, router, capacity):
    tok_count, width = residual.shape
    slots, half = returned.shape
    tile = 256
    whole = lambda shape: pl.BlockSpec(shape, lambda step: (0, 0))
    return pl.pallas_call(
        partial(output_kernel, capacity),
        grid=(tok_count // tile,),
        out_shape=jax.ShapeDtypeStruct((tok_count, half), jnp.bfloat16),
        in_specs=[
            pl.BlockSpec(memory_space=pltpu.SMEM),
            pl.BlockSpec((tile, 128), lambda step: (step, 0)),
            whole(returned.shape),
            pl.BlockSpec((tile, width), lambda step: (step, 0)),
            whole((1, width)),
            whole(router.shape),
        ],
        out_specs=pl.BlockSpec((tile, half), lambda step: (step, 0)),
        compiler_params=params(),
        cost_estimate=pl.CostEstimate(
            flops=2 * tok_count * half * slots, bytes_accessed=6000000, transcendentals=0
        ),
        name="output",
    )(
        where, in_hbm(slot_col), in_hbm(returned), in_hbm(residual), gain.astype(jnp.float32)[None], router
    )


def normed_back_kernel(grads_ref, wq_ref, wk_ref, wv_ref, out_ref):
    own = wq_ref.shape[1]
    out_ref[...] = (
        dot_nt(grads_ref[:, :own], wq_ref[...])
        + dot_nt(grads_ref[:, own : 2 * own], wk_ref[...])
        + dot_nt(grads_ref[:, 2 * own :], wv_ref[...])
    ).astype(jnp.bfloat16)


def normed_back(grads, w_query, w_key, w_value):
    tok_count = grads.shape[0]
    width, own = w_query.shape
    tile = 256
    whole = pl.BlockSpec((width, own), lambda step: (0, 0))
    return pl.pallas_call(
        normed_back_kernel,
        grid=(tok_count // tile,),
        out_shape=jax.ShapeDtypeStruct((tok_count, width), jnp.bfloat16),
        in_specs=[pl.BlockSpec((tile, 3 * own), lambda step: (step, 0))] + [whole] * 3,
        out_specs=pl.BlockSpec((tile, width), lambda step: (step, 0)),
        compiler_params=params(),
        cost_estimate=pl.CostEstimate(
            flops=6 * tok_count * own * width, bytes_accessed=6000000, transcendentals=0
        ),
        name="normed_back",
    )(*(in_hbm(array) for array in (grads, w_query, w_key, w_value)))


def input_back_kernel(tokens_ref, own_ref, other_ref, gain_ref, residual_ref, out_ref):
    ybar = own_ref[...].astype(jnp.float32) + other_ref[...].astype(jnp.float32)
    values = tokens_ref[...].astype(jnp.float32)
    scale = inverse_rms(values)
    scaled = values * scale
    pulled = ybar * gain_ref[...]
    out_ref[...] = residual_ref[...] + scale * (
        pulled - scaled * jnp.mean(pulled * scaled, axis=1, keepdims=True)
    )


def input_back(tokens, own, other, gain, residual_grad):
    tok_count, width = tokens.shape
    tile = 256
    rows = pl.BlockSpec((tile, width), lambda step: (step, 0))
    return pl.pallas_call(
        input_back_kernel,
        grid=(tok_count // tile,),
        out_shape=jax.ShapeDtypeStruct((tok_count, width), jnp.float32),
        in_specs=[rows, rows, rows, pl.BlockSpec((1, width), lambda step: (0, 0)), rows],
        out_specs=rows,
        compiler_params=params(),
        cost_estimate=pl.CostEstimate(
            flops=10 * tok_count * width, bytes_accessed=11000000, transcendentals=0
        ),
        name="input_back",
    )(in_hbm(tokens), own, other, gain.astype(jnp.float32)[None], in_hbm(residual_grad))


def back_kernel(
    bits_ref,
    where_ref,
    col_hbm,
    own_hbm,
    other_hbm,
    residual_hbm,
    grad_hbm,
    wo_hbm,
    q_hbm,
    k_hbm,
    v_hbm,
    mixed_hbm,
    long_hbm,
    short_hbm,
    normed_hbm,
    wq_hbm,
    wk_hbm,
    wv_hbm,
    gain_one_ref,
    gain_two_ref,
    router_ref,
    out_hbm,
    grads_hbm,
    sent_a,
    sent_b,
    sent_c,
    kept_a,
    kept_b,
    kept_c,
    col_ref,
    back_ref,
    residual_ref,
    grad_ref,
    wo_ref,
    q_ref,
    k_ref,
    v_ref,
    mixed_ref,
    long_ref,
    short_ref,
    normed_ref,
    wq_ref,
    wk_ref,
    wv_ref,
    attn_ref,
    heads_ref,
    grads_ref,
    sg_ref,
    tiles_ref,
    far_ref,
    stack_ref,
    small_ref,
    packed_ref,
    total_ref,
    in_sems,
    out_sems,
):
    tok_count, width = residual_ref.shape
    slots, half = own_hbm.shape
    own = mixed_ref.shape[1]
    experts = router_ref.shape[0]
    pairs = own // 128
    tile = 512
    steps = tok_count // tile
    core = where_ref[0]
    first = [
        (own_hbm, back_ref.at[:, half_lanes(core, half)]),
        (other_hbm, back_ref.at[:, half_lanes(1 - core, half)]),
        (col_hbm, col_ref),
        (wo_hbm, wo_ref),
    ]
    tiles = []
    for start in range(0, tok_count, tile):
        rows = slice(start, start + tile)
        tiles.append((residual_hbm.at[rows], residual_ref.at[rows]))
        tiles.append((grad_hbm.at[rows], grad_ref.at[rows]))
    attention = [(q_hbm, q_ref), (k_hbm, k_ref), (v_hbm, v_ref), (mixed_hbm, mixed_ref), (short_hbm, short_ref)]
    for pair in range(pairs):
        both = slice(pair * 2, pair * 2 + 2)
        attention.append((long_hbm.at[both], long_ref.at[both]))
    weights = [(normed_hbm, normed_ref), (wq_hbm, wq_ref), (wk_hbm, wk_ref), (wv_hbm, wv_ref)]
    copies = start_copies(
        [
            (source, target, in_sems.at[index])
            for index, (source, target) in enumerate(first + tiles + attention + weights)
        ]
    )
    base = len(first) + len(tiles)
    outs = []

    for copy in copies[: len(first)]:
        copy.wait()
    gain_two = gain_two_ref[...]
    place = lax.broadcasted_iota(jnp.int32, (tile, slots), 1)

    def tile_out(step):
        rows = pl.ds(pl.multiple_of(step * tile, tile), tile)
        return pltpu.make_async_copy(residual_ref.at[rows], out_hbm.at[rows], out_sems.at[step])

    def one_tile(step, gain_two_grad):
        rows = pl.ds(pl.multiple_of(step * tile, tile), tile)
        at = len(first) + 2 * step
        pltpu.make_async_copy(residual_hbm.at[rows], residual_ref.at[rows], in_sems.at[at]).wait()
        pltpu.make_async_copy(grad_hbm.at[rows], grad_ref.at[rows], in_sems.at[at + 1]).wait()
        hot = jnp.where(place == col_ref[rows, :][:, :1], 1.0, 0.0).astype(jnp.bfloat16)
        ybar = dot_nn(hot, back_ref[...])
        values = residual_ref[rows, :]
        scale = inverse_rms(values)
        scaled = values * scale
        pulled = ybar * gain_two
        back = scale * (pulled - scaled * jnp.mean(pulled * scaled, axis=1, keepdims=True))
        out = back + grad_ref[rows, :].astype(jnp.float32)
        residual_ref[rows, :] = out
        attn = out.astype(jnp.bfloat16)
        attn_ref[rows, :] = attn
        heads_ref[rows, :] = dot_nt(attn, wo_ref[...]).astype(jnp.bfloat16)
        tile_out(step).start()
        return gain_two_grad + jnp.sum(ybar * scaled, axis=0, keepdims=True)

    gain_two_grad = lax.fori_loop(0, steps, one_tile, jnp.zeros((1, width), jnp.float32))
    outs += [tile_out(step) for step in range(steps)]

    for copy in copies[base : base + 5]:
        copy.wait()

    def one_pair(pair, carry):
        both = pl.ds(pair * 2, 2)
        pltpu.make_async_copy(long_hbm.at[both], long_ref.at[both], in_sems.at[base + 5 + pair]).wait()
        attend_back_pair(
            pair, heads_ref, q_ref, k_ref, v_ref, mixed_ref, long_ref, short_ref, grads_ref, tiles_ref, far_ref,
            sg_ref,
        )
        return carry

    lax.fori_loop(0, pairs, one_pair, 0, unroll=True)
    outs += start_copies([(grads_ref, grads_hbm, out_sems.at[steps])])

    grad = contract_rows(mixed_ref[...], attn_ref[...]).astype(jnp.bfloat16)
    for part in range(width // own):
        at = 3 * width + part * own
        stack_ref[at : at + own, :] = grad[:, part * own : part * own + own]
    small_ref[0:experts, :] = router_ref[...]
    small_ref[experts + 1 : experts + 2, :] = gain_two_grad
    for head in range(2 * pairs):
        row = experts + 2 + head
        small_ref[row : row + 1, 0:512] = diagonals(tiles_ref[head])
        small_ref[row : row + 1, 512:640] = far_ref[head, 0:1, :]
        small_ref[row : row + 1, 640:768] = far_ref[head, 1:2, :]
    for copy in copies[base + 5 + pairs :]:
        copy.wait()
    rows = stack_ref.shape[0] // 3
    span = rows // 2

    def send_part(part, sent, kept):
        mine = bits_ref[part]
        sent_rows = pl.ds(pl.multiple_of(part * rows + (1 - mine) * span, span), span)
        kept_rows = pl.ds(pl.multiple_of(part * rows + mine * span, span), span)
        return start_copies(
            [
                (stack_ref.at[sent_rows], sent.at[:span], out_sems.at[steps + 4 + 2 * part]),
                (stack_ref.at[kept_rows], kept, out_sems.at[steps + 5 + 2 * part]),
            ]
        )

    span_rows = 384

    def head_rows(block, carry):
        start = pl.multiple_of(block * span_rows, span_rows)
        piece = pl.ds(start, span_rows)
        grad = contract_rows(normed_ref[:, piece], grads_ref[...])
        total = jnp.zeros((span_rows, 1), jnp.float32)
        for index, w_ref in enumerate((wq_ref, wk_ref, wv_ref)):
            part = grad[:, index * own : index * own + own]
            total = total + jnp.sum(part * w_ref[piece, :].astype(jnp.float32), axis=1, keepdims=True)
            stack_ref[pl.ds(pl.multiple_of(index * width + start, span_rows), span_rows), :] = part.astype(jnp.bfloat16)
        total_ref[piece, :] = jnp.broadcast_to(total, (span_rows, 128))
        return carry

    lax.fori_loop(0, width // span_rows, head_rows, 0, unroll=True)
    for part, (sent, kept) in enumerate(((sent_a, kept_a), (sent_b, kept_b))):
        outs += send_part(part, sent, kept)
    outs += send_part(2, sent_c, kept_c)
    wide = jnp.transpose(total_ref[...])
    small_ref[experts : experts + 1, :] = wide[:1, :] / gain_one_ref[...]
    small = small_ref[...]
    packed_ref[...] = jnp.concatenate([small[:, :own], small[:, own:]], axis=0).astype(jnp.bfloat16)
    outs += start_copies([(packed_ref, sent_a.at[span:], out_sems.at[steps + 3])])
    for copy in outs:
        copy.wait()


def back_pass(
    bits, where, slot_col, back_own, back_other, residual, out_grad, w_out, query_rows, key_rows,
    value_rows, mixed, long_probs, short_probs, normed, w_query, w_key, w_value, gain_one, gain_two,
    router_part,
):
    tok_count, width = normed.shape
    own = mixed.shape[1]
    slots, half = back_own.shape
    heads = long_probs.shape[0]
    count = router_part.shape[0] + 2 + heads
    span = 4 * width // 6
    tile = 512
    steps = tok_count // tile
    half_rows = hbm_out((span, own), jnp.bfloat16)
    pinned = (residual, out_grad, w_out, query_rows, key_rows, value_rows, mixed, long_probs, short_probs, normed,
              w_query, w_key, w_value)
    hbm = pl.BlockSpec(memory_space=pltpu.HBM)
    smem = pl.BlockSpec(memory_space=pltpu.SMEM)

    def scratch(array):
        return pltpu.VMEM(array.shape, array.dtype)

    flops = 2 * tok_count * width * (slots + 5 * own) + 10 * heads * (512 * 512 + 512 * 128) * 64
    out = pl.pallas_call(
        back_kernel,
        out_shape=[
            hbm_out((tok_count, width), jnp.float32),
            hbm_out((tok_count, 3 * own), jnp.bfloat16),
            hbm_out((span + 2 * count, own), jnp.bfloat16),
        ]
        + [half_rows] * 5,
        in_specs=[smem, smem] + [hbm, hbm, pl.BlockSpec(memory_space=pl.ANY)] + [hbm] * 13 + vmem(3),
        out_specs=[hbm] * 8,
        scratch_shapes=[scratch(slot_col), pltpu.VMEM((slots, width), jnp.bfloat16)]
        + [scratch(array) for array in pinned]
        + [
            pltpu.VMEM((tok_count, width), jnp.bfloat16),
            pltpu.VMEM((tok_count, own), jnp.bfloat16),
            pltpu.VMEM((tok_count, 3 * own), jnp.bfloat16),
            pltpu.VMEM((LONG_LEN, LONG_LEN), jnp.bfloat16),
            pltpu.VMEM((heads, 128, 384), jnp.float32),
            pltpu.VMEM((heads, 2, 128), jnp.float32),
            pltpu.VMEM((4 * width, own), jnp.bfloat16),
            pltpu.VMEM((count, width), jnp.float32),
            pltpu.VMEM((2 * count, own), jnp.bfloat16),
            pltpu.VMEM((width, 128), jnp.float32),
            pltpu.SemaphoreType.DMA((2 * steps + 4 + 5 + heads // 2 + 4,)),
            pltpu.SemaphoreType.DMA((steps + 10,)),
        ],
        compiler_params=params(40),
        cost_estimate=pl.CostEstimate(flops=flops, bytes_accessed=25000000, transcendentals=0),
        name="back",
    )(
        bits,
        where,
        in_hbm(slot_col),
        in_hbm(back_own),
        back_other,
        *(in_hbm(array) for array in pinned),
        gain_one.astype(jnp.float32)[None],
        gain_two.astype(jnp.float32)[None],
        router_part,
    )
    return out[0], out[1], out[2:5], out[5:]


def added(left, right):
    return (left.astype(jnp.float32) + right.astype(jnp.float32)).astype(jnp.bfloat16)


def fold_kernel(bits_ref, *refs):
    kept, got, sent, keep = refs[0:3], refs[3:6], refs[7:10], refs[10:13]
    before = refs[6]
    for part in range(3):
        span = kept[part].shape[0] // 2
        mine = bits_ref[part]
        for ref, start in ((sent[part], (1 - mine) * span), (keep[part], mine * span)):
            rows = pl.ds(pl.multiple_of(start, span), span)
            ref[:span, :] = added(kept[part][rows, :], got[part][rows, :])
    rows = kept[0].shape[0]
    sent[0][rows // 2 :, :] = added(before[rows:, :], got[0][rows:, :])


def fold(bits, kept, got, before):
    rows, lanes = kept[0].shape
    extra = before.shape[0] - rows
    half = jax.ShapeDtypeStruct((rows // 2, lanes), jnp.bfloat16)
    out = pl.pallas_call(
        fold_kernel,
        out_shape=[jax.ShapeDtypeStruct((rows // 2 + extra, lanes), jnp.bfloat16)] + [half] * 5,
        in_specs=[pl.BlockSpec(memory_space=pltpu.SMEM)] + vmem(7),
        out_specs=vmem(6),
        compiler_params=params(16),
        name="fold",
    )(bits, *kept, *got, before)
    return out[:3], out[3:]


def pack_kernel(*refs):
    kept, got, before, out = refs[0:3], refs[3:6], refs[6], refs[7]
    rows = kept[0].shape[0]
    for part in range(3):
        out[part * rows : (part + 1) * rows, :] = added(kept[part][...], got[part][:rows, :])
    out[3 * rows :, :] = added(before[rows:, :], got[0][rows:, :])


def pack(kept, got, before):
    rows, lanes = kept[0].shape
    return pl.pallas_call(
        pack_kernel,
        out_shape=jax.ShapeDtypeStruct((2 * rows + before.shape[0], lanes), jnp.bfloat16),
        in_specs=vmem(7),
        out_specs=vmem(1)[0],
        compiler_params=params(16),
        name="pack",
    )(*kept, *got, before)


def unpack_kernel(own_ref, got_ref, *out):
    rows = out[0].shape[0]
    for part in range(3):
        piece = slice(part * rows, (part + 1) * rows)
        out[part][...] = added(own_ref[piece, :], got_ref[piece, :])
    out[3][...] = own_ref[3 * rows :, :].astype(jnp.float32) + got_ref[3 * rows :, :].astype(jnp.float32)


def unpack(own, got, rows):
    lanes = own.shape[1]
    out = pl.pallas_call(
        unpack_kernel,
        out_shape=[jax.ShapeDtypeStruct((rows, lanes), jnp.bfloat16)] * 3
        + [jax.ShapeDtypeStruct((own.shape[0] - 3 * rows, lanes), jnp.float32)],
        in_specs=vmem(2),
        out_specs=vmem(4),
        compiler_params=params(16),
        name="unpack",
    )(own, got)
    return out[:3], out[3]


def join_kernel(bits_ref, *refs):
    own, got, out = refs[0:3], refs[3:6], refs[6:9]
    for part in range(3):
        span = own[part].shape[0]
        mine = bits_ref[part]
        out[part][pl.ds(pl.multiple_of(mine * span, span), span), :] = own[part][...]
        out[part][pl.ds(pl.multiple_of((1 - mine) * span, span), span), :] = got[part][...]


def join(bits, own, got):
    return pl.pallas_call(
        join_kernel,
        out_shape=[jax.ShapeDtypeStruct((p.shape[0] * 2, p.shape[1]), p.dtype) for p in own],
        in_specs=[pl.BlockSpec(memory_space=pltpu.SMEM)] + vmem(6),
        out_specs=vmem(3),
        compiler_params=params(16),
        name="join",
    )(bits, *own, *got)


def finish_kernel(bits_ref, *refs):
    own, got = refs[0:3], refs[3:6]
    results = refs[6:10]
    held, sems = refs[10:14], refs[14]
    span = own[0].shape[0]
    rows = 2 * span
    width, lanes = held[0].shape
    copies = []
    for part in range(3):
        mine = bits_ref[part]
        first = jnp.where(mine == 0, own[part][...], got[part][...])
        second = jnp.where(mine == 0, got[part][...], own[part][...])
        for base, piece in ((part * rows, first), (part * rows + span, second)):
            for index in range(3 + width // lanes):
                start = index * width if index < 3 else 3 * width + (index - 3) * lanes
                size = width if index < 3 else lanes
                low = max(start, base)
                high = min(start + size, base + span)
                if low < high:
                    values = piece[low - base : high - base, :].astype(jnp.float32)
                    if index < 3:
                        held[index][low - start : high - start, :] = values
                    else:
                        place = (index - 3) * lanes
                        held[3][low - start : high - start, place : place + lanes] = values
        for index in range(4):
            last = (index + 1) * width - 1
            if part * rows <= last < (part + 1) * rows:
                copies += start_copies([(held[index], results[index], sems.at[index])])
    for copy in copies:
        copy.wait()


def finish(bits, own, got, width):
    lanes = own[0].shape[1]
    shapes = [(width, lanes)] * 3 + [(lanes, width)]
    return pl.pallas_call(
        finish_kernel,
        out_shape=[hbm_out(shape, jnp.float32) for shape in shapes],
        in_specs=[pl.BlockSpec(memory_space=pltpu.SMEM)] + vmem(6),
        out_specs=[pl.BlockSpec(memory_space=pltpu.HBM)] * 4,
        scratch_shapes=[pltpu.VMEM(shape, jnp.float32) for shape in shapes]
        + [pltpu.SemaphoreType.DMA((4,))],
        compiler_params=params(24),
        name="finish",
    )(bits, *own, *got)


def swap_heads(rows):
    return lax.ppermute(rows, "heads", [(0, 1), (1, 0)])


def trade(rows, bit):
    count = lax.axis_size("seq")
    return lax.ppermute(rows, "seq", [(i, i ^ (1 << bit)) for i in range(count)])


def together(*groups):
    return lax.optimization_barrier(groups)


def contract_rows(left, right):
    return lax.dot_general(
        left, right, (((0,), (0,)), ((), ())), preferred_element_type=jnp.float32
    )


def on_device(
    tokens,
    gain_attn,
    w_query,
    w_key,
    w_value,
    w_out,
    bias_table,
    gain_ffn,
    w_router,
    w_inner,
    w_outer,
    routes,
    seq_lengths,
    out_grad,
):
    tok_count, width = tokens.shape
    bucket_count = bias_table.shape[0]
    experts = w_router.shape[1]
    capacity = max(2, 5 * tok_count // (4 * experts))
    senders = lax.axis_size("seq")
    bits = list(range(senders.bit_length() - 1))
    slots = experts * capacity
    half = width // 2
    own = w_query.shape[1]
    where = jnp.stack([lax.axis_index("heads"), lax.axis_index("seq")]).astype(jnp.int32)

    def exchange(rows):
        return lax.all_to_all(
            rows.reshape(senders, capacity, half), "seq", split_axis=0, concat_axis=0, tiled=True
        ).reshape(slots, half)

    def summed(keep, send):
        return (keep + swap_heads(send).astype(jnp.float32)).astype(jnp.bfloat16)

    slot_row, grad_sent = route(where, routes, out_grad, experts, capacity)
    grad_sent, tokens = together(grad_sent, tokens)
    grad_own = exchange(grad_sent)
    attn_part, normed, query_rows, key_rows, value_rows, mixed, long_probs, short_probs = attend(
        seq_lengths, tokens, gain_attn, w_query, w_key, w_value, w_out, bias_table
    )
    residual, second_sent = second_rows(
        where, tokens, attn_part, swap_heads(attn_part), gain_ffn, slot_row, slots
    )
    second_sent, grad_own = together(second_sent, grad_own)
    arrived_own = exchange(second_sent)

    inner = w_inner[0]
    outer = w_outer[0]
    grad_other = swap_heads(grad_own)
    hidden_grad = hidden_grad_of(where, grad_own, grad_other, outer)
    arrived_own, hidden_grad = together(arrived_own, hidden_grad)
    arrived_other = swap_heads(arrived_own)
    hidden, pre_grad, keep, send, logit_grad = expert(
        where, arrived_own, arrived_other, hidden_grad, inner, w_router
    )
    back_sum, hidden = together(summed(keep, send), hidden)
    back_own = exchange(back_sum)
    out_keep, out_send, router_part, slot_col = expert_out_of(
        where, hidden, arrived_own, arrived_other, logit_grad, slot_row, outer
    )
    out_sum = summed(out_keep, out_send)
    router_half = lax.dynamic_slice_in_dim(
        router_part + swap_heads(router_part), where[0] * (experts // 2), experts // 2, 0
    )
    back_own, out_sum, router_half = together(back_own, out_sum, router_half)
    back_other = swap_heads(back_own)
    returned = exchange(out_sum)

    depth = len(bits) - 1
    turns = [bits[k * depth // 3 : depth] + bits[: k * depth // 3] for k in range(3)]
    place = lax.axis_index("seq")
    mine = [jnp.stack([(place >> turn[k]) & 1 for turn in turns]).astype(jnp.int32) for k in range(depth)]
    residual_grad, head_grads, sent, kept = back_pass(
        mine[0], where, slot_col, back_own, back_other, residual, out_grad, w_out, query_rows, key_rows,
        value_rows, mixed, long_probs, short_probs, normed, w_query, w_key, w_value, gain_attn, gain_ffn,
        router_half,
    )

    def trades(arrays, k):
        return [trade(array, turn[k]) for array, turn in zip(arrays, turns)]

    for k in range(depth):
        got = trades(sent, k)
        if k == 0:
            output = output_of(where, slot_col, returned, residual, gain_ffn, w_router, capacity)
            got, output, head_grads = together(got, output, head_grads)
        if k == 1:
            normed_part = normed_back(head_grads, w_query, w_key, w_value)
            got, normed_part = together(got, normed_part)
        if k + 1 < depth:
            sent, kept = fold(mine[k + 1], kept, got, sent[0])
    normed_other = swap_heads(normed_part)
    packed = pack(kept, got, sent[0])
    packed, normed_other, pre_grad = together(packed, normed_other, pre_grad)
    got = trade(packed, bits[-1])
    inner_grad, outer_grad = expert_grads(
        where, arrived_own, arrived_other, grad_own, grad_other, hidden, pre_grad, w_router
    )
    got, inner_grad = together(got, inner_grad)
    summed_parts, small = unpack(packed, got, kept[0].shape[0])
    small = jnp.concatenate([small[: small.shape[0] // 2], small[small.shape[0] // 2 :]], axis=1)
    small_other = swap_heads(small)
    for k in reversed(range(1, depth)):
        got = trades(summed_parts, k)
        if k == depth - 1:
            got, small = together(got, small)
        if k == 1:
            lower = where[0] == 0
            own_rows, other_rows = small[: experts // 2], small_other[: experts // 2]
            router_grad = jnp.concatenate(
                [jnp.where(lower, own_rows, other_rows), jnp.where(lower, other_rows, own_rows)], axis=0
            ).T
            gain_one_grad = small[experts // 2] + small_other[experts // 2]
            gain_two_grad = small[experts // 2 + 1]
            table_grad = table_from(small[experts // 2 + 2 :], bucket_count)
            got, gain_one_grad, gain_two_grad, router_grad, table_grad = together(
                got, gain_one_grad, gain_two_grad, router_grad, table_grad
            )
        summed_parts = join(mine[k], summed_parts, got)
    got = trades(summed_parts, 0)
    input_grad = input_back(tokens, normed_part, normed_other, gain_attn, residual_grad)
    got, input_grad = together(got, input_grad)
    query_w_grad, key_w_grad, value_w_grad, out_w_grad = finish(mine[0], summed_parts, got, width)
    return (
        output,
        input_grad,
        gain_one_grad,
        query_w_grad,
        key_w_grad,
        value_w_grad,
        out_w_grad,
        table_grad,
        gain_two_grad,
        router_grad,
        inner_grad[None],
        outer_grad[None],
    )


def solution(mesh):
    in_specs = (
        P("seq", None),
        P(),
        P(None, "heads"),
        P(None, "heads"),
        P(None, "heads"),
        P("heads", None),
        P(None, "heads"),
        P(),
        P(),
        P("seq", None, "heads"),
        P("seq", "heads", None),
        P("seq", None),
        P("seq"),
        P("seq", None),
    )
    out_specs = (
        P("seq", "heads"),
        P("seq", None),
        P(),
        P(None, "heads"),
        P(None, "heads"),
        P(None, "heads"),
        P("heads", None),
        P(None, "heads"),
        P(),
        P(),
        P("seq", None, "heads"),
        P("seq", "heads", None),
    )
    return jax.shard_map(
        on_device, mesh=mesh, in_specs=in_specs, out_specs=out_specs, check_vma=False
    )
```

```python
from functools import partial

import jax
import jax.numpy as jnp
from jax import lax
from jax.experimental import pallas as pl
from jax.experimental.pallas import tpu as pltpu
from jax.sharding import PartitionSpec as P

SHORT_LEN = 128
LONG_LEN = 512
SHORT_DEV = 4
LONG_DEV = 1


epsilon = 1e-06
highest = lax.Precision.HIGHEST
far_limits = (12, 16, 23, 32, 46, 64, 91)


def vmem(count):
    return [pl.BlockSpec(memory_space=pltpu.VMEM)] * count


def params(mib=16):
    return pltpu.CompilerParams(vmem_limit_bytes=mib * 1024 * 1024)


def dot_nn(left, right):
    return jnp.dot(left, right, preferred_element_type=jnp.float32)


def dot_nt(left, right):
    return lax.dot_general(
        left, right, (((1,), (1,)), ((), ())), preferred_element_type=jnp.float32
    )


def inverse_rms(values):
    return lax.rsqrt(jnp.mean(values * values, axis=-1, keepdims=True) + epsilon)


def diagonal_buckets(offset):
    distance = jnp.abs(offset)
    far_bucket = jnp.full(offset.shape, 8, jnp.int32)
    for limit in far_limits:
        far_bucket = far_bucket + (distance >= limit).astype(jnp.int32)
    return jnp.where(distance < 8, distance, far_bucket) + jnp.where(offset > 0, 16, 0)


def hbm_out(shape, dtype):
    return pltpu.HBM(shape, dtype)


def in_hbm(array):
    return pltpu.with_memory_space_constraint(array, pltpu.HBM)


def start_copies(pairs):
    copies = [pltpu.make_async_copy(*triple) for triple in pairs]
    for copy in copies:
        copy.start()
    return copies


def attend_kernel(
    block_rows,
    lengths_ref,
    tokens_hbm,
    gain_ref,
    wq_hbm,
    wk_hbm,
    wv_hbm,
    wo_hbm,
    table_ref,
    part_hbm,
    normed_hbm,
    q_hbm,
    k_hbm,
    v_hbm,
    mixed_hbm,
    long_hbm,
    short_hbm,
    tokens_ref,
    joint_ref,
    wo_ref,
    part_ref,
    normed_ref,
    q_ref,
    k_ref,
    v_ref,
    mixed_ref,
    long_ref,
    short_ref,
    diag_ref,
    in_sems,
    out_sems,
):
    tok_count, width = tokens_ref.shape
    own = q_ref.shape[1]
    pairs = own // 128
    short_tok = SHORT_DEV * SHORT_LEN
    tile = 512
    steps = tok_count // tile
    tiles_in = []
    for step in range(steps):
        rows = slice(step * tile, step * tile + tile)
        tiles_in.append((tokens_hbm.at[rows], tokens_ref.at[rows], in_sems.at[step]))
    weights = [
        (source, joint_ref.at[:, index * own : index * own + own])
        for index, source in enumerate((wq_hbm, wk_hbm, wv_hbm))
    ]
    weights.append((wo_hbm, wo_ref))
    copies = start_copies(
        tiles_in + [(src, dst, in_sems.at[steps + index]) for index, (src, dst) in enumerate(weights)]
    )
    weight_copies = copies[steps:]
    outs = []

    offset = lax.broadcasted_iota(jnp.int32, (table_ref.shape[1], 512), 1) - 256
    hot = jnp.where(
        diagonal_buckets(offset)
        == lax.broadcasted_iota(jnp.int32, (table_ref.shape[1], 512), 0),
        1.0,
        0.0,
    )
    diag_ref[...] = dot_nn(table_ref[...], hot.astype(jnp.bfloat16))
    gain = gain_ref[...]

    def normalize(step, carry):
        rows = pl.ds(pl.multiple_of(step * tile, tile), tile)
        pltpu.make_async_copy(tokens_hbm.at[rows], tokens_ref.at[rows], in_sems.at[step]).wait()
        values = tokens_ref[rows, :].astype(jnp.float32)
        normed_ref[rows, :] = (values * inverse_rms(values) * gain).astype(jnp.bfloat16)
        return carry

    lax.fori_loop(0, steps, normalize, 0)
    outs += start_copies([(normed_ref, normed_hbm, out_sems.at[0])])
    for copy in weight_copies[:3]:
        copy.wait()

    def project(step, carry):
        rows = pl.ds(pl.multiple_of(step * tile, tile), tile)
        joint = dot_nn(normed_ref[rows, :], joint_ref[...]).astype(jnp.bfloat16)
        q_ref[rows, :] = joint[:, :own] * jnp.bfloat16(0.125)
        k_ref[rows, :] = joint[:, own : 2 * own]
        v_ref[rows, :] = joint[:, 2 * own :]
        return carry

    lax.fori_loop(0, steps, project, 0)
    outs += start_copies(
        [
            (q_ref, q_hbm, out_sems.at[1]),
            (k_ref, k_hbm, out_sems.at[2]),
            (v_ref, v_hbm, out_sems.at[3]),
        ]
    )
    lane = lax.broadcasted_iota(jnp.int32, (1, 128), 1)
    key_place = lax.broadcasted_iota(jnp.int32, (1, LONG_LEN), 1)
    live_long = key_place < lengths_ref[SHORT_DEV]

    def softmax(scores):
        weights = jnp.exp(scores - jnp.max(scores, axis=1, keepdims=True))
        return (weights * (1.0 / jnp.sum(weights, axis=1, keepdims=True))).astype(jnp.bfloat16)

    def one_pair(pair):
        lanes = slice(pair * 128, pair * 128 + 128)
        tiles = []
        for sub in range(2):
            row = diag_ref[pair * 2 + sub : pair * 2 + sub + 1, :]
            spread = pltpu.roll(
                jnp.broadcast_to(row, (128, 512)), 256, 1, stride=1, stride_axis=0
            )
            tiles.append(
                (
                    spread[:, 0:128],
                    spread[:, 128:256],
                    spread[:, 384:512],
                    jnp.broadcast_to(row[:, 511:512], (128, 128)),
                    jnp.broadcast_to(row[:, 0:1], (128, 128)),
                )
            )
        out = []
        for sub in range(2):
            scores = []
            for block in range(SHORT_DEV):
                rows = slice(block * 128, block * 128 + 128)
                masked = jnp.where((lane >= 64) == (sub == 1), q_ref[rows, lanes], 0)
                live = key_place[:, :128] < lengths_ref[block]
                scores.append(
                    jnp.where(
                        live, dot_nt(masked, k_ref[rows, lanes]) + tiles[sub][0], -1000000000.0
                    )
                )
            probs = softmax(jnp.concatenate(scores, axis=0))
            short_ref[pair * 2 + sub] = probs
            mixed = []
            for block in range(SHORT_DEV):
                rows = slice(block * 128, block * 128 + 128)
                mixed.append(dot_nn(probs[rows], v_ref[rows, lanes]))
            out.append(jnp.concatenate(mixed, axis=0))
        mixed_ref[:short_tok, lanes] = jnp.where(lane < 64, out[0], out[1]).astype(jnp.bfloat16)
        keys = k_ref[short_tok:, lanes]
        values = v_ref[short_tok:, lanes]
        for start in range(0, LONG_LEN, block_rows):
            places = slice(start, start + block_rows)
            rows = slice(short_tok + start, short_tok + start + block_rows)
            queries = q_ref[rows, lanes]
            out = []
            for sub in range(2):
                masked = jnp.where((lane >= 64) == (sub == 1), queries, 0)
                same, above, below, far_above, far_below = tiles[sub]
                bias = jnp.concatenate(
                    [
                        jnp.concatenate(
                            [
                                same
                                if other == block
                                else above
                                if other == block + 1
                                else below
                                if other == block - 1
                                else far_above
                                if other > block
                                else far_below
                                for other in range(LONG_LEN // 128)
                            ],
                            axis=1,
                        )
                        for block in range(start // 128, (start + block_rows) // 128)
                    ],
                    axis=0,
                )
                scores = jnp.where(live_long, dot_nt(masked, keys) + bias, -1000000000.0)
                probs = softmax(scores)
                long_ref[pair * 2 + sub, places, :] = probs
                out.append(dot_nn(probs, values))
            mixed_ref[rows, lanes] = jnp.where(lane < 64, out[0], out[1]).astype(jnp.bfloat16)

    for pair in range(pairs):
        one_pair(pair)
        both = slice(pair * 2, pair * 2 + 2)
        outs += start_copies(
            [
                (long_ref.at[both], long_hbm.at[both], out_sems.at[4 + 2 * pair]),
                (short_ref.at[both], short_hbm.at[both], out_sems.at[5 + 2 * pair]),
            ]
        )
    weight_copies[3].wait()
    base = 4 + 2 * pairs
    outs += start_copies([(mixed_ref, mixed_hbm, out_sems.at[base])])

    def part_copy(step):
        rows = pl.ds(pl.multiple_of(step * tile, tile), tile)
        return pltpu.make_async_copy(part_ref.at[rows], part_hbm.at[rows], out_sems.at[base + 1 + step])

    def project_out(step, carry):
        rows = pl.ds(pl.multiple_of(step * tile, tile), tile)
        part_ref[rows, :] = dot_nn(mixed_ref[rows, :], wo_ref[...]).astype(part_ref.dtype)
        part_copy(step).start()
        return carry

    lax.fori_loop(0, steps, project_out, 0)
    outs += [part_copy(step) for step in range(steps)]
    for copy in outs:
        copy.wait()


def attend(lengths, tokens, gain, w_query, w_key, w_value, w_out, table, block_rows=512):
    tok_count, width = tokens.shape
    own = w_query.shape[1]
    heads = own // 64
    heads_pad = -(-heads // 8) * 8
    table = jnp.pad(table.T, ((0, heads_pad - heads), (0, 0)))
    short_tok = SHORT_DEV * SHORT_LEN
    flops = 2 * tok_count * width * own * 4 + 4 * heads * (512 * 512 + short_tok * 128) * 64
    hbm = pl.BlockSpec(memory_space=pltpu.HBM)
    out_shapes = [
        ((tok_count, width), jnp.bfloat16),
        ((tok_count, width), jnp.bfloat16),
        ((tok_count, own), jnp.bfloat16),
        ((tok_count, own), jnp.bfloat16),
        ((tok_count, own), jnp.bfloat16),
        ((tok_count, own), jnp.bfloat16),
        ((heads, LONG_LEN, LONG_LEN), jnp.bfloat16),
        ((heads, short_tok, SHORT_LEN), jnp.bfloat16),
    ]
    steps = tok_count // 512
    return pl.pallas_call(
        partial(attend_kernel, block_rows),
        out_shape=[jax.ShapeDtypeStruct(*out_shapes[0])]
        + [hbm_out(shape, dtype) for shape, dtype in out_shapes[1:]],
        in_specs=[pl.BlockSpec(memory_space=pltpu.SMEM), hbm]
        + vmem(1)
        + [hbm] * 4
        + vmem(1),
        out_specs=[hbm] * 8,
        scratch_shapes=[pltpu.VMEM(tokens.shape, jnp.bfloat16)]
        + [pltpu.VMEM((width, 3 * own), jnp.bfloat16), pltpu.VMEM(w_out.shape, jnp.bfloat16)]
        + [pltpu.VMEM(shape, dtype) for shape, dtype in out_shapes]
        + [
            pltpu.VMEM((heads_pad, 512), jnp.float32),
            pltpu.SemaphoreType.DMA((steps + 4,)),
            pltpu.SemaphoreType.DMA((5 + 2 * (heads // 2) + steps,)),
        ],
        compiler_params=params(24),
        cost_estimate=pl.CostEstimate(
            flops=flops, bytes_accessed=16000000, transcendentals=heads * 512 * 640
        ),
        name="attend",
    )(
        lengths,
        in_hbm(tokens),
        gain.astype(jnp.float32)[None],
        in_hbm(w_query),
        in_hbm(w_key),
        in_hbm(w_value),
        in_hbm(w_out),
        table,
    )


def score_part(probs, prob_grad):
    mean = jnp.sum(probs * prob_grad, axis=1, keepdims=True) / jnp.sum(probs, axis=1, keepdims=True)
    return probs * (prob_grad - mean)


def attend_back_pair(
    pair, hg_ref, q_ref, k_ref, v_ref, long_ref, short_ref, grads_ref, tiles_ref, far_ref, sg_ref,
):
    short_tok = SHORT_DEV * SHORT_LEN
    lane = lax.broadcasted_iota(jnp.int32, (1, 128), 1)
    lanes = pl.ds(pl.multiple_of(pair * 128, 128), 128)
    blocks = LONG_LEN // 128
    heads_grad = hg_ref[:, lanes]
    q_t = jnp.transpose(q_ref[:, lanes])
    hg_t = jnp.transpose(heads_grad)
    qg = []
    kg_t = []
    vg_t = []
    for sub in range(2):
        head = pair * 2 + sub
        own = (lane >= 64) == (sub == 1)
        rows_t = slice(64 * sub, 64 * sub + 64)
        masked = jnp.where(own, heads_grad, 0)
        grads = [
            dot_nt(masked[block * 128 : block * 128 + 128], v_ref[block * 128 : block * 128 + 128, lanes])
            for block in range(SHORT_DEV)
        ]
        probs = short_ref[head]
        part = score_part(probs.astype(jnp.float32), jnp.concatenate(grads, axis=0))
        same = part[:128]
        for block in range(1, SHORT_DEV):
            same = same + part[block * 128 : block * 128 + 128]
        part = part.astype(jnp.bfloat16)
        qg_parts = []
        kg_parts = []
        vg_parts = []
        for block in range(SHORT_DEV):
            rows = slice(block * 128, block * 128 + 128)
            qg_parts.append(dot_nn(part[rows], k_ref[rows, lanes]))
            kg_parts.append(dot_nn(q_t[rows_t, rows], part[rows]))
            vg_parts.append(dot_nn(hg_t[rows_t, rows], probs[rows]))
        above = jnp.zeros((128, 128), jnp.float32)
        below = above
        far_above = above
        far_below = above
        probs = long_ref[head]
        part = score_part(
            probs.astype(jnp.float32), dot_nt(masked[short_tok:], v_ref[short_tok:, lanes])
        )
        for block in range(blocks):
            for other in range(blocks):
                piece = part[block * 128 : block * 128 + 128, other * 128 : other * 128 + 128]
                if other == block:
                    same = same + piece
                elif other == block + 1:
                    above = above + piece
                elif other == block - 1:
                    below = below + piece
                elif other > block:
                    far_above = far_above + piece
                else:
                    far_below = far_below + piece
        sg_ref[...] = part.astype(jnp.bfloat16)
        qg_parts.append(dot_nn(sg_ref[...], k_ref[short_tok:, lanes]))
        kg_parts.append(dot_nn(q_t[rows_t, short_tok:], sg_ref[...]))
        vg_parts.append(dot_nn(hg_t[rows_t, short_tok:], probs))
        qg.append(jnp.concatenate(qg_parts, axis=0))
        kg_t.append(jnp.concatenate(kg_parts, axis=1))
        vg_t.append(jnp.concatenate(vg_parts, axis=1))
        tiles_ref[head, :, 0:128] = same
        tiles_ref[head, :, 128:256] = above
        tiles_ref[head, :, 256:384] = below
        far_ref[head, 0:1, :] = jnp.sum(far_above, axis=0, keepdims=True)
        far_ref[head, 1:2, :] = jnp.sum(far_below, axis=0, keepdims=True)
    width = q_ref.shape[1]
    grads_ref[:, lanes] = (jnp.where(lane < 64, qg[0], qg[1]) * 0.125).astype(jnp.bfloat16)
    for index, whole in ((1, kg_t), (2, vg_t)):
        place = pl.ds(pl.multiple_of(index * width + pair * 128, 128), 128)
        grads_ref[:, place] = jnp.transpose(jnp.concatenate(whole, axis=0).astype(jnp.bfloat16))


def diagonals(tiles):
    tile = jnp.concatenate(
        [tiles[:, 0:256], jnp.zeros((128, 128), jnp.float32), tiles[:, 256:384]], axis=1
    )
    span = 64
    while span:
        tile = tile[:span] + pltpu.roll(tile[span:], 512 - span, 1)
        span //= 2
    return tile


def table_from(diag, bucket_count):
    lane = jnp.arange(768, dtype=jnp.int32)
    offset = jnp.where(lane < 256, lane, lane - 512)
    offset = jnp.where(lane >= 640, -256, jnp.where(lane >= 512, 256, offset))
    hot = (diagonal_buckets(offset)[:, None] == jnp.arange(bucket_count)[None, :]).astype(jnp.float32)
    return lax.dot_general(
        hot, diag, (((0,), (1,)), ((), ())), precision=highest, preferred_element_type=jnp.float32
    )


def dispatch_rows(send_ref, slot_row, half_rows):
    slots = send_ref.shape[0]
    tok_count = slot_row.shape[1]
    span = slots
    for base in range(0, slots, span):
        place = lax.broadcasted_iota(jnp.int32, (span, tok_count), 0) + base
        hot = jnp.where(place == slot_row, 1.0, 0.0).astype(jnp.bfloat16)
        send_ref[base : base + span, :] = dot_nn(hot, half_rows).astype(jnp.bfloat16)


def half_lanes(core, half):
    return pl.ds(pl.multiple_of(core * half, half), half)


def route_kernel(
    capacity, where_ref, routes_hbm, grad_hbm, row_hbm, send_ref, routes_ref, grad_ref, row_ref, in_sems,
    out_sem,
):
    tok_count = routes_ref.shape[1]
    slots, half = send_ref.shape
    experts = slots // capacity
    fetch, copy = start_copies(
        [
            (routes_hbm, routes_ref, in_sems.at[0]),
            (grad_hbm.at[:, half_lanes(where_ref[0], half)], grad_ref, in_sems.at[1]),
        ]
    )
    fetch.wait()
    routes = routes_ref[...]
    expert = lax.broadcasted_iota(jnp.int32, (experts, tok_count), 0)
    lane = lax.broadcasted_iota(jnp.int32, (1, tok_count), 1)
    hot = jnp.where(expert == routes, 1.0, 0.0)
    total = hot
    step = 1
    while step < tok_count:
        total = total + jnp.where(lane >= step, pltpu.roll(total, step, 1), 0.0)
        step *= 2
    before = jnp.sum(hot * total, axis=0, keepdims=True).astype(jnp.int32) - 1
    slot = jnp.where(before < capacity, routes * capacity + before, slots)
    row_ref[...] = slot
    out = pltpu.make_async_copy(row_ref, row_hbm, out_sem)
    out.start()
    copy.wait()
    dispatch_rows(send_ref, slot, grad_ref[...])
    out.wait()


def route(where, routes, out_grad, experts, capacity):
    tok_count, width = out_grad.shape
    slots = experts * capacity
    return pl.pallas_call(
        partial(route_kernel, capacity),
        out_shape=[
            hbm_out((1, tok_count), jnp.int32),
            jax.ShapeDtypeStruct((slots, width // 2), jnp.bfloat16),
        ],
        in_specs=[
            pl.BlockSpec(memory_space=pltpu.SMEM),
            pl.BlockSpec(memory_space=pltpu.HBM),
            pl.BlockSpec(memory_space=pltpu.HBM),
        ],
        out_specs=[pl.BlockSpec(memory_space=pltpu.HBM)] + vmem(1),
        scratch_shapes=[
            pltpu.VMEM((1, tok_count), jnp.int32),
            pltpu.VMEM((tok_count, width // 2), jnp.bfloat16),
            pltpu.VMEM((1, tok_count), jnp.int32),
            pltpu.SemaphoreType.DMA((2,)),
            pltpu.SemaphoreType.DMA,
        ],
        compiler_params=params(28),
        cost_estimate=pl.CostEstimate(
            flops=slots * tok_count * width, bytes_accessed=4000000, transcendentals=0
        ),
        name="route",
    )(where, in_hbm(routes.reshape(1, tok_count)), in_hbm(out_grad))


def second_kernel(
    where_ref, tokens_hbm, own_ref, other_ref, gain_ref, row_hbm, residual_hbm, send_ref, tokens_ref,
    row_ref, residual_ref, second_ref, in_sems, out_sems,
):
    tile = 256
    tok_count = tokens_ref.shape[0]
    half = send_ref.shape[1]
    tiles_rows = [slice(start, start + tile) for start in range(0, tok_count, tile)]
    copies = start_copies(
        [
            (tokens_hbm.at[rows], tokens_ref.at[rows], in_sems.at[step])
            for step, rows in enumerate(tiles_rows)
        ]
        + [(row_hbm, row_ref, in_sems.at[len(tiles_rows)])]
    )
    outs = []
    gain = gain_ref[...]
    for step, rows in enumerate(tiles_rows):
        attn = own_ref[rows, :].astype(jnp.float32) + other_ref[rows, :].astype(jnp.float32)
        copies[step].wait()
        residual = tokens_ref[rows, :].astype(jnp.float32) + attn
        residual_ref[rows, :] = residual
        outs += start_copies([(residual_ref.at[rows], residual_hbm.at[rows], out_sems.at[step])])
        second_ref[rows, :] = (residual * inverse_rms(residual) * gain).astype(jnp.bfloat16)
    copies[-1].wait()
    dispatch_rows(send_ref, row_ref[...], second_ref[:, half_lanes(where_ref[0], half)])
    for copy in outs:
        copy.wait()


def second_rows(where, tokens, own, other, gain, slot_row, slots):
    tok_count, width = tokens.shape
    steps = tok_count // 256
    hbm = pl.BlockSpec(memory_space=pltpu.HBM)
    return pl.pallas_call(
        second_kernel,
        out_shape=[
            hbm_out((tok_count, width), jnp.float32),
            jax.ShapeDtypeStruct((slots, width // 2), jnp.bfloat16),
        ],
        in_specs=[pl.BlockSpec(memory_space=pltpu.SMEM), hbm] + vmem(3) + [hbm],
        out_specs=[hbm] + vmem(1),
        scratch_shapes=[
            pltpu.VMEM((tok_count, width), jnp.bfloat16),
            pltpu.VMEM((1, tok_count), jnp.int32),
            pltpu.VMEM((tok_count, width), jnp.float32),
            pltpu.VMEM((tok_count, width), jnp.bfloat16),
            pltpu.SemaphoreType.DMA((steps + 1,)),
            pltpu.SemaphoreType.DMA((steps,)),
        ],
        compiler_params=params(28),
        cost_estimate=pl.CostEstimate(
            flops=slots * tok_count * width, bytes_accessed=13000000, transcendentals=0
        ),
        name="second",
    )(where, in_hbm(tokens), own, other, gain.astype(jnp.float32)[None], in_hbm(slot_row))


def hidden_grad_kernel(where_ref, own_ref, other_ref, outer_ref, out_ref, whole_ref):
    half = own_ref.shape[1]
    core = where_ref[0]
    whole_ref[:, half_lanes(core, half)] = own_ref[...]
    whole_ref[:, half_lanes(1 - core, half)] = other_ref[...]
    out_ref[...] = dot_nt(whole_ref[...], outer_ref[...]).astype(jnp.bfloat16)


def hidden_grad_of(where, own, other, outer):
    slots, half = own.shape
    hidden = outer.shape[0]
    tile = 256
    rows = pl.BlockSpec((tile, half), lambda step: (step, 0))
    return pl.pallas_call(
        hidden_grad_kernel,
        grid=(slots // tile,),
        out_shape=hbm_out((slots, hidden), jnp.bfloat16),
        in_specs=[pl.BlockSpec(memory_space=pltpu.SMEM), rows, rows] + vmem(1),
        out_specs=pl.BlockSpec((tile, hidden), lambda step: (step, 0)),
        scratch_shapes=[pltpu.VMEM((tile, 2 * half), jnp.bfloat16)],
        compiler_params=params(),
        cost_estimate=pl.CostEstimate(
            flops=4 * slots * half * hidden, bytes_accessed=12000000, transcendentals=0
        ),
        name="hidden_grad",
    )(where, own, other, outer)


def gate_of(rows, router, index):
    experts = router.shape[1]
    logits = dot_nn(rows, router)
    exp_logit = jnp.exp(logits - jnp.max(logits, axis=1, keepdims=True))
    probs = exp_logit * (1.0 / jnp.sum(exp_logit, axis=1, keepdims=True))
    hit = jnp.where(lax.broadcasted_iota(jnp.int32, (1, experts), 1) == index, 1.0, 0.0)
    return probs, hit, jnp.sum(probs * hit, axis=1, keepdims=True)


def expert_kernel(
    where_ref,
    own_ref,
    other_ref,
    hg_ref,
    inner_ref,
    router_ref,
    hidden_ref,
    pre_grad_ref,
    keep_ref,
    send_ref,
    logit_ref,
    arrived_ref,
    whole_ref,
):
    core = where_ref[0]
    tile, half = own_ref.shape
    own_lanes = half_lanes(core, half)
    other_lanes = half_lanes(1 - core, half)
    arrived_ref[:, own_lanes] = own_ref[...]
    arrived_ref[:, other_lanes] = other_ref[...]
    arrived = arrived_ref[...]
    probs, hit, gate = gate_of(arrived, router_ref[...], where_ref[1])
    curve = 0.7978845608028654
    gate_grad = jnp.zeros((tile, 1), jnp.float32)
    back = jnp.zeros((tile, 2 * half), jnp.float32)
    chunk = 512
    for start in range(0, hg_ref.shape[1], chunk):
        cols = slice(start, start + chunk)
        pre = dot_nn(arrived, inner_ref[:, cols])
        square = pre * pre
        share = 0.5 + 0.5 * jnp.tanh(pre * (curve + (curve * 0.044715) * square))
        hidden_ref[:, cols] = (pre * share).astype(jnp.bfloat16)
        passed = share * hg_ref[:, cols].astype(jnp.float32)
        gate_grad = gate_grad + jnp.sum(pre * passed, axis=1, keepdims=True)
        bend = pre * (2.0 * curve + (6.0 * curve * 0.044715) * square)
        pre_grad = ((gate * passed) * (1.0 + (1.0 - share) * bend)).astype(jnp.bfloat16)
        pre_grad_ref[:, cols] = pre_grad
        back = back + dot_nt(pre_grad, inner_ref[:, cols])
    logit = (probs * (gate_grad * (hit - gate))).astype(jnp.bfloat16)
    logit_ref[...] = logit
    whole_ref[...] = back + dot_nt(logit, router_ref[...])
    send_ref[...] = whole_ref[:, other_lanes].astype(jnp.bfloat16)
    keep_ref[...] = whole_ref[:, own_lanes]


def expert(where, own, other, hidden_grad, inner, router):
    slots, half = own.shape
    width, hidden = inner.shape
    experts = router.shape[1]
    tile = 256
    halves = pl.BlockSpec((tile, half), lambda step: (step, 0))
    units = pl.BlockSpec((tile, hidden), lambda step: (step, 0))
    return pl.pallas_call(
        expert_kernel,
        grid=(slots // tile,),
        out_shape=[
            hbm_out((slots, hidden), jnp.bfloat16),
            hbm_out((slots, hidden), jnp.bfloat16),
            jax.ShapeDtypeStruct((slots, half), jnp.float32),
            jax.ShapeDtypeStruct((slots, half), jnp.bfloat16),
            hbm_out((slots, experts), jnp.bfloat16),
        ],
        in_specs=[
            pl.BlockSpec(memory_space=pltpu.SMEM),
            halves,
            halves,
            units,
            pl.BlockSpec(inner.shape, lambda step: (0, 0), pipeline_mode=pl.Buffered(1)),
        ]
        + vmem(1),
        out_specs=[
            units,
            units,
            halves,
            halves,
            pl.BlockSpec((tile, experts), lambda step: (step, 0)),
        ],
        scratch_shapes=[
            pltpu.VMEM((tile, width), jnp.bfloat16),
            pltpu.VMEM((tile, width), jnp.float32),
        ],
        compiler_params=params(),
        cost_estimate=pl.CostEstimate(
            flops=4 * slots * width * hidden, bytes_accessed=20000000, transcendentals=slots * hidden
        ),
        name="expert",
    )(where, own, other, in_hbm(hidden_grad), in_hbm(inner), router)


def expert_out_kernel(
    where_ref, hidden_ref, own_ref, other_ref, logit_ref, row_ref, outer_ref, keep_ref, send_ref, router_ref,
    col_ref, whole_ref,
):
    core = where_ref[0]
    half = keep_ref.shape[1]
    own_lanes = half_lanes(core, half)
    other_lanes = half_lanes(1 - core, half)
    whole_ref[...] = dot_nn(hidden_ref[...], outer_ref[...])
    send_ref[...] = whole_ref[:, other_lanes].astype(jnp.bfloat16)
    keep_ref[...] = whole_ref[:, own_lanes]

    @pl.when(pl.program_id(0) == 0)
    def _():
        router_ref[...] = jnp.zeros_like(router_ref)
        wide = jnp.broadcast_to(row_ref[...].astype(jnp.float32), (128, row_ref.shape[1]))
        col_ref[...] = jnp.transpose(wide).astype(jnp.int32)

    router_ref[:, own_lanes] += contract_rows(logit_ref[...], own_ref[...])
    router_ref[:, other_lanes] += contract_rows(logit_ref[...], other_ref[...])


def expert_out_of(where, hidden, own, other, logit_grad, slot_row, outer):
    slots, units = hidden.shape
    tok_count = slot_row.shape[1]
    width = outer.shape[1]
    experts = logit_grad.shape[1]
    half = width // 2
    tile = 256
    halves = pl.BlockSpec((tile, half), lambda step: (step, 0))
    return pl.pallas_call(
        expert_out_kernel,
        grid=(slots // tile,),
        out_shape=[
            jax.ShapeDtypeStruct((slots, half), jnp.float32),
            jax.ShapeDtypeStruct((slots, half), jnp.bfloat16),
            hbm_out((experts, width), jnp.float32),
            hbm_out((tok_count, 128), jnp.int32),
        ],
        in_specs=[
            pl.BlockSpec(memory_space=pltpu.SMEM),
            pl.BlockSpec((tile, units), lambda step: (step, 0)),
            halves,
            halves,
            pl.BlockSpec((tile, experts), lambda step: (step, 0)),
            pl.BlockSpec((1, tok_count), lambda step: (0, 0)),
        ]
        + vmem(1),
        out_specs=[
            halves,
            halves,
            pl.BlockSpec((experts, width), lambda step: (0, 0)),
            pl.BlockSpec((tok_count, 128), lambda step: (0, 0)),
        ],
        scratch_shapes=[pltpu.VMEM((tile, width), jnp.float32)],
        compiler_params=params(),
        cost_estimate=pl.CostEstimate(
            flops=2 * slots * width * units, bytes_accessed=9000000, transcendentals=0
        ),
        name="expert_out",
    )(
        where, in_hbm(hidden), in_hbm(own), in_hbm(other), in_hbm(logit_grad), in_hbm(slot_row), outer
    )


def expert_grads_kernel(
    where_ref,
    own_hbm,
    other_hbm,
    grad_own_hbm,
    grad_other_hbm,
    hidden_ref,
    pre_grad_ref,
    router_ref,
    inner_grad_ref,
    outer_grad_ref,
    arrived_ref,
    gated_ref,
    sems,
):
    core = where_ref[0]
    half = own_hbm.shape[1]
    own_lanes = half_lanes(core, half)
    other_lanes = half_lanes(1 - core, half)

    @pl.when(pl.program_id(0) == 0)
    def _():
        copies = [
            pltpu.make_async_copy(own_hbm, arrived_ref.at[:, own_lanes], sems.at[0]),
            pltpu.make_async_copy(other_hbm, arrived_ref.at[:, other_lanes], sems.at[1]),
            pltpu.make_async_copy(grad_own_hbm, gated_ref.at[:, own_lanes], sems.at[2]),
            pltpu.make_async_copy(grad_other_hbm, gated_ref.at[:, other_lanes], sems.at[3]),
        ]
        for copy in copies:
            copy.start()
        for copy in copies:
            copy.wait()
        gate = gate_of(arrived_ref[...], router_ref[...], where_ref[1])[2]
        gated_ref[...] = (gate * gated_ref[...].astype(jnp.float32)).astype(jnp.bfloat16)

    outer_grad_ref[...] = contract_rows(hidden_ref[...], gated_ref[...])
    inner_grad_ref[...] = contract_rows(arrived_ref[...], pre_grad_ref[...])


def expert_grads(where, own, other, grad_own, grad_other, hidden, pre_grad, router):
    slots, half = own.shape
    units = hidden.shape[1]
    width = router.shape[0]
    tile = 256
    hbm = pl.BlockSpec(memory_space=pltpu.HBM)
    whole = lambda shape: pl.BlockSpec(shape, lambda step: (0, 0))
    cols = pl.BlockSpec((slots, tile), lambda step: (0, step))
    return pl.pallas_call(
        expert_grads_kernel,
        grid=(units // tile,),
        out_shape=[
            hbm_out((width, units), jnp.float32),
            hbm_out((units, width), jnp.float32),
        ],
        in_specs=[
            pl.BlockSpec(memory_space=pltpu.SMEM),
            hbm,
            hbm,
            hbm,
            hbm,
            cols,
            cols,
            whole(router.shape),
        ],
        out_specs=[
            pl.BlockSpec((width, tile), lambda step: (0, step)),
            pl.BlockSpec((tile, width), lambda step: (step, 0)),
        ],
        scratch_shapes=[
            pltpu.VMEM((slots, width), jnp.bfloat16),
            pltpu.VMEM((slots, width), jnp.bfloat16),
            pltpu.SemaphoreType.DMA((4,)),
        ],
        compiler_params=params(24),
        cost_estimate=pl.CostEstimate(
            flops=4 * slots * width * units, bytes_accessed=22000000, transcendentals=0
        ),
        name="expert_grads",
    )(
        where,
        in_hbm(own),
        in_hbm(other),
        in_hbm(grad_own),
        in_hbm(grad_other),
        in_hbm(hidden),
        in_hbm(pre_grad),
        router,
    )


def output_kernel(
    capacity, where_ref, col_ref, returned_ref, residual_ref, gain_ref, router_ref, out_ref
):
    slots, half = returned_ref.shape
    tile = residual_ref.shape[0]
    experts = router_ref.shape[1]
    col = col_ref[:, :1]
    place = lax.broadcasted_iota(jnp.int32, (tile, slots), 1)
    hot = jnp.where(place == col, 1.0, 0.0).astype(jnp.bfloat16)
    token_out = dot_nn(hot, returned_ref[...])
    residual = residual_ref[...]
    second = (residual * inverse_rms(residual) * gain_ref[...]).astype(jnp.bfloat16)
    logits = dot_nn(second, router_ref[...])
    exp_logit = jnp.exp(logits - jnp.max(logits, axis=1, keepdims=True))
    first = lax.broadcasted_iota(jnp.int32, (1, experts), 1) * capacity
    hit = jnp.where((col >= first) & (col < first + capacity), exp_logit, 0.0)
    gate = jnp.sum(hit, axis=1, keepdims=True) / jnp.sum(exp_logit, axis=1, keepdims=True)
    own = residual_ref[:, half_lanes(where_ref[0], half)]
    out_ref[...] = (own + gate * token_out).astype(jnp.bfloat16)


def output_of(where, slot_col, returned, residual, gain, router, capacity):
    tok_count, width = residual.shape
    slots, half = returned.shape
    tile = 256
    whole = lambda shape: pl.BlockSpec(shape, lambda step: (0, 0))
    return pl.pallas_call(
        partial(output_kernel, capacity),
        grid=(tok_count // tile,),
        out_shape=jax.ShapeDtypeStruct((tok_count, half), jnp.bfloat16),
        in_specs=[
            pl.BlockSpec(memory_space=pltpu.SMEM),
            pl.BlockSpec((tile, 128), lambda step: (step, 0)),
            whole(returned.shape),
            pl.BlockSpec((tile, width), lambda step: (step, 0)),
            whole((1, width)),
            whole(router.shape),
        ],
        out_specs=pl.BlockSpec((tile, half), lambda step: (step, 0)),
        compiler_params=params(),
        cost_estimate=pl.CostEstimate(
            flops=2 * tok_count * half * slots, bytes_accessed=6000000, transcendentals=0
        ),
        name="output",
    )(
        where, in_hbm(slot_col), in_hbm(returned), in_hbm(residual), gain.astype(jnp.float32)[None], router
    )


def normed_back_kernel(grads_ref, wq_ref, wk_ref, wv_ref, out_ref):
    own = wq_ref.shape[1]
    out_ref[...] = (
        dot_nt(grads_ref[:, :own], wq_ref[...])
        + dot_nt(grads_ref[:, own : 2 * own], wk_ref[...])
        + dot_nt(grads_ref[:, 2 * own :], wv_ref[...])
    ).astype(jnp.bfloat16)


def normed_back(grads, w_query, w_key, w_value):
    tok_count = grads.shape[0]
    width, own = w_query.shape
    tile = 256
    whole = pl.BlockSpec((width, own), lambda step: (0, 0))
    return pl.pallas_call(
        normed_back_kernel,
        grid=(tok_count // tile,),
        out_shape=jax.ShapeDtypeStruct((tok_count, width), jnp.bfloat16),
        in_specs=[pl.BlockSpec((tile, 3 * own), lambda step: (step, 0))] + [whole] * 3,
        out_specs=pl.BlockSpec((tile, width), lambda step: (step, 0)),
        compiler_params=params(),
        cost_estimate=pl.CostEstimate(
            flops=6 * tok_count * own * width, bytes_accessed=6000000, transcendentals=0
        ),
        name="normed_back",
    )(*(in_hbm(array) for array in (grads, w_query, w_key, w_value)))


def input_back_kernel(tokens_ref, own_ref, other_ref, gain_ref, residual_ref, out_ref):
    ybar = own_ref[...].astype(jnp.float32) + other_ref[...].astype(jnp.float32)
    values = tokens_ref[...].astype(jnp.float32)
    scale = inverse_rms(values)
    scaled = values * scale
    pulled = ybar * gain_ref[...]
    out_ref[...] = residual_ref[...] + scale * (
        pulled - scaled * jnp.mean(pulled * scaled, axis=1, keepdims=True)
    )


def input_back(tokens, own, other, gain, residual_grad):
    tok_count, width = tokens.shape
    tile = 256
    rows = pl.BlockSpec((tile, width), lambda step: (step, 0))
    return pl.pallas_call(
        input_back_kernel,
        grid=(tok_count // tile,),
        out_shape=jax.ShapeDtypeStruct((tok_count, width), jnp.float32),
        in_specs=[rows, rows, rows, pl.BlockSpec((1, width), lambda step: (0, 0)), rows],
        out_specs=rows,
        compiler_params=params(),
        cost_estimate=pl.CostEstimate(
            flops=10 * tok_count * width, bytes_accessed=11000000, transcendentals=0
        ),
        name="input_back",
    )(in_hbm(tokens), own, other, gain.astype(jnp.float32)[None], in_hbm(residual_grad))


def back_kernel(
    bits_ref,
    where_ref,
    col_hbm,
    own_hbm,
    other_hbm,
    residual_hbm,
    grad_hbm,
    wo_hbm,
    q_hbm,
    k_hbm,
    v_hbm,
    mixed_hbm,
    long_hbm,
    short_hbm,
    normed_hbm,
    wq_hbm,
    wk_hbm,
    wv_hbm,
    gain_one_ref,
    gain_two_ref,
    router_ref,
    out_hbm,
    grads_hbm,
    sent_a,
    sent_b,
    sent_c,
    kept_a,
    kept_b,
    kept_c,
    col_ref,
    back_ref,
    residual_ref,
    grad_ref,
    wo_ref,
    q_ref,
    k_ref,
    v_ref,
    mixed_ref,
    long_ref,
    short_ref,
    normed_ref,
    wq_ref,
    wk_ref,
    wv_ref,
    attn_ref,
    heads_ref,
    grads_ref,
    sg_ref,
    tiles_ref,
    far_ref,
    stack_ref,
    small_ref,
    packed_ref,
    total_ref,
    in_sems,
    out_sems,
):
    tok_count, width = residual_ref.shape
    slots, half = own_hbm.shape
    own = mixed_ref.shape[1]
    experts = router_ref.shape[0]
    pairs = own // 128
    tile = 512
    steps = tok_count // tile
    core = where_ref[0]
    first = [
        (own_hbm, back_ref.at[:, half_lanes(core, half)]),
        (other_hbm, back_ref.at[:, half_lanes(1 - core, half)]),
        (col_hbm, col_ref),
        (wo_hbm, wo_ref),
    ]
    tiles = []
    for start in range(0, tok_count, tile):
        rows = slice(start, start + tile)
        tiles.append((residual_hbm.at[rows], residual_ref.at[rows]))
        tiles.append((grad_hbm.at[rows], grad_ref.at[rows]))
    attention = [(q_hbm, q_ref), (k_hbm, k_ref), (v_hbm, v_ref), (mixed_hbm, mixed_ref), (short_hbm, short_ref)]
    for pair in range(pairs):
        both = slice(pair * 2, pair * 2 + 2)
        attention.append((long_hbm.at[both], long_ref.at[both]))
    weights = [(normed_hbm, normed_ref), (wq_hbm, wq_ref), (wk_hbm, wk_ref), (wv_hbm, wv_ref)]
    copies = start_copies(
        [
            (source, target, in_sems.at[index])
            for index, (source, target) in enumerate(first + tiles + attention + weights)
        ]
    )
    base = len(first) + len(tiles)
    outs = []

    for copy in copies[: len(first)]:
        copy.wait()
    gain_two = gain_two_ref[...]
    place = lax.broadcasted_iota(jnp.int32, (tile, slots), 1)

    def tile_out(step):
        rows = pl.ds(pl.multiple_of(step * tile, tile), tile)
        return pltpu.make_async_copy(residual_ref.at[rows], out_hbm.at[rows], out_sems.at[step])

    def one_tile(step, gain_two_grad):
        rows = pl.ds(pl.multiple_of(step * tile, tile), tile)
        at = len(first) + 2 * step
        pltpu.make_async_copy(residual_hbm.at[rows], residual_ref.at[rows], in_sems.at[at]).wait()
        pltpu.make_async_copy(grad_hbm.at[rows], grad_ref.at[rows], in_sems.at[at + 1]).wait()
        hot = jnp.where(place == col_ref[rows, :][:, :1], 1.0, 0.0).astype(jnp.bfloat16)
        ybar = dot_nn(hot, back_ref[...])
        values = residual_ref[rows, :]
        scale = inverse_rms(values)
        scaled = values * scale
        pulled = ybar * gain_two
        back = scale * (pulled - scaled * jnp.mean(pulled * scaled, axis=1, keepdims=True))
        out = back + grad_ref[rows, :].astype(jnp.float32)
        residual_ref[rows, :] = out
        attn = out.astype(jnp.bfloat16)
        attn_ref[rows, :] = attn
        heads_ref[rows, :] = dot_nt(attn, wo_ref[...]).astype(jnp.bfloat16)
        tile_out(step).start()
        return gain_two_grad + jnp.sum(ybar * scaled, axis=0, keepdims=True)

    gain_two_grad = lax.fori_loop(0, steps, one_tile, jnp.zeros((1, width), jnp.float32))
    outs += [tile_out(step) for step in range(steps)]

    for copy in copies[base : base + 5]:
        copy.wait()

    def one_pair(pair, carry):
        both = pl.ds(pair * 2, 2)
        pltpu.make_async_copy(long_hbm.at[both], long_ref.at[both], in_sems.at[base + 5 + pair]).wait()
        attend_back_pair(
            pair, heads_ref, q_ref, k_ref, v_ref, long_ref, short_ref, grads_ref, tiles_ref, far_ref,
            sg_ref,
        )
        return carry

    lax.fori_loop(0, pairs, one_pair, 0, unroll=True)
    outs += start_copies([(grads_ref, grads_hbm, out_sems.at[steps])])

    grad = contract_rows(mixed_ref[...], attn_ref[...]).astype(jnp.bfloat16)
    for part in range(width // own):
        at = 3 * width + part * own
        stack_ref[at : at + own, :] = grad[:, part * own : part * own + own]
    small_ref[0:experts, :] = router_ref[...]
    small_ref[experts + 1 : experts + 2, :] = gain_two_grad
    for head in range(2 * pairs):
        row = experts + 2 + head
        small_ref[row : row + 1, 0:512] = diagonals(tiles_ref[head])
        small_ref[row : row + 1, 512:640] = far_ref[head, 0:1, :]
        small_ref[row : row + 1, 640:768] = far_ref[head, 1:2, :]
    for copy in copies[base + 5 + pairs :]:
        copy.wait()
    rows = stack_ref.shape[0] // 3
    span = rows // 2

    def send_part(part, sent, kept):
        mine = bits_ref[part]
        sent_rows = pl.ds(pl.multiple_of(part * rows + (1 - mine) * span, span), span)
        kept_rows = pl.ds(pl.multiple_of(part * rows + mine * span, span), span)
        return start_copies(
            [
                (stack_ref.at[sent_rows], sent.at[:span], out_sems.at[steps + 4 + 2 * part]),
                (stack_ref.at[kept_rows], kept, out_sems.at[steps + 5 + 2 * part]),
            ]
        )

    span_rows = 384

    def head_rows(block, carry):
        start = pl.multiple_of(block * span_rows, span_rows)
        piece = pl.ds(start, span_rows)
        grad = contract_rows(normed_ref[:, piece], grads_ref[...])
        total = jnp.zeros((span_rows, 1), jnp.float32)
        for index, w_ref in enumerate((wq_ref, wk_ref, wv_ref)):
            part = grad[:, index * own : index * own + own]
            total = total + jnp.sum(part * w_ref[piece, :].astype(jnp.float32), axis=1, keepdims=True)
            stack_ref[pl.ds(pl.multiple_of(index * width + start, span_rows), span_rows), :] = part.astype(jnp.bfloat16)
        total_ref[piece, :] = jnp.broadcast_to(total, (span_rows, 128))
        return carry

    lax.fori_loop(0, width // span_rows, head_rows, 0)
    for part, (sent, kept) in enumerate(((sent_a, kept_a), (sent_b, kept_b))):
        outs += send_part(part, sent, kept)
    outs += send_part(2, sent_c, kept_c)
    wide = jnp.transpose(total_ref[...])
    small_ref[experts : experts + 1, :] = wide[:1, :] / gain_one_ref[...]
    small = small_ref[...]
    packed_ref[...] = jnp.concatenate([small[:, :own], small[:, own:]], axis=0).astype(jnp.bfloat16)
    outs += start_copies([(packed_ref, sent_a.at[span:], out_sems.at[steps + 3])])
    for copy in outs:
        copy.wait()


def back_pass(
    bits, where, slot_col, back_own, back_other, residual, out_grad, w_out, query_rows, key_rows,
    value_rows, mixed, long_probs, short_probs, normed, w_query, w_key, w_value, gain_one, gain_two,
    router_part,
):
    tok_count, width = normed.shape
    own = mixed.shape[1]
    slots, half = back_own.shape
    heads = long_probs.shape[0]
    count = router_part.shape[0] + 2 + heads
    span = 4 * width // 6
    tile = 512
    steps = tok_count // tile
    half_rows = hbm_out((span, own), jnp.bfloat16)
    pinned = (residual, out_grad, w_out, query_rows, key_rows, value_rows, mixed, long_probs, short_probs, normed,
              w_query, w_key, w_value)
    hbm = pl.BlockSpec(memory_space=pltpu.HBM)
    smem = pl.BlockSpec(memory_space=pltpu.SMEM)

    def scratch(array):
        return pltpu.VMEM(array.shape, array.dtype)

    flops = 2 * tok_count * width * (slots + 5 * own) + 10 * heads * (512 * 512 + 512 * 128) * 64
    out = pl.pallas_call(
        back_kernel,
        out_shape=[
            hbm_out((tok_count, width), jnp.float32),
            hbm_out((tok_count, 3 * own), jnp.bfloat16),
            hbm_out((span + 2 * count, own), jnp.bfloat16),
        ]
        + [half_rows] * 5,
        in_specs=[smem, smem] + [hbm, hbm, pl.BlockSpec(memory_space=pl.ANY)] + [hbm] * 13 + vmem(3),
        out_specs=[hbm] * 8,
        scratch_shapes=[scratch(slot_col), pltpu.VMEM((slots, width), jnp.bfloat16)]
        + [scratch(array) for array in pinned]
        + [
            pltpu.VMEM((tok_count, width), jnp.bfloat16),
            pltpu.VMEM((tok_count, own), jnp.bfloat16),
            pltpu.VMEM((tok_count, 3 * own), jnp.bfloat16),
            pltpu.VMEM((LONG_LEN, LONG_LEN), jnp.bfloat16),
            pltpu.VMEM((heads, 128, 384), jnp.float32),
            pltpu.VMEM((heads, 2, 128), jnp.float32),
            pltpu.VMEM((4 * width, own), jnp.bfloat16),
            pltpu.VMEM((count, width), jnp.float32),
            pltpu.VMEM((2 * count, own), jnp.bfloat16),
            pltpu.VMEM((width, 128), jnp.float32),
            pltpu.SemaphoreType.DMA((2 * steps + 4 + 5 + heads // 2 + 4,)),
            pltpu.SemaphoreType.DMA((steps + 10,)),
        ],
        compiler_params=params(40),
        cost_estimate=pl.CostEstimate(flops=flops, bytes_accessed=25000000, transcendentals=0),
        name="back",
    )(
        bits,
        where,
        in_hbm(slot_col),
        in_hbm(back_own),
        back_other,
        *(in_hbm(array) for array in pinned),
        gain_one.astype(jnp.float32)[None],
        gain_two.astype(jnp.float32)[None],
        router_part,
    )
    return out[0], out[1], out[2:5], out[5:]


def added(left, right):
    return (left.astype(jnp.float32) + right.astype(jnp.float32)).astype(jnp.bfloat16)


def fold_kernel(bits_ref, *refs):
    kept, got, sent, keep = refs[0:3], refs[3:6], refs[7:10], refs[10:13]
    before = refs[6]
    for part in range(3):
        span = kept[part].shape[0] // 2
        mine = bits_ref[part]
        for ref, start in ((sent[part], (1 - mine) * span), (keep[part], mine * span)):
            rows = pl.ds(pl.multiple_of(start, span), span)
            ref[:span, :] = added(kept[part][rows, :], got[part][rows, :])
    rows = kept[0].shape[0]
    sent[0][rows // 2 :, :] = added(before[rows:, :], got[0][rows:, :])


def fold(bits, kept, got, before):
    rows, lanes = kept[0].shape
    extra = before.shape[0] - rows
    half = jax.ShapeDtypeStruct((rows // 2, lanes), jnp.bfloat16)
    out = pl.pallas_call(
        fold_kernel,
        out_shape=[jax.ShapeDtypeStruct((rows // 2 + extra, lanes), jnp.bfloat16)] + [half] * 5,
        in_specs=[pl.BlockSpec(memory_space=pltpu.SMEM)] + vmem(7),
        out_specs=vmem(6),
        compiler_params=params(16),
        name="fold",
    )(bits, *kept, *got, before)
    return out[:3], out[3:]


def pack_kernel(*refs):
    kept, got, before, out = refs[0:3], refs[3:6], refs[6], refs[7]
    rows = kept[0].shape[0]
    for part in range(3):
        out[part * rows : (part + 1) * rows, :] = added(kept[part][...], got[part][:rows, :])
    out[3 * rows :, :] = added(before[rows:, :], got[0][rows:, :])


def pack(kept, got, before):
    rows, lanes = kept[0].shape
    return pl.pallas_call(
        pack_kernel,
        out_shape=jax.ShapeDtypeStruct((2 * rows + before.shape[0], lanes), jnp.bfloat16),
        in_specs=vmem(7),
        out_specs=vmem(1)[0],
        compiler_params=params(16),
        name="pack",
    )(*kept, *got, before)


def unpack_kernel(own_ref, got_ref, *out):
    rows = out[0].shape[0]
    for part in range(3):
        piece = slice(part * rows, (part + 1) * rows)
        out[part][...] = added(own_ref[piece, :], got_ref[piece, :])
    out[3][...] = own_ref[3 * rows :, :].astype(jnp.float32) + got_ref[3 * rows :, :].astype(jnp.float32)


def unpack(own, got, rows):
    lanes = own.shape[1]
    out = pl.pallas_call(
        unpack_kernel,
        out_shape=[jax.ShapeDtypeStruct((rows, lanes), jnp.bfloat16)] * 3
        + [jax.ShapeDtypeStruct((own.shape[0] - 3 * rows, lanes), jnp.float32)],
        in_specs=vmem(2),
        out_specs=vmem(4),
        compiler_params=params(16),
        name="unpack",
    )(own, got)
    return out[:3], out[3]


def join_kernel(bits_ref, *refs):
    own, got, out = refs[0:3], refs[3:6], refs[6:9]
    for part in range(3):
        span = own[part].shape[0]
        mine = bits_ref[part]
        out[part][pl.ds(pl.multiple_of(mine * span, span), span), :] = own[part][...]
        out[part][pl.ds(pl.multiple_of((1 - mine) * span, span), span), :] = got[part][...]


def join(bits, own, got):
    return pl.pallas_call(
        join_kernel,
        out_shape=[jax.ShapeDtypeStruct((p.shape[0] * 2, p.shape[1]), p.dtype) for p in own],
        in_specs=[pl.BlockSpec(memory_space=pltpu.SMEM)] + vmem(6),
        out_specs=vmem(3),
        compiler_params=params(16),
        name="join",
    )(bits, *own, *got)


def finish_kernel(bits_ref, *refs):
    own, got = refs[0:3], refs[3:6]
    results = refs[6:10]
    held, sems = refs[10:14], refs[14]
    span = own[0].shape[0]
    rows = 2 * span
    width, lanes = held[0].shape
    copies = []
    for part in range(3):
        mine = bits_ref[part]
        first = jnp.where(mine == 0, own[part][...], got[part][...])
        second = jnp.where(mine == 0, got[part][...], own[part][...])
        for base, piece in ((part * rows, first), (part * rows + span, second)):
            for index in range(3 + width // lanes):
                start = index * width if index < 3 else 3 * width + (index - 3) * lanes
                size = width if index < 3 else lanes
                low = max(start, base)
                high = min(start + size, base + span)
                if low < high:
                    values = piece[low - base : high - base, :].astype(jnp.float32)
                    if index < 3:
                        held[index][low - start : high - start, :] = values
                    else:
                        place = (index - 3) * lanes
                        held[3][low - start : high - start, place : place + lanes] = values
        for index in range(4):
            last = (index + 1) * width - 1
            if part * rows <= last < (part + 1) * rows:
                copies += start_copies([(held[index], results[index], sems.at[index])])
    for copy in copies:
        copy.wait()


def finish(bits, own, got, width):
    lanes = own[0].shape[1]
    shapes = [(width, lanes)] * 3 + [(lanes, width)]
    return pl.pallas_call(
        finish_kernel,
        out_shape=[hbm_out(shape, jnp.float32) for shape in shapes],
        in_specs=[pl.BlockSpec(memory_space=pltpu.SMEM)] + vmem(6),
        out_specs=[pl.BlockSpec(memory_space=pltpu.HBM)] * 4,
        scratch_shapes=[pltpu.VMEM(shape, jnp.float32) for shape in shapes]
        + [pltpu.SemaphoreType.DMA((4,))],
        compiler_params=params(24),
        name="finish",
    )(bits, *own, *got)


def swap_heads(rows):
    return lax.ppermute(rows, "heads", [(0, 1), (1, 0)])


def trade(rows, bit):
    count = lax.axis_size("seq")
    return lax.ppermute(rows, "seq", [(i, i ^ (1 << bit)) for i in range(count)])


def together(*groups):
    return lax.optimization_barrier(groups)


def contract_rows(left, right):
    return lax.dot_general(
        left, right, (((0,), (0,)), ((), ())), preferred_element_type=jnp.float32
    )


def on_device(
    tokens,
    gain_attn,
    w_query,
    w_key,
    w_value,
    w_out,
    bias_table,
    gain_ffn,
    w_router,
    w_inner,
    w_outer,
    routes,
    seq_lengths,
    out_grad,
):
    tok_count, width = tokens.shape
    bucket_count = bias_table.shape[0]
    experts = w_router.shape[1]
    capacity = max(2, 5 * tok_count // (4 * experts))
    senders = lax.axis_size("seq")
    bits = list(range(senders.bit_length() - 1))
    slots = experts * capacity
    half = width // 2
    own = w_query.shape[1]
    where = jnp.stack([lax.axis_index("heads"), lax.axis_index("seq")]).astype(jnp.int32)

    def exchange(rows):
        return lax.all_to_all(
            rows.reshape(senders, capacity, half), "seq", split_axis=0, concat_axis=0, tiled=True
        ).reshape(slots, half)

    def summed(keep, send):
        return (keep + swap_heads(send).astype(jnp.float32)).astype(jnp.bfloat16)

    slot_row, grad_sent = route(where, routes, out_grad, experts, capacity)
    grad_sent, tokens = together(grad_sent, tokens)
    grad_own = exchange(grad_sent)
    attn_part, normed, query_rows, key_rows, value_rows, mixed, long_probs, short_probs = attend(
        seq_lengths, tokens, gain_attn, w_query, w_key, w_value, w_out, bias_table
    )
    residual, second_sent = second_rows(
        where, tokens, attn_part, swap_heads(attn_part), gain_ffn, slot_row, slots
    )
    second_sent, grad_own = together(second_sent, grad_own)
    arrived_own = exchange(second_sent)

    inner = w_inner[0]
    outer = w_outer[0]
    grad_other = swap_heads(grad_own)
    hidden_grad = hidden_grad_of(where, grad_own, grad_other, outer)
    arrived_own, hidden_grad = together(arrived_own, hidden_grad)
    arrived_other = swap_heads(arrived_own)
    hidden, pre_grad, keep, send, logit_grad = expert(
        where, arrived_own, arrived_other, hidden_grad, inner, w_router
    )
    back_sum, hidden = together(summed(keep, send), hidden)
    back_own = exchange(back_sum)
    out_keep, out_send, router_part, slot_col = expert_out_of(
        where, hidden, arrived_own, arrived_other, logit_grad, slot_row, outer
    )
    out_sum = summed(out_keep, out_send)
    router_half = lax.dynamic_slice_in_dim(
        router_part + swap_heads(router_part), where[0] * (experts // 2), experts // 2, 0
    )
    back_own, out_sum, router_half = together(back_own, out_sum, router_half)
    back_other = swap_heads(back_own)
    returned = exchange(out_sum)

    depth = len(bits) - 1
    turns = [bits[k * depth // 3 : depth] + bits[: k * depth // 3] for k in range(3)]
    place = lax.axis_index("seq")
    mine = [jnp.stack([(place >> turn[k]) & 1 for turn in turns]).astype(jnp.int32) for k in range(depth)]
    residual_grad, head_grads, sent, kept = back_pass(
        mine[0], where, slot_col, back_own, back_other, residual, out_grad, w_out, query_rows, key_rows,
        value_rows, mixed, long_probs, short_probs, normed, w_query, w_key, w_value, gain_attn, gain_ffn,
        router_half,
    )

    def trades(arrays, k):
        return [trade(array, turn[k]) for array, turn in zip(arrays, turns)]

    for k in range(depth):
        got = trades(sent, k)
        if k == 0:
            output = output_of(where, slot_col, returned, residual, gain_ffn, w_router, capacity)
            got, output, head_grads = together(got, output, head_grads)
        if k == 1:
            normed_part = normed_back(head_grads, w_query, w_key, w_value)
            got, normed_part = together(got, normed_part)
        if k + 1 < depth:
            sent, kept = fold(mine[k + 1], kept, got, sent[0])
    normed_other = swap_heads(normed_part)
    packed = pack(kept, got, sent[0])
    packed, normed_other, pre_grad = together(packed, normed_other, pre_grad)
    got = trade(packed, bits[-1])
    inner_grad, outer_grad = expert_grads(
        where, arrived_own, arrived_other, grad_own, grad_other, hidden, pre_grad, w_router
    )
    got, inner_grad = together(got, inner_grad)
    summed_parts, small = unpack(packed, got, kept[0].shape[0])
    small = jnp.concatenate([small[: small.shape[0] // 2], small[small.shape[0] // 2 :]], axis=1)
    small_other = swap_heads(small)
    for k in reversed(range(1, depth)):
        got = trades(summed_parts, k)
        if k == depth - 1:
            got, small = together(got, small)
        if k == 1:
            lower = where[0] == 0
            own_rows, other_rows = small[: experts // 2], small_other[: experts // 2]
            router_grad = jnp.concatenate(
                [jnp.where(lower, own_rows, other_rows), jnp.where(lower, other_rows, own_rows)], axis=0
            ).T
            gain_one_grad = small[experts // 2] + small_other[experts // 2]
            gain_two_grad = small[experts // 2 + 1]
            table_grad = table_from(small[experts // 2 + 2 :], bucket_count)
            got, gain_one_grad, gain_two_grad, router_grad, table_grad = together(
                got, gain_one_grad, gain_two_grad, router_grad, table_grad
            )
        summed_parts = join(mine[k], summed_parts, got)
    got = trades(summed_parts, 0)
    input_grad = input_back(tokens, normed_part, normed_other, gain_attn, residual_grad)
    got, input_grad = together(got, input_grad)
    query_w_grad, key_w_grad, value_w_grad, out_w_grad = finish(mine[0], summed_parts, got, width)
    return (
        output,
        input_grad,
        gain_one_grad,
        query_w_grad,
        key_w_grad,
        value_w_grad,
        out_w_grad,
        table_grad,
        gain_two_grad,
        router_grad,
        inner_grad[None],
        outer_grad[None],
    )


def solution(mesh):
    in_specs = (
        P("seq", None),
        P(),
        P(None, "heads"),
        P(None, "heads"),
        P(None, "heads"),
        P("heads", None),
        P(None, "heads"),
        P(),
        P(),
        P("seq", None, "heads"),
        P("seq", "heads", None),
        P("seq", None),
        P("seq"),
        P("seq", None),
    )
    out_specs = (
        P("seq", "heads"),
        P("seq", None),
        P(),
        P(None, "heads"),
        P(None, "heads"),
        P(None, "heads"),
        P("heads", None),
        P(None, "heads"),
        P(),
        P(),
        P("seq", None, "heads"),
        P("seq", "heads", None),
    )
    return jax.shard_map(
        on_device, mesh=mesh, in_specs=in_specs, out_specs=out_specs, check_vma=False
    )
```

```python
from functools import partial

import jax
import jax.numpy as jnp
from jax import lax
from jax.experimental import pallas as pl
from jax.experimental.pallas import tpu as pltpu
from jax.sharding import PartitionSpec as P

SHORT_LEN = 128
LONG_LEN = 512
SHORT_DEV = 4
LONG_DEV = 1


epsilon = 1e-06
highest = lax.Precision.HIGHEST
far_limits = (12, 16, 23, 32, 46, 64, 91)


def vmem(count):
    return [pl.BlockSpec(memory_space=pltpu.VMEM)] * count


def params(mib=16):
    return pltpu.CompilerParams(vmem_limit_bytes=mib * 1024 * 1024)


def dot_nn(left, right):
    return jnp.dot(left, right, preferred_element_type=jnp.float32)


def dot_nt(left, right):
    return lax.dot_general(
        left, right, (((1,), (1,)), ((), ())), preferred_element_type=jnp.float32
    )


def inverse_rms(values):
    return lax.rsqrt(jnp.mean(values * values, axis=-1, keepdims=True) + epsilon)


def diagonal_buckets(offset):
    distance = jnp.abs(offset)
    far_bucket = jnp.full(offset.shape, 8, jnp.int32)
    for limit in far_limits:
        far_bucket = far_bucket + (distance >= limit).astype(jnp.int32)
    return jnp.where(distance < 8, distance, far_bucket) + jnp.where(offset > 0, 16, 0)


def hbm_out(shape, dtype):
    return pltpu.HBM(shape, dtype)


def in_hbm(array):
    return pltpu.with_memory_space_constraint(array, pltpu.HBM)


def start_copies(pairs):
    copies = [pltpu.make_async_copy(*triple) for triple in pairs]
    for copy in copies:
        copy.start()
    return copies


def attend_kernel(
    block_rows,
    lengths_ref,
    tokens_hbm,
    gain_ref,
    wq_hbm,
    wk_hbm,
    wv_hbm,
    wo_hbm,
    table_ref,
    part_hbm,
    normed_hbm,
    q_hbm,
    k_hbm,
    v_hbm,
    mixed_hbm,
    long_hbm,
    short_hbm,
    tokens_ref,
    joint_ref,
    wo_ref,
    part_ref,
    normed_ref,
    q_ref,
    k_ref,
    v_ref,
    mixed_ref,
    long_ref,
    short_ref,
    diag_ref,
    in_sems,
    out_sems,
):
    tok_count, width = tokens_ref.shape
    own = q_ref.shape[1]
    pairs = own // 128
    short_tok = SHORT_DEV * SHORT_LEN
    tile = 512
    steps = tok_count // tile
    tiles_in = []
    for step in range(steps):
        rows = slice(step * tile, step * tile + tile)
        tiles_in.append((tokens_hbm.at[rows], tokens_ref.at[rows], in_sems.at[step]))
    weights = [
        (source, joint_ref.at[:, index * own : index * own + own])
        for index, source in enumerate((wq_hbm, wk_hbm, wv_hbm))
    ]
    weights.append((wo_hbm, wo_ref))
    copies = start_copies(
        tiles_in + [(src, dst, in_sems.at[steps + index]) for index, (src, dst) in enumerate(weights)]
    )
    weight_copies = copies[steps:]
    outs = []

    offset = lax.broadcasted_iota(jnp.int32, (table_ref.shape[1], 512), 1) - 256
    hot = jnp.where(
        diagonal_buckets(offset)
        == lax.broadcasted_iota(jnp.int32, (table_ref.shape[1], 512), 0),
        1.0,
        0.0,
    )
    diag_ref[...] = dot_nn(table_ref[...], hot.astype(jnp.bfloat16))
    gain = gain_ref[...]

    def normalize(step, carry):
        rows = pl.ds(pl.multiple_of(step * tile, tile), tile)
        pltpu.make_async_copy(tokens_hbm.at[rows], tokens_ref.at[rows], in_sems.at[step]).wait()
        values = tokens_ref[rows, :].astype(jnp.float32)
        normed_ref[rows, :] = (values * inverse_rms(values) * gain).astype(jnp.bfloat16)
        return carry

    lax.fori_loop(0, steps, normalize, 0)
    outs += start_copies([(normed_ref, normed_hbm, out_sems.at[0])])
    for copy in weight_copies[:3]:
        copy.wait()

    def project(step, carry):
        rows = pl.ds(pl.multiple_of(step * tile, tile), tile)
        joint = dot_nn(normed_ref[rows, :], joint_ref[...]).astype(jnp.bfloat16)
        q_ref[rows, :] = joint[:, :own] * jnp.bfloat16(0.125)
        k_ref[rows, :] = joint[:, own : 2 * own]
        v_ref[rows, :] = joint[:, 2 * own :]
        return carry

    lax.fori_loop(0, steps, project, 0)
    outs += start_copies(
        [
            (q_ref, q_hbm, out_sems.at[1]),
            (k_ref, k_hbm, out_sems.at[2]),
            (v_ref, v_hbm, out_sems.at[3]),
        ]
    )
    lane = lax.broadcasted_iota(jnp.int32, (1, 128), 1)
    key_place = lax.broadcasted_iota(jnp.int32, (1, LONG_LEN), 1)
    live_long = key_place < lengths_ref[SHORT_DEV]

    def softmax(scores):
        weights = jnp.exp(scores - jnp.max(scores, axis=1, keepdims=True))
        return (weights * (1.0 / jnp.sum(weights, axis=1, keepdims=True))).astype(jnp.bfloat16)

    def one_pair(pair):
        lanes = slice(pair * 128, pair * 128 + 128)
        tiles = []
        for sub in range(2):
            row = diag_ref[pair * 2 + sub : pair * 2 + sub + 1, :]
            spread = pltpu.roll(
                jnp.broadcast_to(row, (128, 512)), 256, 1, stride=1, stride_axis=0
            )
            tiles.append(
                (
                    spread[:, 0:128],
                    spread[:, 128:256],
                    spread[:, 384:512],
                    jnp.broadcast_to(row[:, 511:512], (128, 128)),
                    jnp.broadcast_to(row[:, 0:1], (128, 128)),
                )
            )
        out = []
        for sub in range(2):
            scores = []
            for block in range(SHORT_DEV):
                rows = slice(block * 128, block * 128 + 128)
                masked = jnp.where((lane >= 64) == (sub == 1), q_ref[rows, lanes], 0)
                live = key_place[:, :128] < lengths_ref[block]
                scores.append(
                    jnp.where(
                        live, dot_nt(masked, k_ref[rows, lanes]) + tiles[sub][0], -1000000000.0
                    )
                )
            probs = softmax(jnp.concatenate(scores, axis=0))
            short_ref[pair * 2 + sub] = probs
            mixed = []
            for block in range(SHORT_DEV):
                rows = slice(block * 128, block * 128 + 128)
                mixed.append(dot_nn(probs[rows], v_ref[rows, lanes]))
            out.append(jnp.concatenate(mixed, axis=0))
        mixed_ref[:short_tok, lanes] = jnp.where(lane < 64, out[0], out[1]).astype(jnp.bfloat16)
        keys = k_ref[short_tok:, lanes]
        values = v_ref[short_tok:, lanes]
        for start in range(0, LONG_LEN, block_rows):
            places = slice(start, start + block_rows)
            rows = slice(short_tok + start, short_tok + start + block_rows)
            queries = q_ref[rows, lanes]
            out = []
            for sub in range(2):
                masked = jnp.where((lane >= 64) == (sub == 1), queries, 0)
                same, above, below, far_above, far_below = tiles[sub]
                bias = jnp.concatenate(
                    [
                        jnp.concatenate(
                            [
                                same
                                if other == block
                                else above
                                if other == block + 1
                                else below
                                if other == block - 1
                                else far_above
                                if other > block
                                else far_below
                                for other in range(LONG_LEN // 128)
                            ],
                            axis=1,
                        )
                        for block in range(start // 128, (start + block_rows) // 128)
                    ],
                    axis=0,
                )
                scores = jnp.where(live_long, dot_nt(masked, keys) + bias, -1000000000.0)
                probs = softmax(scores)
                long_ref[pair * 2 + sub, places, :] = probs
                out.append(dot_nn(probs, values))
            mixed_ref[rows, lanes] = jnp.where(lane < 64, out[0], out[1]).astype(jnp.bfloat16)

    for pair in range(pairs):
        one_pair(pair)
        both = slice(pair * 2, pair * 2 + 2)
        outs += start_copies(
            [
                (long_ref.at[both], long_hbm.at[both], out_sems.at[4 + 2 * pair]),
                (short_ref.at[both], short_hbm.at[both], out_sems.at[5 + 2 * pair]),
            ]
        )
    weight_copies[3].wait()
    base = 4 + 2 * pairs
    outs += start_copies([(mixed_ref, mixed_hbm, out_sems.at[base])])

    def part_copy(step):
        rows = pl.ds(pl.multiple_of(step * tile, tile), tile)
        return pltpu.make_async_copy(part_ref.at[rows], part_hbm.at[rows], out_sems.at[base + 1 + step])

    def project_out(step, carry):
        rows = pl.ds(pl.multiple_of(step * tile, tile), tile)
        part_ref[rows, :] = dot_nn(mixed_ref[rows, :], wo_ref[...]).astype(part_ref.dtype)
        part_copy(step).start()
        return carry

    lax.fori_loop(0, steps, project_out, 0)
    outs += [part_copy(step) for step in range(steps)]
    for copy in outs:
        copy.wait()


def attend(lengths, tokens, gain, w_query, w_key, w_value, w_out, table, block_rows=512):
    tok_count, width = tokens.shape
    own = w_query.shape[1]
    heads = own // 64
    heads_pad = -(-heads // 8) * 8
    table = jnp.pad(table.T, ((0, heads_pad - heads), (0, 0)))
    short_tok = SHORT_DEV * SHORT_LEN
    flops = 2 * tok_count * width * own * 4 + 4 * heads * (512 * 512 + short_tok * 128) * 64
    hbm = pl.BlockSpec(memory_space=pltpu.HBM)
    out_shapes = [
        ((tok_count, width), jnp.bfloat16),
        ((tok_count, width), jnp.bfloat16),
        ((tok_count, own), jnp.bfloat16),
        ((tok_count, own), jnp.bfloat16),
        ((tok_count, own), jnp.bfloat16),
        ((tok_count, own), jnp.bfloat16),
        ((heads, LONG_LEN, LONG_LEN), jnp.bfloat16),
        ((heads, short_tok, SHORT_LEN), jnp.bfloat16),
    ]
    steps = tok_count // 512
    return pl.pallas_call(
        partial(attend_kernel, block_rows),
        out_shape=[jax.ShapeDtypeStruct(*out_shapes[0])]
        + [hbm_out(shape, dtype) for shape, dtype in out_shapes[1:]],
        in_specs=[pl.BlockSpec(memory_space=pltpu.SMEM), hbm]
        + vmem(1)
        + [hbm] * 4
        + vmem(1),
        out_specs=[hbm] * 8,
        scratch_shapes=[pltpu.VMEM(tokens.shape, jnp.bfloat16)]
        + [pltpu.VMEM((width, 3 * own), jnp.bfloat16), pltpu.VMEM(w_out.shape, jnp.bfloat16)]
        + [pltpu.VMEM(shape, dtype) for shape, dtype in out_shapes]
        + [
            pltpu.VMEM((heads_pad, 512), jnp.float32),
            pltpu.SemaphoreType.DMA((steps + 4,)),
            pltpu.SemaphoreType.DMA((5 + 2 * (heads // 2) + steps,)),
        ],
        compiler_params=params(24),
        cost_estimate=pl.CostEstimate(
            flops=flops, bytes_accessed=16000000, transcendentals=heads * 512 * 640
        ),
        name="attend",
    )(
        lengths,
        in_hbm(tokens),
        gain.astype(jnp.float32)[None],
        in_hbm(w_query),
        in_hbm(w_key),
        in_hbm(w_value),
        in_hbm(w_out),
        table,
    )


def score_part(probs, prob_grad):
    mean = jnp.sum(probs * prob_grad, axis=1, keepdims=True) / jnp.sum(probs, axis=1, keepdims=True)
    return probs * (prob_grad - mean)


def attend_back_pair(
    pair, hg_ref, q_ref, k_ref, v_ref, long_ref, short_ref, grads_ref, tiles_ref, far_ref, sg_ref,
):
    short_tok = SHORT_DEV * SHORT_LEN
    lane = lax.broadcasted_iota(jnp.int32, (1, 128), 1)
    lanes = pl.ds(pl.multiple_of(pair * 128, 128), 128)
    blocks = LONG_LEN // 128
    heads_grad = hg_ref[:, lanes]
    q_t = jnp.transpose(q_ref[:, lanes])
    hg_t = jnp.transpose(heads_grad)
    qg = []
    kg_t = []
    vg_t = []
    for sub in range(2):
        head = pair * 2 + sub
        own = (lane >= 64) == (sub == 1)
        rows_t = slice(64 * sub, 64 * sub + 64)
        masked = jnp.where(own, heads_grad, 0)
        grads = [
            dot_nt(masked[block * 128 : block * 128 + 128], v_ref[block * 128 : block * 128 + 128, lanes])
            for block in range(SHORT_DEV)
        ]
        probs = short_ref[head]
        part = score_part(probs.astype(jnp.float32), jnp.concatenate(grads, axis=0))
        same = part[:128]
        for block in range(1, SHORT_DEV):
            same = same + part[block * 128 : block * 128 + 128]
        part = part.astype(jnp.bfloat16)
        qg_parts = []
        kg_parts = []
        vg_parts = []
        for block in range(SHORT_DEV):
            rows = slice(block * 128, block * 128 + 128)
            qg_parts.append(dot_nn(part[rows], k_ref[rows, lanes]))
            kg_parts.append(dot_nn(q_t[rows_t, rows], part[rows]))
            vg_parts.append(dot_nn(hg_t[rows_t, rows], probs[rows]))
        above = jnp.zeros((128, 128), jnp.float32)
        below = above
        far_above = above
        far_below = above
        probs = long_ref[head]
        part = score_part(
            probs.astype(jnp.float32), dot_nt(masked[short_tok:], v_ref[short_tok:, lanes])
        )
        for block in range(blocks):
            for other in range(blocks):
                piece = part[block * 128 : block * 128 + 128, other * 128 : other * 128 + 128]
                if other == block:
                    same = same + piece
                elif other == block + 1:
                    above = above + piece
                elif other == block - 1:
                    below = below + piece
                elif other > block:
                    far_above = far_above + piece
                else:
                    far_below = far_below + piece
        sg_ref[...] = part.astype(jnp.bfloat16)
        qg_parts.append(dot_nn(sg_ref[...], k_ref[short_tok:, lanes]))
        kg_parts.append(dot_nn(q_t[rows_t, short_tok:], sg_ref[...]))
        vg_parts.append(dot_nn(hg_t[rows_t, short_tok:], probs))
        qg.append(jnp.concatenate(qg_parts, axis=0))
        kg_t.append(jnp.concatenate(kg_parts, axis=1))
        vg_t.append(jnp.concatenate(vg_parts, axis=1))
        tiles_ref[head, :, 0:128] = same
        tiles_ref[head, :, 128:256] = above
        tiles_ref[head, :, 256:384] = below
        far_ref[head, 0:1, :] = jnp.sum(far_above, axis=0, keepdims=True)
        far_ref[head, 1:2, :] = jnp.sum(far_below, axis=0, keepdims=True)
    width = q_ref.shape[1]
    grads_ref[:, lanes] = (jnp.where(lane < 64, qg[0], qg[1]) * 0.125).astype(jnp.bfloat16)
    for index, whole in ((1, kg_t), (2, vg_t)):
        place = pl.ds(pl.multiple_of(index * width + pair * 128, 128), 128)
        grads_ref[:, place] = jnp.transpose(jnp.concatenate(whole, axis=0).astype(jnp.bfloat16))


def diagonals(tiles):
    tile = jnp.concatenate(
        [tiles[:, 0:256], jnp.zeros((128, 128), jnp.float32), tiles[:, 256:384]], axis=1
    )
    span = 64
    while span:
        tile = tile[:span] + pltpu.roll(tile[span:], 512 - span, 1)
        span //= 2
    return tile


def table_from(diag, bucket_count):
    lane = jnp.arange(768, dtype=jnp.int32)
    offset = jnp.where(lane < 256, lane, lane - 512)
    offset = jnp.where(lane >= 640, -256, jnp.where(lane >= 512, 256, offset))
    hot = (diagonal_buckets(offset)[:, None] == jnp.arange(bucket_count)[None, :]).astype(jnp.float32)
    return lax.dot_general(
        hot, diag, (((0,), (1,)), ((), ())), precision=highest, preferred_element_type=jnp.float32
    )


def dispatch_rows(send_ref, slot_row, half_rows):
    slots = send_ref.shape[0]
    tok_count = slot_row.shape[1]
    span = slots
    for base in range(0, slots, span):
        place = lax.broadcasted_iota(jnp.int32, (span, tok_count), 0) + base
        hot = jnp.where(place == slot_row, 1.0, 0.0).astype(jnp.bfloat16)
        send_ref[base : base + span, :] = dot_nn(hot, half_rows).astype(jnp.bfloat16)


def half_lanes(core, half):
    return pl.ds(pl.multiple_of(core * half, half), half)


def route_kernel(
    capacity, where_ref, routes_hbm, grad_hbm, row_hbm, send_ref, routes_ref, grad_ref, row_ref, in_sems,
    out_sem,
):
    tok_count = routes_ref.shape[1]
    slots, half = send_ref.shape
    experts = slots // capacity
    fetch, copy = start_copies(
        [
            (routes_hbm, routes_ref, in_sems.at[0]),
            (grad_hbm.at[:, half_lanes(where_ref[0], half)], grad_ref, in_sems.at[1]),
        ]
    )
    fetch.wait()
    routes = routes_ref[...]
    expert = lax.broadcasted_iota(jnp.int32, (experts, tok_count), 0)
    lane = lax.broadcasted_iota(jnp.int32, (1, tok_count), 1)
    hot = jnp.where(expert == routes, 1.0, 0.0)
    total = hot
    step = 1
    while step < tok_count:
        total = total + jnp.where(lane >= step, pltpu.roll(total, step, 1), 0.0)
        step *= 2
    before = jnp.sum(hot * total, axis=0, keepdims=True).astype(jnp.int32) - 1
    slot = jnp.where(before < capacity, routes * capacity + before, slots)
    row_ref[...] = slot
    out = pltpu.make_async_copy(row_ref, row_hbm, out_sem)
    out.start()
    copy.wait()
    dispatch_rows(send_ref, slot, grad_ref[...])
    out.wait()


def route(where, routes, out_grad, experts, capacity):
    tok_count, width = out_grad.shape
    slots = experts * capacity
    return pl.pallas_call(
        partial(route_kernel, capacity),
        out_shape=[
            hbm_out((1, tok_count), jnp.int32),
            jax.ShapeDtypeStruct((slots, width // 2), jnp.bfloat16),
        ],
        in_specs=[
            pl.BlockSpec(memory_space=pltpu.SMEM),
            pl.BlockSpec(memory_space=pltpu.HBM),
            pl.BlockSpec(memory_space=pltpu.HBM),
        ],
        out_specs=[pl.BlockSpec(memory_space=pltpu.HBM)] + vmem(1),
        scratch_shapes=[
            pltpu.VMEM((1, tok_count), jnp.int32),
            pltpu.VMEM((tok_count, width // 2), jnp.bfloat16),
            pltpu.VMEM((1, tok_count), jnp.int32),
            pltpu.SemaphoreType.DMA((2,)),
            pltpu.SemaphoreType.DMA,
        ],
        compiler_params=params(28),
        cost_estimate=pl.CostEstimate(
            flops=slots * tok_count * width, bytes_accessed=4000000, transcendentals=0
        ),
        name="route",
    )(where, in_hbm(routes.reshape(1, tok_count)), in_hbm(out_grad))


def second_kernel(
    where_ref, tokens_hbm, own_ref, other_ref, gain_ref, row_hbm, residual_hbm, send_ref, tokens_ref,
    row_ref, residual_ref, second_ref, in_sems, out_sems,
):
    tile = 256
    tok_count = tokens_ref.shape[0]
    half = send_ref.shape[1]
    tiles_rows = [slice(start, start + tile) for start in range(0, tok_count, tile)]
    copies = start_copies(
        [
            (tokens_hbm.at[rows], tokens_ref.at[rows], in_sems.at[step])
            for step, rows in enumerate(tiles_rows)
        ]
        + [(row_hbm, row_ref, in_sems.at[len(tiles_rows)])]
    )
    outs = []
    gain = gain_ref[...]
    for step, rows in enumerate(tiles_rows):
        attn = own_ref[rows, :].astype(jnp.float32) + other_ref[rows, :].astype(jnp.float32)
        copies[step].wait()
        residual = tokens_ref[rows, :].astype(jnp.float32) + attn
        residual_ref[rows, :] = residual
        outs += start_copies([(residual_ref.at[rows], residual_hbm.at[rows], out_sems.at[step])])
        second_ref[rows, :] = (residual * inverse_rms(residual) * gain).astype(jnp.bfloat16)
    copies[-1].wait()
    dispatch_rows(send_ref, row_ref[...], second_ref[:, half_lanes(where_ref[0], half)])
    for copy in outs:
        copy.wait()


def second_rows(where, tokens, own, other, gain, slot_row, slots):
    tok_count, width = tokens.shape
    steps = tok_count // 256
    hbm = pl.BlockSpec(memory_space=pltpu.HBM)
    return pl.pallas_call(
        second_kernel,
        out_shape=[
            hbm_out((tok_count, width), jnp.float32),
            jax.ShapeDtypeStruct((slots, width // 2), jnp.bfloat16),
        ],
        in_specs=[pl.BlockSpec(memory_space=pltpu.SMEM), hbm] + vmem(3) + [hbm],
        out_specs=[hbm] + vmem(1),
        scratch_shapes=[
            pltpu.VMEM((tok_count, width), jnp.bfloat16),
            pltpu.VMEM((1, tok_count), jnp.int32),
            pltpu.VMEM((tok_count, width), jnp.float32),
            pltpu.VMEM((tok_count, width), jnp.bfloat16),
            pltpu.SemaphoreType.DMA((steps + 1,)),
            pltpu.SemaphoreType.DMA((steps,)),
        ],
        compiler_params=params(28),
        cost_estimate=pl.CostEstimate(
            flops=slots * tok_count * width, bytes_accessed=13000000, transcendentals=0
        ),
        name="second",
    )(where, in_hbm(tokens), own, other, gain.astype(jnp.float32)[None], in_hbm(slot_row))


def hidden_grad_kernel(where_ref, own_ref, other_ref, outer_ref, out_ref, whole_ref):
    half = own_ref.shape[1]
    core = where_ref[0]
    whole_ref[:, half_lanes(core, half)] = own_ref[...]
    whole_ref[:, half_lanes(1 - core, half)] = other_ref[...]
    out_ref[...] = dot_nt(whole_ref[...], outer_ref[...]).astype(jnp.bfloat16)


def hidden_grad_of(where, own, other, outer):
    slots, half = own.shape
    hidden = outer.shape[0]
    tile = 256
    rows = pl.BlockSpec((tile, half), lambda step: (step, 0))
    return pl.pallas_call(
        hidden_grad_kernel,
        grid=(slots // tile,),
        out_shape=hbm_out((slots, hidden), jnp.bfloat16),
        in_specs=[pl.BlockSpec(memory_space=pltpu.SMEM), rows, rows] + vmem(1),
        out_specs=pl.BlockSpec((tile, hidden), lambda step: (step, 0)),
        scratch_shapes=[pltpu.VMEM((tile, 2 * half), jnp.bfloat16)],
        compiler_params=params(),
        cost_estimate=pl.CostEstimate(
            flops=4 * slots * half * hidden, bytes_accessed=12000000, transcendentals=0
        ),
        name="hidden_grad",
    )(where, own, other, outer)


def gate_of(rows, router, index):
    experts = router.shape[1]
    logits = dot_nn(rows, router)
    exp_logit = jnp.exp(logits - jnp.max(logits, axis=1, keepdims=True))
    probs = exp_logit * (1.0 / jnp.sum(exp_logit, axis=1, keepdims=True))
    hit = jnp.where(lax.broadcasted_iota(jnp.int32, (1, experts), 1) == index, 1.0, 0.0)
    return probs, hit, jnp.sum(probs * hit, axis=1, keepdims=True)


def expert_kernel(
    where_ref,
    own_ref,
    other_ref,
    hg_ref,
    inner_ref,
    router_ref,
    hidden_ref,
    pre_grad_ref,
    keep_ref,
    send_ref,
    logit_ref,
    arrived_ref,
    whole_ref,
):
    core = where_ref[0]
    tile, half = own_ref.shape
    own_lanes = half_lanes(core, half)
    other_lanes = half_lanes(1 - core, half)
    arrived_ref[:, own_lanes] = own_ref[...]
    arrived_ref[:, other_lanes] = other_ref[...]
    arrived = arrived_ref[...]
    probs, hit, gate = gate_of(arrived, router_ref[...], where_ref[1])
    curve = 0.7978845608028654
    gate_grad = jnp.zeros((tile, 1), jnp.float32)
    back = jnp.zeros((tile, 2 * half), jnp.float32)
    chunk = 512
    for start in range(0, hg_ref.shape[1], chunk):
        cols = slice(start, start + chunk)
        pre = dot_nn(arrived, inner_ref[:, cols])
        square = pre * pre
        share = 0.5 + 0.5 * jnp.tanh(pre * (curve + (curve * 0.044715) * square))
        hidden_ref[:, cols] = (pre * share).astype(jnp.bfloat16)
        passed = share * hg_ref[:, cols].astype(jnp.float32)
        gate_grad = gate_grad + jnp.sum(pre * passed, axis=1, keepdims=True)
        bend = pre * (2.0 * curve + (6.0 * curve * 0.044715) * square)
        pre_grad = ((gate * passed) * (1.0 + (1.0 - share) * bend)).astype(jnp.bfloat16)
        pre_grad_ref[:, cols] = pre_grad
        back = back + dot_nt(pre_grad, inner_ref[:, cols])
    logit = (probs * (gate_grad * (hit - gate))).astype(jnp.bfloat16)
    logit_ref[...] = logit
    whole_ref[...] = back + dot_nt(logit, router_ref[...])
    send_ref[...] = whole_ref[:, other_lanes].astype(jnp.bfloat16)
    keep_ref[...] = whole_ref[:, own_lanes]


def expert(where, own, other, hidden_grad, inner, router):
    slots, half = own.shape
    width, hidden = inner.shape
    experts = router.shape[1]
    tile = 256
    halves = pl.BlockSpec((tile, half), lambda step: (step, 0))
    units = pl.BlockSpec((tile, hidden), lambda step: (step, 0))
    return pl.pallas_call(
        expert_kernel,
        grid=(slots // tile,),
        out_shape=[
            hbm_out((slots, hidden), jnp.bfloat16),
            hbm_out((slots, hidden), jnp.bfloat16),
            jax.ShapeDtypeStruct((slots, half), jnp.float32),
            jax.ShapeDtypeStruct((slots, half), jnp.bfloat16),
            hbm_out((slots, experts), jnp.bfloat16),
        ],
        in_specs=[
            pl.BlockSpec(memory_space=pltpu.SMEM),
            halves,
            halves,
            units,
            pl.BlockSpec(inner.shape, lambda step: (0, 0), pipeline_mode=pl.Buffered(1)),
        ]
        + vmem(1),
        out_specs=[
            units,
            units,
            halves,
            halves,
            pl.BlockSpec((tile, experts), lambda step: (step, 0)),
        ],
        scratch_shapes=[
            pltpu.VMEM((tile, width), jnp.bfloat16),
            pltpu.VMEM((tile, width), jnp.float32),
        ],
        compiler_params=params(),
        cost_estimate=pl.CostEstimate(
            flops=4 * slots * width * hidden, bytes_accessed=20000000, transcendentals=slots * hidden
        ),
        name="expert",
    )(where, own, other, in_hbm(hidden_grad), in_hbm(inner), router)


def expert_out_kernel(
    where_ref, hidden_ref, own_ref, other_ref, logit_ref, row_ref, outer_ref, keep_ref, send_ref, router_ref,
    col_ref, whole_ref,
):
    core = where_ref[0]
    half = keep_ref.shape[1]
    own_lanes = half_lanes(core, half)
    other_lanes = half_lanes(1 - core, half)
    whole_ref[...] = dot_nn(hidden_ref[...], outer_ref[...])
    send_ref[...] = whole_ref[:, other_lanes].astype(jnp.bfloat16)
    keep_ref[...] = whole_ref[:, own_lanes]

    @pl.when(pl.program_id(0) == 0)
    def _():
        router_ref[...] = jnp.zeros_like(router_ref)
        wide = jnp.broadcast_to(row_ref[...].astype(jnp.float32), (128, row_ref.shape[1]))
        col_ref[...] = jnp.transpose(wide).astype(jnp.int32)

    router_ref[:, own_lanes] += contract_rows(logit_ref[...], own_ref[...])
    router_ref[:, other_lanes] += contract_rows(logit_ref[...], other_ref[...])


def expert_out_of(where, hidden, own, other, logit_grad, slot_row, outer):
    slots, units = hidden.shape
    tok_count = slot_row.shape[1]
    width = outer.shape[1]
    experts = logit_grad.shape[1]
    half = width // 2
    tile = 256
    halves = pl.BlockSpec((tile, half), lambda step: (step, 0))
    return pl.pallas_call(
        expert_out_kernel,
        grid=(slots // tile,),
        out_shape=[
            jax.ShapeDtypeStruct((slots, half), jnp.float32),
            jax.ShapeDtypeStruct((slots, half), jnp.bfloat16),
            hbm_out((experts, width), jnp.float32),
            hbm_out((tok_count, 128), jnp.int32),
        ],
        in_specs=[
            pl.BlockSpec(memory_space=pltpu.SMEM),
            pl.BlockSpec((tile, units), lambda step: (step, 0)),
            halves,
            halves,
            pl.BlockSpec((tile, experts), lambda step: (step, 0)),
            pl.BlockSpec((1, tok_count), lambda step: (0, 0)),
        ]
        + vmem(1),
        out_specs=[
            halves,
            halves,
            pl.BlockSpec((experts, width), lambda step: (0, 0)),
            pl.BlockSpec((tok_count, 128), lambda step: (0, 0)),
        ],
        scratch_shapes=[pltpu.VMEM((tile, width), jnp.float32)],
        compiler_params=params(),
        cost_estimate=pl.CostEstimate(
            flops=2 * slots * width * units, bytes_accessed=9000000, transcendentals=0
        ),
        name="expert_out",
    )(
        where, in_hbm(hidden), in_hbm(own), in_hbm(other), in_hbm(logit_grad), in_hbm(slot_row), outer
    )


def expert_grads_kernel(
    where_ref,
    own_hbm,
    other_hbm,
    grad_own_hbm,
    grad_other_hbm,
    hidden_ref,
    pre_grad_ref,
    router_ref,
    inner_grad_ref,
    outer_grad_ref,
    arrived_ref,
    gated_ref,
    sems,
):
    core = where_ref[0]
    half = own_hbm.shape[1]
    own_lanes = half_lanes(core, half)
    other_lanes = half_lanes(1 - core, half)

    @pl.when(pl.program_id(0) == 0)
    def _():
        copies = [
            pltpu.make_async_copy(own_hbm, arrived_ref.at[:, own_lanes], sems.at[0]),
            pltpu.make_async_copy(other_hbm, arrived_ref.at[:, other_lanes], sems.at[1]),
            pltpu.make_async_copy(grad_own_hbm, gated_ref.at[:, own_lanes], sems.at[2]),
            pltpu.make_async_copy(grad_other_hbm, gated_ref.at[:, other_lanes], sems.at[3]),
        ]
        for copy in copies:
            copy.start()
        for copy in copies:
            copy.wait()
        gate = gate_of(arrived_ref[...], router_ref[...], where_ref[1])[2]
        gated_ref[...] = (gate * gated_ref[...].astype(jnp.float32)).astype(jnp.bfloat16)

    outer_grad_ref[...] = contract_rows(hidden_ref[...], gated_ref[...])
    inner_grad_ref[...] = contract_rows(arrived_ref[...], pre_grad_ref[...])


def expert_grads(where, own, other, grad_own, grad_other, hidden, pre_grad, router):
    slots, half = own.shape
    units = hidden.shape[1]
    width = router.shape[0]
    tile = 256
    hbm = pl.BlockSpec(memory_space=pltpu.HBM)
    whole = lambda shape: pl.BlockSpec(shape, lambda step: (0, 0))
    cols = pl.BlockSpec((slots, tile), lambda step: (0, step))
    return pl.pallas_call(
        expert_grads_kernel,
        grid=(units // tile,),
        out_shape=[
            hbm_out((width, units), jnp.float32),
            hbm_out((units, width), jnp.float32),
        ],
        in_specs=[
            pl.BlockSpec(memory_space=pltpu.SMEM),
            hbm,
            hbm,
            hbm,
            hbm,
            cols,
            cols,
            whole(router.shape),
        ],
        out_specs=[
            pl.BlockSpec((width, tile), lambda step: (0, step)),
            pl.BlockSpec((tile, width), lambda step: (step, 0)),
        ],
        scratch_shapes=[
            pltpu.VMEM((slots, width), jnp.bfloat16),
            pltpu.VMEM((slots, width), jnp.bfloat16),
            pltpu.SemaphoreType.DMA((4,)),
        ],
        compiler_params=params(24),
        cost_estimate=pl.CostEstimate(
            flops=4 * slots * width * units, bytes_accessed=22000000, transcendentals=0
        ),
        name="expert_grads",
    )(
        where,
        in_hbm(own),
        in_hbm(other),
        in_hbm(grad_own),
        in_hbm(grad_other),
        in_hbm(hidden),
        in_hbm(pre_grad),
        router,
    )


def output_kernel(
    capacity, where_ref, col_ref, returned_ref, residual_ref, gain_ref, router_ref, out_ref
):
    slots, half = returned_ref.shape
    tile = residual_ref.shape[0]
    experts = router_ref.shape[1]
    col = col_ref[:, :1]
    place = lax.broadcasted_iota(jnp.int32, (tile, slots), 1)
    hot = jnp.where(place == col, 1.0, 0.0).astype(jnp.bfloat16)
    token_out = dot_nn(hot, returned_ref[...])
    residual = residual_ref[...]
    second = (residual * inverse_rms(residual) * gain_ref[...]).astype(jnp.bfloat16)
    logits = dot_nn(second, router_ref[...])
    exp_logit = jnp.exp(logits - jnp.max(logits, axis=1, keepdims=True))
    first = lax.broadcasted_iota(jnp.int32, (1, experts), 1) * capacity
    hit = jnp.where((col >= first) & (col < first + capacity), exp_logit, 0.0)
    gate = jnp.sum(hit, axis=1, keepdims=True) / jnp.sum(exp_logit, axis=1, keepdims=True)
    own = residual_ref[:, half_lanes(where_ref[0], half)]
    out_ref[...] = (own + gate * token_out).astype(jnp.bfloat16)


def output_of(where, slot_col, returned, residual, gain, router, capacity):
    tok_count, width = residual.shape
    slots, half = returned.shape
    tile = 256
    whole = lambda shape: pl.BlockSpec(shape, lambda step: (0, 0))
    return pl.pallas_call(
        partial(output_kernel, capacity),
        grid=(tok_count // tile,),
        out_shape=jax.ShapeDtypeStruct((tok_count, half), jnp.bfloat16),
        in_specs=[
            pl.BlockSpec(memory_space=pltpu.SMEM),
            pl.BlockSpec((tile, 128), lambda step: (step, 0)),
            whole(returned.shape),
            pl.BlockSpec((tile, width), lambda step: (step, 0)),
            whole((1, width)),
            whole(router.shape),
        ],
        out_specs=pl.BlockSpec((tile, half), lambda step: (step, 0)),
        compiler_params=params(),
        cost_estimate=pl.CostEstimate(
            flops=2 * tok_count * half * slots, bytes_accessed=6000000, transcendentals=0
        ),
        name="output",
    )(
        where, in_hbm(slot_col), in_hbm(returned), in_hbm(residual), gain.astype(jnp.float32)[None], router
    )


def normed_back_kernel(grads_ref, wq_ref, wk_ref, wv_ref, out_ref):
    own = wq_ref.shape[1]
    out_ref[...] = (
        dot_nt(grads_ref[:, :own], wq_ref[...])
        + dot_nt(grads_ref[:, own : 2 * own], wk_ref[...])
        + dot_nt(grads_ref[:, 2 * own :], wv_ref[...])
    ).astype(jnp.bfloat16)


def normed_back(grads, w_query, w_key, w_value):
    tok_count = grads.shape[0]
    width, own = w_query.shape
    tile = 512
    whole = pl.BlockSpec((width, own), lambda step: (0, 0))
    return pl.pallas_call(
        normed_back_kernel,
        grid=(tok_count // tile,),
        out_shape=jax.ShapeDtypeStruct((tok_count, width), jnp.bfloat16),
        in_specs=[pl.BlockSpec((tile, 3 * own), lambda step: (step, 0))] + [whole] * 3,
        out_specs=pl.BlockSpec((tile, width), lambda step: (step, 0)),
        compiler_params=params(),
        cost_estimate=pl.CostEstimate(
            flops=6 * tok_count * own * width, bytes_accessed=6000000, transcendentals=0
        ),
        name="normed_back",
    )(*(in_hbm(array) for array in (grads, w_query, w_key, w_value)))


def input_back_kernel(tokens_ref, own_ref, other_ref, gain_ref, residual_ref, out_ref):
    ybar = own_ref[...].astype(jnp.float32) + other_ref[...].astype(jnp.float32)
    values = tokens_ref[...].astype(jnp.float32)
    scale = inverse_rms(values)
    scaled = values * scale
    pulled = ybar * gain_ref[...]
    out_ref[...] = residual_ref[...] + scale * (
        pulled - scaled * jnp.mean(pulled * scaled, axis=1, keepdims=True)
    )


def input_back(tokens, own, other, gain, residual_grad):
    tok_count, width = tokens.shape
    tile = 256
    rows = pl.BlockSpec((tile, width), lambda step: (step, 0))
    return pl.pallas_call(
        input_back_kernel,
        grid=(tok_count // tile,),
        out_shape=jax.ShapeDtypeStruct((tok_count, width), jnp.float32),
        in_specs=[rows, rows, rows, pl.BlockSpec((1, width), lambda step: (0, 0)), rows],
        out_specs=rows,
        compiler_params=params(),
        cost_estimate=pl.CostEstimate(
            flops=10 * tok_count * width, bytes_accessed=11000000, transcendentals=0
        ),
        name="input_back",
    )(in_hbm(tokens), own, other, gain.astype(jnp.float32)[None], in_hbm(residual_grad))


def back_kernel(
    bits_ref,
    where_ref,
    col_hbm,
    own_hbm,
    other_hbm,
    residual_hbm,
    grad_hbm,
    wo_hbm,
    q_hbm,
    k_hbm,
    v_hbm,
    mixed_hbm,
    long_hbm,
    short_hbm,
    normed_hbm,
    wq_hbm,
    wk_hbm,
    wv_hbm,
    gain_one_ref,
    gain_two_ref,
    router_ref,
    out_hbm,
    grads_hbm,
    sent_a,
    sent_b,
    sent_c,
    kept_a,
    kept_b,
    kept_c,
    col_ref,
    back_ref,
    residual_ref,
    grad_ref,
    wo_ref,
    q_ref,
    k_ref,
    v_ref,
    mixed_ref,
    long_ref,
    short_ref,
    normed_ref,
    wq_ref,
    wk_ref,
    wv_ref,
    attn_ref,
    heads_ref,
    grads_ref,
    sg_ref,
    tiles_ref,
    far_ref,
    stack_ref,
    small_ref,
    packed_ref,
    total_ref,
    in_sems,
    out_sems,
):
    tok_count, width = residual_ref.shape
    slots, half = own_hbm.shape
    own = mixed_ref.shape[1]
    experts = router_ref.shape[0]
    pairs = own // 128
    tile = 512
    steps = tok_count // tile
    core = where_ref[0]
    first = [
        (own_hbm, back_ref.at[:, half_lanes(core, half)]),
        (other_hbm, back_ref.at[:, half_lanes(1 - core, half)]),
        (col_hbm, col_ref),
        (wo_hbm, wo_ref),
    ]
    tiles = []
    for start in range(0, tok_count, tile):
        rows = slice(start, start + tile)
        tiles.append((residual_hbm.at[rows], residual_ref.at[rows]))
        tiles.append((grad_hbm.at[rows], grad_ref.at[rows]))
    attention = [(q_hbm, q_ref), (k_hbm, k_ref), (v_hbm, v_ref), (mixed_hbm, mixed_ref), (short_hbm, short_ref)]
    for pair in range(pairs):
        both = slice(pair * 2, pair * 2 + 2)
        attention.append((long_hbm.at[both], long_ref.at[both]))
    weights = [(normed_hbm, normed_ref), (wq_hbm, wq_ref), (wk_hbm, wk_ref), (wv_hbm, wv_ref)]
    copies = start_copies(
        [
            (source, target, in_sems.at[index])
            for index, (source, target) in enumerate(first + tiles + attention + weights)
        ]
    )
    base = len(first) + len(tiles)
    outs = []

    for copy in copies[: len(first)]:
        copy.wait()
    gain_two = gain_two_ref[...]
    place = lax.broadcasted_iota(jnp.int32, (tile, slots), 1)

    def tile_out(step):
        rows = pl.ds(pl.multiple_of(step * tile, tile), tile)
        return pltpu.make_async_copy(residual_ref.at[rows], out_hbm.at[rows], out_sems.at[step])

    def one_tile(step, gain_two_grad):
        rows = pl.ds(pl.multiple_of(step * tile, tile), tile)
        at = len(first) + 2 * step
        pltpu.make_async_copy(residual_hbm.at[rows], residual_ref.at[rows], in_sems.at[at]).wait()
        pltpu.make_async_copy(grad_hbm.at[rows], grad_ref.at[rows], in_sems.at[at + 1]).wait()
        hot = jnp.where(place == col_ref[rows, :][:, :1], 1.0, 0.0).astype(jnp.bfloat16)
        ybar = dot_nn(hot, back_ref[...])
        values = residual_ref[rows, :]
        scale = inverse_rms(values)
        scaled = values * scale
        pulled = ybar * gain_two
        back = scale * (pulled - scaled * jnp.mean(pulled * scaled, axis=1, keepdims=True))
        out = back + grad_ref[rows, :].astype(jnp.float32)
        residual_ref[rows, :] = out
        attn = out.astype(jnp.bfloat16)
        attn_ref[rows, :] = attn
        heads_ref[rows, :] = dot_nt(attn, wo_ref[...]).astype(jnp.bfloat16)
        tile_out(step).start()
        return gain_two_grad + jnp.sum(ybar * scaled, axis=0, keepdims=True)

    gain_two_grad = lax.fori_loop(0, steps, one_tile, jnp.zeros((1, width), jnp.float32))
    outs += [tile_out(step) for step in range(steps)]

    for copy in copies[base : base + 5]:
        copy.wait()

    def one_pair(pair, carry):
        both = pl.ds(pair * 2, 2)
        pltpu.make_async_copy(long_hbm.at[both], long_ref.at[both], in_sems.at[base + 5 + pair]).wait()
        attend_back_pair(
            pair, heads_ref, q_ref, k_ref, v_ref, long_ref, short_ref, grads_ref, tiles_ref, far_ref,
            sg_ref,
        )
        return carry

    lax.fori_loop(0, pairs, one_pair, 0, unroll=True)
    outs += start_copies([(grads_ref, grads_hbm, out_sems.at[steps])])

    grad = contract_rows(mixed_ref[...], attn_ref[...]).astype(jnp.bfloat16)
    for part in range(width // own):
        at = 3 * width + part * own
        stack_ref[at : at + own, :] = grad[:, part * own : part * own + own]
    small_ref[0:experts, :] = router_ref[...]
    small_ref[experts + 1 : experts + 2, :] = gain_two_grad
    for head in range(2 * pairs):
        row = experts + 2 + head
        small_ref[row : row + 1, 0:512] = diagonals(tiles_ref[head])
        small_ref[row : row + 1, 512:640] = far_ref[head, 0:1, :]
        small_ref[row : row + 1, 640:768] = far_ref[head, 1:2, :]
    for copy in copies[base + 5 + pairs :]:
        copy.wait()
    rows = stack_ref.shape[0] // 3
    span = rows // 2

    def send_part(part, sent, kept):
        mine = bits_ref[part]
        sent_rows = pl.ds(pl.multiple_of(part * rows + (1 - mine) * span, span), span)
        kept_rows = pl.ds(pl.multiple_of(part * rows + mine * span, span), span)
        return start_copies(
            [
                (stack_ref.at[sent_rows], sent.at[:span], out_sems.at[steps + 4 + 2 * part]),
                (stack_ref.at[kept_rows], kept, out_sems.at[steps + 5 + 2 * part]),
            ]
        )

    span_rows = 384

    def head_rows(block, carry):
        start = pl.multiple_of(block * span_rows, span_rows)
        piece = pl.ds(start, span_rows)
        grad = contract_rows(normed_ref[:, piece], grads_ref[...])
        total = jnp.zeros((span_rows, 1), jnp.float32)
        for index, w_ref in enumerate((wq_ref, wk_ref, wv_ref)):
            part = grad[:, index * own : index * own + own]
            total = total + jnp.sum(part * w_ref[piece, :].astype(jnp.float32), axis=1, keepdims=True)
            stack_ref[pl.ds(pl.multiple_of(index * width + start, span_rows), span_rows), :] = part.astype(jnp.bfloat16)
        total_ref[piece, :] = jnp.broadcast_to(total, (span_rows, 128))
        return carry

    lax.fori_loop(0, width // span_rows, head_rows, 0)
    for part, (sent, kept) in enumerate(((sent_a, kept_a), (sent_b, kept_b))):
        outs += send_part(part, sent, kept)
    outs += send_part(2, sent_c, kept_c)
    wide = jnp.transpose(total_ref[...])
    small_ref[experts : experts + 1, :] = wide[:1, :] / gain_one_ref[...]
    small = small_ref[...]
    packed_ref[...] = jnp.concatenate([small[:, :own], small[:, own:]], axis=0).astype(jnp.bfloat16)
    outs += start_copies([(packed_ref, sent_a.at[span:], out_sems.at[steps + 3])])
    for copy in outs:
        copy.wait()


def back_pass(
    bits, where, slot_col, back_own, back_other, residual, out_grad, w_out, query_rows, key_rows,
    value_rows, mixed, long_probs, short_probs, normed, w_query, w_key, w_value, gain_one, gain_two,
    router_part,
):
    tok_count, width = normed.shape
    own = mixed.shape[1]
    slots, half = back_own.shape
    heads = long_probs.shape[0]
    count = router_part.shape[0] + 2 + heads
    span = 4 * width // 6
    tile = 512
    steps = tok_count // tile
    half_rows = hbm_out((span, own), jnp.bfloat16)
    pinned = (residual, out_grad, w_out, query_rows, key_rows, value_rows, mixed, long_probs, short_probs, normed,
              w_query, w_key, w_value)
    hbm = pl.BlockSpec(memory_space=pltpu.HBM)
    smem = pl.BlockSpec(memory_space=pltpu.SMEM)

    def scratch(array):
        return pltpu.VMEM(array.shape, array.dtype)

    flops = 2 * tok_count * width * (slots + 5 * own) + 10 * heads * (512 * 512 + 512 * 128) * 64
    out = pl.pallas_call(
        back_kernel,
        out_shape=[
            hbm_out((tok_count, width), jnp.float32),
            hbm_out((tok_count, 3 * own), jnp.bfloat16),
            hbm_out((span + 2 * count, own), jnp.bfloat16),
        ]
        + [half_rows] * 5,
        in_specs=[smem, smem] + [hbm, hbm, pl.BlockSpec(memory_space=pl.ANY)] + [hbm] * 13 + vmem(3),
        out_specs=[hbm] * 8,
        scratch_shapes=[scratch(slot_col), pltpu.VMEM((slots, width), jnp.bfloat16)]
        + [scratch(array) for array in pinned]
        + [
            pltpu.VMEM((tok_count, width), jnp.bfloat16),
            pltpu.VMEM((tok_count, own), jnp.bfloat16),
            pltpu.VMEM((tok_count, 3 * own), jnp.bfloat16),
            pltpu.VMEM((LONG_LEN, LONG_LEN), jnp.bfloat16),
            pltpu.VMEM((heads, 128, 384), jnp.float32),
            pltpu.VMEM((heads, 2, 128), jnp.float32),
            pltpu.VMEM((4 * width, own), jnp.bfloat16),
            pltpu.VMEM((count, width), jnp.float32),
            pltpu.VMEM((2 * count, own), jnp.bfloat16),
            pltpu.VMEM((width, 128), jnp.float32),
            pltpu.SemaphoreType.DMA((2 * steps + 4 + 5 + heads // 2 + 4,)),
            pltpu.SemaphoreType.DMA((steps + 10,)),
        ],
        compiler_params=params(40),
        cost_estimate=pl.CostEstimate(flops=flops, bytes_accessed=25000000, transcendentals=0),
        name="back",
    )(
        bits,
        where,
        in_hbm(slot_col),
        in_hbm(back_own),
        back_other,
        *(in_hbm(array) for array in pinned),
        gain_one.astype(jnp.float32)[None],
        gain_two.astype(jnp.float32)[None],
        router_part,
    )
    return out[0], out[1], out[2:5], out[5:]


def added(left, right):
    return (left.astype(jnp.float32) + right.astype(jnp.float32)).astype(jnp.bfloat16)


def fold_kernel(bits_ref, *refs):
    kept, got, sent, keep = refs[0:3], refs[3:6], refs[7:10], refs[10:13]
    before = refs[6]
    for part in range(3):
        span = kept[part].shape[0] // 2
        mine = bits_ref[part]
        for ref, start in ((sent[part], (1 - mine) * span), (keep[part], mine * span)):
            rows = pl.ds(pl.multiple_of(start, span), span)
            ref[:span, :] = added(kept[part][rows, :], got[part][rows, :])
    rows = kept[0].shape[0]
    sent[0][rows // 2 :, :] = added(before[rows:, :], got[0][rows:, :])


def fold(bits, kept, got, before):
    rows, lanes = kept[0].shape
    extra = before.shape[0] - rows
    half = jax.ShapeDtypeStruct((rows // 2, lanes), jnp.bfloat16)
    out = pl.pallas_call(
        fold_kernel,
        out_shape=[jax.ShapeDtypeStruct((rows // 2 + extra, lanes), jnp.bfloat16)] + [half] * 5,
        in_specs=[pl.BlockSpec(memory_space=pltpu.SMEM)] + vmem(7),
        out_specs=vmem(6),
        compiler_params=params(16),
        name="fold",
    )(bits, *kept, *got, before)
    return out[:3], out[3:]


def pack_kernel(*refs):
    kept, got, before, out = refs[0:3], refs[3:6], refs[6], refs[7]
    rows = kept[0].shape[0]
    for part in range(3):
        out[part * rows : (part + 1) * rows, :] = added(kept[part][...], got[part][:rows, :])
    out[3 * rows :, :] = added(before[rows:, :], got[0][rows:, :])


def pack(kept, got, before):
    rows, lanes = kept[0].shape
    return pl.pallas_call(
        pack_kernel,
        out_shape=jax.ShapeDtypeStruct((2 * rows + before.shape[0], lanes), jnp.bfloat16),
        in_specs=vmem(7),
        out_specs=vmem(1)[0],
        compiler_params=params(16),
        name="pack",
    )(*kept, *got, before)


def unpack_kernel(own_ref, got_ref, *out):
    rows = out[0].shape[0]
    for part in range(3):
        piece = slice(part * rows, (part + 1) * rows)
        out[part][...] = added(own_ref[piece, :], got_ref[piece, :])
    out[3][...] = own_ref[3 * rows :, :].astype(jnp.float32) + got_ref[3 * rows :, :].astype(jnp.float32)


def unpack(own, got, rows):
    lanes = own.shape[1]
    out = pl.pallas_call(
        unpack_kernel,
        out_shape=[jax.ShapeDtypeStruct((rows, lanes), jnp.bfloat16)] * 3
        + [jax.ShapeDtypeStruct((own.shape[0] - 3 * rows, lanes), jnp.float32)],
        in_specs=vmem(2),
        out_specs=vmem(4),
        compiler_params=params(16),
        name="unpack",
    )(own, got)
    return out[:3], out[3]


def join_kernel(bits_ref, *refs):
    own, got, out = refs[0:3], refs[3:6], refs[6:9]
    for part in range(3):
        span = own[part].shape[0]
        mine = bits_ref[part]
        out[part][pl.ds(pl.multiple_of(mine * span, span), span), :] = own[part][...]
        out[part][pl.ds(pl.multiple_of((1 - mine) * span, span), span), :] = got[part][...]


def join(bits, own, got):
    return pl.pallas_call(
        join_kernel,
        out_shape=[jax.ShapeDtypeStruct((p.shape[0] * 2, p.shape[1]), p.dtype) for p in own],
        in_specs=[pl.BlockSpec(memory_space=pltpu.SMEM)] + vmem(6),
        out_specs=vmem(3),
        compiler_params=params(16),
        name="join",
    )(bits, *own, *got)


def finish_kernel(bits_ref, *refs):
    own, got = refs[0:3], refs[3:6]
    results = refs[6:10]
    held, sems = refs[10:14], refs[14]
    span = own[0].shape[0]
    rows = 2 * span
    width, lanes = held[0].shape
    copies = []
    for part in range(3):
        mine = bits_ref[part]
        first = jnp.where(mine == 0, own[part][...], got[part][...])
        second = jnp.where(mine == 0, got[part][...], own[part][...])
        for base, piece in ((part * rows, first), (part * rows + span, second)):
            for index in range(3 + width // lanes):
                start = index * width if index < 3 else 3 * width + (index - 3) * lanes
                size = width if index < 3 else lanes
                low = max(start, base)
                high = min(start + size, base + span)
                if low < high:
                    values = piece[low - base : high - base, :].astype(jnp.float32)
                    if index < 3:
                        held[index][low - start : high - start, :] = values
                    else:
                        place = (index - 3) * lanes
                        held[3][low - start : high - start, place : place + lanes] = values
        for index in range(4):
            last = (index + 1) * width - 1
            if part * rows <= last < (part + 1) * rows:
                copies += start_copies([(held[index], results[index], sems.at[index])])
    for copy in copies:
        copy.wait()


def finish(bits, own, got, width):
    lanes = own[0].shape[1]
    shapes = [(width, lanes)] * 3 + [(lanes, width)]
    return pl.pallas_call(
        finish_kernel,
        out_shape=[hbm_out(shape, jnp.float32) for shape in shapes],
        in_specs=[pl.BlockSpec(memory_space=pltpu.SMEM)] + vmem(6),
        out_specs=[pl.BlockSpec(memory_space=pltpu.HBM)] * 4,
        scratch_shapes=[pltpu.VMEM(shape, jnp.float32) for shape in shapes]
        + [pltpu.SemaphoreType.DMA((4,))],
        compiler_params=params(24),
        name="finish",
    )(bits, *own, *got)


def swap_heads(rows):
    return lax.ppermute(rows, "heads", [(0, 1), (1, 0)])


def trade(rows, bit):
    count = lax.axis_size("seq")
    return lax.ppermute(rows, "seq", [(i, i ^ (1 << bit)) for i in range(count)])


def together(*groups):
    return lax.optimization_barrier(groups)


def contract_rows(left, right):
    return lax.dot_general(
        left, right, (((0,), (0,)), ((), ())), preferred_element_type=jnp.float32
    )


def on_device(
    tokens,
    gain_attn,
    w_query,
    w_key,
    w_value,
    w_out,
    bias_table,
    gain_ffn,
    w_router,
    w_inner,
    w_outer,
    routes,
    seq_lengths,
    out_grad,
):
    tok_count, width = tokens.shape
    bucket_count = bias_table.shape[0]
    experts = w_router.shape[1]
    capacity = max(2, 5 * tok_count // (4 * experts))
    senders = lax.axis_size("seq")
    bits = list(range(senders.bit_length() - 1))
    slots = experts * capacity
    half = width // 2
    own = w_query.shape[1]
    where = jnp.stack([lax.axis_index("heads"), lax.axis_index("seq")]).astype(jnp.int32)

    def exchange(rows):
        return lax.all_to_all(
            rows.reshape(senders, capacity, half), "seq", split_axis=0, concat_axis=0, tiled=True
        ).reshape(slots, half)

    def summed(keep, send):
        return (keep + swap_heads(send).astype(jnp.float32)).astype(jnp.bfloat16)

    slot_row, grad_sent = route(where, routes, out_grad, experts, capacity)
    grad_sent, tokens = together(grad_sent, tokens)
    grad_own = exchange(grad_sent)
    attn_part, normed, query_rows, key_rows, value_rows, mixed, long_probs, short_probs = attend(
        seq_lengths, tokens, gain_attn, w_query, w_key, w_value, w_out, bias_table
    )
    residual, second_sent = second_rows(
        where, tokens, attn_part, swap_heads(attn_part), gain_ffn, slot_row, slots
    )
    second_sent, grad_own = together(second_sent, grad_own)
    arrived_own = exchange(second_sent)

    inner = w_inner[0]
    outer = w_outer[0]
    grad_other = swap_heads(grad_own)
    hidden_grad = hidden_grad_of(where, grad_own, grad_other, outer)
    arrived_own, hidden_grad = together(arrived_own, hidden_grad)
    arrived_other = swap_heads(arrived_own)
    hidden, pre_grad, keep, send, logit_grad = expert(
        where, arrived_own, arrived_other, hidden_grad, inner, w_router
    )
    back_sum, hidden = together(summed(keep, send), hidden)
    back_own = exchange(back_sum)
    out_keep, out_send, router_part, slot_col = expert_out_of(
        where, hidden, arrived_own, arrived_other, logit_grad, slot_row, outer
    )
    out_sum = summed(out_keep, out_send)
    router_half = lax.dynamic_slice_in_dim(
        router_part + swap_heads(router_part), where[0] * (experts // 2), experts // 2, 0
    )
    back_own, out_sum, router_half = together(back_own, out_sum, router_half)
    back_other = swap_heads(back_own)
    returned = exchange(out_sum)

    depth = len(bits) - 1
    turns = [bits[k * depth // 3 : depth] + bits[: k * depth // 3] for k in range(3)]
    place = lax.axis_index("seq")
    mine = [jnp.stack([(place >> turn[k]) & 1 for turn in turns]).astype(jnp.int32) for k in range(depth)]
    residual_grad, head_grads, sent, kept = back_pass(
        mine[0], where, slot_col, back_own, back_other, residual, out_grad, w_out, query_rows, key_rows,
        value_rows, mixed, long_probs, short_probs, normed, w_query, w_key, w_value, gain_attn, gain_ffn,
        router_half,
    )

    def trades(arrays, k):
        return [trade(array, turn[k]) for array, turn in zip(arrays, turns)]

    for k in range(depth):
        got = trades(sent, k)
        if k == 0:
            output = output_of(where, slot_col, returned, residual, gain_ffn, w_router, capacity)
            got, output, head_grads = together(got, output, head_grads)
        if k == 1:
            normed_part = normed_back(head_grads, w_query, w_key, w_value)
            got, normed_part = together(got, normed_part)
        if k + 1 < depth:
            sent, kept = fold(mine[k + 1], kept, got, sent[0])
    normed_other = swap_heads(normed_part)
    packed = pack(kept, got, sent[0])
    packed, normed_other, pre_grad = together(packed, normed_other, pre_grad)
    got = trade(packed, bits[-1])
    inner_grad, outer_grad = expert_grads(
        where, arrived_own, arrived_other, grad_own, grad_other, hidden, pre_grad, w_router
    )
    got, inner_grad = together(got, inner_grad)
    summed_parts, small = unpack(packed, got, kept[0].shape[0])
    small = jnp.concatenate([small[: small.shape[0] // 2], small[small.shape[0] // 2 :]], axis=1)
    small_other = swap_heads(small)
    for k in reversed(range(1, depth)):
        got = trades(summed_parts, k)
        if k == depth - 1:
            got, small = together(got, small)
        if k == 1:
            lower = where[0] == 0
            own_rows, other_rows = small[: experts // 2], small_other[: experts // 2]
            router_grad = jnp.concatenate(
                [jnp.where(lower, own_rows, other_rows), jnp.where(lower, other_rows, own_rows)], axis=0
            ).T
            gain_one_grad = small[experts // 2] + small_other[experts // 2]
            gain_two_grad = small[experts // 2 + 1]
            table_grad = table_from(small[experts // 2 + 2 :], bucket_count)
            got, gain_one_grad, gain_two_grad, router_grad, table_grad = together(
                got, gain_one_grad, gain_two_grad, router_grad, table_grad
            )
        summed_parts = join(mine[k], summed_parts, got)
    got = trades(summed_parts, 0)
    input_grad = input_back(tokens, normed_part, normed_other, gain_attn, residual_grad)
    got, input_grad = together(got, input_grad)
    query_w_grad, key_w_grad, value_w_grad, out_w_grad = finish(mine[0], summed_parts, got, width)
    return (
        output,
        input_grad,
        gain_one_grad,
        query_w_grad,
        key_w_grad,
        value_w_grad,
        out_w_grad,
        table_grad,
        gain_two_grad,
        router_grad,
        inner_grad[None],
        outer_grad[None],
    )


def solution(mesh):
    in_specs = (
        P("seq", None),
        P(),
        P(None, "heads"),
        P(None, "heads"),
        P(None, "heads"),
        P("heads", None),
        P(None, "heads"),
        P(),
        P(),
        P("seq", None, "heads"),
        P("seq", "heads", None),
        P("seq", None),
        P("seq"),
        P("seq", None),
    )
    out_specs = (
        P("seq", "heads"),
        P("seq", None),
        P(),
        P(None, "heads"),
        P(None, "heads"),
        P(None, "heads"),
        P("heads", None),
        P(None, "heads"),
        P(),
        P(),
        P("seq", None, "heads"),
        P("seq", "heads", None),
    )
    return jax.shard_map(
        on_device, mesh=mesh, in_specs=in_specs, out_specs=out_specs, check_vma=False
    )
```
